32 devices in a mesh: role: 4 (over y, core), seq: 2 (over x), mp: 4 (over z).
Axes of the slice: x: 2, y: 2, z: 4, core: 2. Of those that a mesh axis runs over, the one named last changes fastest.
Arguments:
- gen_heads: bfloat16 [128, 4096], P(None, 'seq'), may hold values from -6 to 6
- gen_resid: bfloat16 [128, 5120], P('seq', 'mp'), may hold values from -6 to 6
- gen_out_w: bfloat16 [4096, 5120], P('seq', 'mp'), may hold values from -0.09375 to 0.09375
- gen_time_w: bfloat16 [256, 5120], P(None, 'mp'), may hold values from -0.375 to 0.375
- noise: bfloat16 [128, 5120], P('seq', 'mp'), may hold values from -6 to 6
- steps: int32 [3], replicated, may hold values from 20 to 979
- teacher_qkv: bfloat16 [5120, 3, 4096], P('mp', None, 'seq'), may hold values from -0.078125 to 0.078125
- teacher_out: bfloat16 [4096, 5120], P('seq', 'mp'), may hold values from -0.09375 to 0.09375
- teacher_time: bfloat16 [256, 3, 5120], P(None, None, 'mp'), may hold values from -0.375 to 0.375
- teacher_norm: float32 [2, 4096], P(None, 'seq'), may hold values from 0.5 to 1.5
- critic_qkv: bfloat16 [5120, 3, 4096], P('mp', None, 'seq'), may hold values from -0.078125 to 0.078125
- critic_out: bfloat16 [4096, 5120], P('seq', 'mp'), may hold values from -0.09375 to 0.09375
- critic_time: bfloat16 [256, 3, 5120], P(None, None, 'mp'), may hold values from -0.375 to 0.375
- critic_norm: float32 [2, 4096], P(None, 'seq'), may hold values from 0.5 to 1.5
Outputs:
- latent: bfloat16 [128, 5120], P('seq', 'mp')
- weight_grad: bfloat16 [4096, 5120], P('seq', 'mp')
The draws below stay inside these ranges and needn't reach their ends.
All inputs are finite; a program needn't handle non-finite values.
Results may differ from the reference program's by a relative error of at most 0.012.
Values may be sent and summed in bfloat16 or wider, within the bound.
No kernel may reach another device: no remote copies, remote signals or barrier semaphores. Data moves between devices by JAX's collectives and lax.ppermute only.
A program may use at most 128 MiB of HBM per device.

```python
import math
import jax
import jax.numpy as jnp
from jax import lax

D = 5120
HEAD_DIM = 128
FREQ = 256
HEADS = 32
LENGTH = 128


def shard_levels(own_key, shape, cuts, low, largest):
    factor_of = 1.0
    for position, parts in cuts:
        heights = jax.random.uniform(jax.random.fold_in(jax.random.fold_in(own_key, 6), position), (parts,), jnp.float32, low / len(cuts), largest / len(cuts))
        factor_of = factor_of * jnp.repeat(jnp.exp(heights), shape[position] // parts).reshape((-1,) + (1,) * (len(shape) - 1 - position))
    return factor_of


def normal_values(rng, dims, spread, most, split=(), held_as=jnp.bfloat16):
    result = spread * jax.random.normal(rng, dims, jnp.float32)
    if split:
        result = result * shard_levels(rng, dims, split, -0.22, 0.18)
    return jnp.clip(result, -most, most).astype(held_as)


def setup_inputs(seed: int = 0) -> dict:
    seeds = jax.random.split(jax.random.key(seed), 15)
    gen_heads = normal_values(seeds[0], (LENGTH, HEADS * HEAD_DIM), 1.0, 6.0, ((1, 2),))
    gen_resid = normal_values(seeds[1], (LENGTH, D), 1.0, 6.0, ((0, 2), (1, 4)))
    gen_out_w = normal_values(seeds[2], (HEADS * HEAD_DIM, D), (HEADS * HEAD_DIM) ** -0.5, 0.09375, ((0, 2), (1, 4)))
    gen_time_w = normal_values(seeds[3], (FREQ, D), FREQ ** -0.5, 0.375, ((1, 4),))
    noise = normal_values(seeds[4], (LENGTH, D), 1.0, 6.0, ((0, 2), (1, 4)))
    steps = jax.random.randint(seeds[5], (3,), 20, 980).astype(jnp.int32)
    teacher_qkv = normal_values(seeds[6], (D, 3, HEADS * HEAD_DIM), D ** -0.5, 0.078125, ((0, 4), (2, 2)))
    teacher_out = normal_values(seeds[7], (HEADS * HEAD_DIM, D), (HEADS * HEAD_DIM) ** -0.5, 0.09375, ((0, 2), (1, 4)))
    teacher_time = normal_values(seeds[8], (FREQ, 3, D), FREQ ** -0.5, 0.375, ((2, 4),))
    teacher_norm = jnp.clip(1.0 + 0.1 * jax.random.normal(seeds[9], (2, HEADS * HEAD_DIM), jnp.float32), 0.5, 1.5)
    critic_qkv = normal_values(seeds[10], (D, 3, HEADS * HEAD_DIM), D ** -0.5, 0.078125, ((0, 4), (2, 2)))
    critic_out = normal_values(seeds[11], (HEADS * HEAD_DIM, D), (HEADS * HEAD_DIM) ** -0.5, 0.09375, ((0, 2), (1, 4)))
    critic_time = normal_values(seeds[12], (FREQ, 3, D), FREQ ** -0.5, 0.375, ((2, 4),))
    critic_norm = jnp.clip(1.0 + 0.1 * jax.random.normal(seeds[13], (2, HEADS * HEAD_DIM), jnp.float32), 0.5, 1.5)
    return {"gen_heads": gen_heads, "gen_resid": gen_resid, "gen_out_w": gen_out_w, "gen_time_w": gen_time_w, "noise": noise, "steps": steps, "teacher_qkv": teacher_qkv, "teacher_out": teacher_out, "teacher_time": teacher_time, "teacher_norm": teacher_norm, "critic_qkv": critic_qkv, "critic_out": critic_out, "critic_time": critic_time, "critic_norm": critic_norm}


def time_embed(step_value):
    half_width = FREQ // 2
    positions = jnp.arange(half_width, dtype=jnp.float32)
    frequencies = jnp.exp(positions * (-math.log(10000.0) / half_width))
    angles = step_value.astype(jnp.float32) * frequencies
    return jnp.concatenate([jnp.cos(angles), jnp.sin(angles)]).astype(jnp.bfloat16)

def head_norm(values, gains):
    factor = lax.rsqrt(lax.optimization_barrier(jnp.mean(values * values, axis=-1, keepdims=True)) + 1e-06)
    return (values * factor * gains).astype(jnp.bfloat16)

def one_head(operands):
    query_head, key_head, value_head = operands
    logits = jnp.dot(query_head, key_head.T, preferred_element_type=jnp.float32) * (1.0 / math.sqrt(HEAD_DIM))
    expanded = jnp.exp(logits)
    probs = (expanded / lax.optimization_barrier(jnp.sum(expanded, axis=1, keepdims=True))).astype(jnp.bfloat16)
    return jnp.dot(probs, value_head, preferred_element_type=jnp.float32).astype(jnp.bfloat16)

def score_pass(latent, noise, level, w_qkv, w_out, w_time, w_norm):
    noise_level = level.astype(jnp.float32) / 1000.0
    noisy = ((1.0 - noise_level) * latent.astype(jnp.float32) + noise_level * noise.astype(jnp.float32)).astype(jnp.bfloat16)
    modulation = jnp.einsum('f,fkd->kd', time_embed(level).astype(jnp.float32), w_time.astype(jnp.float32))
    shift_vec = modulation[0]
    scale_vec = modulation[1]
    gate_vec = modulation[2]
    mean_square = lax.optimization_barrier(jnp.mean(jnp.square(noisy.astype(jnp.float32)), axis=1))
    scaled = (noisy.astype(jnp.float32) * (1.0 + scale_vec)).astype(jnp.bfloat16)
    flat_w = w_qkv.reshape(D, 3 * HEADS * HEAD_DIM)
    projected = jnp.dot(scaled, flat_w, preferred_element_type=jnp.float32)
    shift_proj = jnp.dot(shift_vec.astype(jnp.bfloat16)[None, :], flat_w, preferred_element_type=jnp.float32)[0]
    mixed = projected * lax.rsqrt(mean_square + 1e-06)[:, None] + shift_proj
    mixed = mixed.reshape(LENGTH, 3, HEADS, HEAD_DIM)
    gains = w_norm.reshape(2, HEADS, HEAD_DIM)
    query_norm = head_norm(mixed[:, 0], gains[0])
    key_norm = head_norm(mixed[:, 1], gains[1])
    value_rows = mixed[:, 2].astype(jnp.bfloat16)
    head_out = lax.map(one_head, (query_norm.transpose(1, 0, 2), key_norm.transpose(1, 0, 2), value_rows.transpose(1, 0, 2)))
    head_out = head_out.transpose(1, 0, 2).reshape(LENGTH, HEADS * HEAD_DIM)
    return gate_vec * jnp.dot(head_out, w_out, preferred_element_type=jnp.float32)

def reference(gen_heads, gen_resid, gen_out_w, gen_time_w, noise, steps, teacher_qkv, teacher_out, teacher_time, teacher_norm, critic_qkv, critic_out, critic_time, critic_norm):
    gen_gate = jnp.dot(time_embed(steps[0])[None, :], gen_time_w, preferred_element_type=jnp.float32)[0]
    gen_proj = jnp.dot(gen_heads, gen_out_w, preferred_element_type=jnp.float32)
    latent = (gen_resid.astype(jnp.float32) + gen_gate * gen_proj).astype(jnp.bfloat16)
    total = jnp.zeros((LENGTH, D), jnp.float32)
    for pass_index in range(4):
        level = steps[1 + pass_index // 2]
        if pass_index % 2 == 1:
            predicted = score_pass(latent, noise, level, critic_qkv, critic_out, critic_time, critic_norm)
            total = total + 0.5 * predicted
        else:
            predicted = score_pass(latent, noise, level, teacher_qkv, teacher_out, teacher_time, teacher_norm)
            total = total - 0.5 * predicted
    grad_rows = (gen_gate * total).astype(jnp.bfloat16)
    weight_grad = jnp.dot(gen_heads.T, grad_rows, preferred_element_type=jnp.float32)
    return (latent, weight_grad.astype(jnp.bfloat16))
```

```python
import math

import jax
import jax.numpy as jnp
from jax import lax
from jax.experimental import pallas as pl
from jax.experimental.pallas import tpu as pltpu
from jax.sharding import PartitionSpec as P

D = 5120
HEAD_DIM = 128


def time_embed(step_value, width):
    half_width = width // 2
    positions = jnp.arange(half_width, dtype=jnp.float32)
    frequencies = jnp.exp(positions * (-math.log(10000.0) / half_width))
    angles = step_value.astype(jnp.float32) * frequencies
    return jnp.concatenate([jnp.cos(angles), jnp.sin(angles)]).astype(jnp.bfloat16)


def head_norm(values, gains):
    factor = lax.rsqrt(jnp.mean(values * values, axis=-1, keepdims=True) + 1e-06)
    return (values * factor * gains).astype(jnp.bfloat16)


def attend(query_norm, key_norm, value_rows):
    full_length, heads_here, head_width = query_norm.shape
    query_blocks = query_norm.reshape(
        full_length // full_length, full_length, heads_here, head_width
    )

    def one_block(query_block):
        logits = jnp.einsum(
            "qhd,khd->hqk", query_block, key_norm, preferred_element_type=jnp.float32
        ) * (1.0 / math.sqrt(head_width))
        expanded = jnp.exp(logits)
        probs = (expanded / jnp.sum(expanded, axis=2, keepdims=True)).astype(jnp.bfloat16)
        return jnp.einsum(
            "hqk,khd->qhd", probs, value_rows, preferred_element_type=jnp.float32
        ).astype(jnp.bfloat16)

    head_out = lax.map(one_block, query_blocks)
    return head_out.reshape(full_length, heads_here * head_width)


def pass_per_role(
    gen_heads,
    gen_resid,
    gen_out_w,
    gen_time_w,
    noise,
    steps,
    teacher_qkv,
    teacher_out,
    teacher_time,
    teacher_norm,
    critic_qkv,
    critic_out,
    critic_time,
    critic_norm,
):
    full_length = gen_heads.shape[0]
    head_cols = gen_heads.shape[1]
    embed_width = gen_time_w.shape[0]
    gen_gate = jnp.dot(
        time_embed(steps[0], embed_width)[None, :], gen_time_w, preferred_element_type=jnp.float32
    )[0]
    block = gen_heads
    gen_proj = lax.psum_scatter(
        jnp.dot(block, gen_out_w, preferred_element_type=jnp.float32),
        "seq",
        scatter_dimension=0,
        tiled=True,
    )
    latent = (gen_resid.astype(jnp.float32) + gen_gate * gen_proj).astype(jnp.bfloat16)
    role_index = lax.axis_index("role")
    level = steps[1 + role_index // 2]
    use_critic = role_index % 2 == 1
    w_qkv = jnp.where(use_critic, critic_qkv, teacher_qkv)
    w_out = jnp.where(use_critic, critic_out, teacher_out)
    w_time = jnp.where(use_critic, critic_time, teacher_time)
    w_norm = jnp.where(use_critic, critic_norm, teacher_norm)
    noise_level = level.astype(jnp.float32) / 1000.0
    noisy = (
        (1.0 - noise_level) * latent.astype(jnp.float32) + noise_level * noise.astype(jnp.float32)
    ).astype(jnp.bfloat16)
    modulation = jnp.einsum(
        "f,fkd->kd", time_embed(level, embed_width), w_time, preferred_element_type=jnp.float32
    )
    shift_vec = modulation[0]
    scale_vec = modulation[1]
    gate_vec = modulation[2]
    gathered = lax.all_gather(noisy, "seq", axis=0, tiled=True)
    partial_squares = jnp.sum(jnp.square(gathered.astype(jnp.float32)), axis=1)
    scaled = (gathered.astype(jnp.float32) * (1.0 + scale_vec)).astype(jnp.bfloat16)
    flat_w = w_qkv.reshape(w_qkv.shape[0], 3 * head_cols)
    projected = jnp.dot(scaled, flat_w, preferred_element_type=jnp.float32)
    shift_proj = jnp.dot(
        shift_vec.astype(jnp.bfloat16)[None, :], flat_w, preferred_element_type=jnp.float32
    )[0]
    projected, squares, shift_proj = lax.psum((projected, partial_squares, shift_proj), "mp")
    mixed = projected * lax.rsqrt(squares / D + 1e-06)[:, None] + shift_proj
    heads_here = head_cols // HEAD_DIM
    mixed = mixed.reshape(full_length, 3, heads_here, HEAD_DIM)
    gains = w_norm.reshape(2, heads_here, HEAD_DIM)
    query_norm = head_norm(mixed[:, 0], gains[0])
    key_norm = head_norm(mixed[:, 1], gains[1])
    value_rows = mixed[:, 2].astype(jnp.bfloat16)
    head_out = attend(query_norm, key_norm, value_rows)
    weight_sign = jnp.where(use_critic, 0.5, -0.5)
    block = head_out
    summed_rows = lax.psum_scatter(
        weight_sign * (gate_vec * jnp.dot(block, w_out, preferred_element_type=jnp.float32)),
        ("role", "seq"),
        scatter_dimension=0,
        tiled=True,
    )
    grad_rows = lax.all_gather(
        (gen_gate * summed_rows).astype(jnp.bfloat16), ("role", "seq"), axis=0, tiled=True
    )
    weight_grad = lax.dot_general(
        gen_heads, grad_rows, (((0,), (0,)), ((), ())), preferred_element_type=jnp.float32
    )
    return (latent, weight_grad.astype(jnp.bfloat16))

VMEM_LIMIT = 40 * 1024 * 1024
EXTRA_ROWS = 16


def vmem_spec():
    return pl.BlockSpec(memory_space=pltpu.VMEM)


def smem_spec():
    return pl.BlockSpec(memory_space=pltpu.SMEM)


def params(limit=VMEM_LIMIT):
    return pltpu.CompilerParams(vmem_limit_bytes=limit)


def dot32(a, b):
    return jnp.dot(a, b, preferred_element_type=jnp.float32)


def gen_kernel(where, heads, weight, time_w, embed, resid, full, sent, gate):
    rows = resid.shape[0]
    gate_rows = dot32(embed[...], time_w[...])
    gate[...] = gate_rows
    full[...] = gate_rows[0:1] * dot32(heads[...], weight[...])
    at = pl.ds(pl.multiple_of(where[0] * rows, rows), rows)
    full[at, :] = full[at, :] + resid[...].astype(jnp.float32)
    sent[...] = full[...].astype(jnp.bfloat16)


def gen_part(where, heads, weight, time_w, embed, resid, tile):
    length, depth = heads.shape
    width = weight.shape[1]
    freq = time_w.shape[0]
    grid_spec = pltpu.PrefetchScalarGridSpec(
        num_scalar_prefetch=1,
        grid=(width // tile,),
        in_specs=[
            pl.BlockSpec((length, depth), lambda n, w: (0, 0)),
            pl.BlockSpec((depth, tile), lambda n, w: (0, n)),
            pl.BlockSpec((freq, tile), lambda n, w: (0, n)),
            pl.BlockSpec((8, freq), lambda n, w: (0, 0)),
            pl.BlockSpec((resid.shape[0], tile), lambda n, w: (0, n)),
        ],
        out_specs=[
            pl.BlockSpec((length, tile), lambda n, w: (0, n)),
            pl.BlockSpec((length, tile), lambda n, w: (0, n)),
            pl.BlockSpec((8, tile), lambda n, w: (0, n)),
        ],
    )
    return pl.pallas_call(
        gen_kernel,
        grid_spec=grid_spec,
        out_shape=[
            jax.ShapeDtypeStruct((length, width), jnp.float32),
            jax.ShapeDtypeStruct((length, width), jnp.bfloat16),
            jax.ShapeDtypeStruct((8, width), jnp.float32),
        ],
        compiler_params=params(),
        name="gen_part",
    )(where, heads, weight, time_w, embed, resid)


def mod_kernel(embed, time_a, time_b, mods):
    for k in range(3):
        mods[0, k] = dot32(embed[...], time_a[k])
        mods[1, k] = dot32(embed[...], time_b[k])


def mod_part(embed, time_a, time_b):
    width = time_a.shape[2]
    return pl.pallas_call(
        mod_kernel,
        in_specs=[vmem_spec()] * 3,
        out_specs=vmem_spec(),
        out_shape=jax.ShapeDtypeStruct((2, 3, 8, width), jnp.float32),
        compiler_params=params(24 * 1024 * 1024),
        name="mod_part",
    )(embed, time_a, time_b)


def qkv_kernel(where, levels, full, other, noise, mods, weight_a, weight_b, latent, sent, noisy):
    length = full.shape[0]
    own = latent.shape[0]
    groups, _, _, cols = sent.shape
    unit = cols // 3
    tokens = 2 * length
    values = (full[...] + other[...].astype(jnp.float32)).astype(jnp.bfloat16)
    spread = values.astype(jnp.float32)
    noise_rows = noise[...].astype(jnp.float32)
    for level in range(2):
        share = levels[level]
        noisy[pl.ds(level * length, length), :] = (1.0 - share) * spread + share * noise_rows
    at = pl.ds(pl.multiple_of(where[0] * own, own), own)
    latent[...] = (full[at, :] + other[at, :].astype(jnp.float32)).astype(jnp.bfloat16)
    mixed = noisy[...].astype(jnp.bfloat16).astype(jnp.float32)
    squares = jnp.sum(mixed * mixed, axis=1, keepdims=True)
    squares = jnp.broadcast_to(squares, (tokens, unit)).T[0:1]
    squares = jnp.concatenate([squares, jnp.zeros((1, cols - tokens), jnp.float32)], axis=1)
    row_id = lax.broadcasted_iota(jnp.int32, (EXTRA_ROWS, cols), 0)
    for index, weight in enumerate((weight_a, weight_b)):
        scale = mods[index, 1]
        shift = mods[index, 0]
        top = mixed[:length] * (1.0 + scale[1:2])
        low = mixed[length:] * (1.0 + scale[2:3])
        extra = jnp.concatenate([shift[1:3], jnp.zeros((EXTRA_ROWS - 2, shift.shape[1]), jnp.float32)], axis=0)
        rows = jnp.concatenate([top, low, extra], axis=0).astype(jnp.bfloat16)
        for part in range(3):
            result = dot32(rows, weight[part])
            for group in range(groups):
                piece = result[:, group * unit : (group + 1) * unit]
                at_cols = pl.ds(part * unit, unit)
                sent[group, index, pl.ds(0, tokens), at_cols] = piece[:tokens].astype(jnp.bfloat16)
                ids = row_id[:, :unit]
                tail = jnp.where(ids == 2, squares[:, part * unit : (part + 1) * unit], piece[tokens:])
                sent[group, index, pl.ds(tokens, EXTRA_ROWS), at_cols] = tail.astype(jnp.bfloat16)


def qkv_part(where, levels, full, other, noise, mods, weight_a, weight_b, own, groups):
    length, width = full.shape
    cols = 3 * weight_a.shape[2] // groups
    return pl.pallas_call(
        qkv_kernel,
        in_specs=[smem_spec(), smem_spec()] + [vmem_spec()] * 6,
        out_specs=[vmem_spec()] * 2,
        out_shape=[
            jax.ShapeDtypeStruct((own, width), jnp.bfloat16),
            jax.ShapeDtypeStruct((groups, 2, 2 * length + EXTRA_ROWS, cols), jnp.bfloat16),
        ],
        scratch_shapes=[pltpu.VMEM((2 * length, width), jnp.float32)],
        compiler_params=params(),
        name="qkv_part",
    )(where, levels, full, other, noise, mods, weight_a, weight_b)


def attend_kernel(width, mixed, gains, out):
    unit = out.shape[3]
    length = out.shape[2]
    tokens = 2 * length
    for index in range(2):
        extra = mixed[index, pl.ds(tokens, EXTRA_ROWS), :].astype(jnp.float32)
        squares = jnp.broadcast_to(extra[2:3, :tokens], (unit, tokens)).T
        factor = lax.rsqrt(squares * (1.0 / width) + 1e-06)
        for level in range(2):
            at = pl.ds(level * length, length)
            scale = factor[level * length : (level + 1) * length]

            def pick(part):
                piece = mixed[index, at, pl.ds(part * unit, unit)].astype(jnp.float32)
                shift = extra[level : level + 1, part * unit : (part + 1) * unit]
                return piece * scale + shift

            def normed(part):
                rows = pick(part)
                mean = jnp.mean(rows * rows, axis=1, keepdims=True)
                return (rows * lax.rsqrt(mean + 1e-06) * gains[index, part : part + 1, :]).astype(jnp.bfloat16)

            query, key = normed(0), normed(1)
            value = pick(2).astype(jnp.bfloat16)
            logits = lax.dot_general(
                query, key, (((1,), (1,)), ((), ())), preferred_element_type=jnp.float32
            ) * (1.0 / math.sqrt(unit))
            expanded = jnp.exp(logits)
            probs = (expanded / jnp.sum(expanded, axis=1, keepdims=True)).astype(jnp.bfloat16)
            out[index, level] = dot32(probs, value).astype(jnp.bfloat16)


def attend_part(mixed, gains, width, length):
    unit = mixed.shape[2] // 3
    return pl.pallas_call(
        lambda *refs: attend_kernel(width, *refs),
        in_specs=[vmem_spec()] * 2,
        out_specs=vmem_spec(),
        out_shape=jax.ShapeDtypeStruct((2, 2, length, unit), jnp.bfloat16),
        compiler_params=params(16 * 1024 * 1024),
        name="attend_part",
    )(mixed, gains)


def out_kernel(place, heads, weight_a, weight_b, mods, kept, sent, total):
    groups, _, _, length, unit = heads.shape
    count = sent.shape[0] + 1
    block = kept.shape[0]
    for index, weight in enumerate((weight_a, weight_b)):
        rows = jnp.concatenate(
            [jnp.concatenate([heads[g, index, level] for g in range(groups)], axis=1) for level in range(2)], axis=0
        )
        result = dot32(rows, weight[...])
        gates = mods[index, 2]
        signed = gates[1:2] * result[:length] + gates[2:3] * result[length:]
        if index == 0:
            total[...] = -0.5 * signed
        else:
            total[...] = total[...] + 0.5 * signed
    for hop in range(count):
        other = jnp.bitwise_xor(place[0], hop)
        rows = total[pl.ds(pl.multiple_of(other * block, block), block), :]
        if hop == 0:
            kept[...] = rows
        else:
            sent[hop - 1] = rows.astype(jnp.bfloat16)


def out_part(place, heads, weight_a, weight_b, mods, count):
    length = heads.shape[3]
    width = weight_a.shape[1]
    block = length // count
    return pl.pallas_call(
        out_kernel,
        in_specs=[smem_spec()] + [vmem_spec()] * 4,
        out_specs=[vmem_spec()] * 2,
        out_shape=[
            jax.ShapeDtypeStruct((block, width), jnp.float32),
            jax.ShapeDtypeStruct((count - 1, block, width), jnp.bfloat16),
        ],
        scratch_shapes=[pltpu.VMEM((length, width), jnp.float32)],
        compiler_params=params(24 * 1024 * 1024),
        name="out_part",
    )(place, heads, weight_a, weight_b, mods)


def grad_kernel(place, heads_t, *refs):
    blocks, out, rows = refs[:-2], refs[-2], refs[-1]
    block = blocks[0].shape[0]

    @pl.when(pl.program_id(0) == 0)
    def _():
        for hop, piece in enumerate(blocks):
            other = jnp.bitwise_xor(place[0], hop)
            rows[pl.ds(pl.multiple_of(other * block, block), block), :] = piece[...]

    out[...] = dot32(heads_t[...], rows[...]).astype(jnp.bfloat16)


def grad_part(place, heads_t, blocks, tile):
    depth, length = heads_t.shape
    block, width = blocks[0].shape
    grid_spec = pltpu.PrefetchScalarGridSpec(
        num_scalar_prefetch=1,
        grid=(depth // tile,),
        in_specs=[pl.BlockSpec((tile, length), lambda n, w: (n, 0))]
        + [pl.BlockSpec((block, width), lambda n, w: (0, 0))] * len(blocks),
        out_specs=pl.BlockSpec((tile, width), lambda n, w: (n, 0)),
        scratch_shapes=[pltpu.VMEM((length, width), jnp.bfloat16)],
    )
    return pl.pallas_call(
        grad_kernel,
        grid_spec=grid_spec,
        out_shape=jax.ShapeDtypeStruct((depth, width), jnp.bfloat16),
        compiler_params=params(24 * 1024 * 1024),
        name="grad_part",
    )(place, heads_t, *blocks)


def heads_per_role(
    gen_heads,
    gen_resid,
    gen_out_w,
    gen_time_w,
    noise,
    steps,
    teacher_qkv,
    teacher_out,
    teacher_time,
    teacher_norm,
    critic_qkv,
    critic_out,
    critic_time,
    critic_norm,
):
    length = gen_heads.shape[0]
    own = gen_resid.shape[0]
    roles, seqs, groups = lax.axis_size("role"), lax.axis_size("seq"), lax.axis_size("mp")
    role, seq, mp = lax.axis_index("role"), lax.axis_index("seq"), lax.axis_index("mp")
    head_cols = gen_heads.shape[1]
    part_cols = head_cols // roles
    width = D
    freq = gen_time_w.shape[0]
    seq_at = seq.astype(jnp.int32).reshape(1)
    place = (role * seqs + seq).astype(jnp.int32).reshape(1)
    count = roles * seqs

    swap = [(i, 1 - i) for i in range(seqs)]
    noise_other = lax.ppermute(noise, "seq", swap)
    first = jnp.where(seq == 0, noise, noise_other)
    second = jnp.where(seq == 0, noise_other, noise)
    noise_full = jnp.concatenate([first, second], axis=0)

    embed = jax.vmap(lambda t: time_embed(t, freq))(steps)
    embed = jnp.concatenate([embed, jnp.zeros((5, freq), jnp.bfloat16)], axis=0)
    levels = steps[1:3].astype(jnp.float32) / 1000.0
    full, sent, gate = gen_part(seq_at, gen_heads, gen_out_w, gen_time_w, embed, gen_resid, 256)
    other = lax.ppermute(sent, "seq", swap)

    start = role * part_cols
    weight_a = lax.dynamic_slice_in_dim(teacher_qkv.transpose(1, 0, 2), start, part_cols, axis=2)
    weight_b = lax.dynamic_slice_in_dim(critic_qkv.transpose(1, 0, 2), start, part_cols, axis=2)
    mods = mod_part(embed, teacher_time.transpose(1, 0, 2), critic_time.transpose(1, 0, 2))
    latent, partial = qkv_part(seq_at, levels, full, other, noise_full, mods, weight_a, weight_b, own, groups)

    mixed = lax.psum_scatter(partial, "mp", scatter_dimension=0, tiled=True)[0]
    out_a = lax.dynamic_slice_in_dim(teacher_out, start, part_cols, axis=0)
    out_b = lax.dynamic_slice_in_dim(critic_out, start, part_cols, axis=0)
    unit = part_cols // groups
    gains = jnp.stack([teacher_norm, critic_norm])
    gains = lax.dynamic_slice_in_dim(gains, start + mp * unit, unit, axis=2)
    head_out = attend_part(mixed, gains, width, length)
    heads_all = lax.all_gather(head_out, "mp", axis=0)
    kept, parts = out_part(place, heads_all, out_a, out_b, mods, count)
    axes = ("role", "seq")
    total = kept
    for hop in range(1, count):
        arrived = lax.ppermute(parts[hop - 1], axes, [(i, i ^ hop) for i in range(count)])
        total = total + arrived.astype(jnp.float32)
    rows = (gate[0:1] * total).astype(jnp.bfloat16)
    blocks = [rows]
    for hop in range(1, count):
        blocks.append(lax.ppermute(rows, axes, [(i, i ^ hop) for i in range(count)]))
    weight_grad = grad_part(place, gen_heads.T, blocks, head_cols // 8)
    return latent, weight_grad


def solution(mesh):
    in_specs = (
        P(None, "seq"),
        P("seq", "mp"),
        P("seq", "mp"),
        P(None, "mp"),
        P("seq", "mp"),
        P(),
        P("mp", None, "seq"),
        P("seq", "mp"),
        P(None, None, "mp"),
        P(None, "seq"),
        P("mp", None, "seq"),
        P("seq", "mp"),
        P(None, None, "mp"),
        P(None, "seq"),
    )
    out_specs = (P("seq", "mp"), P("seq", "mp"))
    roles, seqs, groups = mesh.shape["role"], mesh.shape["seq"], mesh.shape["mp"]

    def on_device(*arrays):
        heads_here = arrays[0].shape[1] // HEAD_DIM
        length = arrays[0].shape[0]
        count = roles * seqs
        fits = (
            seqs == 2
            and heads_here == roles * groups
            and count & (count - 1) == 0
            and length == HEAD_DIM
            and length % (16 * count) == 0
        )
        return heads_per_role(*arrays) if fits else pass_per_role(*arrays)

    return jax.shard_map(
        on_device, mesh=mesh, in_specs=in_specs, out_specs=out_specs, check_vma=False
    )
```

```python
import math

import jax
import jax.numpy as jnp
from jax import lax
from jax.experimental import pallas as pl
from jax.experimental.pallas import tpu as pltpu
from jax.sharding import PartitionSpec as P

D = 5120
HEAD_DIM = 128


def time_embed(step_value, width):
    half_width = width // 2
    positions = jnp.arange(half_width, dtype=jnp.float32)
    frequencies = jnp.exp(positions * (-math.log(10000.0) / half_width))
    angles = step_value.astype(jnp.float32) * frequencies
    return jnp.concatenate([jnp.cos(angles), jnp.sin(angles)]).astype(jnp.bfloat16)


def head_norm(values, gains):
    factor = lax.rsqrt(jnp.mean(values * values, axis=-1, keepdims=True) + 1e-06)
    return (values * factor * gains).astype(jnp.bfloat16)


def attend(query_norm, key_norm, value_rows):
    full_length, heads_here, head_width = query_norm.shape
    query_blocks = query_norm.reshape(
        full_length // full_length, full_length, heads_here, head_width
    )

    def one_block(query_block):
        logits = jnp.einsum(
            "qhd,khd->hqk", query_block, key_norm, preferred_element_type=jnp.float32
        ) * (1.0 / math.sqrt(head_width))
        expanded = jnp.exp(logits)
        probs = (expanded / jnp.sum(expanded, axis=2, keepdims=True)).astype(jnp.bfloat16)
        return jnp.einsum(
            "hqk,khd->qhd", probs, value_rows, preferred_element_type=jnp.float32
        ).astype(jnp.bfloat16)

    head_out = lax.map(one_block, query_blocks)
    return head_out.reshape(full_length, heads_here * head_width)


def pass_per_role(
    gen_heads,
    gen_resid,
    gen_out_w,
    gen_time_w,
    noise,
    steps,
    teacher_qkv,
    teacher_out,
    teacher_time,
    teacher_norm,
    critic_qkv,
    critic_out,
    critic_time,
    critic_norm,
):
    full_length = gen_heads.shape[0]
    head_cols = gen_heads.shape[1]
    embed_width = gen_time_w.shape[0]
    gen_gate = jnp.dot(
        time_embed(steps[0], embed_width)[None, :], gen_time_w, preferred_element_type=jnp.float32
    )[0]
    block = gen_heads
    gen_proj = lax.psum_scatter(
        jnp.dot(block, gen_out_w, preferred_element_type=jnp.float32),
        "seq",
        scatter_dimension=0,
        tiled=True,
    )
    latent = (gen_resid.astype(jnp.float32) + gen_gate * gen_proj).astype(jnp.bfloat16)
    role_index = lax.axis_index("role")
    level = steps[1 + role_index // 2]
    use_critic = role_index % 2 == 1
    w_qkv = jnp.where(use_critic, critic_qkv, teacher_qkv)
    w_out = jnp.where(use_critic, critic_out, teacher_out)
    w_time = jnp.where(use_critic, critic_time, teacher_time)
    w_norm = jnp.where(use_critic, critic_norm, teacher_norm)
    noise_level = level.astype(jnp.float32) / 1000.0
    noisy = (
        (1.0 - noise_level) * latent.astype(jnp.float32) + noise_level * noise.astype(jnp.float32)
    ).astype(jnp.bfloat16)
    modulation = jnp.einsum(
        "f,fkd->kd", time_embed(level, embed_width), w_time, preferred_element_type=jnp.float32
    )
    shift_vec = modulation[0]
    scale_vec = modulation[1]
    gate_vec = modulation[2]
    gathered = lax.all_gather(noisy, "seq", axis=0, tiled=True)
    partial_squares = jnp.sum(jnp.square(gathered.astype(jnp.float32)), axis=1)
    scaled = (gathered.astype(jnp.float32) * (1.0 + scale_vec)).astype(jnp.bfloat16)
    flat_w = w_qkv.reshape(w_qkv.shape[0], 3 * head_cols)
    projected = jnp.dot(scaled, flat_w, preferred_element_type=jnp.float32)
    shift_proj = jnp.dot(
        shift_vec.astype(jnp.bfloat16)[None, :], flat_w, preferred_element_type=jnp.float32
    )[0]
    projected, squares, shift_proj = lax.psum((projected, partial_squares, shift_proj), "mp")
    mixed = projected * lax.rsqrt(squares / D + 1e-06)[:, None] + shift_proj
    heads_here = head_cols // HEAD_DIM
    mixed = mixed.reshape(full_length, 3, heads_here, HEAD_DIM)
    gains = w_norm.reshape(2, heads_here, HEAD_DIM)
    query_norm = head_norm(mixed[:, 0], gains[0])
    key_norm = head_norm(mixed[:, 1], gains[1])
    value_rows = mixed[:, 2].astype(jnp.bfloat16)
    head_out = attend(query_norm, key_norm, value_rows)
    weight_sign = jnp.where(use_critic, 0.5, -0.5)
    block = head_out
    summed_rows = lax.psum_scatter(
        weight_sign * (gate_vec * jnp.dot(block, w_out, preferred_element_type=jnp.float32)),
        ("role", "seq"),
        scatter_dimension=0,
        tiled=True,
    )
    grad_rows = lax.all_gather(
        (gen_gate * summed_rows).astype(jnp.bfloat16), ("role", "seq"), axis=0, tiled=True
    )
    weight_grad = lax.dot_general(
        gen_heads, grad_rows, (((0,), (0,)), ((), ())), preferred_element_type=jnp.float32
    )
    return (latent, weight_grad.astype(jnp.bfloat16))

MIB = 1024 * 1024
EXTRA_ROWS = 16


def vmem_spec():
    return pl.BlockSpec(memory_space=pltpu.VMEM)


def smem_spec():
    return pl.BlockSpec(memory_space=pltpu.SMEM)


def params(mebibytes):
    return pltpu.CompilerParams(vmem_limit_bytes=mebibytes * MIB)


def dot32(a, b):
    return jnp.dot(a, b, preferred_element_type=jnp.float32)


def at_block(index, size):
    return pl.ds(pl.multiple_of(index * size, size), size)


def gen_kernel(where, heads, weight, time_w, embed, resid, noise, full, sent):
    step = pl.program_id(0)
    length = full.shape[0]
    own = resid.shape[0]

    @pl.when(step == 0)
    def _():
        full[...] = jnp.zeros_like(full)

    full[...] += dot32(heads[...], weight[...])

    @pl.when(step == pl.num_programs(0) - 1)
    def _():
        full[...] = full[...] * dot32(embed[...], time_w[...])[0:1]
        at = at_block(where[0], own)
        full[at, :] = full[at, :] + resid[...].astype(jnp.float32)
        sent[pl.ds(0, length), :] = full[...].astype(jnp.bfloat16)
        sent[pl.ds(length, own), :] = noise[...]


def gen_part(where, heads, weight, time_w, embed, resid, noise, steps):
    length, depth = heads.shape
    width = weight.shape[1] // 2
    freq = time_w.shape[0]
    own = resid.shape[0]
    tile = depth // steps
    grid_spec = pltpu.PrefetchScalarGridSpec(
        num_scalar_prefetch=1,
        grid=(steps,),
        in_specs=[
            pl.BlockSpec((length, tile), lambda n, w: (0, n)),
            pl.BlockSpec((tile, width), lambda n, w: (n, w[1])),
            pl.BlockSpec((freq, width), lambda n, w: (0, w[1])),
            pl.BlockSpec((8, freq), lambda n, w: (0, 0)),
            pl.BlockSpec((own, width), lambda n, w: (0, w[1])),
            pl.BlockSpec((own, width), lambda n, w: (0, w[1])),
        ],
        out_specs=[
            pl.BlockSpec((length, width), lambda n, w: (0, 0)),
            pl.BlockSpec((length + own, width), lambda n, w: (0, 0)),
        ],
    )
    return pl.pallas_call(
        gen_kernel,
        grid_spec=grid_spec,
        out_shape=[
            jax.ShapeDtypeStruct((length, width), jnp.float32),
            jax.ShapeDtypeStruct((length + own, width), jnp.bfloat16),
        ],
        compiler_params=params(56),
        name="gen_part",
    )(where, heads, weight, time_w, embed, resid, noise)


def mod_kernel(embed, time_a, time_b, time_w, mods, gate):
    gate[...] = dot32(embed[...], time_w[...])
    for k in range(3):
        mods[0, k] = dot32(embed[...], time_a[k])
        mods[1, k] = dot32(embed[...], time_b[k])


def mod_part(embed, time_a, time_b, time_w):
    width = time_a.shape[2]
    return pl.pallas_call(
        mod_kernel,
        in_specs=[vmem_spec()] * 4,
        out_specs=[vmem_spec()] * 2,
        out_shape=[
            jax.ShapeDtypeStruct((2, 3, 8, width), jnp.float32),
            jax.ShapeDtypeStruct((8, width), jnp.float32),
        ],
        compiler_params=params(16),
        name="mod_part",
    )(embed, time_a, time_b, time_w)


def project(index, mine, noisy, squares, mods, weight, kept, sent, result):
    tokens = noisy.shape[0]
    length = tokens // 2
    unit = squares.shape[1] // 2
    groups = weight.shape[2] // unit
    scale = mods[index, 1]
    shift = mods[index, 0]
    spread = noisy.astype(jnp.float32)
    top = spread[:length] * (1.0 + scale[1:2])
    low = spread[length:] * (1.0 + scale[2:3])
    extra = jnp.concatenate([shift[1:3], jnp.zeros((EXTRA_ROWS - 2, shift.shape[1]), jnp.float32)], axis=0)
    rows = jnp.concatenate([top, low, extra], axis=0).astype(jnp.bfloat16)
    row_id = lax.broadcasted_iota(jnp.int32, (EXTRA_ROWS, unit), 0)
    for part in range(3):
        result[...] = dot32(rows, weight[part])
        cols = pl.ds(part * unit, unit)
        for slot in range(groups):
            at = at_block(jnp.bitwise_xor(mine, slot), unit)
            goal = sent if slot % 2 else kept
            for level in range(2):
                goal[level][slot // 2, pl.ds(0, length), cols] = result[pl.ds(level * length, length), at].astype(
                    jnp.bfloat16
                )
                tail = jnp.where(row_id == 0, result[pl.ds(tokens + level, 1), at], 0.0)
                tail = jnp.where(row_id == 1, squares[0:1, level * length : (level + 1) * length], tail)
                goal[level][slot // 2, pl.ds(length, EXTRA_ROWS), cols] = tail.astype(jnp.bfloat16)


def first_kernel(where, levels, half, swapped, arrived, noise, mods, weight, *refs):
    latent, noisy, squares, kept_a, kept_b, sent_a, sent_b, values, noises, result = refs
    length, cols = half.shape
    own = latent.shape[0]
    tokens = 2 * length
    seq, core, mine = where[0], where[1], where[2]
    values[:, at_block(core, cols)] = half[...]
    values[:, at_block(1 - core, cols)] = swapped[pl.ds(0, length), :]
    latent[...] = values[at_block(seq, own), :]
    noises[at_block(seq, own), :] = noise[...]
    theirs = at_block(1 - seq, own)
    noises[theirs, at_block(core, cols)] = arrived[pl.ds(length, own), :]
    noises[theirs, at_block(1 - core, cols)] = swapped[pl.ds(length, own), :]
    spread = values[...].astype(jnp.float32)
    noise_rows = noises[...].astype(jnp.float32)
    mixed = jnp.concatenate(
        [(1.0 - levels[level]) * spread + levels[level] * noise_rows for level in range(2)], axis=0
    ).astype(jnp.bfloat16)
    noisy[...] = mixed
    wide = mixed.astype(jnp.float32)
    sums = jnp.sum(wide * wide, axis=1, keepdims=True)
    sums = jnp.broadcast_to(sums, (tokens, length)).T[0:8]
    squares[...] = sums
    project(0, mine, mixed, sums, mods, weight, (kept_a, kept_b), (sent_a, sent_b), result)


def second_kernel(where, noisy, squares, mods, weight, kept_a, kept_b, sent_a, sent_b, result):
    project(1, where[2], noisy[...], squares[...], mods, weight, (kept_a, kept_b), (sent_a, sent_b), result)


def chunk_shapes(length, weight):
    unit = length
    groups = weight.shape[2] // unit
    return [jax.ShapeDtypeStruct((groups // 2, length + EXTRA_ROWS, 3 * unit), jnp.bfloat16)] * 4


def first_part(where, levels, half, swapped, arrived, noise, mods, weight):
    length, cols = half.shape
    own, width = noise.shape
    tokens = 2 * length
    return pl.pallas_call(
        first_kernel,
        in_specs=[smem_spec(), smem_spec()] + [vmem_spec()] * 6,
        out_specs=[vmem_spec()] * 7,
        out_shape=[
            jax.ShapeDtypeStruct((own, width), jnp.bfloat16),
            jax.ShapeDtypeStruct((tokens, width), jnp.bfloat16),
            jax.ShapeDtypeStruct((8, tokens), jnp.float32),
        ]
        + chunk_shapes(length, weight),
        scratch_shapes=[
            pltpu.VMEM((length, width), jnp.bfloat16),
            pltpu.VMEM((length, width), jnp.bfloat16),
            pltpu.VMEM((tokens + EXTRA_ROWS, weight.shape[2]), jnp.float32),
        ],
        compiler_params=params(24),
        name="first_part",
    )(where, levels, half, swapped, arrived, noise, mods, weight)


def second_part(where, noisy, squares, mods, weight):
    tokens = noisy.shape[0]
    return pl.pallas_call(
        second_kernel,
        in_specs=[smem_spec()] + [vmem_spec()] * 4,
        out_specs=[vmem_spec()] * 4,
        out_shape=chunk_shapes(tokens // 2, weight),
        scratch_shapes=[pltpu.VMEM((tokens + EXTRA_ROWS, weight.shape[2]), jnp.float32)],
        compiler_params=params(24),
        name="second_part",
    )(where, noisy, squares, mods, weight)


def attend_kernel(width, kept_a, other_a, kept_b, other_b, gains, out):
    _, length, unit = out.shape
    for level, (kept, other) in enumerate(((kept_a, other_a), (kept_b, other_b))):
        mixed = kept[...] + other[...].astype(jnp.float32)
        squares = jnp.broadcast_to(mixed[length + 1 : length + 2, :unit], (unit, unit)).T
        factor = lax.rsqrt(squares * (1.0 / width) + 1e-06)

        def pick(part):
            cols = slice(part * unit, (part + 1) * unit)
            return mixed[:length, cols] * factor + mixed[length : length + 1, cols]

        def normed(part):
            rows = pick(part)
            mean = jnp.mean(rows * rows, axis=1, keepdims=True)
            return (rows * lax.rsqrt(mean + 1e-06) * gains[part : part + 1, :]).astype(jnp.bfloat16)

        query, key = normed(0), normed(1)
        value = pick(2).astype(jnp.bfloat16)
        logits = lax.dot_general(
            query, key, (((1,), (1,)), ((), ())), preferred_element_type=jnp.float32
        ) * (1.0 / math.sqrt(unit))
        expanded = jnp.exp(logits)
        probs = (expanded / jnp.sum(expanded, axis=1, keepdims=True)).astype(jnp.bfloat16)
        out[level] = dot32(probs, value).astype(jnp.bfloat16)


def attend_part(chunks, gains, width):
    kept_a, kept_b = chunks[0][0], chunks[1][0]
    unit = kept_a.shape[1] // 3
    length = kept_a.shape[0] - EXTRA_ROWS
    return pl.pallas_call(
        lambda *refs: attend_kernel(width, *refs),
        in_specs=[vmem_spec()] * 5,
        out_specs=vmem_spec(),
        out_shape=jax.ShapeDtypeStruct((2, length, unit), jnp.bfloat16),
        compiler_params=params(8),
        name="attend_part",
    )(kept_a, chunks[0][1], kept_b, chunks[1][1], gains)


def out_kernel(where, *refs):
    heads_a, heads_b = refs[0:4], refs[4:8]
    weight_a, weight_b, mods, kept, sent, rows, total = refs[8:]
    _, length, unit = heads_a[0].shape
    core, mine = where[1], where[2]
    for index, (heads, weight) in enumerate(((heads_a, weight_a), (heads_b, weight_b))):
        for slot, head in enumerate(heads):
            at = at_block(jnp.bitwise_xor(mine, slot), unit)
            for level in range(2):
                rows[pl.ds(level * length, length), at] = head[level]
        result = dot32(rows[...], weight[...])
        gates = mods[index, 2]
        signed = gates[1:2] * result[:length] + gates[2:3] * result[length:]
        if index == 0:
            total[...] = -0.5 * signed
        else:
            total[...] = total[...] + 0.5 * signed
    cols = kept.shape[1]
    kept[...] = total[:, at_block(core, cols)]
    sent[...] = total[:, at_block(1 - core, cols)].astype(jnp.bfloat16)


def out_part(where, heads_a, heads_b, weight_a, weight_b, mods):
    _, length, unit = heads_a[0].shape
    depth, width = weight_a.shape
    return pl.pallas_call(
        out_kernel,
        in_specs=[smem_spec()] + [vmem_spec()] * 11,
        out_specs=[vmem_spec()] * 2,
        out_shape=[
            jax.ShapeDtypeStruct((length, width // 2), jnp.float32),
            jax.ShapeDtypeStruct((length, width // 2), jnp.bfloat16),
        ],
        scratch_shapes=[
            pltpu.VMEM((2 * length, depth), jnp.bfloat16),
            pltpu.VMEM((length, width), jnp.float32),
        ],
        compiler_params=params(16),
        name="out_part",
    )(where, *heads_a, *heads_b, weight_a, weight_b, mods)


def grad_kernel(where, heads_t, mine, theirs, out, rows):
    cols = mine.shape[1]

    @pl.when(pl.program_id(0) == 0)
    def _():
        rows[:, at_block(where[1], cols)] = mine[...]
        rows[:, at_block(1 - where[1], cols)] = theirs[...]

    out[...] = dot32(heads_t[...], rows[...]).astype(jnp.bfloat16)


def grad_part(where, heads_t, mine, theirs, steps):
    depth, length = heads_t.shape
    cols = mine.shape[1]
    tile = depth // steps
    grid_spec = pltpu.PrefetchScalarGridSpec(
        num_scalar_prefetch=1,
        grid=(steps,),
        in_specs=[
            pl.BlockSpec((tile, length), lambda n, w: (n, 0)),
            pl.BlockSpec((length, cols), lambda n, w: (0, 0)),
            pl.BlockSpec((length, cols), lambda n, w: (0, 0)),
        ],
        out_specs=pl.BlockSpec((tile, 2 * cols), lambda n, w: (n, 0)),
        scratch_shapes=[pltpu.VMEM((length, 2 * cols), jnp.bfloat16)],
    )
    return pl.pallas_call(
        grad_kernel,
        grid_spec=grid_spec,
        out_shape=jax.ShapeDtypeStruct((depth, 2 * cols), jnp.bfloat16),
        compiler_params=params(24),
        name="grad_part",
    )(where, heads_t, mine, theirs)


def exchange(array, axis, bit):
    return lax.ppermute(array, axis, [(i, i ^ bit) for i in range(lax.axis_size(axis))])


def both(mine, theirs):
    return mine.astype(jnp.float32) + theirs.astype(jnp.float32)


def heads_per_role(
    gen_heads,
    gen_resid,
    gen_out_w,
    gen_time_w,
    noise,
    steps,
    teacher_qkv,
    teacher_out,
    teacher_time,
    teacher_norm,
    critic_qkv,
    critic_out,
    critic_time,
    critic_norm,
):
    length = gen_heads.shape[0]
    roles, groups = lax.axis_size("role"), lax.axis_size("mp")
    role, seq, mp = lax.axis_index("role"), lax.axis_index("seq"), lax.axis_index("mp")
    part_cols = gen_heads.shape[1] // roles
    freq = gen_time_w.shape[0]
    core = role % 2
    where = jnp.stack([seq, core, mp]).astype(jnp.int32)
    half_cols = gen_resid.shape[1] // 2

    embed = jax.vmap(lambda t: time_embed(t, freq))(steps)
    embed = jnp.concatenate([embed, jnp.zeros((5, freq), jnp.bfloat16)], axis=0)
    levels = steps[1:3].astype(jnp.float32) / 1000.0
    full, sent = gen_part(where, gen_heads, gen_out_w, gen_time_w, embed, gen_resid, noise, 4)
    arrived = exchange(sent, "seq", 1)

    start = role * part_cols
    weight_a = lax.dynamic_slice_in_dim(teacher_qkv.transpose(1, 0, 2), start, part_cols, axis=2)
    weight_b = lax.dynamic_slice_in_dim(critic_qkv.transpose(1, 0, 2), start, part_cols, axis=2)
    mods, gate = mod_part(embed, teacher_time.transpose(1, 0, 2), critic_time.transpose(1, 0, 2), gen_time_w)

    half = both(full, arrived[:length]).astype(jnp.bfloat16)
    swapped = exchange(jnp.concatenate([half, arrived[length:]], axis=0), "role", 1)
    first = first_part(where, levels, half, swapped, arrived, noise, mods, weight_a)
    latent, noisy, squares = first[:3]
    second = second_part(where, noisy, squares, mods, weight_b)

    out_a = lax.dynamic_slice_in_dim(teacher_out, start, part_cols, axis=0)
    out_b = lax.dynamic_slice_in_dim(critic_out, start, part_cols, axis=0)
    unit = part_cols // groups
    gathered = []
    for chunks, gains in ((first[3:], teacher_norm), (second, critic_norm)):
        kept, sends = chunks[:2], chunks[2:]
        pieces = []
        for level in range(2):
            summed = both(kept[level], exchange(sends[level], "mp", 1))
            pieces.append((summed[0], exchange(summed[1].astype(jnp.bfloat16), "mp", 2)))
        gains = lax.dynamic_slice_in_dim(gains, start + mp * unit, unit, axis=1)
        head_out = attend_part(pieces, gains, D)
        near = exchange(head_out, "mp", 1)
        far = exchange(head_out, "mp", 2)
        gathered.append((head_out, near, far, exchange(far, "mp", 1)))

    kept, sent = out_part(where, *gathered, out_a, out_b, mods)
    total = both(kept, exchange(sent, "role", 1)).astype(jnp.bfloat16)
    middle = length // 2
    top, low = total[:middle], total[middle:]
    top = both(top, exchange(top, "seq", 1)).astype(jnp.bfloat16)
    low = both(low, exchange(low, "role", 2)).astype(jnp.bfloat16)
    top = both(top, exchange(top, "role", 2))
    low = both(low, exchange(low, "seq", 1))
    gate_row = lax.dynamic_slice_in_dim(gate, core * half_cols, half_cols, axis=1)[0:1]
    rows = (gate_row * jnp.concatenate([top, low], axis=0)).astype(jnp.bfloat16)
    weight_grad = grad_part(where, gen_heads.T, rows, exchange(rows, "role", 1), 4)
    return latent, weight_grad


def solution(mesh):
    in_specs = (
        P(None, "seq"),
        P("seq", "mp"),
        P("seq", "mp"),
        P(None, "mp"),
        P("seq", "mp"),
        P(),
        P("mp", None, "seq"),
        P("seq", "mp"),
        P(None, None, "mp"),
        P(None, "seq"),
        P("mp", None, "seq"),
        P("seq", "mp"),
        P(None, None, "mp"),
        P(None, "seq"),
    )
    out_specs = (P("seq", "mp"), P("seq", "mp"))
    roles, seqs, groups = mesh.shape["role"], mesh.shape["seq"], mesh.shape["mp"]

    def on_device(*arrays):
        heads_here = arrays[0].shape[1] // HEAD_DIM
        length = arrays[0].shape[0]
        fits = (roles, seqs, groups) == (4, 2, 4) and heads_here == roles * groups and length == HEAD_DIM
        return heads_per_role(*arrays) if fits else pass_per_role(*arrays)

    return jax.shard_map(
        on_device, mesh=mesh, in_specs=in_specs, out_specs=out_specs, check_vma=False
    )
```

```python
import math

import jax
import jax.numpy as jnp
from jax import lax
from jax.experimental import pallas as pl
from jax.experimental.pallas import tpu as pltpu
from jax.sharding import PartitionSpec as P

D = 5120
HEAD_DIM = 128


def time_embed(step_value, width):
    half_width = width // 2
    positions = jnp.arange(half_width, dtype=jnp.float32)
    frequencies = jnp.exp(positions * (-math.log(10000.0) / half_width))
    angles = step_value.astype(jnp.float32) * frequencies
    return jnp.concatenate([jnp.cos(angles), jnp.sin(angles)]).astype(jnp.bfloat16)


def head_norm(values, gains):
    factor = lax.rsqrt(jnp.mean(values * values, axis=-1, keepdims=True) + 1e-06)
    return (values * factor * gains).astype(jnp.bfloat16)


def attend(query_norm, key_norm, value_rows):
    full_length, heads_here, head_width = query_norm.shape
    query_blocks = query_norm.reshape(
        full_length // full_length, full_length, heads_here, head_width
    )

    def one_block(query_block):
        logits = jnp.einsum(
            "qhd,khd->hqk", query_block, key_norm, preferred_element_type=jnp.float32
        ) * (1.0 / math.sqrt(head_width))
        expanded = jnp.exp(logits)
        probs = (expanded / jnp.sum(expanded, axis=2, keepdims=True)).astype(jnp.bfloat16)
        return jnp.einsum(
            "hqk,khd->qhd", probs, value_rows, preferred_element_type=jnp.float32
        ).astype(jnp.bfloat16)

    head_out = lax.map(one_block, query_blocks)
    return head_out.reshape(full_length, heads_here * head_width)


def pass_per_role(
    gen_heads,
    gen_resid,
    gen_out_w,
    gen_time_w,
    noise,
    steps,
    teacher_qkv,
    teacher_out,
    teacher_time,
    teacher_norm,
    critic_qkv,
    critic_out,
    critic_time,
    critic_norm,
):
    full_length = gen_heads.shape[0]
    head_cols = gen_heads.shape[1]
    embed_width = gen_time_w.shape[0]
    gen_gate = jnp.dot(
        time_embed(steps[0], embed_width)[None, :], gen_time_w, preferred_element_type=jnp.float32
    )[0]
    block = gen_heads
    gen_proj = lax.psum_scatter(
        jnp.dot(block, gen_out_w, preferred_element_type=jnp.float32),
        "seq",
        scatter_dimension=0,
        tiled=True,
    )
    latent = (gen_resid.astype(jnp.float32) + gen_gate * gen_proj).astype(jnp.bfloat16)
    role_index = lax.axis_index("role")
    level = steps[1 + role_index // 2]
    use_critic = role_index % 2 == 1
    w_qkv = jnp.where(use_critic, critic_qkv, teacher_qkv)
    w_out = jnp.where(use_critic, critic_out, teacher_out)
    w_time = jnp.where(use_critic, critic_time, teacher_time)
    w_norm = jnp.where(use_critic, critic_norm, teacher_norm)
    noise_level = level.astype(jnp.float32) / 1000.0
    noisy = (
        (1.0 - noise_level) * latent.astype(jnp.float32) + noise_level * noise.astype(jnp.float32)
    ).astype(jnp.bfloat16)
    modulation = jnp.einsum(
        "f,fkd->kd", time_embed(level, embed_width), w_time, preferred_element_type=jnp.float32
    )
    shift_vec = modulation[0]
    scale_vec = modulation[1]
    gate_vec = modulation[2]
    gathered = lax.all_gather(noisy, "seq", axis=0, tiled=True)
    partial_squares = jnp.sum(jnp.square(gathered.astype(jnp.float32)), axis=1)
    scaled = (gathered.astype(jnp.float32) * (1.0 + scale_vec)).astype(jnp.bfloat16)
    flat_w = w_qkv.reshape(w_qkv.shape[0], 3 * head_cols)
    projected = jnp.dot(scaled, flat_w, preferred_element_type=jnp.float32)
    shift_proj = jnp.dot(
        shift_vec.astype(jnp.bfloat16)[None, :], flat_w, preferred_element_type=jnp.float32
    )[0]
    projected, squares, shift_proj = lax.psum((projected, partial_squares, shift_proj), "mp")
    mixed = projected * lax.rsqrt(squares / D + 1e-06)[:, None] + shift_proj
    heads_here = head_cols // HEAD_DIM
    mixed = mixed.reshape(full_length, 3, heads_here, HEAD_DIM)
    gains = w_norm.reshape(2, heads_here, HEAD_DIM)
    query_norm = head_norm(mixed[:, 0], gains[0])
    key_norm = head_norm(mixed[:, 1], gains[1])
    value_rows = mixed[:, 2].astype(jnp.bfloat16)
    head_out = attend(query_norm, key_norm, value_rows)
    weight_sign = jnp.where(use_critic, 0.5, -0.5)
    block = head_out
    summed_rows = lax.psum_scatter(
        weight_sign * (gate_vec * jnp.dot(block, w_out, preferred_element_type=jnp.float32)),
        ("role", "seq"),
        scatter_dimension=0,
        tiled=True,
    )
    grad_rows = lax.all_gather(
        (gen_gate * summed_rows).astype(jnp.bfloat16), ("role", "seq"), axis=0, tiled=True
    )
    weight_grad = lax.dot_general(
        gen_heads, grad_rows, (((0,), (0,)), ((), ())), preferred_element_type=jnp.float32
    )
    return (latent, weight_grad.astype(jnp.bfloat16))

MIB = 1024 * 1024
EXTRA_ROWS = 16


def vmem_spec():
    return pl.BlockSpec(memory_space=pltpu.VMEM)


def smem_spec():
    return pl.BlockSpec(memory_space=pltpu.SMEM)


def params(mebibytes):
    return pltpu.CompilerParams(vmem_limit_bytes=mebibytes * MIB)


def dot32(a, b):
    return jnp.dot(a, b, preferred_element_type=jnp.float32)


def at_block(index, size):
    return pl.ds(pl.multiple_of(index * size, size), size)


def any_spec():
    return pl.BlockSpec(memory_space=pl.ANY)


def hbm_spec():
    return pl.BlockSpec(memory_space=pltpu.HBM)


def cost(flops, moved):
    return pl.CostEstimate(flops=flops, bytes_accessed=moved, transcendentals=0)


GEN_CUTS = 4


def gen_kernel(seq, core, embed, heads, weight, time_w, resid, noise, full, sent, heads_v, weight_v, time_v, resid_v, sems):
    length, width = full.shape
    own = resid_v.shape[0]
    cols = at_block(core[0], width)
    tile = weight_v.shape[0] // GEN_CUTS
    copies = [pltpu.make_async_copy(heads, heads_v, sems.at[GEN_CUTS])]
    for k in range(GEN_CUTS):
        rows = pl.ds(k * tile, tile)
        copies.append(pltpu.make_async_copy(weight.at[rows, cols], weight_v.at[rows, :], sems.at[k]))
    copies.append(pltpu.make_async_copy(time_w.at[:, cols], time_v, sems.at[GEN_CUTS + 1]))
    copies.append(pltpu.make_async_copy(resid.at[:, cols], resid_v, sems.at[GEN_CUTS + 2]))
    copies.append(pltpu.make_async_copy(noise.at[:, cols], sent.at[pl.ds(length, own), :], sems.at[GEN_CUTS + 3]))
    for copy in copies:
        copy.start()
    copies[0].wait()
    total = None
    for k in range(GEN_CUTS):
        copies[1 + k].wait()
        rows = pl.ds(k * tile, tile)
        term = dot32(heads_v[:, rows], weight_v[rows, :])
        total = term if total is None else total + term
    for copy in copies[1 + GEN_CUTS :]:
        copy.wait()
    full[...] = total * dot32(embed[...], time_v[...])[0:1]
    at = at_block(seq[0], own)
    full[at, :] = full[at, :] + resid_v[...].astype(jnp.float32)
    sent[pl.ds(0, length), :] = full[...].astype(jnp.bfloat16)


def gen_part(seq, core, embed, heads, weight, time_w, resid, noise):
    length, depth = heads.shape
    width = weight.shape[1] // 2
    freq = time_w.shape[0]
    own = resid.shape[0]
    return pl.pallas_call(
        gen_kernel,
        in_specs=[smem_spec(), smem_spec(), vmem_spec()] + [hbm_spec()] * 5,
        out_specs=[vmem_spec()] * 2,
        out_shape=[
            jax.ShapeDtypeStruct((length, width), jnp.float32),
            jax.ShapeDtypeStruct((length + own, width), jnp.bfloat16),
        ],
        scratch_shapes=[
            pltpu.VMEM((length, depth), jnp.bfloat16),
            pltpu.VMEM((depth, width), jnp.bfloat16),
            pltpu.VMEM((freq, width), jnp.bfloat16),
            pltpu.VMEM((own, width), jnp.bfloat16),
            pltpu.SemaphoreType.DMA((GEN_CUTS + 4,)),
        ],
        compiler_params=params(16),
        name="gen_part",
    )(seq, core, embed, heads, weight, time_w, resid, noise)


def load_kernel(role, embed, after, *refs):
    qkv_a, qkv_b, out_a, out_b, time_a, time_b, time_w = refs[:7]
    own_qkv_a, own_qkv_b, own_out_a, own_out_b, mods, gate = refs[7:13]
    time_v, gate_v, sems = refs[13:]
    cols = at_block(role[0], own_qkv_a.shape[2])
    rows = at_block(role[0], own_out_a.shape[0])
    pairs = (
        (time_a, time_v.at[0]),
        (time_b, time_v.at[1]),
        (time_w, gate_v),
        (qkv_a.at[:, :, cols], own_qkv_a),
        (qkv_b.at[:, :, cols], own_qkv_b),
        (out_a.at[rows, :], own_out_a),
        (out_b.at[rows, :], own_out_b),
    )
    copies = [pltpu.make_async_copy(source, goal, sems.at[k]) for k, (source, goal) in enumerate(pairs)]
    for copy in copies:
        copy.start()
    for index in range(2):
        copies[index].wait()
        for k in range(3):
            mods[index, k] = dot32(embed[...], time_v[index, k])
    copies[2].wait()
    gate[...] = dot32(embed[...], gate_v[...])
    for copy in copies[3:]:
        copy.wait()


def load_part(role, embed, after, qkv_a, qkv_b, out_a, out_b, time_a, time_b, time_w, roles):
    parts, depth, heads_cols = qkv_a.shape
    part_cols = heads_cols // roles
    width = time_w.shape[1]
    freq = time_w.shape[0]
    moved = 4 * (parts * depth * part_cols + part_cols * width + parts * freq * width)
    return pl.pallas_call(
        load_kernel,
        in_specs=[smem_spec(), vmem_spec(), any_spec()] + [hbm_spec()] * 7,
        out_specs=[vmem_spec()] * 6,
        out_shape=[jax.ShapeDtypeStruct((parts, depth, part_cols), jnp.bfloat16)] * 2
        + [jax.ShapeDtypeStruct((part_cols, width), jnp.bfloat16)] * 2
        + [
            jax.ShapeDtypeStruct((2, parts, 8, width), jnp.float32),
            jax.ShapeDtypeStruct((8, width), jnp.float32),
        ],
        scratch_shapes=[
            pltpu.VMEM((2, parts, freq, width), jnp.bfloat16),
            pltpu.VMEM((freq, width), jnp.bfloat16),
            pltpu.SemaphoreType.DMA((7,)),
        ],
        compiler_params=params(24),
        cost_estimate=cost(moved, moved),
        name="load_part",
    )(role, embed, after, qkv_a, qkv_b, out_a, out_b, time_a, time_b, time_w)


def join_kernel(full, arrived, after, joined):
    length = full.shape[0]
    own = arrived.shape[0] - length
    top = full[...] + arrived[pl.ds(0, length), :].astype(jnp.float32)
    joined[pl.ds(0, length), :] = top.astype(jnp.bfloat16)
    joined[pl.ds(length, own), :] = arrived[pl.ds(length, own), :]


def join_part(full, arrived, after):
    return pl.pallas_call(
        join_kernel,
        in_specs=[vmem_spec(), vmem_spec(), any_spec()],
        out_specs=vmem_spec(),
        out_shape=jax.ShapeDtypeStruct(arrived.shape, jnp.bfloat16),
        compiler_params=params(8),
        name="join_part",
    )(full, arrived, after)


def project(index, mine, noisy, squares, mods, weight, kept, sent, result):
    tokens = noisy.shape[0]
    length = tokens // 2
    unit = squares.shape[1] // 2
    groups = weight.shape[2] // unit
    scale = mods[index, 1]
    shift = mods[index, 0]
    spread = noisy.astype(jnp.float32)
    top = spread[:length] * (1.0 + scale[1:2])
    low = spread[length:] * (1.0 + scale[2:3])
    extra = jnp.concatenate([shift[1:3], jnp.zeros((EXTRA_ROWS - 2, shift.shape[1]), jnp.float32)], axis=0)
    rows = jnp.concatenate([top, low, extra], axis=0).astype(jnp.bfloat16)
    row_id = lax.broadcasted_iota(jnp.int32, (EXTRA_ROWS, unit), 0)
    for part in range(3):
        result[...] = dot32(rows, weight[part])
        cols = pl.ds(part * unit, unit)
        for slot in range(groups):
            at = at_block(jnp.bitwise_xor(mine, slot), unit)
            goal = sent if slot % 2 else kept
            for level in range(2):
                goal[level][slot // 2, pl.ds(0, length), cols] = result[pl.ds(level * length, length), at].astype(
                    jnp.bfloat16
                )
            tail = jnp.where(row_id < 2, result[pl.ds(tokens, EXTRA_ROWS), at], 0.0)
            for level in range(2):
                tail = jnp.where(row_id == 2 + level, squares[0:1, level * length : (level + 1) * length], tail)
            goal[0][slot // 2, pl.ds(length, EXTRA_ROWS), cols] = tail.astype(jnp.bfloat16)


def first_kernel(seq, core, mine, levels, joined, swapped, noise, mods, weight, *refs):
    latent, noisy, squares, kept_a, kept_b, sent_a, sent_b, values, noises, result = refs
    length, cols = values.shape[0], joined.shape[1]
    own = latent.shape[0]
    tokens = 2 * length
    left, right = at_block(core[0], cols), at_block(1 - core[0], cols)
    values[:, left] = joined[pl.ds(0, length), :]
    values[:, right] = swapped[pl.ds(0, length), :]
    latent[...] = values[at_block(seq[0], own), :]
    noises[at_block(seq[0], own), :] = noise[...]
    theirs = at_block(1 - seq[0], own)
    noises[theirs, left] = joined[pl.ds(length, own), :]
    noises[theirs, right] = swapped[pl.ds(length, own), :]
    spread = values[...].astype(jnp.float32)
    noise_rows = noises[...].astype(jnp.float32)
    mixed = jnp.concatenate(
        [(1.0 - levels[level]) * spread + levels[level] * noise_rows for level in range(2)], axis=0
    ).astype(jnp.bfloat16)
    noisy[...] = mixed
    wide = mixed.astype(jnp.float32)
    sums = jnp.sum(wide * wide, axis=1, keepdims=True)
    sums = jnp.broadcast_to(sums, (tokens, length)).T[0:8]
    squares[...] = sums
    project(0, mine[0], mixed, sums, mods, weight, (kept_a, kept_b), (sent_a, sent_b), result)


def second_kernel(mine, noisy, squares, mods, weight, kept_a, kept_b, sent_a, sent_b, result):
    project(1, mine[0], noisy[...], squares[...], mods, weight, (kept_a, kept_b), (sent_a, sent_b), result)


def chunk_shapes(length, weight):
    unit = length
    groups = weight.shape[2] // unit
    shapes = [
        jax.ShapeDtypeStruct((groups // 2, rows, 3 * unit), jnp.bfloat16) for rows in (length + EXTRA_ROWS, length)
    ]
    return shapes * 2


def first_part(seq, core, mine, levels, joined, swapped, noise, mods, weight):
    own, width = noise.shape
    length = joined.shape[0] - own
    tokens = 2 * length
    return pl.pallas_call(
        first_kernel,
        in_specs=[smem_spec()] * 4 + [vmem_spec()] * 5,
        out_specs=[vmem_spec()] * 7,
        out_shape=[
            jax.ShapeDtypeStruct((own, width), jnp.bfloat16),
            jax.ShapeDtypeStruct((tokens, width), jnp.bfloat16),
            jax.ShapeDtypeStruct((8, tokens), jnp.float32),
        ]
        + chunk_shapes(length, weight),
        scratch_shapes=[
            pltpu.VMEM((length, width), jnp.bfloat16),
            pltpu.VMEM((length, width), jnp.bfloat16),
            pltpu.VMEM((tokens + EXTRA_ROWS, weight.shape[2]), jnp.float32),
        ],
        compiler_params=params(24),
        name="first_part",
    )(seq, core, mine, levels, joined, swapped, noise, mods, weight)


def second_part(mine, noisy, squares, mods, weight):
    tokens = noisy.shape[0]
    return pl.pallas_call(
        second_kernel,
        in_specs=[smem_spec()] + [vmem_spec()] * 4,
        out_specs=[vmem_spec()] * 4,
        out_shape=chunk_shapes(tokens // 2, weight),
        scratch_shapes=[pltpu.VMEM((tokens + EXTRA_ROWS, weight.shape[2]), jnp.float32)],
        compiler_params=params(24),
        name="second_part",
    )(mine, noisy, squares, mods, weight)


def attend_kernel(width, kept_a, other_a, kept_b, other_b, gains, out):
    _, length, unit = out.shape
    extra = None
    for level, (kept, other) in enumerate(((kept_a, other_a), (kept_b, other_b))):
        mixed = kept[...] + other[...].astype(jnp.float32)
        if level == 0:
            extra = mixed[length:]
        squares = jnp.broadcast_to(extra[2 + level : 3 + level, :unit], (unit, unit)).T
        factor = lax.rsqrt(squares * (1.0 / width) + 1e-06)

        def pick(part):
            cols = slice(part * unit, (part + 1) * unit)
            return mixed[:length, cols] * factor + extra[level : level + 1, cols]

        def normed(part):
            rows = pick(part)
            mean = jnp.mean(rows * rows, axis=1, keepdims=True)
            return (rows * lax.rsqrt(mean + 1e-06) * gains[part : part + 1, :]).astype(jnp.bfloat16)

        query, key = normed(0), normed(1)
        value = pick(2).astype(jnp.bfloat16)
        logits = lax.dot_general(
            query, key, (((1,), (1,)), ((), ())), preferred_element_type=jnp.float32
        ) * (1.0 / math.sqrt(unit))
        expanded = jnp.exp(logits)
        probs = (expanded / jnp.sum(expanded, axis=1, keepdims=True)).astype(jnp.bfloat16)
        out[level] = dot32(probs, value).astype(jnp.bfloat16)


def attend_part(chunks, gains, width):
    kept_a, kept_b = chunks[0][0], chunks[1][0]
    unit = kept_a.shape[1] // 3
    length = kept_a.shape[0] - EXTRA_ROWS
    return pl.pallas_call(
        lambda *refs: attend_kernel(width, *refs),
        in_specs=[vmem_spec()] * 5,
        out_specs=vmem_spec(),
        out_shape=jax.ShapeDtypeStruct((2, length, unit), jnp.bfloat16),
        compiler_params=params(8),
        name="attend_part",
    )(kept_a, chunks[0][1], kept_b, chunks[1][1], gains)


def out_kernel(core, mine, *refs):
    heads_a, heads_b = refs[0:4], refs[4:8]
    weight_a, weight_b, mods, kept, sent, rows, total = refs[8:]
    _, length, unit = heads_a[0].shape
    for index, (heads, weight) in enumerate(((heads_a, weight_a), (heads_b, weight_b))):
        for slot, head in enumerate(heads):
            at = at_block(jnp.bitwise_xor(mine[0], slot), unit)
            for level in range(2):
                rows[pl.ds(level * length, length), at] = head[level]
        result = dot32(rows[...], weight[...])
        gates = mods[index, 2]
        signed = gates[1:2] * result[:length] + gates[2:3] * result[length:]
        if index == 0:
            total[...] = -0.5 * signed
        else:
            total[...] = total[...] + 0.5 * signed
    cols = kept.shape[1]
    kept[...] = total[:, at_block(core[0], cols)]
    sent[...] = total[:, at_block(1 - core[0], cols)].astype(jnp.bfloat16)


def out_part(core, mine, heads_a, heads_b, weight_a, weight_b, mods):
    _, length, unit = heads_a[0].shape
    depth, width = weight_a.shape
    return pl.pallas_call(
        out_kernel,
        in_specs=[smem_spec()] * 2 + [vmem_spec()] * 11,
        out_specs=[vmem_spec()] * 2,
        out_shape=[
            jax.ShapeDtypeStruct((length, width // 2), jnp.float32),
            jax.ShapeDtypeStruct((length, width // 2), jnp.bfloat16),
        ],
        scratch_shapes=[
            pltpu.VMEM((2 * length, depth), jnp.bfloat16),
            pltpu.VMEM((length, width), jnp.float32),
        ],
        compiler_params=params(16),
        name="out_part",
    )(core, mine, *heads_a, *heads_b, weight_a, weight_b, mods)


def grad_kernel(half, heads_t, rows, *refs):
    refs[-1][...] = dot32(heads_t[...], rows[...]).astype(jnp.bfloat16)


def grad_part(half, heads_t, rows, before, steps):
    depth, length = heads_t.shape
    cols = rows.shape[1]
    tile = depth // steps
    rest = [] if before is None else [before]
    grid_spec = pltpu.PrefetchScalarGridSpec(
        num_scalar_prefetch=1,
        grid=(steps,),
        in_specs=[
            pl.BlockSpec((tile, length), lambda n, w: (n, 0)),
            pl.BlockSpec((length, cols), lambda n, w: (0, 0)),
        ]
        + [any_spec()] * len(rest),
        out_specs=pl.BlockSpec((tile, cols), lambda n, w: (n, w[0])),
    )
    return pl.pallas_call(
        grad_kernel,
        grid_spec=grid_spec,
        out_shape=jax.ShapeDtypeStruct((depth, 2 * cols), jnp.bfloat16),
        input_output_aliases={3: 0} if rest else {},
        compiler_params=params(24),
        name="grad_part",
    )(half, heads_t, rows, *rest)


def exchange(array, axis, bit):
    return lax.ppermute(array, axis, [(i, i ^ bit) for i in range(lax.axis_size(axis))])


def both(mine, theirs):
    return mine.astype(jnp.float32) + theirs.astype(jnp.float32)


def heads_per_role(
    gen_heads,
    gen_resid,
    gen_out_w,
    gen_time_w,
    noise,
    steps,
    teacher_qkv,
    teacher_out,
    teacher_time,
    teacher_norm,
    critic_qkv,
    critic_out,
    critic_time,
    critic_norm,
):
    length = gen_heads.shape[0]
    roles, groups = lax.axis_size("role"), lax.axis_size("mp")
    role, seq, mp = lax.axis_index("role"), lax.axis_index("seq"), lax.axis_index("mp")
    part_cols = gen_heads.shape[1] // roles
    freq = gen_time_w.shape[0]
    role_at, seq_at, mine = [v.astype(jnp.int32).reshape(1) for v in (role, seq, mp)]
    core = role_at % 2
    half_cols = gen_resid.shape[1] // 2

    embed = jax.vmap(lambda t: time_embed(t, freq))(steps)
    embed = jnp.concatenate([embed, jnp.zeros((5, freq), jnp.bfloat16)], axis=0)
    levels = steps[1:3].astype(jnp.float32) / 1000.0
    full, sent = gen_part(seq_at, core, embed, gen_heads, gen_out_w, gen_time_w, gen_resid, noise)
    arrived = exchange(sent, "seq", 1)
    planes = [w.transpose(1, 0, 2) for w in (teacher_qkv, critic_qkv, teacher_time, critic_time)]
    weight_a, weight_b, out_a, out_b, mods, gate = load_part(
        role_at, embed, full, planes[0], planes[1], teacher_out, critic_out, planes[2], planes[3], gen_time_w, roles
    )
    joined = join_part(full, arrived, gate)
    swapped = exchange(joined, "role", 1)
    first = first_part(seq_at, core, mine, levels, joined, swapped, noise, mods, weight_a)
    latent, noisy, squares = first[:3]
    second = second_part(mine, noisy, squares, mods, weight_b)

    start = role * part_cols
    unit = part_cols // groups
    gathered = []
    for chunks, gains in ((first[3:], teacher_norm), (second, critic_norm)):
        kept, sends = chunks[:2], chunks[2:]
        pieces = []
        for level in range(2):
            summed = both(kept[level], exchange(sends[level], "mp", 1))
            pieces.append((summed[0], exchange(summed[1].astype(jnp.bfloat16), "mp", 2)))
        gains = lax.dynamic_slice_in_dim(gains, start + mp * unit, unit, axis=1)
        head_out = attend_part(pieces, gains, D)
        near = exchange(head_out, "mp", 1)
        far = exchange(head_out, "mp", 2)
        gathered.append((head_out, near, far, exchange(far, "mp", 1)))

    kept, sent = out_part(core, mine, *gathered, out_a, out_b, mods)
    total = both(kept, exchange(sent, "role", 1)).astype(jnp.bfloat16)
    middle = length // 2
    top, low = total[:middle], total[middle:]
    top = both(top, exchange(top, "seq", 1)).astype(jnp.bfloat16)
    low = both(low, exchange(low, "role", 2)).astype(jnp.bfloat16)
    top = both(top, exchange(top, "role", 2))
    low = both(low, exchange(low, "seq", 1))
    gate_row = lax.dynamic_slice_in_dim(gate, core[0] * half_cols, half_cols, axis=1)[0:1]
    rows = (gate_row * jnp.concatenate([top, low], axis=0)).astype(jnp.bfloat16)
    heads_t = gen_heads.T
    theirs = exchange(rows, "role", 1)
    weight_grad = grad_part(core, heads_t, rows, None, 2)
    weight_grad = grad_part(1 - core, heads_t, theirs, weight_grad, 2)
    return latent, weight_grad


def solution(mesh):
    in_specs = (
        P(None, "seq"),
        P("seq", "mp"),
        P("seq", "mp"),
        P(None, "mp"),
        P("seq", "mp"),
        P(),
        P("mp", None, "seq"),
        P("seq", "mp"),
        P(None, None, "mp"),
        P(None, "seq"),
        P("mp", None, "seq"),
        P("seq", "mp"),
        P(None, None, "mp"),
        P(None, "seq"),
    )
    out_specs = (P("seq", "mp"), P("seq", "mp"))
    roles, seqs, groups = mesh.shape["role"], mesh.shape["seq"], mesh.shape["mp"]

    def on_device(*arrays):
        heads_here = arrays[0].shape[1] // HEAD_DIM
        length = arrays[0].shape[0]
        fits = (roles, seqs, groups) == (4, 2, 4) and heads_here == roles * groups and length == HEAD_DIM
        return heads_per_role(*arrays) if fits else pass_per_role(*arrays)

    return jax.shard_map(
        on_device, mesh=mesh, in_specs=in_specs, out_specs=out_specs, check_vma=False
    )
```

```python
import math

import jax
import jax.numpy as jnp
from jax import lax
from jax.experimental import pallas as pl
from jax.experimental.pallas import tpu as pltpu
from jax.sharding import PartitionSpec as P

D = 5120
HEAD_DIM = 128


def time_embed(step_value, width):
    half_width = width // 2
    positions = jnp.arange(half_width, dtype=jnp.float32)
    frequencies = jnp.exp(positions * (-math.log(10000.0) / half_width))
    angles = step_value.astype(jnp.float32) * frequencies
    return jnp.concatenate([jnp.cos(angles), jnp.sin(angles)]).astype(jnp.bfloat16)


def head_norm(values, gains):
    factor = lax.rsqrt(jnp.mean(values * values, axis=-1, keepdims=True) + 1e-06)
    return (values * factor * gains).astype(jnp.bfloat16)


def attend(query_norm, key_norm, value_rows):
    full_length, heads_here, head_width = query_norm.shape
    query_blocks = query_norm.reshape(
        full_length // full_length, full_length, heads_here, head_width
    )

    def one_block(query_block):
        logits = jnp.einsum(
            "qhd,khd->hqk", query_block, key_norm, preferred_element_type=jnp.float32
        ) * (1.0 / math.sqrt(head_width))
        expanded = jnp.exp(logits)
        probs = (expanded / jnp.sum(expanded, axis=2, keepdims=True)).astype(jnp.bfloat16)
        return jnp.einsum(
            "hqk,khd->qhd", probs, value_rows, preferred_element_type=jnp.float32
        ).astype(jnp.bfloat16)

    head_out = lax.map(one_block, query_blocks)
    return head_out.reshape(full_length, heads_here * head_width)


def pass_per_role(
    gen_heads,
    gen_resid,
    gen_out_w,
    gen_time_w,
    noise,
    steps,
    teacher_qkv,
    teacher_out,
    teacher_time,
    teacher_norm,
    critic_qkv,
    critic_out,
    critic_time,
    critic_norm,
):
    full_length = gen_heads.shape[0]
    head_cols = gen_heads.shape[1]
    embed_width = gen_time_w.shape[0]
    gen_gate = jnp.dot(
        time_embed(steps[0], embed_width)[None, :], gen_time_w, preferred_element_type=jnp.float32
    )[0]
    block = gen_heads
    gen_proj = lax.psum_scatter(
        jnp.dot(block, gen_out_w, preferred_element_type=jnp.float32),
        "seq",
        scatter_dimension=0,
        tiled=True,
    )
    latent = (gen_resid.astype(jnp.float32) + gen_gate * gen_proj).astype(jnp.bfloat16)
    role_index = lax.axis_index("role")
    level = steps[1 + role_index // 2]
    use_critic = role_index % 2 == 1
    w_qkv = jnp.where(use_critic, critic_qkv, teacher_qkv)
    w_out = jnp.where(use_critic, critic_out, teacher_out)
    w_time = jnp.where(use_critic, critic_time, teacher_time)
    w_norm = jnp.where(use_critic, critic_norm, teacher_norm)
    noise_level = level.astype(jnp.float32) / 1000.0
    noisy = (
        (1.0 - noise_level) * latent.astype(jnp.float32) + noise_level * noise.astype(jnp.float32)
    ).astype(jnp.bfloat16)
    modulation = jnp.einsum(
        "f,fkd->kd", time_embed(level, embed_width), w_time, preferred_element_type=jnp.float32
    )
    shift_vec = modulation[0]
    scale_vec = modulation[1]
    gate_vec = modulation[2]
    gathered = lax.all_gather(noisy, "seq", axis=0, tiled=True)
    partial_squares = jnp.sum(jnp.square(gathered.astype(jnp.float32)), axis=1)
    scaled = (gathered.astype(jnp.float32) * (1.0 + scale_vec)).astype(jnp.bfloat16)
    flat_w = w_qkv.reshape(w_qkv.shape[0], 3 * head_cols)
    projected = jnp.dot(scaled, flat_w, preferred_element_type=jnp.float32)
    shift_proj = jnp.dot(
        shift_vec.astype(jnp.bfloat16)[None, :], flat_w, preferred_element_type=jnp.float32
    )[0]
    projected, squares, shift_proj = lax.psum((projected, partial_squares, shift_proj), "mp")
    mixed = projected * lax.rsqrt(squares / D + 1e-06)[:, None] + shift_proj
    heads_here = head_cols // HEAD_DIM
    mixed = mixed.reshape(full_length, 3, heads_here, HEAD_DIM)
    gains = w_norm.reshape(2, heads_here, HEAD_DIM)
    query_norm = head_norm(mixed[:, 0], gains[0])
    key_norm = head_norm(mixed[:, 1], gains[1])
    value_rows = mixed[:, 2].astype(jnp.bfloat16)
    head_out = attend(query_norm, key_norm, value_rows)
    weight_sign = jnp.where(use_critic, 0.5, -0.5)
    block = head_out
    summed_rows = lax.psum_scatter(
        weight_sign * (gate_vec * jnp.dot(block, w_out, preferred_element_type=jnp.float32)),
        ("role", "seq"),
        scatter_dimension=0,
        tiled=True,
    )
    grad_rows = lax.all_gather(
        (gen_gate * summed_rows).astype(jnp.bfloat16), ("role", "seq"), axis=0, tiled=True
    )
    weight_grad = lax.dot_general(
        gen_heads, grad_rows, (((0,), (0,)), ((), ())), preferred_element_type=jnp.float32
    )
    return (latent, weight_grad.astype(jnp.bfloat16))

MIB = 1024 * 1024
EXTRA_ROWS = 16


def vmem_spec():
    return pl.BlockSpec(memory_space=pltpu.VMEM)


def smem_spec():
    return pl.BlockSpec(memory_space=pltpu.SMEM)


def params(mebibytes):
    return pltpu.CompilerParams(vmem_limit_bytes=mebibytes * MIB)


def dot32(a, b):
    return jnp.dot(a, b, preferred_element_type=jnp.float32)


def at_block(index, size):
    return pl.ds(pl.multiple_of(index * size, size), size)


def any_spec():
    return pl.BlockSpec(memory_space=pl.ANY)


def hbm_spec():
    return pl.BlockSpec(memory_space=pltpu.HBM)


def cost(flops, moved):
    return pl.CostEstimate(flops=flops, bytes_accessed=moved, transcendentals=0)


GEN_CUTS = 4


def gen_kernel(seq, core, embed, heads, weight, time_w, resid, noise, full, sent, heads_v, weight_v, time_v, resid_v, sems):
    length, width = full.shape
    own = resid_v.shape[0]
    cols = at_block(core[0], width)
    tile = weight_v.shape[0] // GEN_CUTS
    copies = [pltpu.make_async_copy(heads, heads_v, sems.at[GEN_CUTS])]
    for k in range(GEN_CUTS):
        rows = pl.ds(k * tile, tile)
        copies.append(pltpu.make_async_copy(weight.at[rows, cols], weight_v.at[rows, :], sems.at[k]))
    copies.append(pltpu.make_async_copy(time_w.at[:, cols], time_v, sems.at[GEN_CUTS + 1]))
    copies.append(pltpu.make_async_copy(resid.at[:, cols], resid_v, sems.at[GEN_CUTS + 2]))
    copies.append(pltpu.make_async_copy(noise.at[:, cols], sent.at[pl.ds(length, own), :], sems.at[GEN_CUTS + 3]))
    for copy in copies:
        copy.start()
    copies[0].wait()
    total = None
    for k in range(GEN_CUTS):
        copies[1 + k].wait()
        rows = pl.ds(k * tile, tile)
        term = dot32(heads_v[:, rows], weight_v[rows, :])
        total = term if total is None else total + term
    for copy in copies[1 + GEN_CUTS :]:
        copy.wait()
    full[...] = total * dot32(embed[...], time_v[...])[0:1]
    at = at_block(seq[0], own)
    full[at, :] = full[at, :] + resid_v[...].astype(jnp.float32)
    sent[pl.ds(0, length), :] = full[...].astype(jnp.bfloat16)


def gen_part(seq, core, embed, heads, weight, time_w, resid, noise):
    length, depth = heads.shape
    width = weight.shape[1] // 2
    freq = time_w.shape[0]
    own = resid.shape[0]
    return pl.pallas_call(
        gen_kernel,
        in_specs=[smem_spec(), smem_spec(), vmem_spec()] + [hbm_spec()] * 5,
        out_specs=[vmem_spec()] * 2,
        out_shape=[
            jax.ShapeDtypeStruct((length, width), jnp.float32),
            jax.ShapeDtypeStruct((length + own, width), jnp.bfloat16),
        ],
        scratch_shapes=[
            pltpu.VMEM((length, depth), jnp.bfloat16),
            pltpu.VMEM((depth, width), jnp.bfloat16),
            pltpu.VMEM((freq, width), jnp.bfloat16),
            pltpu.VMEM((own, width), jnp.bfloat16),
            pltpu.SemaphoreType.DMA((GEN_CUTS + 4,)),
        ],
        compiler_params=params(56),
        name="gen_part",
    )(seq, core, embed, heads, weight, time_w, resid, noise)


def mod_kernel(embed, time_a, time_b, time_w, after, mods, gate):
    gate[...] = dot32(embed[...], time_w[...])
    for k in range(3):
        mods[0, k] = dot32(embed[...], time_a[k])
        mods[1, k] = dot32(embed[...], time_b[k])


def mod_part(embed, time_a, time_b, time_w, after):
    width = time_a.shape[2]
    moved = 2 * (time_a.size + time_b.size + time_w.size)
    return pl.pallas_call(
        mod_kernel,
        in_specs=[vmem_spec()] * 4 + [any_spec()],
        out_specs=[vmem_spec()] * 2,
        out_shape=[
            jax.ShapeDtypeStruct((2, 3, 8, width), jnp.float32),
            jax.ShapeDtypeStruct((8, width), jnp.float32),
        ],
        compiler_params=params(16),
        cost_estimate=cost(8 * moved, moved),
        name="mod_part",
    )(embed, time_a, time_b, time_w, after)


def join_kernel(full, arrived, after, joined):
    length = full.shape[0]
    own = arrived.shape[0] - length
    top = full[...] + arrived[pl.ds(0, length), :].astype(jnp.float32)
    joined[pl.ds(0, length), :] = top.astype(jnp.bfloat16)
    joined[pl.ds(length, own), :] = arrived[pl.ds(length, own), :]


def join_part(full, arrived, after):
    return pl.pallas_call(
        join_kernel,
        in_specs=[vmem_spec(), vmem_spec(), any_spec()],
        out_specs=vmem_spec(),
        out_shape=jax.ShapeDtypeStruct(arrived.shape, jnp.bfloat16),
        compiler_params=params(8),
        name="join_part",
    )(full, arrived, after)


def project(index, mine, noisy, squares, mods, weight, copies, kept, sent, result):
    tokens = noisy.shape[0]
    length = tokens // 2
    unit = squares.shape[1] // 2
    groups = weight.shape[2] // unit
    scale = mods[index, 1]
    shift = mods[index, 0]
    spread = noisy.astype(jnp.float32)
    top = spread[:length] * (1.0 + scale[1:2])
    low = spread[length:] * (1.0 + scale[2:3])
    extra = jnp.concatenate([shift[1:3], jnp.zeros((EXTRA_ROWS - 2, shift.shape[1]), jnp.float32)], axis=0)
    rows = jnp.concatenate([top, low, extra], axis=0).astype(jnp.bfloat16)
    row_id = lax.broadcasted_iota(jnp.int32, (EXTRA_ROWS, unit), 0)
    for part in range(3):
        copies[part].wait()
        result[...] = dot32(rows, weight[part])
        cols = pl.ds(part * unit, unit)
        for slot in range(groups):
            at = at_block(jnp.bitwise_xor(mine, slot), unit)
            goal = sent if slot % 2 else kept
            for level in range(2):
                goal[level][slot // 2, pl.ds(0, length), cols] = result[pl.ds(level * length, length), at].astype(
                    jnp.bfloat16
                )
            tail = jnp.where(row_id < 2, result[pl.ds(tokens, EXTRA_ROWS), at], 0.0)
            for level in range(2):
                tail = jnp.where(row_id == 2 + level, squares[0:1, level * length : (level + 1) * length], tail)
            goal[0][slot // 2, pl.ds(length, EXTRA_ROWS), cols] = tail.astype(jnp.bfloat16)


def weight_copies(role, planes, weight, sems):
    cols = at_block(role[0], weight.shape[3])
    copies = [
        [
            pltpu.make_async_copy(planes[index].at[part, :, cols], weight.at[index, part], sems.at[3 * index + part])
            for part in range(3)
        ]
        for index in range(2)
    ]
    for copy in copies[0] + copies[1]:
        copy.start()
    return copies


def qkv_kernel(role, seq, core, mine, levels, joined, swapped, noise, mods, planes_a, planes_b, latent, *refs):
    chunks, (values, noises, result, weight, sems) = refs[:8], refs[8:]
    copies = weight_copies(role, (planes_a, planes_b), weight, sems)
    length, cols = values.shape[0], joined.shape[1]
    own = latent.shape[0]
    tokens = 2 * length
    left, right = at_block(core[0], cols), at_block(1 - core[0], cols)
    values[:, left] = joined[pl.ds(0, length), :]
    values[:, right] = swapped[pl.ds(0, length), :]
    latent[...] = values[at_block(seq[0], own), :]
    noises[at_block(seq[0], own), :] = noise[...]
    theirs = at_block(1 - seq[0], own)
    noises[theirs, left] = joined[pl.ds(length, own), :]
    noises[theirs, right] = swapped[pl.ds(length, own), :]
    spread = values[...].astype(jnp.float32)
    noise_rows = noises[...].astype(jnp.float32)
    mixed = jnp.concatenate(
        [(1.0 - levels[level]) * spread + levels[level] * noise_rows for level in range(2)], axis=0
    ).astype(jnp.bfloat16)
    wide = mixed.astype(jnp.float32)
    sums = jnp.sum(wide * wide, axis=1, keepdims=True)
    sums = jnp.broadcast_to(sums, (tokens, length)).T[0:8]
    for index in range(2):
        kept, sent = chunks[4 * index : 4 * index + 2], chunks[4 * index + 2 : 4 * index + 4]
        project(index, mine[0], mixed, sums, mods, weight.at[index], copies[index], kept, sent, result)


def chunk_shapes(length, cols):
    groups = cols // length
    shapes = [
        jax.ShapeDtypeStruct((groups // 2, rows, 3 * length), jnp.bfloat16) for rows in (length + EXTRA_ROWS, length)
    ]
    return shapes * 2


def qkv_part(role, seq, core, mine, levels, joined, swapped, noise, mods, planes_a, planes_b, cols):
    own, width = noise.shape
    length = joined.shape[0] - own
    tokens = 2 * length
    return pl.pallas_call(
        qkv_kernel,
        in_specs=[smem_spec()] * 5 + [vmem_spec()] * 4 + [hbm_spec()] * 2,
        out_specs=[vmem_spec()] * 9,
        out_shape=[jax.ShapeDtypeStruct((own, width), jnp.bfloat16)] + chunk_shapes(length, cols) * 2,
        scratch_shapes=[
            pltpu.VMEM((length, width), jnp.bfloat16),
            pltpu.VMEM((length, width), jnp.bfloat16),
            pltpu.VMEM((tokens + EXTRA_ROWS, cols), jnp.float32),
            pltpu.VMEM((2, 3, width, cols), jnp.bfloat16),
            pltpu.SemaphoreType.DMA((6,)),
        ],
        compiler_params=params(48),
        name="qkv_part",
    )(role, seq, core, mine, levels, joined, swapped, noise, mods, planes_a, planes_b)


def add_kernel(mine, theirs, *refs):
    kept, sent = refs[-3:-1] if len(refs) > 2 else refs
    kept[...] = mine[0].astype(jnp.float32) + theirs[0].astype(jnp.float32)
    sent[...] = (mine[1].astype(jnp.float32) + theirs[1].astype(jnp.float32)).astype(jnp.bfloat16)


def add_part(mine, theirs, later=None):
    rest = [] if later is None else [later]
    shape = mine.shape[1:]
    return pl.pallas_call(
        add_kernel,
        in_specs=[vmem_spec()] * 2 + [any_spec()] * len(rest),
        out_specs=[vmem_spec()] * 2 + [any_spec()] * len(rest),
        out_shape=[jax.ShapeDtypeStruct(shape, jnp.float32), jax.ShapeDtypeStruct(shape, jnp.bfloat16)]
        + [jax.ShapeDtypeStruct(x.shape, x.dtype) for x in rest],
        input_output_aliases={2: 2} if rest else {},
        compiler_params=params(8),
        name="add_part",
    )(mine, theirs, *rest)


def attend_kernel(width, kept_a, other_a, kept_b, other_b, gains, after, out):
    _, length, unit = out.shape
    extra = None
    for level, (kept, other) in enumerate(((kept_a, other_a), (kept_b, other_b))):
        mixed = kept[...] + other[...].astype(jnp.float32)
        if level == 0:
            extra = mixed[length:]
        squares = jnp.broadcast_to(extra[2 + level : 3 + level, :unit], (unit, unit)).T
        factor = lax.rsqrt(squares * (1.0 / width) + 1e-06)

        def pick(part):
            cols = slice(part * unit, (part + 1) * unit)
            return mixed[:length, cols] * factor + extra[level : level + 1, cols]

        def normed(part):
            rows = pick(part)
            mean = jnp.mean(rows * rows, axis=1, keepdims=True)
            return (rows * lax.rsqrt(mean + 1e-06) * gains[part : part + 1, :]).astype(jnp.bfloat16)

        query, key = normed(0), normed(1)
        value = pick(2).astype(jnp.bfloat16)
        logits = lax.dot_general(
            query, key, (((1,), (1,)), ((), ())), preferred_element_type=jnp.float32
        ) * (1.0 / math.sqrt(unit))
        expanded = jnp.exp(logits)
        probs = (expanded / jnp.sum(expanded, axis=1, keepdims=True)).astype(jnp.bfloat16)
        out[level] = dot32(probs, value).astype(jnp.bfloat16)


def attend_part(chunks, gains, after, width):
    kept_a, kept_b = chunks[0][0], chunks[1][0]
    unit = kept_a.shape[1] // 3
    length = kept_a.shape[0] - EXTRA_ROWS
    return pl.pallas_call(
        lambda *refs: attend_kernel(width, *refs),
        in_specs=[vmem_spec()] * 5 + [any_spec()],
        out_specs=vmem_spec(),
        out_shape=jax.ShapeDtypeStruct((2, length, unit), jnp.bfloat16),
        compiler_params=params(8),
        name="attend_part",
    )(kept_a, chunks[0][1], kept_b, chunks[1][1], gains, after)


def out_kernel(core, mine, *refs):
    heads_a, heads_b = refs[0:4], refs[4:8]
    weight_a, weight_b, mods, kept, sent, rows, total = refs[8:]
    _, length, unit = heads_a[0].shape
    for index, (heads, weight) in enumerate(((heads_a, weight_a), (heads_b, weight_b))):
        for slot, head in enumerate(heads):
            at = at_block(jnp.bitwise_xor(mine[0], slot), unit)
            for level in range(2):
                rows[pl.ds(level * length, length), at] = head[level]
        result = dot32(rows[...], weight[...])
        gates = mods[index, 2]
        signed = gates[1:2] * result[:length] + gates[2:3] * result[length:]
        if index == 0:
            total[...] = -0.5 * signed
        else:
            total[...] = total[...] + 0.5 * signed
    cols = kept.shape[1]
    kept[...] = total[:, at_block(core[0], cols)]
    sent[...] = total[:, at_block(1 - core[0], cols)].astype(jnp.bfloat16)


def out_part(core, mine, heads_a, heads_b, weight_a, weight_b, mods):
    _, length, unit = heads_a[0].shape
    depth, width = weight_a.shape
    return pl.pallas_call(
        out_kernel,
        in_specs=[smem_spec()] * 2 + [vmem_spec()] * 11,
        out_specs=[vmem_spec()] * 2,
        out_shape=[
            jax.ShapeDtypeStruct((length, width // 2), jnp.float32),
            jax.ShapeDtypeStruct((length, width // 2), jnp.bfloat16),
        ],
        scratch_shapes=[
            pltpu.VMEM((2 * length, depth), jnp.bfloat16),
            pltpu.VMEM((length, width), jnp.float32),
        ],
        compiler_params=params(16),
        name="out_part",
    )(core, mine, *heads_a, *heads_b, weight_a, weight_b, mods)


def grad_kernel(half, heads_t, rows, *refs):
    refs[-1][...] = dot32(heads_t[...], rows[...]).astype(jnp.bfloat16)


def grad_part(half, heads_t, rows, before, steps):
    depth, length = heads_t.shape
    cols = rows.shape[1]
    tile = depth // steps
    rest = [] if before is None else [before]
    grid_spec = pltpu.PrefetchScalarGridSpec(
        num_scalar_prefetch=1,
        grid=(steps,),
        in_specs=[
            pl.BlockSpec((tile, length), lambda n, w: (n, 0)),
            pl.BlockSpec((length, cols), lambda n, w: (0, 0)),
        ]
        + [any_spec()] * len(rest),
        out_specs=pl.BlockSpec((tile, cols), lambda n, w: (n, w[0])),
    )
    return pl.pallas_call(
        grad_kernel,
        grid_spec=grid_spec,
        out_shape=jax.ShapeDtypeStruct((depth, 2 * cols), jnp.bfloat16),
        input_output_aliases={3: 0} if rest else {},
        compiler_params=params(24),
        name="grad_part",
    )(half, heads_t, rows, *rest)


def exchange(array, axis, bit):
    return lax.ppermute(array, axis, [(i, i ^ bit) for i in range(lax.axis_size(axis))])


def both(mine, theirs):
    return mine.astype(jnp.float32) + theirs.astype(jnp.float32)


def heads_per_role(
    gen_heads,
    gen_resid,
    gen_out_w,
    gen_time_w,
    noise,
    steps,
    teacher_qkv,
    teacher_out,
    teacher_time,
    teacher_norm,
    critic_qkv,
    critic_out,
    critic_time,
    critic_norm,
):
    length = gen_heads.shape[0]
    roles, groups = lax.axis_size("role"), lax.axis_size("mp")
    role, seq, mp = lax.axis_index("role"), lax.axis_index("seq"), lax.axis_index("mp")
    part_cols = gen_heads.shape[1] // roles
    freq = gen_time_w.shape[0]
    role_at, seq_at, mine = [v.astype(jnp.int32).reshape(1) for v in (role, seq, mp)]
    core = role_at % 2
    half_cols = gen_resid.shape[1] // 2

    embed = jax.vmap(lambda t: time_embed(t, freq))(steps)
    embed = jnp.concatenate([embed, jnp.zeros((5, freq), jnp.bfloat16)], axis=0)
    levels = steps[1:3].astype(jnp.float32) / 1000.0
    full, sent = gen_part(seq_at, core, embed, gen_heads, gen_out_w, gen_time_w, gen_resid, noise)
    arrived = exchange(sent, "seq", 1)
    planes = [w.transpose(1, 0, 2) for w in (teacher_qkv, critic_qkv, teacher_time, critic_time)]
    mods, gate = mod_part(embed, planes[2], planes[3], gen_time_w, full)
    joined = join_part(full, arrived, gate)
    swapped = exchange(joined, "role", 1)
    start = role * part_cols
    out_a, out_b = [lax.dynamic_slice_in_dim(w, start, part_cols, axis=0) for w in (teacher_out, critic_out)]
    unit = part_cols // groups
    gains = [lax.dynamic_slice_in_dim(g, start + mp * unit, unit, axis=1) for g in (teacher_norm, critic_norm)]

    latent, *chunks = qkv_part(
        role_at, seq_at, core, mine, levels, joined, swapped, noise, mods, planes[0], planes[1], part_cols
    )
    first, second = chunks[:4], chunks[4:]
    kept_a, send_a, third = add_part(first[0], exchange(first[2], "mp", 1), second[2])
    kept_b, send_b, last = add_part(first[1], exchange(first[3], "mp", 1), second[3])
    kept_c, send_c = add_part(second[0], exchange(third, "mp", 1))
    kept_d, send_d = add_part(second[1], exchange(last, "mp", 1))
    sums = [(kept, exchange(send, "mp", 2)) for kept, send in ((kept_a, send_a), (kept_b, send_b))]
    head_a = attend_part(sums, gains[0], out_a, D)
    sums = [(kept, exchange(send, "mp", 2)) for kept, send in ((kept_c, send_c), (kept_d, send_d))]
    head_b = attend_part(sums, gains[1], out_b, D)
    gathered = [[head] + [exchange(head, "mp", bits) for bits in range(1, groups)] for head in (head_a, head_b)]

    kept, sent = out_part(core, mine, *gathered, out_a, out_b, mods)
    total = both(kept, exchange(sent, "role", 1)).astype(jnp.bfloat16)
    along_x = exchange(total, "seq", 1)
    along_y = exchange(total, "role", 2)
    across = lax.ppermute(
        total, ("role", "seq"), [(i, i ^ (2 * lax.axis_size("seq") + 1)) for i in range(roles * lax.axis_size("seq"))]
    )
    total = both(total, along_x) + both(along_y, across)
    gate_row = lax.dynamic_slice_in_dim(gate, core[0] * half_cols, half_cols, axis=1)[0:1]
    rows = (gate_row * total).astype(jnp.bfloat16)
    heads_t = gen_heads.T
    theirs = exchange(rows, "role", 1)
    weight_grad = grad_part(core, heads_t, rows, None, 2)
    weight_grad = grad_part(1 - core, heads_t, theirs, weight_grad, 2)
    return latent, weight_grad


def solution(mesh):
    in_specs = (
        P(None, "seq"),
        P("seq", "mp"),
        P("seq", "mp"),
        P(None, "mp"),
        P("seq", "mp"),
        P(),
        P("mp", None, "seq"),
        P("seq", "mp"),
        P(None, None, "mp"),
        P(None, "seq"),
        P("mp", None, "seq"),
        P("seq", "mp"),
        P(None, None, "mp"),
        P(None, "seq"),
    )
    out_specs = (P("seq", "mp"), P("seq", "mp"))
    roles, seqs, groups = mesh.shape["role"], mesh.shape["seq"], mesh.shape["mp"]

    def on_device(*arrays):
        heads_here = arrays[0].shape[1] // HEAD_DIM
        length = arrays[0].shape[0]
        fits = (roles, seqs, groups) == (4, 2, 4) and heads_here == roles * groups and length == HEAD_DIM
        return heads_per_role(*arrays) if fits else pass_per_role(*arrays)

    return jax.shard_map(
        on_device, mesh=mesh, in_specs=in_specs, out_specs=out_specs, check_vma=False
    )
```

```python
import math

import jax
import jax.numpy as jnp
from jax import lax
from jax.experimental import pallas as pl
from jax.experimental.pallas import tpu as pltpu
from jax.sharding import PartitionSpec as P

D = 5120
HEAD_DIM = 128


def time_embed(step_value, width):
    half_width = width // 2
    positions = jnp.arange(half_width, dtype=jnp.float32)
    frequencies = jnp.exp(positions * (-math.log(10000.0) / half_width))
    angles = step_value.astype(jnp.float32) * frequencies
    return jnp.concatenate([jnp.cos(angles), jnp.sin(angles)]).astype(jnp.bfloat16)


def head_norm(values, gains):
    factor = lax.rsqrt(jnp.mean(values * values, axis=-1, keepdims=True) + 1e-06)
    return (values * factor * gains).astype(jnp.bfloat16)


def attend(query_norm, key_norm, value_rows):
    full_length, heads_here, head_width = query_norm.shape
    query_blocks = query_norm.reshape(
        full_length // full_length, full_length, heads_here, head_width
    )

    def one_block(query_block):
        logits = jnp.einsum(
            "qhd,khd->hqk", query_block, key_norm, preferred_element_type=jnp.float32
        ) * (1.0 / math.sqrt(head_width))
        expanded = jnp.exp(logits)
        probs = (expanded / jnp.sum(expanded, axis=2, keepdims=True)).astype(jnp.bfloat16)
        return jnp.einsum(
            "hqk,khd->qhd", probs, value_rows, preferred_element_type=jnp.float32
        ).astype(jnp.bfloat16)

    head_out = lax.map(one_block, query_blocks)
    return head_out.reshape(full_length, heads_here * head_width)


def pass_per_role(
    gen_heads,
    gen_resid,
    gen_out_w,
    gen_time_w,
    noise,
    steps,
    teacher_qkv,
    teacher_out,
    teacher_time,
    teacher_norm,
    critic_qkv,
    critic_out,
    critic_time,
    critic_norm,
):
    full_length = gen_heads.shape[0]
    head_cols = gen_heads.shape[1]
    embed_width = gen_time_w.shape[0]
    gen_gate = jnp.dot(
        time_embed(steps[0], embed_width)[None, :], gen_time_w, preferred_element_type=jnp.float32
    )[0]
    block = gen_heads
    gen_proj = lax.psum_scatter(
        jnp.dot(block, gen_out_w, preferred_element_type=jnp.float32),
        "seq",
        scatter_dimension=0,
        tiled=True,
    )
    latent = (gen_resid.astype(jnp.float32) + gen_gate * gen_proj).astype(jnp.bfloat16)
    role_index = lax.axis_index("role")
    level = steps[1 + role_index // 2]
    use_critic = role_index % 2 == 1
    w_qkv = jnp.where(use_critic, critic_qkv, teacher_qkv)
    w_out = jnp.where(use_critic, critic_out, teacher_out)
    w_time = jnp.where(use_critic, critic_time, teacher_time)
    w_norm = jnp.where(use_critic, critic_norm, teacher_norm)
    noise_level = level.astype(jnp.float32) / 1000.0
    noisy = (
        (1.0 - noise_level) * latent.astype(jnp.float32) + noise_level * noise.astype(jnp.float32)
    ).astype(jnp.bfloat16)
    modulation = jnp.einsum(
        "f,fkd->kd", time_embed(level, embed_width), w_time, preferred_element_type=jnp.float32
    )
    shift_vec = modulation[0]
    scale_vec = modulation[1]
    gate_vec = modulation[2]
    gathered = lax.all_gather(noisy, "seq", axis=0, tiled=True)
    partial_squares = jnp.sum(jnp.square(gathered.astype(jnp.float32)), axis=1)
    scaled = (gathered.astype(jnp.float32) * (1.0 + scale_vec)).astype(jnp.bfloat16)
    flat_w = w_qkv.reshape(w_qkv.shape[0], 3 * head_cols)
    projected = jnp.dot(scaled, flat_w, preferred_element_type=jnp.float32)
    shift_proj = jnp.dot(
        shift_vec.astype(jnp.bfloat16)[None, :], flat_w, preferred_element_type=jnp.float32
    )[0]
    projected, squares, shift_proj = lax.psum((projected, partial_squares, shift_proj), "mp")
    mixed = projected * lax.rsqrt(squares / D + 1e-06)[:, None] + shift_proj
    heads_here = head_cols // HEAD_DIM
    mixed = mixed.reshape(full_length, 3, heads_here, HEAD_DIM)
    gains = w_norm.reshape(2, heads_here, HEAD_DIM)
    query_norm = head_norm(mixed[:, 0], gains[0])
    key_norm = head_norm(mixed[:, 1], gains[1])
    value_rows = mixed[:, 2].astype(jnp.bfloat16)
    head_out = attend(query_norm, key_norm, value_rows)
    weight_sign = jnp.where(use_critic, 0.5, -0.5)
    block = head_out
    summed_rows = lax.psum_scatter(
        weight_sign * (gate_vec * jnp.dot(block, w_out, preferred_element_type=jnp.float32)),
        ("role", "seq"),
        scatter_dimension=0,
        tiled=True,
    )
    grad_rows = lax.all_gather(
        (gen_gate * summed_rows).astype(jnp.bfloat16), ("role", "seq"), axis=0, tiled=True
    )
    weight_grad = lax.dot_general(
        gen_heads, grad_rows, (((0,), (0,)), ((), ())), preferred_element_type=jnp.float32
    )
    return (latent, weight_grad.astype(jnp.bfloat16))

MIB = 1024 * 1024
EXTRA_ROWS = 16


def vmem_spec():
    return pl.BlockSpec(memory_space=pltpu.VMEM)


def smem_spec():
    return pl.BlockSpec(memory_space=pltpu.SMEM)


def params(mebibytes):
    return pltpu.CompilerParams(vmem_limit_bytes=mebibytes * MIB)


def dot32(a, b):
    return jnp.dot(a, b, preferred_element_type=jnp.float32)


def at_block(index, size):
    return pl.ds(pl.multiple_of(index * size, size), size)


def any_spec():
    return pl.BlockSpec(memory_space=pl.ANY)


def hbm_spec():
    return pl.BlockSpec(memory_space=pltpu.HBM)


def cost(flops, moved):
    return pl.CostEstimate(flops=flops, bytes_accessed=moved, transcendentals=0)


GEN_CUTS = 4
AHEAD = 2


def gen_kernel(seq, core, embed, heads, weight, time_w, resid, noise, full, sent, heads_v, weight_v, time_v, resid_v, sems):
    length, width = full.shape
    own = resid_v.shape[0]
    cols = at_block(core[0], width)
    tile = weight_v.shape[0] // GEN_CUTS
    copies = [pltpu.make_async_copy(heads, heads_v, sems.at[GEN_CUTS])]
    for k in range(GEN_CUTS):
        rows = pl.ds(k * tile, tile)
        copies.append(pltpu.make_async_copy(weight.at[rows, cols], weight_v.at[rows, :], sems.at[k]))
    copies.append(pltpu.make_async_copy(time_w.at[:, cols], time_v, sems.at[GEN_CUTS + 1]))
    copies.append(pltpu.make_async_copy(resid.at[:, cols], resid_v, sems.at[GEN_CUTS + 2]))
    copies.append(pltpu.make_async_copy(noise.at[:, cols], sent.at[pl.ds(length, own), :], sems.at[GEN_CUTS + 3]))
    for copy in copies[: 1 + AHEAD]:
        copy.start()
    copies[0].wait()
    total = None
    for k in range(GEN_CUTS):
        copies[1 + k].wait()
        following = copies[1 + k + AHEAD : 2 + k + AHEAD] if k + AHEAD < GEN_CUTS - 1 else copies[GEN_CUTS:]
        for copy in following if k + AHEAD < GEN_CUTS else []:
            copy.start()
        rows = pl.ds(k * tile, tile)
        term = dot32(heads_v[:, rows], weight_v[rows, :])
        total = term if total is None else total + term
    for copy in copies[1 + GEN_CUTS :]:
        copy.wait()
    full[...] = total * dot32(embed[...], time_v[...])[0:1]
    at = at_block(seq[0], own)
    full[at, :] = full[at, :] + resid_v[...].astype(jnp.float32)
    sent[pl.ds(0, length), :] = full[...].astype(jnp.bfloat16)


def gen_part(seq, core, embed, heads, weight, time_w, resid, noise):
    length, depth = heads.shape
    width = weight.shape[1] // 2
    freq = time_w.shape[0]
    own = resid.shape[0]
    return pl.pallas_call(
        gen_kernel,
        in_specs=[smem_spec(), smem_spec(), vmem_spec()] + [hbm_spec()] * 5,
        out_specs=[vmem_spec()] * 2,
        out_shape=[
            jax.ShapeDtypeStruct((length, width), jnp.float32),
            jax.ShapeDtypeStruct((length + own, width), jnp.bfloat16),
        ],
        scratch_shapes=[
            pltpu.VMEM((length, depth), jnp.bfloat16),
            pltpu.VMEM((depth, width), jnp.bfloat16),
            pltpu.VMEM((freq, width), jnp.bfloat16),
            pltpu.VMEM((own, width), jnp.bfloat16),
            pltpu.SemaphoreType.DMA((GEN_CUTS + 4,)),
        ],
        compiler_params=params(56),
        name="gen_part",
    )(seq, core, embed, heads, weight, time_w, resid, noise)


def mod_kernel(embed, time_a, time_b, time_w, after, mods, gate):
    gate[...] = dot32(embed[...], time_w[...])
    for k in range(3):
        mods[0, k] = dot32(embed[...], time_a[k])
        mods[1, k] = dot32(embed[...], time_b[k])


def mod_part(embed, time_a, time_b, time_w, after):
    width = time_a.shape[2]
    moved = 2 * (time_a.size + time_b.size + time_w.size)
    return pl.pallas_call(
        mod_kernel,
        in_specs=[vmem_spec()] * 4 + [any_spec()],
        out_specs=[vmem_spec()] * 2,
        out_shape=[
            jax.ShapeDtypeStruct((2, 3, 8, width), jnp.float32),
            jax.ShapeDtypeStruct((8, width), jnp.float32),
        ],
        compiler_params=params(16),
        cost_estimate=cost(8 * moved, moved),
        name="mod_part",
    )(embed, time_a, time_b, time_w, after)


def join_kernel(full, arrived, after, joined):
    length = full.shape[0]
    own = arrived.shape[0] - length
    top = full[...] + arrived[pl.ds(0, length), :].astype(jnp.float32)
    joined[pl.ds(0, length), :] = top.astype(jnp.bfloat16)
    joined[pl.ds(length, own), :] = arrived[pl.ds(length, own), :]


def join_part(full, arrived, after):
    return pl.pallas_call(
        join_kernel,
        in_specs=[vmem_spec(), vmem_spec(), any_spec()],
        out_specs=vmem_spec(),
        out_shape=jax.ShapeDtypeStruct(arrived.shape, jnp.bfloat16),
        compiler_params=params(8),
        name="join_part",
    )(full, arrived, after)


def project(index, mine, noisy, squares, mods, weight, copies, kept, sent, result):
    tokens = noisy.shape[0]
    length = tokens // 2
    unit = squares.shape[1] // 2
    groups = weight.shape[2] // unit
    scale = mods[index, 1]
    shift = mods[index, 0]
    spread = noisy.astype(jnp.float32)
    top = spread[:length] * (1.0 + scale[1:2])
    low = spread[length:] * (1.0 + scale[2:3])
    extra = jnp.concatenate([shift[1:3], jnp.zeros((EXTRA_ROWS - 2, shift.shape[1]), jnp.float32)], axis=0)
    rows = jnp.concatenate([top, low, extra], axis=0).astype(jnp.bfloat16)
    row_id = lax.broadcasted_iota(jnp.int32, (EXTRA_ROWS, unit), 0)
    for part in range(3):
        turn = 3 * index + part
        copies[turn].wait()
        if turn + AHEAD < len(copies):
            copies[turn + AHEAD].start()
        result[...] = dot32(rows, weight[part])
        cols = pl.ds(part * unit, unit)
        for slot in range(groups):
            at = at_block(jnp.bitwise_xor(mine, slot), unit)
            goal = sent if slot % 2 else kept
            for level in range(2):
                goal[level][slot // 2, pl.ds(0, length), cols] = result[pl.ds(level * length, length), at].astype(
                    jnp.bfloat16
                )
            tail = jnp.where(row_id < 2, result[pl.ds(tokens, EXTRA_ROWS), at], 0.0)
            for level in range(2):
                tail = jnp.where(row_id == 2 + level, squares[0:1, level * length : (level + 1) * length], tail)
            goal[0][slot // 2, pl.ds(length, EXTRA_ROWS), cols] = tail.astype(jnp.bfloat16)


def weight_copies(role, planes, weight, sems):
    cols = at_block(role[0], weight.shape[3])
    copies = [
        [
            pltpu.make_async_copy(planes[index].at[part, :, cols], weight.at[index, part], sems.at[3 * index + part])
            for part in range(3)
        ]
        for index in range(2)
    ]
    copies = copies[0] + copies[1]
    for copy in copies[:AHEAD]:
        copy.start()
    return copies


def qkv_kernel(role, seq, core, mine, levels, joined, swapped, noise, mods, planes_a, planes_b, latent, *refs):
    chunks, (values, noises, result, weight, sems) = refs[:8], refs[8:]
    copies = weight_copies(role, (planes_a, planes_b), weight, sems)
    length, cols = values.shape[0], joined.shape[1]
    own = latent.shape[0]
    tokens = 2 * length
    left, right = at_block(core[0], cols), at_block(1 - core[0], cols)
    values[:, left] = joined[pl.ds(0, length), :]
    values[:, right] = swapped[pl.ds(0, length), :]
    latent[...] = values[at_block(seq[0], own), :]
    noises[at_block(seq[0], own), :] = noise[...]
    theirs = at_block(1 - seq[0], own)
    noises[theirs, left] = joined[pl.ds(length, own), :]
    noises[theirs, right] = swapped[pl.ds(length, own), :]
    spread = values[...].astype(jnp.float32)
    noise_rows = noises[...].astype(jnp.float32)
    mixed = jnp.concatenate(
        [(1.0 - levels[level]) * spread + levels[level] * noise_rows for level in range(2)], axis=0
    ).astype(jnp.bfloat16)
    wide = mixed.astype(jnp.float32)
    sums = jnp.sum(wide * wide, axis=1, keepdims=True)
    sums = jnp.broadcast_to(sums, (tokens, length)).T[0:8]
    for index in range(2):
        kept, sent = chunks[4 * index : 4 * index + 2], chunks[4 * index + 2 : 4 * index + 4]
        project(index, mine[0], mixed, sums, mods, weight.at[index], copies, kept, sent, result)


def chunk_shapes(length, cols):
    groups = cols // length
    shapes = [
        jax.ShapeDtypeStruct((groups // 2, rows, 3 * length), jnp.bfloat16) for rows in (length + EXTRA_ROWS, length)
    ]
    return shapes * 2


def qkv_part(role, seq, core, mine, levels, joined, swapped, noise, mods, planes_a, planes_b, cols):
    own, width = noise.shape
    length = joined.shape[0] - own
    tokens = 2 * length
    return pl.pallas_call(
        qkv_kernel,
        in_specs=[smem_spec()] * 5 + [vmem_spec()] * 4 + [hbm_spec()] * 2,
        out_specs=[vmem_spec()] * 9,
        out_shape=[jax.ShapeDtypeStruct((own, width), jnp.bfloat16)] + chunk_shapes(length, cols) * 2,
        scratch_shapes=[
            pltpu.VMEM((length, width), jnp.bfloat16),
            pltpu.VMEM((length, width), jnp.bfloat16),
            pltpu.VMEM((tokens + EXTRA_ROWS, cols), jnp.float32),
            pltpu.VMEM((2, 3, width, cols), jnp.bfloat16),
            pltpu.SemaphoreType.DMA((6,)),
        ],
        compiler_params=params(48),
        name="qkv_part",
    )(role, seq, core, mine, levels, joined, swapped, noise, mods, planes_a, planes_b)


def add_kernel(passed, mine, theirs, *refs):
    kept, sent = refs[-2 - passed :][:2]
    if passed:
        refs[-1][...] = refs[0][...]
    kept[...] = mine[0].astype(jnp.float32) + theirs[0].astype(jnp.float32)
    sent[...] = (mine[1].astype(jnp.float32) + theirs[1].astype(jnp.float32)).astype(jnp.bfloat16)


def add_part(mine, theirs, later=None, after=()):
    rest = [] if later is None else [later]
    shape = mine.shape[1:]
    return pl.pallas_call(
        lambda *refs: add_kernel(len(rest), *refs),
        in_specs=[vmem_spec()] * (2 + len(rest)) + [any_spec()] * len(after),
        out_specs=[vmem_spec()] * (2 + len(rest)),
        out_shape=[jax.ShapeDtypeStruct(shape, jnp.float32), jax.ShapeDtypeStruct(shape, jnp.bfloat16)]
        + [jax.ShapeDtypeStruct(x.shape, x.dtype) for x in rest],
        compiler_params=params(8),
        name="add_part",
    )(mine, theirs, *rest, *after)


def attend_kernel(width, kept_a, other_a, kept_b, other_b, gains, after_a, after_b, out):
    _, length, unit = out.shape
    extra = None
    for level, (kept, other) in enumerate(((kept_a, other_a), (kept_b, other_b))):
        mixed = kept[...] + other[...].astype(jnp.float32)
        if level == 0:
            extra = mixed[length:]
        squares = jnp.broadcast_to(extra[2 + level : 3 + level, :unit], (unit, unit)).T
        factor = lax.rsqrt(squares * (1.0 / width) + 1e-06)

        def pick(part):
            cols = slice(part * unit, (part + 1) * unit)
            return mixed[:length, cols] * factor + extra[level : level + 1, cols]

        def normed(part):
            rows = pick(part)
            mean = jnp.mean(rows * rows, axis=1, keepdims=True)
            return (rows * lax.rsqrt(mean + 1e-06) * gains[part : part + 1, :]).astype(jnp.bfloat16)

        query, key = normed(0), normed(1)
        value = pick(2).astype(jnp.bfloat16)
        logits = lax.dot_general(
            query, key, (((1,), (1,)), ((), ())), preferred_element_type=jnp.float32
        ) * (1.0 / math.sqrt(unit))
        expanded = jnp.exp(logits)
        probs = (expanded / jnp.sum(expanded, axis=1, keepdims=True)).astype(jnp.bfloat16)
        out[level] = dot32(probs, value).astype(jnp.bfloat16)


def attend_part(chunks, gains, after, width):
    kept_a, kept_b = chunks[0][0], chunks[1][0]
    unit = kept_a.shape[1] // 3
    length = kept_a.shape[0] - EXTRA_ROWS
    return pl.pallas_call(
        lambda *refs: attend_kernel(width, *refs),
        in_specs=[vmem_spec()] * 5 + [any_spec()] * 2,
        out_specs=vmem_spec(),
        out_shape=jax.ShapeDtypeStruct((2, length, unit), jnp.bfloat16),
        compiler_params=params(8),
        name="attend_part",
    )(kept_a, chunks[0][1], kept_b, chunks[1][1], gains, *after)


def out_kernel(core, mine, *refs):
    heads_a, heads_b = refs[0:4], refs[4:8]
    weight_a, weight_b, mods, kept, sent, rows, total = refs[8:]
    _, length, unit = heads_a[0].shape
    for index, (heads, weight) in enumerate(((heads_a, weight_a), (heads_b, weight_b))):
        for slot, head in enumerate(heads):
            at = at_block(jnp.bitwise_xor(mine[0], slot), unit)
            for level in range(2):
                rows[pl.ds(level * length, length), at] = head[level]
        result = dot32(rows[...], weight[...])
        gates = mods[index, 2]
        signed = gates[1:2] * result[:length] + gates[2:3] * result[length:]
        if index == 0:
            total[...] = -0.5 * signed
        else:
            total[...] = total[...] + 0.5 * signed
    cols = kept.shape[1]
    kept[...] = total[:, at_block(core[0], cols)]
    sent[...] = total[:, at_block(1 - core[0], cols)].astype(jnp.bfloat16)


def out_part(core, mine, heads_a, heads_b, weight_a, weight_b, mods):
    _, length, unit = heads_a[0].shape
    depth, width = weight_a.shape
    return pl.pallas_call(
        out_kernel,
        in_specs=[smem_spec()] * 2 + [vmem_spec()] * 11,
        out_specs=[vmem_spec()] * 2,
        out_shape=[
            jax.ShapeDtypeStruct((length, width // 2), jnp.float32),
            jax.ShapeDtypeStruct((length, width // 2), jnp.bfloat16),
        ],
        scratch_shapes=[
            pltpu.VMEM((2 * length, depth), jnp.bfloat16),
            pltpu.VMEM((length, width), jnp.float32),
        ],
        compiler_params=params(16),
        name="out_part",
    )(core, mine, *heads_a, *heads_b, weight_a, weight_b, mods)


def grad_kernel(half, heads_t, rows, *refs):
    refs[-1][...] = dot32(heads_t[...], rows[...]).astype(jnp.bfloat16)


def grad_part(half, heads_t, rows, before, steps):
    depth, length = heads_t.shape
    cols = rows.shape[1]
    tile = depth // steps
    rest = [] if before is None else [before]
    grid_spec = pltpu.PrefetchScalarGridSpec(
        num_scalar_prefetch=1,
        grid=(steps,),
        in_specs=[
            pl.BlockSpec((tile, length), lambda n, w: (n, 0)),
            pl.BlockSpec((length, cols), lambda n, w: (0, 0)),
        ]
        + [any_spec()] * len(rest),
        out_specs=pl.BlockSpec((tile, cols), lambda n, w: (n, w[0])),
    )
    return pl.pallas_call(
        grad_kernel,
        grid_spec=grid_spec,
        out_shape=jax.ShapeDtypeStruct((depth, 2 * cols), jnp.bfloat16),
        input_output_aliases={3: 0} if rest else {},
        compiler_params=params(24),
        name="grad_part",
    )(half, heads_t, rows, *rest)


def exchange(array, axis, bit):
    return lax.ppermute(array, axis, [(i, i ^ bit) for i in range(lax.axis_size(axis))])


def both(mine, theirs):
    return mine.astype(jnp.float32) + theirs.astype(jnp.float32)


def heads_per_role(
    gen_heads,
    gen_resid,
    gen_out_w,
    gen_time_w,
    noise,
    steps,
    teacher_qkv,
    teacher_out,
    teacher_time,
    teacher_norm,
    critic_qkv,
    critic_out,
    critic_time,
    critic_norm,
):
    length = gen_heads.shape[0]
    roles, groups = lax.axis_size("role"), lax.axis_size("mp")
    role, seq, mp = lax.axis_index("role"), lax.axis_index("seq"), lax.axis_index("mp")
    part_cols = gen_heads.shape[1] // roles
    freq = gen_time_w.shape[0]
    role_at, seq_at, mine = [v.astype(jnp.int32).reshape(1) for v in (role, seq, mp)]
    core = role_at % 2
    half_cols = gen_resid.shape[1] // 2

    embed = jax.vmap(lambda t: time_embed(t, freq))(steps)
    embed = jnp.concatenate([embed, jnp.zeros((5, freq), jnp.bfloat16)], axis=0)
    levels = steps[1:3].astype(jnp.float32) / 1000.0
    full, sent = gen_part(seq_at, core, embed, gen_heads, gen_out_w, gen_time_w, gen_resid, noise)
    arrived = exchange(sent, "seq", 1)
    planes = [w.transpose(1, 0, 2) for w in (teacher_qkv, critic_qkv, teacher_time, critic_time)]
    mods, gate = mod_part(embed, planes[2], planes[3], gen_time_w, full)
    joined = join_part(full, arrived, gate)
    swapped = exchange(joined, "role", 1)
    start = role * part_cols
    out_a, out_b = [lax.dynamic_slice_in_dim(w, start, part_cols, axis=0) for w in (teacher_out, critic_out)]
    unit = part_cols // groups
    gains = [lax.dynamic_slice_in_dim(g, start + mp * unit, unit, axis=1) for g in (teacher_norm, critic_norm)]

    latent, *chunks = qkv_part(
        role_at, seq_at, core, mine, levels, joined, swapped, noise, mods, planes[0], planes[1], part_cols
    )
    first, second = chunks[:4], chunks[4:]
    early = (out_a, out_b, *gains)
    kept_a, send_a, third = add_part(first[0], exchange(first[2], "mp", 1), second[2], early)
    kept_b, send_b, last = add_part(first[1], exchange(first[3], "mp", 1), second[3])
    kept_c, send_c = add_part(second[0], exchange(third, "mp", 1))
    kept_d, send_d = add_part(second[1], exchange(last, "mp", 1))
    sums = [(kept, exchange(send, "mp", 2)) for kept, send in ((kept_a, send_a), (kept_b, send_b))]
    head_a = attend_part(sums, gains[0], (send_c, send_d), D)
    sums = [(kept, exchange(send, "mp", 2)) for kept, send in ((kept_c, send_c), (kept_d, send_d))]
    head_b = attend_part(sums, gains[1], (out_a, out_b), D)
    gathered = [[head] + [exchange(head, "mp", bits) for bits in range(1, groups)] for head in (head_a, head_b)]

    kept, sent = out_part(core, mine, *gathered, out_a, out_b, mods)
    total = both(kept, exchange(sent, "role", 1)).astype(jnp.bfloat16)
    along_x = exchange(total, "seq", 1)
    along_y = exchange(total, "role", 2)
    across = lax.ppermute(
        total, ("role", "seq"), [(i, i ^ (2 * lax.axis_size("seq") + 1)) for i in range(roles * lax.axis_size("seq"))]
    )
    total = both(total, along_x) + both(along_y, across)
    gate_row = lax.dynamic_slice_in_dim(gate, core[0] * half_cols, half_cols, axis=1)[0:1]
    rows = (gate_row * total).astype(jnp.bfloat16)
    heads_t = gen_heads.T
    theirs = exchange(rows, "role", 1)
    weight_grad = grad_part(core, heads_t, rows, None, 2)
    weight_grad = grad_part(1 - core, heads_t, theirs, weight_grad, 2)
    return latent, weight_grad


def solution(mesh):
    in_specs = (
        P(None, "seq"),
        P("seq", "mp"),
        P("seq", "mp"),
        P(None, "mp"),
        P("seq", "mp"),
        P(),
        P("mp", None, "seq"),
        P("seq", "mp"),
        P(None, None, "mp"),
        P(None, "seq"),
        P("mp", None, "seq"),
        P("seq", "mp"),
        P(None, None, "mp"),
        P(None, "seq"),
    )
    out_specs = (P("seq", "mp"), P("seq", "mp"))
    roles, seqs, groups = mesh.shape["role"], mesh.shape["seq"], mesh.shape["mp"]

    def on_device(*arrays):
        heads_here = arrays[0].shape[1] // HEAD_DIM
        length = arrays[0].shape[0]
        fits = (roles, seqs, groups) == (4, 2, 4) and heads_here == roles * groups and length == HEAD_DIM
        return heads_per_role(*arrays) if fits else pass_per_role(*arrays)

    return jax.shard_map(
        on_device, mesh=mesh, in_specs=in_specs, out_specs=out_specs, check_vma=False
    )
```

```python
import math

import jax
import jax.numpy as jnp
from jax import lax
from jax.experimental import pallas as pl
from jax.experimental.pallas import tpu as pltpu
from jax.sharding import PartitionSpec as P

D = 5120
HEAD_DIM = 128


def time_embed(step_value, width):
    half_width = width // 2
    positions = jnp.arange(half_width, dtype=jnp.float32)
    frequencies = jnp.exp(positions * (-math.log(10000.0) / half_width))
    angles = step_value.astype(jnp.float32) * frequencies
    return jnp.concatenate([jnp.cos(angles), jnp.sin(angles)]).astype(jnp.bfloat16)


def head_norm(values, gains):
    factor = lax.rsqrt(jnp.mean(values * values, axis=-1, keepdims=True) + 1e-06)
    return (values * factor * gains).astype(jnp.bfloat16)


def attend(query_norm, key_norm, value_rows):
    full_length, heads_here, head_width = query_norm.shape
    query_blocks = query_norm.reshape(
        full_length // full_length, full_length, heads_here, head_width
    )

    def one_block(query_block):
        logits = jnp.einsum(
            "qhd,khd->hqk", query_block, key_norm, preferred_element_type=jnp.float32
        ) * (1.0 / math.sqrt(head_width))
        expanded = jnp.exp(logits)
        probs = (expanded / jnp.sum(expanded, axis=2, keepdims=True)).astype(jnp.bfloat16)
        return jnp.einsum(
            "hqk,khd->qhd", probs, value_rows, preferred_element_type=jnp.float32
        ).astype(jnp.bfloat16)

    head_out = lax.map(one_block, query_blocks)
    return head_out.reshape(full_length, heads_here * head_width)


def pass_per_role(
    gen_heads,
    gen_resid,
    gen_out_w,
    gen_time_w,
    noise,
    steps,
    teacher_qkv,
    teacher_out,
    teacher_time,
    teacher_norm,
    critic_qkv,
    critic_out,
    critic_time,
    critic_norm,
):
    full_length = gen_heads.shape[0]
    head_cols = gen_heads.shape[1]
    embed_width = gen_time_w.shape[0]
    gen_gate = jnp.dot(
        time_embed(steps[0], embed_width)[None, :], gen_time_w, preferred_element_type=jnp.float32
    )[0]
    block = gen_heads
    gen_proj = lax.psum_scatter(
        jnp.dot(block, gen_out_w, preferred_element_type=jnp.float32),
        "seq",
        scatter_dimension=0,
        tiled=True,
    )
    latent = (gen_resid.astype(jnp.float32) + gen_gate * gen_proj).astype(jnp.bfloat16)
    role_index = lax.axis_index("role")
    level = steps[1 + role_index // 2]
    use_critic = role_index % 2 == 1
    w_qkv = jnp.where(use_critic, critic_qkv, teacher_qkv)
    w_out = jnp.where(use_critic, critic_out, teacher_out)
    w_time = jnp.where(use_critic, critic_time, teacher_time)
    w_norm = jnp.where(use_critic, critic_norm, teacher_norm)
    noise_level = level.astype(jnp.float32) / 1000.0
    noisy = (
        (1.0 - noise_level) * latent.astype(jnp.float32) + noise_level * noise.astype(jnp.float32)
    ).astype(jnp.bfloat16)
    modulation = jnp.einsum(
        "f,fkd->kd", time_embed(level, embed_width), w_time, preferred_element_type=jnp.float32
    )
    shift_vec = modulation[0]
    scale_vec = modulation[1]
    gate_vec = modulation[2]
    gathered = lax.all_gather(noisy, "seq", axis=0, tiled=True)
    partial_squares = jnp.sum(jnp.square(gathered.astype(jnp.float32)), axis=1)
    scaled = (gathered.astype(jnp.float32) * (1.0 + scale_vec)).astype(jnp.bfloat16)
    flat_w = w_qkv.reshape(w_qkv.shape[0], 3 * head_cols)
    projected = jnp.dot(scaled, flat_w, preferred_element_type=jnp.float32)
    shift_proj = jnp.dot(
        shift_vec.astype(jnp.bfloat16)[None, :], flat_w, preferred_element_type=jnp.float32
    )[0]
    projected, squares, shift_proj = lax.psum((projected, partial_squares, shift_proj), "mp")
    mixed = projected * lax.rsqrt(squares / D + 1e-06)[:, None] + shift_proj
    heads_here = head_cols // HEAD_DIM
    mixed = mixed.reshape(full_length, 3, heads_here, HEAD_DIM)
    gains = w_norm.reshape(2, heads_here, HEAD_DIM)
    query_norm = head_norm(mixed[:, 0], gains[0])
    key_norm = head_norm(mixed[:, 1], gains[1])
    value_rows = mixed[:, 2].astype(jnp.bfloat16)
    head_out = attend(query_norm, key_norm, value_rows)
    weight_sign = jnp.where(use_critic, 0.5, -0.5)
    block = head_out
    summed_rows = lax.psum_scatter(
        weight_sign * (gate_vec * jnp.dot(block, w_out, preferred_element_type=jnp.float32)),
        ("role", "seq"),
        scatter_dimension=0,
        tiled=True,
    )
    grad_rows = lax.all_gather(
        (gen_gate * summed_rows).astype(jnp.bfloat16), ("role", "seq"), axis=0, tiled=True
    )
    weight_grad = lax.dot_general(
        gen_heads, grad_rows, (((0,), (0,)), ((), ())), preferred_element_type=jnp.float32
    )
    return (latent, weight_grad.astype(jnp.bfloat16))

MIB = 1024 * 1024
EXTRA_ROWS = 16


def vmem_spec():
    return pl.BlockSpec(memory_space=pltpu.VMEM)


def smem_spec():
    return pl.BlockSpec(memory_space=pltpu.SMEM)


def params(mebibytes):
    return pltpu.CompilerParams(vmem_limit_bytes=mebibytes * MIB)


def dot32(a, b):
    return jnp.dot(a, b, preferred_element_type=jnp.float32)


def at_block(index, size):
    return pl.ds(pl.multiple_of(index * size, size), size)


def any_spec():
    return pl.BlockSpec(memory_space=pl.ANY)


def hbm_spec():
    return pl.BlockSpec(memory_space=pltpu.HBM)


def cost(flops, moved):
    return pl.CostEstimate(flops=flops, bytes_accessed=moved, transcendentals=0)


GEN_CUTS = 8


def gen_kernel(seq, core, embed, heads, weight, time_w, resid, noise, full, sent, heads_v, weight_v, time_v, resid_v, sems):
    length, width = full.shape
    own = resid_v.shape[0]
    cols = at_block(core[0], width)
    tile = weight_v.shape[0] // GEN_CUTS
    copies = [pltpu.make_async_copy(heads, heads_v, sems.at[GEN_CUTS])]
    for k in range(GEN_CUTS):
        rows = pl.ds(k * tile, tile)
        copies.append(pltpu.make_async_copy(weight.at[rows, cols], weight_v.at[rows, :], sems.at[k]))
    copies.append(pltpu.make_async_copy(time_w.at[:, cols], time_v, sems.at[GEN_CUTS + 1]))
    copies.append(pltpu.make_async_copy(resid.at[:, cols], resid_v, sems.at[GEN_CUTS + 2]))
    copies.append(pltpu.make_async_copy(noise.at[:, cols], sent.at[pl.ds(length, own), :], sems.at[GEN_CUTS + 3]))
    for copy in copies:
        copy.start()
    copies[0].wait()
    total = None
    for k in range(GEN_CUTS):
        copies[1 + k].wait()
        rows = pl.ds(k * tile, tile)
        term = dot32(heads_v[:, rows], weight_v[rows, :])
        total = term if total is None else total + term
    for copy in copies[1 + GEN_CUTS :]:
        copy.wait()
    full[...] = total * dot32(embed[...], time_v[...])[0:1]
    at = at_block(seq[0], own)
    full[at, :] = full[at, :] + resid_v[...].astype(jnp.float32)
    sent[pl.ds(0, length), :] = full[...].astype(jnp.bfloat16)


def gen_part(seq, core, embed, heads, weight, time_w, resid, noise):
    length, depth = heads.shape
    width = weight.shape[1] // 2
    freq = time_w.shape[0]
    own = resid.shape[0]
    return pl.pallas_call(
        gen_kernel,
        in_specs=[smem_spec(), smem_spec(), vmem_spec()] + [hbm_spec()] * 5,
        out_specs=[vmem_spec()] * 2,
        out_shape=[
            jax.ShapeDtypeStruct((length, width), jnp.float32),
            jax.ShapeDtypeStruct((length + own, width), jnp.bfloat16),
        ],
        scratch_shapes=[
            pltpu.VMEM((length, depth), jnp.bfloat16),
            pltpu.VMEM((depth, width), jnp.bfloat16),
            pltpu.VMEM((freq, width), jnp.bfloat16),
            pltpu.VMEM((own, width), jnp.bfloat16),
            pltpu.SemaphoreType.DMA((GEN_CUTS + 4,)),
        ],
        compiler_params=params(56),
        name="gen_part",
    )(seq, core, embed, heads, weight, time_w, resid, noise)


def mod_kernel(embed, time_a, time_b, time_w, after, mods, gate):
    gate[...] = dot32(embed[...], time_w[...])
    for k in range(3):
        mods[0, k] = dot32(embed[...], time_a[k])
        mods[1, k] = dot32(embed[...], time_b[k])


def mod_part(embed, time_a, time_b, time_w, after):
    width = time_a.shape[2]
    moved = 2 * (time_a.size + time_b.size + time_w.size)
    return pl.pallas_call(
        mod_kernel,
        in_specs=[vmem_spec()] * 4 + [any_spec()],
        out_specs=[vmem_spec()] * 2,
        out_shape=[
            jax.ShapeDtypeStruct((2, 3, 8, width), jnp.float32),
            jax.ShapeDtypeStruct((8, width), jnp.float32),
        ],
        compiler_params=params(16),
        cost_estimate=cost(8 * moved, moved),
        name="mod_part",
    )(embed, time_a, time_b, time_w, after)


def join_kernel(full, arrived, after_a, after_b, after_c, joined):
    length = full.shape[0]
    own = arrived.shape[0] - length
    top = full[...] + arrived[pl.ds(0, length), :].astype(jnp.float32)
    joined[pl.ds(0, length), :] = top.astype(jnp.bfloat16)
    joined[pl.ds(length, own), :] = arrived[pl.ds(length, own), :]


def join_part(full, arrived, *after):
    return pl.pallas_call(
        join_kernel,
        in_specs=[vmem_spec(), vmem_spec()] + [any_spec()] * 3,
        out_specs=vmem_spec(),
        out_shape=jax.ShapeDtypeStruct(arrived.shape, jnp.bfloat16),
        compiler_params=params(8),
        name="join_part",
    )(full, arrived, *after)


def project(index, mine, noisy, squares, mods, weight, kept, sent, result):
    tokens = noisy.shape[0]
    length = tokens // 2
    unit = squares.shape[1] // 2
    groups = weight.shape[2] // unit
    scale = mods[index, 1]
    shift = mods[index, 0]
    spread = noisy.astype(jnp.float32)
    top = spread[:length] * (1.0 + scale[1:2])
    low = spread[length:] * (1.0 + scale[2:3])
    extra = jnp.concatenate([shift[1:3], jnp.zeros((EXTRA_ROWS - 2, shift.shape[1]), jnp.float32)], axis=0)
    rows = jnp.concatenate([top, low, extra], axis=0).astype(jnp.bfloat16)
    row_id = lax.broadcasted_iota(jnp.int32, (EXTRA_ROWS, unit), 0)
    for part in range(3):
        result[...] = dot32(rows, weight[part])
        cols = pl.ds(part * unit, unit)
        for slot in range(groups):
            at = at_block(jnp.bitwise_xor(mine, slot), unit)
            goal = sent if slot % 2 else kept
            for level in range(2):
                goal[level][slot // 2, pl.ds(0, length), cols] = result[pl.ds(level * length, length), at].astype(
                    jnp.bfloat16
                )
            tail = jnp.where(row_id < 2, result[pl.ds(tokens, EXTRA_ROWS), at], 0.0)
            for level in range(2):
                tail = jnp.where(row_id == 2 + level, squares[0:1, level * length : (level + 1) * length], tail)
            goal[0][slot // 2, pl.ds(length, EXTRA_ROWS), cols] = tail.astype(jnp.bfloat16)


def qkv_kernel(seq, core, mine, levels, joined, swapped, noise, mods, weight_a, weight_b, latent, *refs):
    chunks, (values, noises, result) = refs[:8], refs[8:]
    length, cols = values.shape[0], joined.shape[1]
    own = latent.shape[0]
    tokens = 2 * length
    left, right = at_block(core[0], cols), at_block(1 - core[0], cols)
    values[:, left] = joined[pl.ds(0, length), :]
    values[:, right] = swapped[pl.ds(0, length), :]
    latent[...] = values[at_block(seq[0], own), :]
    noises[at_block(seq[0], own), :] = noise[...]
    theirs = at_block(1 - seq[0], own)
    noises[theirs, left] = joined[pl.ds(length, own), :]
    noises[theirs, right] = swapped[pl.ds(length, own), :]
    spread = values[...].astype(jnp.float32)
    noise_rows = noises[...].astype(jnp.float32)
    mixed = jnp.concatenate(
        [(1.0 - levels[level]) * spread + levels[level] * noise_rows for level in range(2)], axis=0
    ).astype(jnp.bfloat16)
    wide = mixed.astype(jnp.float32)
    sums = jnp.sum(wide * wide, axis=1, keepdims=True)
    sums = jnp.broadcast_to(sums, (tokens, length)).T[0:8]
    for index, weight in enumerate((weight_a, weight_b)):
        kept, sent = chunks[4 * index : 4 * index + 2], chunks[4 * index + 2 : 4 * index + 4]
        project(index, mine[0], mixed, sums, mods, weight, kept, sent, result)


def chunk_shapes(length, cols):
    groups = cols // length
    shapes = [
        jax.ShapeDtypeStruct((groups // 2, rows, 3 * length), jnp.bfloat16) for rows in (length + EXTRA_ROWS, length)
    ]
    return shapes * 2


def qkv_part(seq, core, mine, levels, joined, swapped, noise, mods, weight_a, weight_b):
    own, width = noise.shape
    length = joined.shape[0] - own
    tokens = 2 * length
    cols = weight_a.shape[2]
    return pl.pallas_call(
        qkv_kernel,
        in_specs=[smem_spec()] * 4 + [vmem_spec()] * 6,
        out_specs=[vmem_spec()] * 9,
        out_shape=[jax.ShapeDtypeStruct((own, width), jnp.bfloat16)] + chunk_shapes(length, cols) * 2,
        scratch_shapes=[
            pltpu.VMEM((length, width), jnp.bfloat16),
            pltpu.VMEM((length, width), jnp.bfloat16),
            pltpu.VMEM((tokens + EXTRA_ROWS, cols), jnp.float32),
        ],
        compiler_params=params(24),
        name="qkv_part",
    )(seq, core, mine, levels, joined, swapped, noise, mods, weight_a, weight_b)


def attend_kernel(width, kept_a, other_a, kept_b, other_b, gains, out):
    _, length, unit = out.shape
    extra = None
    for level, (kept, other) in enumerate(((kept_a, other_a), (kept_b, other_b))):
        mixed = kept[...] + other[...].astype(jnp.float32)
        if level == 0:
            extra = mixed[length:]
        squares = jnp.broadcast_to(extra[2 + level : 3 + level, :unit], (unit, unit)).T
        factor = lax.rsqrt(squares * (1.0 / width) + 1e-06)

        def pick(part):
            cols = slice(part * unit, (part + 1) * unit)
            return mixed[:length, cols] * factor + extra[level : level + 1, cols]

        def normed(part):
            rows = pick(part)
            mean = jnp.mean(rows * rows, axis=1, keepdims=True)
            return (rows * lax.rsqrt(mean + 1e-06) * gains[part : part + 1, :]).astype(jnp.bfloat16)

        query, key = normed(0), normed(1)
        value = pick(2).astype(jnp.bfloat16)
        logits = lax.dot_general(
            query, key, (((1,), (1,)), ((), ())), preferred_element_type=jnp.float32
        ) * (1.0 / math.sqrt(unit))
        expanded = jnp.exp(logits)
        probs = (expanded / jnp.sum(expanded, axis=1, keepdims=True)).astype(jnp.bfloat16)
        out[level] = dot32(probs, value).astype(jnp.bfloat16)


def attend_part(chunks, gains, width):
    kept_a, kept_b = chunks[0][0], chunks[1][0]
    unit = kept_a.shape[1] // 3
    length = kept_a.shape[0] - EXTRA_ROWS
    return pl.pallas_call(
        lambda *refs: attend_kernel(width, *refs),
        in_specs=[vmem_spec()] * 5,
        out_specs=vmem_spec(),
        out_shape=jax.ShapeDtypeStruct((2, length, unit), jnp.bfloat16),
        compiler_params=params(8),
        name="attend_part",
    )(kept_a, chunks[0][1], kept_b, chunks[1][1], gains)


def out_kernel(core, mine, *refs):
    heads_a, heads_b = refs[0:4], refs[4:8]
    weight_a, weight_b, mods, kept, sent, rows, total = refs[8:]
    _, length, unit = heads_a[0].shape
    for index, (heads, weight) in enumerate(((heads_a, weight_a), (heads_b, weight_b))):
        for slot, head in enumerate(heads):
            at = at_block(jnp.bitwise_xor(mine[0], slot), unit)
            for level in range(2):
                rows[pl.ds(level * length, length), at] = head[level]
        result = dot32(rows[...], weight[...])
        gates = mods[index, 2]
        signed = gates[1:2] * result[:length] + gates[2:3] * result[length:]
        if index == 0:
            total[...] = -0.5 * signed
        else:
            total[...] = total[...] + 0.5 * signed
    cols = kept.shape[1]
    kept[...] = total[:, at_block(core[0], cols)]
    sent[...] = total[:, at_block(1 - core[0], cols)].astype(jnp.bfloat16)


def out_part(core, mine, heads_a, heads_b, weight_a, weight_b, mods):
    _, length, unit = heads_a[0].shape
    depth, width = weight_a.shape
    return pl.pallas_call(
        out_kernel,
        in_specs=[smem_spec()] * 2 + [vmem_spec()] * 11,
        out_specs=[vmem_spec()] * 2,
        out_shape=[
            jax.ShapeDtypeStruct((length, width // 2), jnp.float32),
            jax.ShapeDtypeStruct((length, width // 2), jnp.bfloat16),
        ],
        scratch_shapes=[
            pltpu.VMEM((2 * length, depth), jnp.bfloat16),
            pltpu.VMEM((length, width), jnp.float32),
        ],
        compiler_params=params(16),
        name="out_part",
    )(core, mine, *heads_a, *heads_b, weight_a, weight_b, mods)


def grad_kernel(half, heads_t, rows, *refs):
    refs[-1][...] = dot32(heads_t[...], rows[...]).astype(jnp.bfloat16)


def grad_part(half, heads_t, rows, before, steps):
    depth, length = heads_t.shape
    cols = rows.shape[1]
    tile = depth // steps
    rest = [] if before is None else [before]
    grid_spec = pltpu.PrefetchScalarGridSpec(
        num_scalar_prefetch=1,
        grid=(steps,),
        in_specs=[
            pl.BlockSpec((tile, length), lambda n, w: (n, 0)),
            pl.BlockSpec((length, cols), lambda n, w: (0, 0)),
        ]
        + [any_spec()] * len(rest),
        out_specs=pl.BlockSpec((tile, cols), lambda n, w: (n, w[0])),
    )
    return pl.pallas_call(
        grad_kernel,
        grid_spec=grid_spec,
        out_shape=jax.ShapeDtypeStruct((depth, 2 * cols), jnp.bfloat16),
        input_output_aliases={3: 0} if rest else {},
        compiler_params=params(24),
        name="grad_part",
    )(half, heads_t, rows, *rest)


def exchange(array, axis, bit):
    return lax.ppermute(array, axis, [(i, i ^ bit) for i in range(lax.axis_size(axis))])


def both(mine, theirs):
    return mine.astype(jnp.float32) + theirs.astype(jnp.float32)


def heads_per_role(
    gen_heads,
    gen_resid,
    gen_out_w,
    gen_time_w,
    noise,
    steps,
    teacher_qkv,
    teacher_out,
    teacher_time,
    teacher_norm,
    critic_qkv,
    critic_out,
    critic_time,
    critic_norm,
):
    length = gen_heads.shape[0]
    roles, groups = lax.axis_size("role"), lax.axis_size("mp")
    role, seq, mp = lax.axis_index("role"), lax.axis_index("seq"), lax.axis_index("mp")
    part_cols = gen_heads.shape[1] // roles
    freq = gen_time_w.shape[0]
    seq_at, mine = [v.astype(jnp.int32).reshape(1) for v in (seq, mp)]
    core = (role % 2).astype(jnp.int32).reshape(1)
    half_cols = gen_resid.shape[1] // 2

    embed = jax.vmap(lambda t: time_embed(t, freq))(steps)
    embed = jnp.concatenate([embed, jnp.zeros((5, freq), jnp.bfloat16)], axis=0)
    levels = steps[1:3].astype(jnp.float32) / 1000.0
    full, sent = gen_part(seq_at, core, embed, gen_heads, gen_out_w, gen_time_w, gen_resid, noise)
    arrived = exchange(sent, "seq", 1)
    planes = [w.transpose(1, 0, 2) for w in (teacher_qkv, critic_qkv, teacher_time, critic_time)]
    mods, gate = mod_part(embed, planes[2], planes[3], gen_time_w, full)
    start = role * part_cols
    later, _ = lax.optimization_barrier((start, full))
    weight_a, weight_b = [lax.dynamic_slice_in_dim(w, later, part_cols, axis=2) for w in planes[:2]]
    joined = join_part(full, arrived, gate, weight_a, weight_b)
    swapped = exchange(joined, "role", 1)
    unit = part_cols // groups

    latent, *chunks = qkv_part(seq_at, core, mine, levels, joined, swapped, noise, mods, weight_a, weight_b)
    first, second = chunks[:4], chunks[4:]
    arrivals = [exchange(send, "mp", 1) for send in first[2:]]
    out_a, out_b = [lax.dynamic_slice_in_dim(w, start, part_cols, axis=0) for w in (teacher_out, critic_out)]
    gains = [lax.dynamic_slice_in_dim(g, start + mp * unit, unit, axis=1) for g in (teacher_norm, critic_norm)]
    arrivals[0], out_a, out_b, *gains = lax.optimization_barrier((arrivals[0], out_a, out_b, *gains))
    third, arrivals[0] = lax.optimization_barrier((second[2], arrivals[0]))
    last, arrivals[1] = lax.optimization_barrier((second[3], arrivals[1]))
    arrivals += [exchange(third, "mp", 1), exchange(last, "mp", 1)]
    kept, sends = [], []
    for mine_rows, theirs in zip(first[:2] + second[:2], arrivals):
        summed = both(mine_rows, theirs)
        kept.append(summed[0])
        sends.append(summed[1].astype(jnp.bfloat16))
    pieces = [(rows, exchange(send, "mp", 2)) for rows, send in zip(kept, sends)]
    kept_b, _, _ = lax.optimization_barrier((pieces[1][0], sends[2], sends[3]))
    head_a = attend_part((pieces[0], (kept_b, pieces[1][1])), gains[0], D)
    head_b = attend_part(pieces[2:], gains[1], D)
    gathered = [[head] + [exchange(head, "mp", bits) for bits in range(1, groups)] for head in (head_a, head_b)]

    kept, sent = out_part(core, mine, *gathered, out_a, out_b, mods)
    total = both(kept, exchange(sent, "role", 1)).astype(jnp.bfloat16)
    along_x = exchange(total, "seq", 1)
    along_y = exchange(total, "role", 2)
    across = lax.ppermute(
        total, ("role", "seq"), [(i, i ^ (2 * lax.axis_size("seq") + 1)) for i in range(roles * lax.axis_size("seq"))]
    )
    total = both(total, along_x) + both(along_y, across)
    gate_row = lax.dynamic_slice_in_dim(gate, core[0] * half_cols, half_cols, axis=1)[0:1]
    rows = (gate_row * total).astype(jnp.bfloat16)
    heads_t = gen_heads.T
    theirs = exchange(rows, "role", 1)
    weight_grad = grad_part(core, heads_t, rows, None, 2)
    weight_grad = grad_part(1 - core, heads_t, theirs, weight_grad, 2)
    return latent, weight_grad


def solution(mesh):
    in_specs = (
        P(None, "seq"),
        P("seq", "mp"),
        P("seq", "mp"),
        P(None, "mp"),
        P("seq", "mp"),
        P(),
        P("mp", None, "seq"),
        P("seq", "mp"),
        P(None, None, "mp"),
        P(None, "seq"),
        P("mp", None, "seq"),
        P("seq", "mp"),
        P(None, None, "mp"),
        P(None, "seq"),
    )
    out_specs = (P("seq", "mp"), P("seq", "mp"))
    roles, seqs, groups = mesh.shape["role"], mesh.shape["seq"], mesh.shape["mp"]

    def on_device(*arrays):
        heads_here = arrays[0].shape[1] // HEAD_DIM
        length = arrays[0].shape[0]
        fits = (roles, seqs, groups) == (4, 2, 4) and heads_here == roles * groups and length == HEAD_DIM
        return heads_per_role(*arrays) if fits else pass_per_role(*arrays)

    return jax.shard_map(
        on_device, mesh=mesh, in_specs=in_specs, out_specs=out_specs, check_vma=False
    )
```

```python
import math

import jax
import jax.numpy as jnp
from jax import lax
from jax.experimental import pallas as pl
from jax.experimental.pallas import tpu as pltpu
from jax.sharding import PartitionSpec as P

D = 5120
HEAD_DIM = 128


def time_embed(step_value, width):
    half_width = width // 2
    positions = jnp.arange(half_width, dtype=jnp.float32)
    frequencies = jnp.exp(positions * (-math.log(10000.0) / half_width))
    angles = step_value.astype(jnp.float32) * frequencies
    return jnp.concatenate([jnp.cos(angles), jnp.sin(angles)]).astype(jnp.bfloat16)


def head_norm(values, gains):
    factor = lax.rsqrt(jnp.mean(values * values, axis=-1, keepdims=True) + 1e-06)
    return (values * factor * gains).astype(jnp.bfloat16)


def attend(query_norm, key_norm, value_rows):
    full_length, heads_here, head_width = query_norm.shape
    query_blocks = query_norm.reshape(
        full_length // full_length, full_length, heads_here, head_width
    )

    def one_block(query_block):
        logits = jnp.einsum(
            "qhd,khd->hqk", query_block, key_norm, preferred_element_type=jnp.float32
        ) * (1.0 / math.sqrt(head_width))
        expanded = jnp.exp(logits)
        probs = (expanded / jnp.sum(expanded, axis=2, keepdims=True)).astype(jnp.bfloat16)
        return jnp.einsum(
            "hqk,khd->qhd", probs, value_rows, preferred_element_type=jnp.float32
        ).astype(jnp.bfloat16)

    head_out = lax.map(one_block, query_blocks)
    return head_out.reshape(full_length, heads_here * head_width)


def pass_per_role(
    gen_heads,
    gen_resid,
    gen_out_w,
    gen_time_w,
    noise,
    steps,
    teacher_qkv,
    teacher_out,
    teacher_time,
    teacher_norm,
    critic_qkv,
    critic_out,
    critic_time,
    critic_norm,
):
    full_length = gen_heads.shape[0]
    head_cols = gen_heads.shape[1]
    embed_width = gen_time_w.shape[0]
    gen_gate = jnp.dot(
        time_embed(steps[0], embed_width)[None, :], gen_time_w, preferred_element_type=jnp.float32
    )[0]
    block = gen_heads
    gen_proj = lax.psum_scatter(
        jnp.dot(block, gen_out_w, preferred_element_type=jnp.float32),
        "seq",
        scatter_dimension=0,
        tiled=True,
    )
    latent = (gen_resid.astype(jnp.float32) + gen_gate * gen_proj).astype(jnp.bfloat16)
    role_index = lax.axis_index("role")
    level = steps[1 + role_index // 2]
    use_critic = role_index % 2 == 1
    w_qkv = jnp.where(use_critic, critic_qkv, teacher_qkv)
    w_out = jnp.where(use_critic, critic_out, teacher_out)
    w_time = jnp.where(use_critic, critic_time, teacher_time)
    w_norm = jnp.where(use_critic, critic_norm, teacher_norm)
    noise_level = level.astype(jnp.float32) / 1000.0
    noisy = (
        (1.0 - noise_level) * latent.astype(jnp.float32) + noise_level * noise.astype(jnp.float32)
    ).astype(jnp.bfloat16)
    modulation = jnp.einsum(
        "f,fkd->kd", time_embed(level, embed_width), w_time, preferred_element_type=jnp.float32
    )
    shift_vec = modulation[0]
    scale_vec = modulation[1]
    gate_vec = modulation[2]
    gathered = lax.all_gather(noisy, "seq", axis=0, tiled=True)
    partial_squares = jnp.sum(jnp.square(gathered.astype(jnp.float32)), axis=1)
    scaled = (gathered.astype(jnp.float32) * (1.0 + scale_vec)).astype(jnp.bfloat16)
    flat_w = w_qkv.reshape(w_qkv.shape[0], 3 * head_cols)
    projected = jnp.dot(scaled, flat_w, preferred_element_type=jnp.float32)
    shift_proj = jnp.dot(
        shift_vec.astype(jnp.bfloat16)[None, :], flat_w, preferred_element_type=jnp.float32
    )[0]
    projected, squares, shift_proj = lax.psum((projected, partial_squares, shift_proj), "mp")
    mixed = projected * lax.rsqrt(squares / D + 1e-06)[:, None] + shift_proj
    heads_here = head_cols // HEAD_DIM
    mixed = mixed.reshape(full_length, 3, heads_here, HEAD_DIM)
    gains = w_norm.reshape(2, heads_here, HEAD_DIM)
    query_norm = head_norm(mixed[:, 0], gains[0])
    key_norm = head_norm(mixed[:, 1], gains[1])
    value_rows = mixed[:, 2].astype(jnp.bfloat16)
    head_out = attend(query_norm, key_norm, value_rows)
    weight_sign = jnp.where(use_critic, 0.5, -0.5)
    block = head_out
    summed_rows = lax.psum_scatter(
        weight_sign * (gate_vec * jnp.dot(block, w_out, preferred_element_type=jnp.float32)),
        ("role", "seq"),
        scatter_dimension=0,
        tiled=True,
    )
    grad_rows = lax.all_gather(
        (gen_gate * summed_rows).astype(jnp.bfloat16), ("role", "seq"), axis=0, tiled=True
    )
    weight_grad = lax.dot_general(
        gen_heads, grad_rows, (((0,), (0,)), ((), ())), preferred_element_type=jnp.float32
    )
    return (latent, weight_grad.astype(jnp.bfloat16))

MIB = 1024 * 1024
EXTRA_ROWS = 16


def vmem_spec():
    return pl.BlockSpec(memory_space=pltpu.VMEM)


def smem_spec():
    return pl.BlockSpec(memory_space=pltpu.SMEM)


def params(mebibytes):
    return pltpu.CompilerParams(vmem_limit_bytes=mebibytes * MIB)


def dot32(a, b):
    return jnp.dot(a, b, preferred_element_type=jnp.float32)


def at_block(index, size):
    return pl.ds(pl.multiple_of(index * size, size), size)


def any_spec():
    return pl.BlockSpec(memory_space=pl.ANY)


def cost(flops, moved):
    return pl.CostEstimate(flops=flops, bytes_accessed=moved, transcendentals=0)


def pack_kernel(seq, core, product, embed, time_w, resid, noise, full, sent):
    length, width = full.shape
    own = resid.shape[0]
    cols = at_block(core[0], width)
    full[...] = product[...] * dot32(embed[...], time_w[:, cols])[0:1]
    at = at_block(seq[0], own)
    full[at, :] = full[at, :] + resid[:, cols].astype(jnp.float32)
    sent[pl.ds(0, length), :] = full[...].astype(jnp.bfloat16)
    sent[pl.ds(length, own), :] = noise[:, cols]


def pack_part(seq, core, product, embed, time_w, resid, noise):
    length, width = product.shape
    own = resid.shape[0]
    return pl.pallas_call(
        pack_kernel,
        in_specs=[smem_spec()] * 2 + [vmem_spec()] * 5,
        out_specs=[vmem_spec()] * 2,
        out_shape=[
            jax.ShapeDtypeStruct((length, width), jnp.float32),
            jax.ShapeDtypeStruct((length + own, width), jnp.bfloat16),
        ],
        compiler_params=params(8),
        name="pack_part",
    )(seq, core, product, embed, time_w, resid, noise)


def mod_kernel(embed, time_a, time_b, time_w, after, mods, gate):
    gate[...] = dot32(embed[...], time_w[...])
    for k in range(3):
        mods[0, k] = dot32(embed[...], time_a[k])
        mods[1, k] = dot32(embed[...], time_b[k])


def mod_part(embed, time_a, time_b, time_w, after):
    width = time_a.shape[2]
    moved = 2 * (time_a.size + time_b.size + time_w.size)
    return pl.pallas_call(
        mod_kernel,
        in_specs=[vmem_spec()] * 4 + [any_spec()],
        out_specs=[vmem_spec()] * 2,
        out_shape=[
            jax.ShapeDtypeStruct((2, 3, 8, width), jnp.float32),
            jax.ShapeDtypeStruct((8, width), jnp.float32),
        ],
        compiler_params=params(16),
        cost_estimate=cost(8 * moved, moved),
        name="mod_part",
    )(embed, time_a, time_b, time_w, after)


def join_kernel(full, arrived, after_a, after_b, after_c, joined):
    length = full.shape[0]
    own = arrived.shape[0] - length
    top = full[...] + arrived[pl.ds(0, length), :].astype(jnp.float32)
    joined[pl.ds(0, length), :] = top.astype(jnp.bfloat16)
    joined[pl.ds(length, own), :] = arrived[pl.ds(length, own), :]


def join_part(full, arrived, *after):
    return pl.pallas_call(
        join_kernel,
        in_specs=[vmem_spec(), vmem_spec()] + [any_spec()] * 3,
        out_specs=vmem_spec(),
        out_shape=jax.ShapeDtypeStruct(arrived.shape, jnp.bfloat16),
        compiler_params=params(8),
        name="join_part",
    )(full, arrived, *after)


def project(index, stride, mine, noisy, squares, mods, weight, kept, sent, result):
    tokens = noisy.shape[0]
    length = tokens // 2
    unit = squares.shape[1] // 2
    groups = weight.shape[2] // unit
    scale = mods[index, 1]
    shift = mods[index, 0]
    spread = noisy.astype(jnp.float32)
    top = spread[:length] * (1.0 + scale[1:2])
    low = spread[length:] * (1.0 + scale[2:3])
    extra = jnp.concatenate([shift[1:3], jnp.zeros((EXTRA_ROWS - 2, shift.shape[1]), jnp.float32)], axis=0)
    rows = jnp.concatenate([top, low, extra], axis=0).astype(jnp.bfloat16)
    row_id = lax.broadcasted_iota(jnp.int32, (EXTRA_ROWS, unit), 0)
    for part in range(3):
        result[...] = dot32(rows, weight[part])
        cols = pl.ds(part * unit, unit)
        for slot in range(groups):
            at = at_block(jnp.bitwise_xor(mine, slot), unit)
            goal = sent if slot & stride else kept
            place = slot // 2 if stride == 1 else slot % 2
            goal[place, pl.ds(0, tokens), cols] = result[pl.ds(0, tokens), at].astype(jnp.bfloat16)
            tail = jnp.where(row_id < 2, result[pl.ds(tokens, EXTRA_ROWS), at], 0.0)
            for level in range(2):
                tail = jnp.where(row_id == 2 + level, squares[0:1, level * length : (level + 1) * length], tail)
            goal[place, pl.ds(tokens, EXTRA_ROWS), cols] = tail.astype(jnp.bfloat16)


def qkv_kernel(seq, core, mine, levels, joined, swapped, noise, mods, weight_a, weight_b, latent, *refs):
    chunks, (values, noises, result) = refs[:4], refs[4:]
    length, cols = values.shape[0], joined.shape[1]
    own = latent.shape[0]
    tokens = 2 * length
    left, right = at_block(core[0], cols), at_block(1 - core[0], cols)
    values[:, left] = joined[pl.ds(0, length), :]
    values[:, right] = swapped[pl.ds(0, length), :]
    latent[...] = values[at_block(seq[0], own), :]
    noises[at_block(seq[0], own), :] = noise[...]
    theirs = at_block(1 - seq[0], own)
    noises[theirs, left] = joined[pl.ds(length, own), :]
    noises[theirs, right] = swapped[pl.ds(length, own), :]
    spread = values[...].astype(jnp.float32)
    noise_rows = noises[...].astype(jnp.float32)
    mixed = jnp.concatenate(
        [(1.0 - levels[level]) * spread + levels[level] * noise_rows for level in range(2)], axis=0
    ).astype(jnp.bfloat16)
    wide = mixed.astype(jnp.float32)
    sums = jnp.sum(wide * wide, axis=1, keepdims=True)
    sums = jnp.broadcast_to(sums, (tokens, length)).T[0:8]
    for index, weight in enumerate((weight_a, weight_b)):
        project(index, index + 1, mine[0], mixed, sums, mods, weight, *chunks[2 * index : 2 * index + 2], result)


def qkv_part(seq, core, mine, levels, joined, swapped, noise, mods, weight_a, weight_b):
    own, width = noise.shape
    length = joined.shape[0] - own
    tokens = 2 * length
    cols = weight_a.shape[2]
    return pl.pallas_call(
        qkv_kernel,
        in_specs=[smem_spec()] * 4 + [vmem_spec()] * 6,
        out_specs=[vmem_spec()] * 5,
        out_shape=[jax.ShapeDtypeStruct((own, width), jnp.bfloat16)]
        + [jax.ShapeDtypeStruct((cols // length // 2, tokens + EXTRA_ROWS, 3 * length), jnp.bfloat16)] * 4,
        scratch_shapes=[
            pltpu.VMEM((length, width), jnp.bfloat16),
            pltpu.VMEM((length, width), jnp.bfloat16),
            pltpu.VMEM((tokens + EXTRA_ROWS, cols), jnp.float32),
        ],
        compiler_params=params(20),
        name="qkv_part",
    )(seq, core, mine, levels, joined, swapped, noise, mods, weight_a, weight_b)


def attend_kernel(width, kept_a, other_a, kept_b, other_b, gains, out):
    _, _, length, unit = out.shape
    tokens = 2 * length
    for index, (kept, other) in enumerate(((kept_a, other_a), (kept_b, other_b))):
        mixed = kept[...] + other[...].astype(jnp.float32)
        extra = mixed[tokens:]
        for level in range(2):
            rows_at = slice(level * length, (level + 1) * length)
            squares = jnp.broadcast_to(extra[2 + level : 3 + level, :unit], (unit, unit)).T
            factor = lax.rsqrt(squares * (1.0 / width) + 1e-06)

            def pick(part):
                cols = slice(part * unit, (part + 1) * unit)
                return mixed[rows_at, cols] * factor + extra[level : level + 1, cols]

            def normed(part):
                rows = pick(part)
                mean = jnp.mean(rows * rows, axis=1, keepdims=True)
                return (rows * lax.rsqrt(mean + 1e-06) * gains[index, part : part + 1, :]).astype(jnp.bfloat16)

            query, key = normed(0), normed(1)
            value = pick(2).astype(jnp.bfloat16)
            logits = lax.dot_general(
                query, key, (((1,), (1,)), ((), ())), preferred_element_type=jnp.float32
            ) * (1.0 / math.sqrt(unit))
            expanded = jnp.exp(logits)
            probs = (expanded / jnp.sum(expanded, axis=1, keepdims=True)).astype(jnp.bfloat16)
            out[index, level] = dot32(probs, value).astype(jnp.bfloat16)


def attend_part(kept_a, other_a, kept_b, other_b, gains, width):
    unit = kept_a.shape[1] // 3
    length = (kept_a.shape[0] - EXTRA_ROWS) // 2
    return pl.pallas_call(
        lambda *refs: attend_kernel(width, *refs),
        in_specs=[vmem_spec()] * 5,
        out_specs=vmem_spec(),
        out_shape=jax.ShapeDtypeStruct((2, 2, length, unit), jnp.bfloat16),
        compiler_params=params(8),
        name="attend_part",
    )(kept_a, other_a, kept_b, other_b, gains)


def out_kernel(core, mine, *refs):
    heads = refs[0:4]
    weight_a, weight_b, mods, kept, sent, rows, total = refs[4:]
    _, _, length, unit = heads[0].shape
    for index, weight in enumerate((weight_a, weight_b)):
        for slot, head in enumerate(heads):
            at = at_block(jnp.bitwise_xor(mine[0], slot), unit)
            for level in range(2):
                rows[pl.ds(level * length, length), at] = head[index, level]
        result = dot32(rows[...], weight[...])
        gates = mods[index, 2]
        signed = gates[1:2] * result[:length] + gates[2:3] * result[length:]
        if index == 0:
            total[...] = -0.5 * signed
        else:
            total[...] = total[...] + 0.5 * signed
    cols = kept.shape[1]
    kept[...] = total[:, at_block(core[0], cols)]
    sent[...] = total[:, at_block(1 - core[0], cols)].astype(jnp.bfloat16)


def out_part(core, mine, heads, weight_a, weight_b, mods):
    length = heads[0].shape[2]
    depth, width = weight_a.shape
    return pl.pallas_call(
        out_kernel,
        in_specs=[smem_spec()] * 2 + [vmem_spec()] * 7,
        out_specs=[vmem_spec()] * 2,
        out_shape=[
            jax.ShapeDtypeStruct((length, width // 2), jnp.float32),
            jax.ShapeDtypeStruct((length, width // 2), jnp.bfloat16),
        ],
        scratch_shapes=[
            pltpu.VMEM((2 * length, depth), jnp.bfloat16),
            pltpu.VMEM((length, width), jnp.float32),
        ],
        compiler_params=params(16),
        name="out_part",
    )(core, mine, *heads, weight_a, weight_b, mods)


def grad_kernel(half, heads_t, rows, *refs):
    refs[-1][...] = dot32(heads_t[...], rows[...]).astype(jnp.bfloat16)


def grad_part(half, heads_t, rows, before, steps):
    depth, length = heads_t.shape
    cols = rows.shape[1]
    tile = depth // steps
    rest = [] if before is None else [before]
    grid_spec = pltpu.PrefetchScalarGridSpec(
        num_scalar_prefetch=1,
        grid=(steps,),
        in_specs=[
            pl.BlockSpec((tile, length), lambda n, w: (n, 0)),
            pl.BlockSpec((length, cols), lambda n, w: (0, 0)),
        ]
        + [any_spec()] * len(rest),
        out_specs=pl.BlockSpec((tile, cols), lambda n, w: (n, w[0])),
    )
    return pl.pallas_call(
        grad_kernel,
        grid_spec=grid_spec,
        out_shape=jax.ShapeDtypeStruct((depth, 2 * cols), jnp.bfloat16),
        input_output_aliases={3: 0} if rest else {},
        compiler_params=params(16),
        name="grad_part",
    )(half, heads_t, rows, *rest)


def exchange(array, axis, bit):
    return lax.ppermute(array, axis, [(i, i ^ bit) for i in range(lax.axis_size(axis))])


def both(mine, theirs):
    return mine.astype(jnp.float32) + theirs.astype(jnp.float32)


def heads_per_role(
    gen_heads,
    gen_resid,
    gen_out_w,
    gen_time_w,
    noise,
    steps,
    teacher_qkv,
    teacher_out,
    teacher_time,
    teacher_norm,
    critic_qkv,
    critic_out,
    critic_time,
    critic_norm,
):
    length = gen_heads.shape[0]
    roles, groups = lax.axis_size("role"), lax.axis_size("mp")
    role, seq, mp = lax.axis_index("role"), lax.axis_index("seq"), lax.axis_index("mp")
    part_cols = gen_heads.shape[1] // roles
    freq = gen_time_w.shape[0]
    seq_at, mine = [v.astype(jnp.int32).reshape(1) for v in (seq, mp)]
    core = (role % 2).astype(jnp.int32).reshape(1)
    half_cols = gen_resid.shape[1] // 2

    embed = jax.vmap(lambda t: time_embed(t, freq))(steps)
    embed = jnp.concatenate([embed, jnp.zeros((5, freq), jnp.bfloat16)], axis=0)
    levels = steps[1:3].astype(jnp.float32) / 1000.0
    weight = lax.dynamic_slice_in_dim(gen_out_w, core[0] * half_cols, half_cols, axis=1)
    full, sent = pack_part(seq_at, core, dot32(gen_heads, weight), embed, gen_time_w, gen_resid, noise)
    arrived = exchange(sent, "seq", 1)
    planes = [w.transpose(1, 0, 2) for w in (teacher_qkv, critic_qkv, teacher_time, critic_time)]
    mods, gate = mod_part(embed, planes[2], planes[3], gen_time_w, full)
    start = role * part_cols
    later, _ = lax.optimization_barrier((start, full))
    weight_a, weight_b = [lax.dynamic_slice_in_dim(w, later, part_cols, axis=2) for w in planes[:2]]
    joined = join_part(full, arrived, gate, weight_a, weight_b)
    swapped = exchange(joined, "role", 1)
    unit = part_cols // groups

    latent, kept_a, sent_a, kept_b, sent_b = qkv_part(
        seq_at, core, mine, levels, joined, swapped, noise, mods, weight_a, weight_b
    )
    arrived_a, arrived_b = exchange(sent_a, "mp", 1), exchange(sent_b, "mp", 2)
    out_a, out_b = [lax.dynamic_slice_in_dim(w, start, part_cols, axis=0) for w in (teacher_out, critic_out)]
    gains = jnp.stack([teacher_norm, critic_norm])
    gains = lax.dynamic_slice_in_dim(gains, start + mp * unit, unit, axis=2)
    arrived_a, arrived_b, out_a, out_b, gains = lax.optimization_barrier((arrived_a, arrived_b, out_a, out_b, gains))
    sum_a, sum_b = both(kept_a, arrived_a), both(kept_b, arrived_b)
    last_a = exchange(sum_a[1].astype(jnp.bfloat16), "mp", 2)
    last_b = exchange(sum_b[1].astype(jnp.bfloat16), "mp", 1)
    head = attend_part(sum_a[0], last_a, sum_b[0], last_b, gains, D)
    gathered = [head] + [exchange(head, "mp", bits) for bits in range(1, groups)]

    kept, sent = out_part(core, mine, gathered, out_a, out_b, mods)
    total = both(kept, exchange(sent, "role", 1)).astype(jnp.bfloat16)
    along_x = exchange(total, "seq", 1)
    along_y = exchange(total, "role", 2)
    across = lax.ppermute(
        total, ("role", "seq"), [(i, i ^ (2 * lax.axis_size("seq") + 1)) for i in range(roles * lax.axis_size("seq"))]
    )
    total = both(total, along_x) + both(along_y, across)
    gate_row = lax.dynamic_slice_in_dim(gate, core[0] * half_cols, half_cols, axis=1)[0:1]
    rows = (gate_row * total).astype(jnp.bfloat16)
    heads_t = gen_heads.T
    theirs = exchange(rows, "role", 1)
    weight_grad = grad_part(core, heads_t, rows, None, 2)
    weight_grad = grad_part(1 - core, heads_t, theirs, weight_grad, 2)
    return latent, weight_grad


def solution(mesh):
    in_specs = (
        P(None, "seq"),
        P("seq", "mp"),
        P("seq", "mp"),
        P(None, "mp"),
        P("seq", "mp"),
        P(),
        P("mp", None, "seq"),
        P("seq", "mp"),
        P(None, None, "mp"),
        P(None, "seq"),
        P("mp", None, "seq"),
        P("seq", "mp"),
        P(None, None, "mp"),
        P(None, "seq"),
    )
    out_specs = (P("seq", "mp"), P("seq", "mp"))
    roles, seqs, groups = mesh.shape["role"], mesh.shape["seq"], mesh.shape["mp"]

    def on_device(*arrays):
        heads_here = arrays[0].shape[1] // HEAD_DIM
        length = arrays[0].shape[0]
        fits = (roles, seqs, groups) == (4, 2, 4) and heads_here == roles * groups and length == HEAD_DIM
        return heads_per_role(*arrays) if fits else pass_per_role(*arrays)

    return jax.shard_map(
        on_device, mesh=mesh, in_specs=in_specs, out_specs=out_specs, check_vma=False
    )
```

```python
import math

import jax
import jax.numpy as jnp
from jax import lax
from jax.experimental import pallas as pl
from jax.experimental.pallas import tpu as pltpu
from jax.sharding import PartitionSpec as P

D = 5120
HEAD_DIM = 128


def time_embed(step_value, width):
    half_width = width // 2
    positions = jnp.arange(half_width, dtype=jnp.float32)
    frequencies = jnp.exp(positions * (-math.log(10000.0) / half_width))
    angles = step_value.astype(jnp.float32) * frequencies
    return jnp.concatenate([jnp.cos(angles), jnp.sin(angles)]).astype(jnp.bfloat16)


def head_norm(values, gains):
    factor = lax.rsqrt(jnp.mean(values * values, axis=-1, keepdims=True) + 1e-06)
    return (values * factor * gains).astype(jnp.bfloat16)


def attend(query_norm, key_norm, value_rows):
    full_length, heads_here, head_width = query_norm.shape
    query_blocks = query_norm.reshape(
        full_length // full_length, full_length, heads_here, head_width
    )

    def one_block(query_block):
        logits = jnp.einsum(
            "qhd,khd->hqk", query_block, key_norm, preferred_element_type=jnp.float32
        ) * (1.0 / math.sqrt(head_width))
        expanded = jnp.exp(logits)
        probs = (expanded / jnp.sum(expanded, axis=2, keepdims=True)).astype(jnp.bfloat16)
        return jnp.einsum(
            "hqk,khd->qhd", probs, value_rows, preferred_element_type=jnp.float32
        ).astype(jnp.bfloat16)

    head_out = lax.map(one_block, query_blocks)
    return head_out.reshape(full_length, heads_here * head_width)


def pass_per_role(
    gen_heads,
    gen_resid,
    gen_out_w,
    gen_time_w,
    noise,
    steps,
    teacher_qkv,
    teacher_out,
    teacher_time,
    teacher_norm,
    critic_qkv,
    critic_out,
    critic_time,
    critic_norm,
):
    full_length = gen_heads.shape[0]
    head_cols = gen_heads.shape[1]
    embed_width = gen_time_w.shape[0]
    gen_gate = jnp.dot(
        time_embed(steps[0], embed_width)[None, :], gen_time_w, preferred_element_type=jnp.float32
    )[0]
    block = gen_heads
    gen_proj = lax.psum_scatter(
        jnp.dot(block, gen_out_w, preferred_element_type=jnp.float32),
        "seq",
        scatter_dimension=0,
        tiled=True,
    )
    latent = (gen_resid.astype(jnp.float32) + gen_gate * gen_proj).astype(jnp.bfloat16)
    role_index = lax.axis_index("role")
    level = steps[1 + role_index // 2]
    use_critic = role_index % 2 == 1
    w_qkv = jnp.where(use_critic, critic_qkv, teacher_qkv)
    w_out = jnp.where(use_critic, critic_out, teacher_out)
    w_time = jnp.where(use_critic, critic_time, teacher_time)
    w_norm = jnp.where(use_critic, critic_norm, teacher_norm)
    noise_level = level.astype(jnp.float32) / 1000.0
    noisy = (
        (1.0 - noise_level) * latent.astype(jnp.float32) + noise_level * noise.astype(jnp.float32)
    ).astype(jnp.bfloat16)
    modulation = jnp.einsum(
        "f,fkd->kd", time_embed(level, embed_width), w_time, preferred_element_type=jnp.float32
    )
    shift_vec = modulation[0]
    scale_vec = modulation[1]
    gate_vec = modulation[2]
    gathered = lax.all_gather(noisy, "seq", axis=0, tiled=True)
    partial_squares = jnp.sum(jnp.square(gathered.astype(jnp.float32)), axis=1)
    scaled = (gathered.astype(jnp.float32) * (1.0 + scale_vec)).astype(jnp.bfloat16)
    flat_w = w_qkv.reshape(w_qkv.shape[0], 3 * head_cols)
    projected = jnp.dot(scaled, flat_w, preferred_element_type=jnp.float32)
    shift_proj = jnp.dot(
        shift_vec.astype(jnp.bfloat16)[None, :], flat_w, preferred_element_type=jnp.float32
    )[0]
    projected, squares, shift_proj = lax.psum((projected, partial_squares, shift_proj), "mp")
    mixed = projected * lax.rsqrt(squares / D + 1e-06)[:, None] + shift_proj
    heads_here = head_cols // HEAD_DIM
    mixed = mixed.reshape(full_length, 3, heads_here, HEAD_DIM)
    gains = w_norm.reshape(2, heads_here, HEAD_DIM)
    query_norm = head_norm(mixed[:, 0], gains[0])
    key_norm = head_norm(mixed[:, 1], gains[1])
    value_rows = mixed[:, 2].astype(jnp.bfloat16)
    head_out = attend(query_norm, key_norm, value_rows)
    weight_sign = jnp.where(use_critic, 0.5, -0.5)
    block = head_out
    summed_rows = lax.psum_scatter(
        weight_sign * (gate_vec * jnp.dot(block, w_out, preferred_element_type=jnp.float32)),
        ("role", "seq"),
        scatter_dimension=0,
        tiled=True,
    )
    grad_rows = lax.all_gather(
        (gen_gate * summed_rows).astype(jnp.bfloat16), ("role", "seq"), axis=0, tiled=True
    )
    weight_grad = lax.dot_general(
        gen_heads, grad_rows, (((0,), (0,)), ((), ())), preferred_element_type=jnp.float32
    )
    return (latent, weight_grad.astype(jnp.bfloat16))

MIB = 1024 * 1024
EXTRA_ROWS = 16


def vmem_spec():
    return pl.BlockSpec(memory_space=pltpu.VMEM)


def smem_spec():
    return pl.BlockSpec(memory_space=pltpu.SMEM)


def params(mebibytes):
    return pltpu.CompilerParams(vmem_limit_bytes=mebibytes * MIB)


def dot32(a, b):
    return jnp.dot(a, b, preferred_element_type=jnp.float32)


def at_block(index, size):
    return pl.ds(pl.multiple_of(index * size, size), size)


def any_spec():
    return pl.BlockSpec(memory_space=pl.ANY)


def cost(flops, moved):
    return pl.CostEstimate(flops=flops, bytes_accessed=moved, transcendentals=0)


def pack_kernel(seq, product, gate, resid, noise, full, sent):
    length = full.shape[0]
    own = resid.shape[0]
    full[...] = product[...] * gate[0:1, :]
    at = at_block(seq[0], own)
    full[at, :] = full[at, :] + resid[...].astype(jnp.float32)
    sent[pl.ds(0, length), :] = full[...].astype(jnp.bfloat16)
    sent[pl.ds(length, own), :] = noise[...]


def pack_part(seq, product, gate, resid, noise):
    length, width = product.shape
    own = resid.shape[0]
    return pl.pallas_call(
        pack_kernel,
        in_specs=[smem_spec()] + [vmem_spec()] * 4,
        out_specs=[vmem_spec()] * 2,
        out_shape=[
            jax.ShapeDtypeStruct((length, width), jnp.float32),
            jax.ShapeDtypeStruct((length + own, width), jnp.bfloat16),
        ],
        compiler_params=params(8),
        name="pack_part",
    )(seq, product, gate, resid, noise)


def mod_kernel(embed, time_a, time_b, mods):
    for k in range(3):
        mods[0, k] = dot32(embed[...], time_a[k])
        mods[1, k] = dot32(embed[...], time_b[k])


def mod_part(embed, time_a, time_b):
    width = time_a.shape[2]
    return pl.pallas_call(
        mod_kernel,
        in_specs=[vmem_spec()] * 3,
        out_specs=vmem_spec(),
        out_shape=jax.ShapeDtypeStruct((2, 3, 8, width), jnp.float32),
        compiler_params=params(8),
        name="mod_part",
    )(embed, time_a, time_b)


def join_kernel(full, arrived, joined):
    length = full.shape[0]
    own = arrived.shape[0] - length
    top = full[...] + arrived[pl.ds(0, length), :].astype(jnp.float32)
    joined[pl.ds(0, length), :] = top.astype(jnp.bfloat16)
    joined[pl.ds(length, own), :] = arrived[pl.ds(length, own), :]


def join_part(full, arrived):
    return pl.pallas_call(
        join_kernel,
        in_specs=[vmem_spec(), vmem_spec()],
        out_specs=vmem_spec(),
        out_shape=jax.ShapeDtypeStruct(arrived.shape, jnp.bfloat16),
        compiler_params=params(8),
        name="join_part",
    )(full, arrived)


def project(index, stride, mine, noisy, squares, mods, weight, kept, sent, result):
    tokens = noisy.shape[0]
    length = tokens // 2
    unit = squares.shape[1] // 2
    groups = weight.shape[2] // unit
    scale = mods[index, 1]
    shift = mods[index, 0]
    spread = noisy.astype(jnp.float32)
    top = spread[:length] * (1.0 + scale[1:2])
    low = spread[length:] * (1.0 + scale[2:3])
    extra = jnp.concatenate([shift[1:3], jnp.zeros((EXTRA_ROWS - 2, shift.shape[1]), jnp.float32)], axis=0)
    rows = jnp.concatenate([top, low, extra], axis=0).astype(jnp.bfloat16)
    row_id = lax.broadcasted_iota(jnp.int32, (EXTRA_ROWS, unit), 0)
    for part in range(3):
        result[...] = dot32(rows, weight[part])
        cols = pl.ds(part * unit, unit)
        for slot in range(groups):
            at = at_block(jnp.bitwise_xor(mine, slot), unit)
            goal = sent if slot & stride else kept
            place = slot // 2 if stride == 1 else slot % 2
            goal[place, pl.ds(0, tokens), cols] = result[pl.ds(0, tokens), at].astype(jnp.bfloat16)
            tail = jnp.where(row_id < 2, result[pl.ds(tokens, EXTRA_ROWS), at], 0.0)
            for level in range(2):
                tail = jnp.where(row_id == 2 + level, squares[0:1, level * length : (level + 1) * length], tail)
            goal[place, pl.ds(tokens, EXTRA_ROWS), cols] = tail.astype(jnp.bfloat16)


def qkv_kernel(seq, core, mine, levels, joined, swapped, noise, mods, weight_a, weight_b, latent, *refs):
    chunks, (values, noises, result) = refs[:4], refs[4:]
    length, cols = values.shape[0], joined.shape[1]
    own = latent.shape[0]
    tokens = 2 * length
    left, right = at_block(core[0], cols), at_block(1 - core[0], cols)
    values[:, left] = joined[pl.ds(0, length), :]
    values[:, right] = swapped[pl.ds(0, length), :]
    latent[...] = values[at_block(seq[0], own), :]
    noises[at_block(seq[0], own), :] = noise[...]
    theirs = at_block(1 - seq[0], own)
    noises[theirs, left] = joined[pl.ds(length, own), :]
    noises[theirs, right] = swapped[pl.ds(length, own), :]
    spread = values[...].astype(jnp.float32)
    noise_rows = noises[...].astype(jnp.float32)
    mixed = jnp.concatenate(
        [(1.0 - levels[level]) * spread + levels[level] * noise_rows for level in range(2)], axis=0
    ).astype(jnp.bfloat16)
    wide = mixed.astype(jnp.float32)
    sums = jnp.sum(wide * wide, axis=1, keepdims=True)
    sums = jnp.broadcast_to(sums, (tokens, length)).T[0:8]
    for index, weight in enumerate((weight_a, weight_b)):
        project(index, index + 1, mine[0], mixed, sums, mods, weight, *chunks[2 * index : 2 * index + 2], result)


def qkv_part(seq, core, mine, levels, joined, swapped, noise, mods, weight_a, weight_b):
    own, width = noise.shape
    length = joined.shape[0] - own
    tokens = 2 * length
    cols = weight_a.shape[2]
    return pl.pallas_call(
        qkv_kernel,
        in_specs=[smem_spec()] * 4 + [vmem_spec()] * 6,
        out_specs=[vmem_spec()] * 5,
        out_shape=[jax.ShapeDtypeStruct((own, width), jnp.bfloat16)]
        + [jax.ShapeDtypeStruct((cols // length // 2, tokens + EXTRA_ROWS, 3 * length), jnp.bfloat16)] * 4,
        scratch_shapes=[
            pltpu.VMEM((length, width), jnp.bfloat16),
            pltpu.VMEM((length, width), jnp.bfloat16),
            pltpu.VMEM((tokens + EXTRA_ROWS, cols), jnp.float32),
        ],
        compiler_params=params(20),
        name="qkv_part",
    )(seq, core, mine, levels, joined, swapped, noise, mods, weight_a, weight_b)


def attend_kernel(width, kept_a, other_a, kept_b, other_b, gains, out):
    _, _, length, unit = out.shape
    tokens = 2 * length
    for index, (kept, other) in enumerate(((kept_a, other_a), (kept_b, other_b))):
        mixed = kept[...] + other[...].astype(jnp.float32)
        extra = mixed[tokens:]
        for level in range(2):
            rows_at = slice(level * length, (level + 1) * length)
            squares = jnp.broadcast_to(extra[2 + level : 3 + level, :unit], (unit, unit)).T
            factor = lax.rsqrt(squares * (1.0 / width) + 1e-06)

            def pick(part):
                cols = slice(part * unit, (part + 1) * unit)
                return mixed[rows_at, cols] * factor + extra[level : level + 1, cols]

            def normed(part):
                rows = pick(part)
                mean = jnp.mean(rows * rows, axis=1, keepdims=True)
                return (rows * lax.rsqrt(mean + 1e-06) * gains[index, part : part + 1, :]).astype(jnp.bfloat16)

            query, key = normed(0), normed(1)
            value = pick(2).astype(jnp.bfloat16)
            logits = lax.dot_general(
                query, key, (((1,), (1,)), ((), ())), preferred_element_type=jnp.float32
            ) * (1.0 / math.sqrt(unit))
            expanded = jnp.exp(logits)
            probs = (expanded / jnp.sum(expanded, axis=1, keepdims=True)).astype(jnp.bfloat16)
            out[index, level] = dot32(probs, value).astype(jnp.bfloat16)


def attend_part(kept_a, other_a, kept_b, other_b, gains, width):
    unit = kept_a.shape[1] // 3
    length = (kept_a.shape[0] - EXTRA_ROWS) // 2
    return pl.pallas_call(
        lambda *refs: attend_kernel(width, *refs),
        in_specs=[vmem_spec()] * 5,
        out_specs=vmem_spec(),
        out_shape=jax.ShapeDtypeStruct((2, 2, length, unit), jnp.bfloat16),
        compiler_params=params(8),
        name="attend_part",
    )(kept_a, other_a, kept_b, other_b, gains)


def out_kernel(core, mine, *refs):
    heads = refs[0:4]
    weight_a, weight_b, mods, kept, sent, rows, total = refs[4:]
    _, _, length, unit = heads[0].shape
    for index, weight in enumerate((weight_a, weight_b)):
        for slot, head in enumerate(heads):
            at = at_block(jnp.bitwise_xor(mine[0], slot), unit)
            for level in range(2):
                rows[pl.ds(level * length, length), at] = head[index, level]
        result = dot32(rows[...], weight[...])
        gates = mods[index, 2]
        signed = gates[1:2] * result[:length] + gates[2:3] * result[length:]
        if index == 0:
            total[...] = -0.5 * signed
        else:
            total[...] = total[...] + 0.5 * signed
    cols = kept.shape[1]
    kept[...] = total[:, at_block(core[0], cols)]
    sent[...] = total[:, at_block(1 - core[0], cols)].astype(jnp.bfloat16)


def out_part(core, mine, heads, weight_a, weight_b, mods):
    length = heads[0].shape[2]
    depth, width = weight_a.shape
    return pl.pallas_call(
        out_kernel,
        in_specs=[smem_spec()] * 2 + [vmem_spec()] * 7,
        out_specs=[vmem_spec()] * 2,
        out_shape=[
            jax.ShapeDtypeStruct((length, width // 2), jnp.float32),
            jax.ShapeDtypeStruct((length, width // 2), jnp.bfloat16),
        ],
        scratch_shapes=[
            pltpu.VMEM((2 * length, depth), jnp.bfloat16),
            pltpu.VMEM((length, width), jnp.float32),
        ],
        compiler_params=params(16),
        name="out_part",
    )(core, mine, *heads, weight_a, weight_b, mods)


def grad_kernel(half, heads_t, rows, *refs):
    refs[-1][...] = dot32(heads_t[...], rows[...]).astype(jnp.bfloat16)


def grad_part(half, heads_t, rows, before, steps):
    depth, length = heads_t.shape
    cols = rows.shape[1]
    tile = depth // steps
    rest = [] if before is None else [before]
    grid_spec = pltpu.PrefetchScalarGridSpec(
        num_scalar_prefetch=1,
        grid=(steps,),
        in_specs=[
            pl.BlockSpec((tile, length), lambda n, w: (n, 0)),
            pl.BlockSpec((length, cols), lambda n, w: (0, 0)),
        ]
        + [any_spec()] * len(rest),
        out_specs=pl.BlockSpec((tile, cols), lambda n, w: (n, w[0])),
    )
    return pl.pallas_call(
        grad_kernel,
        grid_spec=grid_spec,
        out_shape=jax.ShapeDtypeStruct((depth, 2 * cols), jnp.bfloat16),
        input_output_aliases={3: 0} if rest else {},
        compiler_params=params(16),
        name="grad_part",
    )(half, heads_t, rows, *rest)


def exchange(array, axis, bit):
    return lax.ppermute(array, axis, [(i, i ^ bit) for i in range(lax.axis_size(axis))])


def both(mine, theirs):
    return mine.astype(jnp.float32) + theirs.astype(jnp.float32)


def heads_per_role(
    gen_heads,
    gen_resid,
    gen_out_w,
    gen_time_w,
    noise,
    steps,
    teacher_qkv,
    teacher_out,
    teacher_time,
    teacher_norm,
    critic_qkv,
    critic_out,
    critic_time,
    critic_norm,
):
    length = gen_heads.shape[0]
    roles, groups = lax.axis_size("role"), lax.axis_size("mp")
    role, seq, mp = lax.axis_index("role"), lax.axis_index("seq"), lax.axis_index("mp")
    part_cols = gen_heads.shape[1] // roles
    freq = gen_time_w.shape[0]
    seq_at, mine = [v.astype(jnp.int32).reshape(1) for v in (seq, mp)]
    core = (role % 2).astype(jnp.int32).reshape(1)
    half_cols = gen_resid.shape[1] // 2

    embed = jax.vmap(lambda t: time_embed(t, freq))(steps)
    embed = jnp.concatenate([embed, jnp.zeros((5, freq), jnp.bfloat16)], axis=0)
    levels = steps[1:3].astype(jnp.float32) / 1000.0
    begin = core[0] * half_cols
    weight, time_half, resid_half, noise_half = [
        lax.dynamic_slice_in_dim(w, begin, half_cols, axis=1) for w in (gen_out_w, gen_time_w, gen_resid, noise)
    ]
    gate = dot32(embed, time_half)
    full, sent = pack_part(seq_at, dot32(gen_heads, weight), gate, resid_half, noise_half)
    arrived = exchange(sent, "seq", 1)
    start = role * part_cols
    later, embed, _ = lax.optimization_barrier((start, embed, full))
    planes = [w.transpose(1, 0, 2) for w in (teacher_qkv, critic_qkv, teacher_time, critic_time)]
    mods = mod_part(embed, planes[2], planes[3])
    weight_a, weight_b = [lax.dynamic_slice_in_dim(w, later, part_cols, axis=2) for w in planes[:2]]
    arrived, mods, weight_a, weight_b = lax.optimization_barrier((arrived, mods, weight_a, weight_b))
    joined = join_part(full, arrived)
    swapped = exchange(joined, "role", 1)
    unit = part_cols // groups

    latent, kept_a, sent_a, kept_b, sent_b = qkv_part(
        seq_at, core, mine, levels, joined, swapped, noise, mods, weight_a, weight_b
    )
    arrived_a, arrived_b = exchange(sent_a, "mp", 1), exchange(sent_b, "mp", 2)
    out_a, out_b = [lax.dynamic_slice_in_dim(w, start, part_cols, axis=0) for w in (teacher_out, critic_out)]
    gains = jnp.stack([teacher_norm, critic_norm])
    gains = lax.dynamic_slice_in_dim(gains, start + mp * unit, unit, axis=2)
    arrived_a, arrived_b, out_a, out_b, gains = lax.optimization_barrier((arrived_a, arrived_b, out_a, out_b, gains))
    sum_a, sum_b = both(kept_a, arrived_a), both(kept_b, arrived_b)
    last_a = exchange(sum_a[1].astype(jnp.bfloat16), "mp", 2)
    last_b = exchange(sum_b[1].astype(jnp.bfloat16), "mp", 1)
    head = attend_part(sum_a[0], last_a, sum_b[0], last_b, gains, D)
    near, far = exchange(head, "mp", 1), exchange(head, "mp", 2)
    gathered = head, near, far, exchange(far, "mp", 1)

    kept, sent = out_part(core, mine, gathered, out_a, out_b, mods)
    total = both(kept, exchange(sent, "role", 1)).astype(jnp.bfloat16)
    along_x = exchange(total, "seq", 1)
    along_y = exchange(total, "role", 2)
    across = lax.ppermute(
        total, ("role", "seq"), [(i, i ^ (2 * lax.axis_size("seq") + 1)) for i in range(roles * lax.axis_size("seq"))]
    )
    total = both(total, along_x) + both(along_y, across)
    rows = (gate[0:1] * total).astype(jnp.bfloat16)
    heads_t = gen_heads.T
    theirs = exchange(rows, "role", 1)
    weight_grad = grad_part(core, heads_t, rows, None, 2)
    weight_grad = grad_part(1 - core, heads_t, theirs, weight_grad, 2)
    return latent, weight_grad


def solution(mesh):
    in_specs = (
        P(None, "seq"),
        P("seq", "mp"),
        P("seq", "mp"),
        P(None, "mp"),
        P("seq", "mp"),
        P(),
        P("mp", None, "seq"),
        P("seq", "mp"),
        P(None, None, "mp"),
        P(None, "seq"),
        P("mp", None, "seq"),
        P("seq", "mp"),
        P(None, None, "mp"),
        P(None, "seq"),
    )
    out_specs = (P("seq", "mp"), P("seq", "mp"))
    roles, seqs, groups = mesh.shape["role"], mesh.shape["seq"], mesh.shape["mp"]

    def on_device(*arrays):
        heads_here = arrays[0].shape[1] // HEAD_DIM
        length = arrays[0].shape[0]
        fits = (roles, seqs, groups) == (4, 2, 4) and heads_here == roles * groups and length == HEAD_DIM
        return heads_per_role(*arrays) if fits else pass_per_role(*arrays)

    return jax.shard_map(
        on_device, mesh=mesh, in_specs=in_specs, out_specs=out_specs, check_vma=False
    )
```

```python
import math

import jax
import jax.numpy as jnp
from jax import lax
from jax.experimental import pallas as pl
from jax.experimental.pallas import tpu as pltpu
from jax.sharding import PartitionSpec as P

D = 5120
HEAD_DIM = 128


def time_embed(step_value, width):
    half_width = width // 2
    positions = jnp.arange(half_width, dtype=jnp.float32)
    frequencies = jnp.exp(positions * (-math.log(10000.0) / half_width))
    angles = step_value.astype(jnp.float32) * frequencies
    return jnp.concatenate([jnp.cos(angles), jnp.sin(angles)]).astype(jnp.bfloat16)


def head_norm(values, gains):
    factor = lax.rsqrt(jnp.mean(values * values, axis=-1, keepdims=True) + 1e-06)
    return (values * factor * gains).astype(jnp.bfloat16)


def attend(query_norm, key_norm, value_rows):
    full_length, heads_here, head_width = query_norm.shape
    query_blocks = query_norm.reshape(
        full_length // full_length, full_length, heads_here, head_width
    )

    def one_block(query_block):
        logits = jnp.einsum(
            "qhd,khd->hqk", query_block, key_norm, preferred_element_type=jnp.float32
        ) * (1.0 / math.sqrt(head_width))
        expanded = jnp.exp(logits)
        probs = (expanded / jnp.sum(expanded, axis=2, keepdims=True)).astype(jnp.bfloat16)
        return jnp.einsum(
            "hqk,khd->qhd", probs, value_rows, preferred_element_type=jnp.float32
        ).astype(jnp.bfloat16)

    head_out = lax.map(one_block, query_blocks)
    return head_out.reshape(full_length, heads_here * head_width)


def pass_per_role(
    gen_heads,
    gen_resid,
    gen_out_w,
    gen_time_w,
    noise,
    steps,
    teacher_qkv,
    teacher_out,
    teacher_time,
    teacher_norm,
    critic_qkv,
    critic_out,
    critic_time,
    critic_norm,
):
    full_length = gen_heads.shape[0]
    head_cols = gen_heads.shape[1]
    embed_width = gen_time_w.shape[0]
    gen_gate = jnp.dot(
        time_embed(steps[0], embed_width)[None, :], gen_time_w, preferred_element_type=jnp.float32
    )[0]
    block = gen_heads
    gen_proj = lax.psum_scatter(
        jnp.dot(block, gen_out_w, preferred_element_type=jnp.float32),
        "seq",
        scatter_dimension=0,
        tiled=True,
    )
    latent = (gen_resid.astype(jnp.float32) + gen_gate * gen_proj).astype(jnp.bfloat16)
    role_index = lax.axis_index("role")
    level = steps[1 + role_index // 2]
    use_critic = role_index % 2 == 1
    w_qkv = jnp.where(use_critic, critic_qkv, teacher_qkv)
    w_out = jnp.where(use_critic, critic_out, teacher_out)
    w_time = jnp.where(use_critic, critic_time, teacher_time)
    w_norm = jnp.where(use_critic, critic_norm, teacher_norm)
    noise_level = level.astype(jnp.float32) / 1000.0
    noisy = (
        (1.0 - noise_level) * latent.astype(jnp.float32) + noise_level * noise.astype(jnp.float32)
    ).astype(jnp.bfloat16)
    modulation = jnp.einsum(
        "f,fkd->kd", time_embed(level, embed_width), w_time, preferred_element_type=jnp.float32
    )
    shift_vec = modulation[0]
    scale_vec = modulation[1]
    gate_vec = modulation[2]
    gathered = lax.all_gather(noisy, "seq", axis=0, tiled=True)
    partial_squares = jnp.sum(jnp.square(gathered.astype(jnp.float32)), axis=1)
    scaled = (gathered.astype(jnp.float32) * (1.0 + scale_vec)).astype(jnp.bfloat16)
    flat_w = w_qkv.reshape(w_qkv.shape[0], 3 * head_cols)
    projected = jnp.dot(scaled, flat_w, preferred_element_type=jnp.float32)
    shift_proj = jnp.dot(
        shift_vec.astype(jnp.bfloat16)[None, :], flat_w, preferred_element_type=jnp.float32
    )[0]
    projected, squares, shift_proj = lax.psum((projected, partial_squares, shift_proj), "mp")
    mixed = projected * lax.rsqrt(squares / D + 1e-06)[:, None] + shift_proj
    heads_here = head_cols // HEAD_DIM
    mixed = mixed.reshape(full_length, 3, heads_here, HEAD_DIM)
    gains = w_norm.reshape(2, heads_here, HEAD_DIM)
    query_norm = head_norm(mixed[:, 0], gains[0])
    key_norm = head_norm(mixed[:, 1], gains[1])
    value_rows = mixed[:, 2].astype(jnp.bfloat16)
    head_out = attend(query_norm, key_norm, value_rows)
    weight_sign = jnp.where(use_critic, 0.5, -0.5)
    block = head_out
    summed_rows = lax.psum_scatter(
        weight_sign * (gate_vec * jnp.dot(block, w_out, preferred_element_type=jnp.float32)),
        ("role", "seq"),
        scatter_dimension=0,
        tiled=True,
    )
    grad_rows = lax.all_gather(
        (gen_gate * summed_rows).astype(jnp.bfloat16), ("role", "seq"), axis=0, tiled=True
    )
    weight_grad = lax.dot_general(
        gen_heads, grad_rows, (((0,), (0,)), ((), ())), preferred_element_type=jnp.float32
    )
    return (latent, weight_grad.astype(jnp.bfloat16))

MIB = 1024 * 1024
EXTRA_ROWS = 16


def vmem_spec():
    return pl.BlockSpec(memory_space=pltpu.VMEM)


def smem_spec():
    return pl.BlockSpec(memory_space=pltpu.SMEM)


def params(mebibytes):
    return pltpu.CompilerParams(vmem_limit_bytes=mebibytes * MIB)


def dot32(a, b):
    return jnp.dot(a, b, preferred_element_type=jnp.float32)


def at_block(index, size):
    return pl.ds(pl.multiple_of(index * size, size), size)


def any_spec():
    return pl.BlockSpec(memory_space=pl.ANY)


def cost(flops, moved):
    return pl.CostEstimate(flops=flops, bytes_accessed=moved, transcendentals=0)


def pack_kernel(seq, product, gate, resid, noise, full, sent):
    length = full.shape[0]
    own = resid.shape[0]
    full[...] = product[...] * gate[0:1, :]
    at = at_block(seq[0], own)
    full[at, :] = full[at, :] + resid[...].astype(jnp.float32)
    sent[pl.ds(0, length), :] = full[...].astype(jnp.bfloat16)
    sent[pl.ds(length, own), :] = noise[...]


def pack_part(seq, product, gate, resid, noise):
    length, width = product.shape
    own = resid.shape[0]
    return pl.pallas_call(
        pack_kernel,
        in_specs=[smem_spec()] + [vmem_spec()] * 4,
        out_specs=[vmem_spec()] * 2,
        out_shape=[
            jax.ShapeDtypeStruct((length, width), jnp.float32),
            jax.ShapeDtypeStruct((length + own, width), jnp.bfloat16),
        ],
        compiler_params=params(8),
        name="pack_part",
    )(seq, product, gate, resid, noise)


def mod_kernel(embed, time_a, time_b, mods):
    for k in range(3):
        mods[0, k] = dot32(embed[...], time_a[k])
        mods[1, k] = dot32(embed[...], time_b[k])


def mod_part(embed, time_a, time_b):
    width = time_a.shape[2]
    return pl.pallas_call(
        mod_kernel,
        in_specs=[vmem_spec()] * 3,
        out_specs=vmem_spec(),
        out_shape=jax.ShapeDtypeStruct((2, 3, 8, width), jnp.float32),
        compiler_params=params(8),
        name="mod_part",
    )(embed, time_a, time_b)


def join_kernel(full, arrived, joined):
    length = full.shape[0]
    own = arrived.shape[0] - length
    top = full[...] + arrived[pl.ds(0, length), :].astype(jnp.float32)
    joined[pl.ds(0, length), :] = top.astype(jnp.bfloat16)
    joined[pl.ds(length, own), :] = arrived[pl.ds(length, own), :]


def join_part(full, arrived):
    return pl.pallas_call(
        join_kernel,
        in_specs=[vmem_spec(), vmem_spec()],
        out_specs=vmem_spec(),
        out_shape=jax.ShapeDtypeStruct(arrived.shape, jnp.bfloat16),
        compiler_params=params(8),
        name="join_part",
    )(full, arrived)


def project(index, stride, mine, noisy, squares, mods, weight, kept, sent, result):
    tokens = noisy.shape[0]
    length = tokens // 2
    unit = squares.shape[1] // 2
    groups = weight.shape[2] // unit
    scale = mods[index, 1]
    shift = mods[index, 0]
    spread = noisy.astype(jnp.float32)
    top = spread[:length] * (1.0 + scale[1:2])
    low = spread[length:] * (1.0 + scale[2:3])
    extra = jnp.concatenate([shift[1:3], jnp.zeros((EXTRA_ROWS - 2, shift.shape[1]), jnp.float32)], axis=0)
    rows = jnp.concatenate([top, low, extra], axis=0).astype(jnp.bfloat16)
    row_id = lax.broadcasted_iota(jnp.int32, (EXTRA_ROWS, unit), 0)
    for part in range(3):
        result[...] = dot32(rows, weight[part])
        cols = pl.ds(part * unit, unit)
        for slot in range(groups):
            at = at_block(jnp.bitwise_xor(mine, slot), unit)
            goal = sent if slot & stride else kept
            place = slot // 2 if stride == 1 else slot % 2
            goal[place, pl.ds(0, tokens), cols] = result[pl.ds(0, tokens), at].astype(jnp.bfloat16)
            tail = jnp.where(row_id < 2, result[pl.ds(tokens, EXTRA_ROWS), at], 0.0)
            for level in range(2):
                tail = jnp.where(row_id == 2 + level, squares[0:1, level * length : (level + 1) * length], tail)
            goal[place, pl.ds(tokens, EXTRA_ROWS), cols] = tail.astype(jnp.bfloat16)


def qkv_kernel(seq, core, mine, levels, joined, swapped, noise, mods, weight_a, weight_b, latent, *refs):
    chunks, (values, noises, result) = refs[:4], refs[4:]
    length, cols = values.shape[0], joined.shape[1]
    own = latent.shape[0]
    tokens = 2 * length
    left, right = at_block(core[0], cols), at_block(1 - core[0], cols)
    values[:, left] = joined[pl.ds(0, length), :]
    values[:, right] = swapped[pl.ds(0, length), :]
    latent[...] = values[at_block(seq[0], own), :]
    noises[at_block(seq[0], own), :] = noise[...]
    theirs = at_block(1 - seq[0], own)
    noises[theirs, left] = joined[pl.ds(length, own), :]
    noises[theirs, right] = swapped[pl.ds(length, own), :]
    spread = values[...].astype(jnp.float32)
    noise_rows = noises[...].astype(jnp.float32)
    mixed = jnp.concatenate(
        [(1.0 - levels[level]) * spread + levels[level] * noise_rows for level in range(2)], axis=0
    ).astype(jnp.bfloat16)
    wide = mixed.astype(jnp.float32)
    sums = jnp.sum(wide * wide, axis=1, keepdims=True)
    sums = jnp.broadcast_to(sums, (tokens, length)).T[0:8]
    for index, weight in enumerate((weight_a, weight_b)):
        project(index, index + 1, mine[0], mixed, sums, mods, weight, *chunks[2 * index : 2 * index + 2], result)


def qkv_part(seq, core, mine, levels, joined, swapped, noise, mods, weight_a, weight_b):
    own, width = noise.shape
    length = joined.shape[0] - own
    tokens = 2 * length
    cols = weight_a.shape[2]
    return pl.pallas_call(
        qkv_kernel,
        in_specs=[smem_spec()] * 4 + [vmem_spec()] * 6,
        out_specs=[vmem_spec()] * 5,
        out_shape=[jax.ShapeDtypeStruct((own, width), jnp.bfloat16)]
        + [jax.ShapeDtypeStruct((cols // length // 2, tokens + EXTRA_ROWS, 3 * length), jnp.bfloat16)] * 4,
        scratch_shapes=[
            pltpu.VMEM((length, width), jnp.bfloat16),
            pltpu.VMEM((length, width), jnp.bfloat16),
            pltpu.VMEM((tokens + EXTRA_ROWS, cols), jnp.float32),
        ],
        compiler_params=params(20),
        name="qkv_part",
    )(seq, core, mine, levels, joined, swapped, noise, mods, weight_a, weight_b)


def attend_kernel(width, kept_a, other_a, kept_b, other_b, gains, out):
    _, _, length, unit = out.shape
    tokens = 2 * length
    for index, (kept, other) in enumerate(((kept_a, other_a), (kept_b, other_b))):
        mixed = kept[...] + other[...].astype(jnp.float32)
        extra = mixed[tokens:]
        for level in range(2):
            rows_at = slice(level * length, (level + 1) * length)
            squares = jnp.broadcast_to(extra[2 + level : 3 + level, :unit], (unit, unit)).T
            factor = lax.rsqrt(squares * (1.0 / width) + 1e-06)

            def pick(part):
                cols = slice(part * unit, (part + 1) * unit)
                return mixed[rows_at, cols] * factor + extra[level : level + 1, cols]

            def normed(part):
                rows = pick(part)
                mean = jnp.mean(rows * rows, axis=1, keepdims=True)
                return (rows * lax.rsqrt(mean + 1e-06) * gains[index, part : part + 1, :]).astype(jnp.bfloat16)

            query, key = normed(0), normed(1)
            value = pick(2).astype(jnp.bfloat16)
            logits = lax.dot_general(
                query, key, (((1,), (1,)), ((), ())), preferred_element_type=jnp.float32
            ) * (1.0 / math.sqrt(unit))
            expanded = jnp.exp(logits)
            probs = (expanded / jnp.sum(expanded, axis=1, keepdims=True)).astype(jnp.bfloat16)
            out[index, level] = dot32(probs, value).astype(jnp.bfloat16)


def attend_part(kept_a, other_a, kept_b, other_b, gains, width):
    unit = kept_a.shape[1] // 3
    length = (kept_a.shape[0] - EXTRA_ROWS) // 2
    return pl.pallas_call(
        lambda *refs: attend_kernel(width, *refs),
        in_specs=[vmem_spec()] * 5,
        out_specs=vmem_spec(),
        out_shape=jax.ShapeDtypeStruct((2, 2, length, unit), jnp.bfloat16),
        compiler_params=params(8),
        name="attend_part",
    )(kept_a, other_a, kept_b, other_b, gains)


def out_kernel(core, mine, *refs):
    heads = refs[0:4]
    weight_a, weight_b, mods, kept, sent, rows, total = refs[4:]
    _, _, length, unit = heads[0].shape
    for index, weight in enumerate((weight_a, weight_b)):
        for slot, head in enumerate(heads):
            at = at_block(jnp.bitwise_xor(mine[0], slot), unit)
            for level in range(2):
                rows[pl.ds(level * length, length), at] = head[index, level]
        result = dot32(rows[...], weight[...])
        gates = mods[index, 2]
        signed = gates[1:2] * result[:length] + gates[2:3] * result[length:]
        if index == 0:
            total[...] = -0.5 * signed
        else:
            total[...] = total[...] + 0.5 * signed
    cols = kept.shape[1]
    kept[...] = total[:, at_block(core[0], cols)]
    sent[...] = total[:, at_block(1 - core[0], cols)].astype(jnp.bfloat16)


def out_part(core, mine, heads, weight_a, weight_b, mods):
    length = heads[0].shape[2]
    depth, width = weight_a.shape
    return pl.pallas_call(
        out_kernel,
        in_specs=[smem_spec()] * 2 + [vmem_spec()] * 7,
        out_specs=[vmem_spec()] * 2,
        out_shape=[
            jax.ShapeDtypeStruct((length, width // 2), jnp.float32),
            jax.ShapeDtypeStruct((length, width // 2), jnp.bfloat16),
        ],
        scratch_shapes=[
            pltpu.VMEM((2 * length, depth), jnp.bfloat16),
            pltpu.VMEM((length, width), jnp.float32),
        ],
        compiler_params=params(16),
        name="out_part",
    )(core, mine, *heads, weight_a, weight_b, mods)


def grad_kernel(half, heads_t, rows, *refs):
    refs[-1][...] = dot32(heads_t[...], rows[...]).astype(jnp.bfloat16)


def grad_part(half, heads_t, rows, before, steps):
    depth, length = heads_t.shape
    cols = rows.shape[1]
    tile = depth // steps
    rest = [] if before is None else [before]
    grid_spec = pltpu.PrefetchScalarGridSpec(
        num_scalar_prefetch=1,
        grid=(steps,),
        in_specs=[
            pl.BlockSpec((tile, length), lambda n, w: (n, 0)),
            pl.BlockSpec((length, cols), lambda n, w: (0, 0)),
        ]
        + [any_spec()] * len(rest),
        out_specs=pl.BlockSpec((tile, cols), lambda n, w: (n, w[0])),
    )
    return pl.pallas_call(
        grad_kernel,
        grid_spec=grid_spec,
        out_shape=jax.ShapeDtypeStruct((depth, 2 * cols), jnp.bfloat16),
        input_output_aliases={3: 0} if rest else {},
        compiler_params=params(16),
        name="grad_part",
    )(half, heads_t, rows, *rest)


def exchange(array, axis, bit):
    return lax.ppermute(array, axis, [(i, i ^ bit) for i in range(lax.axis_size(axis))])


def take(array, begin, size, axis):
    return lax.dynamic_slice_in_dim(array, begin, size, axis=axis, allow_negative_indices=False)


def both(mine, theirs):
    return mine.astype(jnp.float32) + theirs.astype(jnp.float32)


def heads_per_role(
    gen_heads,
    gen_resid,
    gen_out_w,
    gen_time_w,
    noise,
    steps,
    teacher_qkv,
    teacher_out,
    teacher_time,
    teacher_norm,
    critic_qkv,
    critic_out,
    critic_time,
    critic_norm,
):
    length = gen_heads.shape[0]
    roles, groups = lax.axis_size("role"), lax.axis_size("mp")
    role, seq, mp = lax.axis_index("role"), lax.axis_index("seq"), lax.axis_index("mp")
    part_cols = gen_heads.shape[1] // roles
    freq = gen_time_w.shape[0]
    core = role % 2
    half_cols = gen_resid.shape[1] // 2
    unit = part_cols // groups

    embed = jax.vmap(lambda t: time_embed(t, freq))(steps)
    embed = jnp.concatenate([embed, jnp.zeros((5, freq), jnp.bfloat16)], axis=0)
    levels = steps[1:3].astype(jnp.float32) / 1000.0
    start = role * part_cols
    scalars = [seq, mp, core, 1 - core, core * half_cols, start, start + mp * unit]
    embed, levels, *scalars = lax.optimization_barrier((embed, levels, *scalars))
    seq_at, mine, core, other_core = [v.astype(jnp.int32).reshape(1) for v in scalars[:4]]
    begin, start, gain_at = scalars[4:]
    weight, time_half, resid_half, noise_half = [
        take(w, begin, half_cols, 1) for w in (gen_out_w, gen_time_w, gen_resid, noise)
    ]
    gate = dot32(embed, time_half)
    full, sent = pack_part(seq_at, dot32(gen_heads, weight), gate, resid_half, noise_half)
    arrived = exchange(sent, "seq", 1)
    later, embed, _ = lax.optimization_barrier((start, embed, full))
    planes = [w.transpose(1, 0, 2) for w in (teacher_qkv, critic_qkv, teacher_time, critic_time)]
    mods = mod_part(embed, planes[2], planes[3])
    weight_a, weight_b = [take(w, later, part_cols, 2) for w in planes[:2]]
    arrived, mods, weight_a, weight_b = lax.optimization_barrier((arrived, mods, weight_a, weight_b))
    joined = join_part(full, arrived)
    swapped = exchange(joined, "role", 1)

    latent, kept_a, sent_a, kept_b, sent_b = qkv_part(
        seq_at, core, mine, levels, joined, swapped, noise, mods, weight_a, weight_b
    )
    arrived_a, arrived_b = exchange(sent_a, "mp", 1), exchange(sent_b, "mp", 2)
    out_a, out_b = [take(w, start, part_cols, 0) for w in (teacher_out, critic_out)]
    gains = jnp.stack([teacher_norm, critic_norm])
    gains = take(gains, gain_at, unit, 2)
    arrived_a, arrived_b, out_a, out_b, gains = lax.optimization_barrier((arrived_a, arrived_b, out_a, out_b, gains))
    sum_a, sum_b = both(kept_a, arrived_a), both(kept_b, arrived_b)
    last_a = exchange(sum_a[1].astype(jnp.bfloat16), "mp", 2)
    last_b = exchange(sum_b[1].astype(jnp.bfloat16), "mp", 1)
    head = attend_part(sum_a[0], last_a, sum_b[0], last_b, gains, D)
    near, far = exchange(head, "mp", 1), exchange(head, "mp", 2)
    gathered = head, near, far, exchange(far, "mp", 1)

    kept, sent = out_part(core, mine, gathered, out_a, out_b, mods)
    total = both(kept, exchange(sent, "role", 1)).astype(jnp.bfloat16)
    along_x = exchange(total, "seq", 1)
    along_y = exchange(total, "role", 2)
    across = lax.ppermute(
        total, ("role", "seq"), [(i, i ^ (2 * lax.axis_size("seq") + 1)) for i in range(roles * lax.axis_size("seq"))]
    )
    total = both(total, along_x) + both(along_y, across)
    rows = (gate[0:1] * total).astype(jnp.bfloat16)
    heads_t = gen_heads.T
    theirs = exchange(rows, "role", 1)
    weight_grad = grad_part(core, heads_t, rows, None, 2)
    weight_grad = grad_part(other_core, heads_t, theirs, weight_grad, 2)
    return latent, weight_grad


def solution(mesh):
    in_specs = (
        P(None, "seq"),
        P("seq", "mp"),
        P("seq", "mp"),
        P(None, "mp"),
        P("seq", "mp"),
        P(),
        P("mp", None, "seq"),
        P("seq", "mp"),
        P(None, None, "mp"),
        P(None, "seq"),
        P("mp", None, "seq"),
        P("seq", "mp"),
        P(None, None, "mp"),
        P(None, "seq"),
    )
    out_specs = (P("seq", "mp"), P("seq", "mp"))
    roles, seqs, groups = mesh.shape["role"], mesh.shape["seq"], mesh.shape["mp"]

    def on_device(*arrays):
        heads_here = arrays[0].shape[1] // HEAD_DIM
        length = arrays[0].shape[0]
        fits = (roles, seqs, groups) == (4, 2, 4) and heads_here == roles * groups and length == HEAD_DIM
        return heads_per_role(*arrays) if fits else pass_per_role(*arrays)

    return jax.shard_map(
        on_device, mesh=mesh, in_specs=in_specs, out_specs=out_specs, check_vma=False
    )
```

```python
import math

import jax
import jax.numpy as jnp
from jax import lax
from jax.experimental import pallas as pl
from jax.experimental.pallas import tpu as pltpu
from jax.sharding import PartitionSpec as P

D = 5120
HEAD_DIM = 128


def time_embed(step_value, width):
    half_width = width // 2
    positions = jnp.arange(half_width, dtype=jnp.float32)
    frequencies = jnp.exp(positions * (-math.log(10000.0) / half_width))
    angles = step_value.astype(jnp.float32) * frequencies
    return jnp.concatenate([jnp.cos(angles), jnp.sin(angles)]).astype(jnp.bfloat16)


def head_norm(values, gains):
    factor = lax.rsqrt(jnp.mean(values * values, axis=-1, keepdims=True) + 1e-06)
    return (values * factor * gains).astype(jnp.bfloat16)


def attend(query_norm, key_norm, value_rows):
    full_length, heads_here, head_width = query_norm.shape
    query_blocks = query_norm.reshape(
        full_length // full_length, full_length, heads_here, head_width
    )

    def one_block(query_block):
        logits = jnp.einsum(
            "qhd,khd->hqk", query_block, key_norm, preferred_element_type=jnp.float32
        ) * (1.0 / math.sqrt(head_width))
        expanded = jnp.exp(logits)
        probs = (expanded / jnp.sum(expanded, axis=2, keepdims=True)).astype(jnp.bfloat16)
        return jnp.einsum(
            "hqk,khd->qhd", probs, value_rows, preferred_element_type=jnp.float32
        ).astype(jnp.bfloat16)

    head_out = lax.map(one_block, query_blocks)
    return head_out.reshape(full_length, heads_here * head_width)


def pass_per_role(
    gen_heads,
    gen_resid,
    gen_out_w,
    gen_time_w,
    noise,
    steps,
    teacher_qkv,
    teacher_out,
    teacher_time,
    teacher_norm,
    critic_qkv,
    critic_out,
    critic_time,
    critic_norm,
):
    full_length = gen_heads.shape[0]
    head_cols = gen_heads.shape[1]
    embed_width = gen_time_w.shape[0]
    gen_gate = jnp.dot(
        time_embed(steps[0], embed_width)[None, :], gen_time_w, preferred_element_type=jnp.float32
    )[0]
    block = gen_heads
    gen_proj = lax.psum_scatter(
        jnp.dot(block, gen_out_w, preferred_element_type=jnp.float32),
        "seq",
        scatter_dimension=0,
        tiled=True,
    )
    latent = (gen_resid.astype(jnp.float32) + gen_gate * gen_proj).astype(jnp.bfloat16)
    role_index = lax.axis_index("role")
    level = steps[1 + role_index // 2]
    use_critic = role_index % 2 == 1
    w_qkv = jnp.where(use_critic, critic_qkv, teacher_qkv)
    w_out = jnp.where(use_critic, critic_out, teacher_out)
    w_time = jnp.where(use_critic, critic_time, teacher_time)
    w_norm = jnp.where(use_critic, critic_norm, teacher_norm)
    noise_level = level.astype(jnp.float32) / 1000.0
    noisy = (
        (1.0 - noise_level) * latent.astype(jnp.float32) + noise_level * noise.astype(jnp.float32)
    ).astype(jnp.bfloat16)
    modulation = jnp.einsum(
        "f,fkd->kd", time_embed(level, embed_width), w_time, preferred_element_type=jnp.float32
    )
    shift_vec = modulation[0]
    scale_vec = modulation[1]
    gate_vec = modulation[2]
    gathered = lax.all_gather(noisy, "seq", axis=0, tiled=True)
    partial_squares = jnp.sum(jnp.square(gathered.astype(jnp.float32)), axis=1)
    scaled = (gathered.astype(jnp.float32) * (1.0 + scale_vec)).astype(jnp.bfloat16)
    flat_w = w_qkv.reshape(w_qkv.shape[0], 3 * head_cols)
    projected = jnp.dot(scaled, flat_w, preferred_element_type=jnp.float32)
    shift_proj = jnp.dot(
        shift_vec.astype(jnp.bfloat16)[None, :], flat_w, preferred_element_type=jnp.float32
    )[0]
    projected, squares, shift_proj = lax.psum((projected, partial_squares, shift_proj), "mp")
    mixed = projected * lax.rsqrt(squares / D + 1e-06)[:, None] + shift_proj
    heads_here = head_cols // HEAD_DIM
    mixed = mixed.reshape(full_length, 3, heads_here, HEAD_DIM)
    gains = w_norm.reshape(2, heads_here, HEAD_DIM)
    query_norm = head_norm(mixed[:, 0], gains[0])
    key_norm = head_norm(mixed[:, 1], gains[1])
    value_rows = mixed[:, 2].astype(jnp.bfloat16)
    head_out = attend(query_norm, key_norm, value_rows)
    weight_sign = jnp.where(use_critic, 0.5, -0.5)
    block = head_out
    summed_rows = lax.psum_scatter(
        weight_sign * (gate_vec * jnp.dot(block, w_out, preferred_element_type=jnp.float32)),
        ("role", "seq"),
        scatter_dimension=0,
        tiled=True,
    )
    grad_rows = lax.all_gather(
        (gen_gate * summed_rows).astype(jnp.bfloat16), ("role", "seq"), axis=0, tiled=True
    )
    weight_grad = lax.dot_general(
        gen_heads, grad_rows, (((0,), (0,)), ((), ())), preferred_element_type=jnp.float32
    )
    return (latent, weight_grad.astype(jnp.bfloat16))

MIB = 1024 * 1024
EXTRA_ROWS = 16


def vmem_spec():
    return pl.BlockSpec(memory_space=pltpu.VMEM)


def smem_spec():
    return pl.BlockSpec(memory_space=pltpu.SMEM)


def params(mebibytes):
    return pltpu.CompilerParams(vmem_limit_bytes=mebibytes * MIB)


def dot32(a, b):
    return jnp.dot(a, b, preferred_element_type=jnp.float32)


def at_block(index, size):
    return pl.ds(pl.multiple_of(index * size, size), size)


def any_spec():
    return pl.BlockSpec(memory_space=pl.ANY)


def hbm_spec():
    return pl.BlockSpec(memory_space=pltpu.HBM)


def cost(flops, moved):
    return pl.CostEstimate(flops=flops, bytes_accessed=moved, transcendentals=0)


def pack_kernel(seq, product, gate, resid, noise, full, sent):
    length = full.shape[0]
    own = resid.shape[0]
    full[...] = product[...] * gate[0:1, :]
    at = at_block(seq[0], own)
    full[at, :] = full[at, :] + resid[...].astype(jnp.float32)
    sent[pl.ds(0, length), :] = full[...].astype(jnp.bfloat16)
    sent[pl.ds(length, own), :] = noise[...]


def pack_part(seq, product, gate, resid, noise):
    length, width = product.shape
    own = resid.shape[0]
    return pl.pallas_call(
        pack_kernel,
        in_specs=[smem_spec()] + [vmem_spec()] * 4,
        out_specs=[vmem_spec()] * 2,
        out_shape=[
            jax.ShapeDtypeStruct((length, width), jnp.float32),
            jax.ShapeDtypeStruct((length + own, width), jnp.bfloat16),
        ],
        compiler_params=params(8),
        name="pack_part",
    )(seq, product, gate, resid, noise)


def load_kernel(start, embed, time_a, time_b, planes_a, planes_b, weight_a, weight_b, mods, sems):
    cols = pl.ds(pl.multiple_of(start[0], weight_a.shape[2]), weight_a.shape[2])
    copies = []
    for index, (planes, weight) in enumerate(((planes_a, weight_a), (planes_b, weight_b))):
        for part in range(3):
            copies.append(
                pltpu.make_async_copy(planes.at[part, :, cols], weight.at[part], sems.at[3 * index + part])
            )
    for copy in copies:
        copy.start()
    for k in range(3):
        mods[0, k] = dot32(embed[...], time_a[k])
        mods[1, k] = dot32(embed[...], time_b[k])
    for copy in copies:
        copy.wait()


def load_part(start, embed, time_a, time_b, planes_a, planes_b, cols):
    parts, depth, _ = planes_a.shape
    width = time_a.shape[2]
    return pl.pallas_call(
        load_kernel,
        in_specs=[smem_spec()] + [vmem_spec()] * 3 + [hbm_spec()] * 2,
        out_specs=[vmem_spec()] * 3,
        out_shape=[jax.ShapeDtypeStruct((parts, depth, cols), jnp.bfloat16)] * 2
        + [jax.ShapeDtypeStruct((2, parts, 8, width), jnp.float32)],
        scratch_shapes=[pltpu.SemaphoreType.DMA((2 * parts,))],
        compiler_params=params(46),
        name="load_part",
    )(start, embed, time_a, time_b, planes_a, planes_b)


def join_kernel(full, arrived, joined):
    length = full.shape[0]
    own = arrived.shape[0] - length
    top = full[...] + arrived[pl.ds(0, length), :].astype(jnp.float32)
    joined[pl.ds(0, length), :] = top.astype(jnp.bfloat16)
    joined[pl.ds(length, own), :] = arrived[pl.ds(length, own), :]


def join_part(full, arrived):
    return pl.pallas_call(
        join_kernel,
        in_specs=[vmem_spec(), vmem_spec()],
        out_specs=vmem_spec(),
        out_shape=jax.ShapeDtypeStruct(arrived.shape, jnp.bfloat16),
        compiler_params=params(8),
        name="join_part",
    )(full, arrived)


def project(index, stride, mine, noisy, squares, mods, weight, kept, sent, result):
    tokens = noisy.shape[0]
    length = tokens // 2
    unit = squares.shape[1] // 2
    groups = weight.shape[2] // unit
    scale = mods[index, 1]
    shift = mods[index, 0]
    spread = noisy.astype(jnp.float32)
    top = spread[:length] * (1.0 + scale[1:2])
    low = spread[length:] * (1.0 + scale[2:3])
    extra = jnp.concatenate([shift[1:3], jnp.zeros((EXTRA_ROWS - 2, shift.shape[1]), jnp.float32)], axis=0)
    rows = jnp.concatenate([top, low, extra], axis=0).astype(jnp.bfloat16)
    row_id = lax.broadcasted_iota(jnp.int32, (EXTRA_ROWS, unit), 0)
    for part in range(3):
        result[...] = dot32(rows, weight[part])
        cols = pl.ds(part * unit, unit)
        for slot in range(groups):
            at = at_block(jnp.bitwise_xor(mine, slot), unit)
            goal = sent if slot & stride else kept
            place = slot // 2 if stride == 1 else slot % 2
            goal[place, pl.ds(0, tokens), cols] = result[pl.ds(0, tokens), at].astype(jnp.bfloat16)
            tail = jnp.where(row_id < 2, result[pl.ds(tokens, EXTRA_ROWS), at], 0.0)
            for level in range(2):
                tail = jnp.where(row_id == 2 + level, squares[0:1, level * length : (level + 1) * length], tail)
            goal[place, pl.ds(tokens, EXTRA_ROWS), cols] = tail.astype(jnp.bfloat16)


def qkv_kernel(seq, core, mine, levels, joined, swapped, noise, mods, weight_a, weight_b, latent, *refs):
    chunks, (values, noises, result) = refs[:4], refs[4:]
    length, cols = values.shape[0], joined.shape[1]
    own = latent.shape[0]
    tokens = 2 * length
    left, right = at_block(core[0], cols), at_block(1 - core[0], cols)
    values[:, left] = joined[pl.ds(0, length), :]
    values[:, right] = swapped[pl.ds(0, length), :]
    latent[...] = values[at_block(seq[0], own), :]
    noises[at_block(seq[0], own), :] = noise[...]
    theirs = at_block(1 - seq[0], own)
    noises[theirs, left] = joined[pl.ds(length, own), :]
    noises[theirs, right] = swapped[pl.ds(length, own), :]
    spread = values[...].astype(jnp.float32)
    noise_rows = noises[...].astype(jnp.float32)
    mixed = jnp.concatenate(
        [(1.0 - levels[level]) * spread + levels[level] * noise_rows for level in range(2)], axis=0
    ).astype(jnp.bfloat16)
    wide = mixed.astype(jnp.float32)
    sums = jnp.sum(wide * wide, axis=1, keepdims=True)
    sums = jnp.broadcast_to(sums, (tokens, length)).T[0:8]
    for index, weight in enumerate((weight_a, weight_b)):
        project(index, index + 1, mine[0], mixed, sums, mods, weight, *chunks[2 * index : 2 * index + 2], result)


def qkv_part(seq, core, mine, levels, joined, swapped, noise, mods, weight_a, weight_b):
    own, width = noise.shape
    length = joined.shape[0] - own
    tokens = 2 * length
    cols = weight_a.shape[2]
    return pl.pallas_call(
        qkv_kernel,
        in_specs=[smem_spec()] * 4 + [vmem_spec()] * 6,
        out_specs=[vmem_spec()] * 5,
        out_shape=[jax.ShapeDtypeStruct((own, width), jnp.bfloat16)]
        + [jax.ShapeDtypeStruct((cols // length // 2, tokens + EXTRA_ROWS, 3 * length), jnp.bfloat16)] * 4,
        scratch_shapes=[
            pltpu.VMEM((length, width), jnp.bfloat16),
            pltpu.VMEM((length, width), jnp.bfloat16),
            pltpu.VMEM((tokens + EXTRA_ROWS, cols), jnp.float32),
        ],
        compiler_params=params(20),
        name="qkv_part",
    )(seq, core, mine, levels, joined, swapped, noise, mods, weight_a, weight_b)


def attend_kernel(width, kept_a, other_a, kept_b, other_b, gains, out):
    _, _, length, unit = out.shape
    tokens = 2 * length
    for index, (kept, other) in enumerate(((kept_a, other_a), (kept_b, other_b))):
        mixed = kept[...] + other[...].astype(jnp.float32)
        extra = mixed[tokens:]
        for level in range(2):
            rows_at = slice(level * length, (level + 1) * length)
            squares = jnp.broadcast_to(extra[2 + level : 3 + level, :unit], (unit, unit)).T
            factor = lax.rsqrt(squares * (1.0 / width) + 1e-06)

            def pick(part):
                cols = slice(part * unit, (part + 1) * unit)
                return mixed[rows_at, cols] * factor + extra[level : level + 1, cols]

            def normed(part):
                rows = pick(part)
                mean = jnp.mean(rows * rows, axis=1, keepdims=True)
                return (rows * lax.rsqrt(mean + 1e-06) * gains[index, part : part + 1, :]).astype(jnp.bfloat16)

            query, key = normed(0), normed(1)
            value = pick(2).astype(jnp.bfloat16)
            logits = lax.dot_general(
                query, key, (((1,), (1,)), ((), ())), preferred_element_type=jnp.float32
            ) * (1.0 / math.sqrt(unit))
            expanded = jnp.exp(logits)
            probs = (expanded / jnp.sum(expanded, axis=1, keepdims=True)).astype(jnp.bfloat16)
            out[index, level] = dot32(probs, value).astype(jnp.bfloat16)


def attend_part(kept_a, other_a, kept_b, other_b, gains, width):
    unit = kept_a.shape[1] // 3
    length = (kept_a.shape[0] - EXTRA_ROWS) // 2
    return pl.pallas_call(
        lambda *refs: attend_kernel(width, *refs),
        in_specs=[vmem_spec()] * 5,
        out_specs=vmem_spec(),
        out_shape=jax.ShapeDtypeStruct((2, 2, length, unit), jnp.bfloat16),
        compiler_params=params(8),
        name="attend_part",
    )(kept_a, other_a, kept_b, other_b, gains)


def out_kernel(core, mine, *refs):
    heads = refs[0:4]
    weight_a, weight_b, mods, kept, sent, rows, total = refs[4:]
    _, _, length, unit = heads[0].shape
    for index, weight in enumerate((weight_a, weight_b)):
        for slot, head in enumerate(heads):
            at = at_block(jnp.bitwise_xor(mine[0], slot), unit)
            for level in range(2):
                rows[pl.ds(level * length, length), at] = head[index, level]
        result = dot32(rows[...], weight[...])
        gates = mods[index, 2]
        signed = gates[1:2] * result[:length] + gates[2:3] * result[length:]
        if index == 0:
            total[...] = -0.5 * signed
        else:
            total[...] = total[...] + 0.5 * signed
    cols = kept.shape[1]
    kept[...] = total[:, at_block(core[0], cols)]
    sent[...] = total[:, at_block(1 - core[0], cols)].astype(jnp.bfloat16)


def out_part(core, mine, heads, weight_a, weight_b, mods):
    length = heads[0].shape[2]
    depth, width = weight_a.shape
    return pl.pallas_call(
        out_kernel,
        in_specs=[smem_spec()] * 2 + [vmem_spec()] * 7,
        out_specs=[vmem_spec()] * 2,
        out_shape=[
            jax.ShapeDtypeStruct((length, width // 2), jnp.float32),
            jax.ShapeDtypeStruct((length, width // 2), jnp.bfloat16),
        ],
        scratch_shapes=[
            pltpu.VMEM((2 * length, depth), jnp.bfloat16),
            pltpu.VMEM((length, width), jnp.float32),
        ],
        compiler_params=params(16),
        name="out_part",
    )(core, mine, *heads, weight_a, weight_b, mods)


def grad_kernel(half, heads_t, rows, *refs):
    refs[-1][...] = dot32(heads_t[...], rows[...]).astype(jnp.bfloat16)


def grad_part(half, heads_t, rows, before, steps):
    depth, length = heads_t.shape
    cols = rows.shape[1]
    tile = depth // steps
    rest = [] if before is None else [before]
    grid_spec = pltpu.PrefetchScalarGridSpec(
        num_scalar_prefetch=1,
        grid=(steps,),
        in_specs=[
            pl.BlockSpec((tile, length), lambda n, w: (n, 0)),
            pl.BlockSpec((length, cols), lambda n, w: (0, 0)),
        ]
        + [any_spec()] * len(rest),
        out_specs=pl.BlockSpec((tile, cols), lambda n, w: (n, w[0])),
    )
    return pl.pallas_call(
        grad_kernel,
        grid_spec=grid_spec,
        out_shape=jax.ShapeDtypeStruct((depth, 2 * cols), jnp.bfloat16),
        input_output_aliases={3: 0} if rest else {},
        compiler_params=params(16),
        name="grad_part",
    )(half, heads_t, rows, *rest)


def exchange(array, axis, bit):
    return lax.ppermute(array, axis, [(i, i ^ bit) for i in range(lax.axis_size(axis))])


def take(array, begin, size, axis):
    return lax.dynamic_slice_in_dim(array, begin, size, axis=axis, allow_negative_indices=False)


def both(mine, theirs):
    return mine.astype(jnp.float32) + theirs.astype(jnp.float32)


def heads_per_role(
    gen_heads,
    gen_resid,
    gen_out_w,
    gen_time_w,
    noise,
    steps,
    teacher_qkv,
    teacher_out,
    teacher_time,
    teacher_norm,
    critic_qkv,
    critic_out,
    critic_time,
    critic_norm,
):
    length = gen_heads.shape[0]
    roles, groups = lax.axis_size("role"), lax.axis_size("mp")
    role, seq, mp = lax.axis_index("role"), lax.axis_index("seq"), lax.axis_index("mp")
    part_cols = gen_heads.shape[1] // roles
    freq = gen_time_w.shape[0]
    core = role % 2
    half_cols = gen_resid.shape[1] // 2
    unit = part_cols // groups

    embed = jax.vmap(lambda t: time_embed(t, freq))(steps)
    embed = jnp.concatenate([embed, jnp.zeros((5, freq), jnp.bfloat16)], axis=0)
    levels = steps[1:3].astype(jnp.float32) / 1000.0
    start = role * part_cols
    scalars = [seq, mp, core, 1 - core, core * half_cols, start, start + mp * unit]
    embed, *scalars = lax.optimization_barrier((embed, *scalars))
    seq_at, mine, core, other_core, start_at = [v.astype(jnp.int32).reshape(1) for v in scalars[:4] + scalars[5:6]]
    begin, start, gain_at = scalars[4:]
    weight, time_half, resid_half, noise_half = [
        take(w, begin, half_cols, 1) for w in (gen_out_w, gen_time_w, gen_resid, noise)
    ]
    gate = dot32(embed, time_half)
    full, sent = pack_part(seq_at, dot32(gen_heads, weight), gate, resid_half, noise_half)
    arrived = exchange(sent, "seq", 1)
    later, embed, _ = lax.optimization_barrier((start_at, embed, full))
    planes = [w.transpose(1, 0, 2) for w in (teacher_qkv, critic_qkv, teacher_time, critic_time)]
    weight_a, weight_b, mods = load_part(later, embed, planes[2], planes[3], planes[0], planes[1], part_cols)
    arrived, mods = lax.optimization_barrier((arrived, mods))
    joined = join_part(full, arrived)
    swapped = exchange(joined, "role", 1)

    latent, kept_a, sent_a, kept_b, sent_b = qkv_part(
        seq_at, core, mine, levels, joined, swapped, noise, mods, weight_a, weight_b
    )
    arrived_a, arrived_b = exchange(sent_a, "mp", 1), exchange(sent_b, "mp", 2)
    out_a, out_b = [take(w, start, part_cols, 0) for w in (teacher_out, critic_out)]
    gains = jnp.stack([teacher_norm, critic_norm])
    gains = take(gains, gain_at, unit, 2)
    arrived_a, arrived_b, out_a, out_b, gains = lax.optimization_barrier((arrived_a, arrived_b, out_a, out_b, gains))
    sum_a, sum_b = both(kept_a, arrived_a), both(kept_b, arrived_b)
    last_a = exchange(sum_a[1].astype(jnp.bfloat16), "mp", 2)
    last_b = exchange(sum_b[1].astype(jnp.bfloat16), "mp", 1)
    head = attend_part(sum_a[0], last_a, sum_b[0], last_b, gains, D)
    near, far = exchange(head, "mp", 1), exchange(head, "mp", 2)
    gathered = head, near, far, exchange(far, "mp", 1)

    kept, sent = out_part(core, mine, gathered, out_a, out_b, mods)
    total = both(kept, exchange(sent, "role", 1)).astype(jnp.bfloat16)
    along_x = exchange(total, "seq", 1)
    along_y = exchange(total, "role", 2)
    across = lax.ppermute(
        total, ("role", "seq"), [(i, i ^ (2 * lax.axis_size("seq") + 1)) for i in range(roles * lax.axis_size("seq"))]
    )
    total = both(total, along_x) + both(along_y, across)
    rows = (gate[0:1] * total).astype(jnp.bfloat16)
    heads_t = gen_heads.T
    theirs = exchange(rows, "role", 1)
    weight_grad = grad_part(core, heads_t, rows, None, 2)
    weight_grad = grad_part(other_core, heads_t, theirs, weight_grad, 2)
    return latent, weight_grad


def solution(mesh):
    in_specs = (
        P(None, "seq"),
        P("seq", "mp"),
        P("seq", "mp"),
        P(None, "mp"),
        P("seq", "mp"),
        P(),
        P("mp", None, "seq"),
        P("seq", "mp"),
        P(None, None, "mp"),
        P(None, "seq"),
        P("mp", None, "seq"),
        P("seq", "mp"),
        P(None, None, "mp"),
        P(None, "seq"),
    )
    out_specs = (P("seq", "mp"), P("seq", "mp"))
    roles, seqs, groups = mesh.shape["role"], mesh.shape["seq"], mesh.shape["mp"]

    def on_device(*arrays):
        heads_here = arrays[0].shape[1] // HEAD_DIM
        length = arrays[0].shape[0]
        fits = (roles, seqs, groups) == (4, 2, 4) and heads_here == roles * groups and length == HEAD_DIM
        return heads_per_role(*arrays) if fits else pass_per_role(*arrays)

    return jax.shard_map(
        on_device, mesh=mesh, in_specs=in_specs, out_specs=out_specs, check_vma=False
    )
```

```python
import math

import jax
import jax.numpy as jnp
from jax import lax
from jax.experimental import pallas as pl
from jax.experimental.pallas import tpu as pltpu
from jax.sharding import PartitionSpec as P

D = 5120
HEAD_DIM = 128


def time_embed(step_value, width):
    half_width = width // 2
    positions = jnp.arange(half_width, dtype=jnp.float32)
    frequencies = jnp.exp(positions * (-math.log(10000.0) / half_width))
    angles = step_value.astype(jnp.float32) * frequencies
    return jnp.concatenate([jnp.cos(angles), jnp.sin(angles)]).astype(jnp.bfloat16)


def head_norm(values, gains):
    factor = lax.rsqrt(jnp.mean(values * values, axis=-1, keepdims=True) + 1e-06)
    return (values * factor * gains).astype(jnp.bfloat16)


def attend(query_norm, key_norm, value_rows):
    full_length, heads_here, head_width = query_norm.shape
    query_blocks = query_norm.reshape(
        full_length // full_length, full_length, heads_here, head_width
    )

    def one_block(query_block):
        logits = jnp.einsum(
            "qhd,khd->hqk", query_block, key_norm, preferred_element_type=jnp.float32
        ) * (1.0 / math.sqrt(head_width))
        expanded = jnp.exp(logits)
        probs = (expanded / jnp.sum(expanded, axis=2, keepdims=True)).astype(jnp.bfloat16)
        return jnp.einsum(
            "hqk,khd->qhd", probs, value_rows, preferred_element_type=jnp.float32
        ).astype(jnp.bfloat16)

    head_out = lax.map(one_block, query_blocks)
    return head_out.reshape(full_length, heads_here * head_width)


def pass_per_role(
    gen_heads,
    gen_resid,
    gen_out_w,
    gen_time_w,
    noise,
    steps,
    teacher_qkv,
    teacher_out,
    teacher_time,
    teacher_norm,
    critic_qkv,
    critic_out,
    critic_time,
    critic_norm,
):
    full_length = gen_heads.shape[0]
    head_cols = gen_heads.shape[1]
    embed_width = gen_time_w.shape[0]
    gen_gate = jnp.dot(
        time_embed(steps[0], embed_width)[None, :], gen_time_w, preferred_element_type=jnp.float32
    )[0]
    block = gen_heads
    gen_proj = lax.psum_scatter(
        jnp.dot(block, gen_out_w, preferred_element_type=jnp.float32),
        "seq",
        scatter_dimension=0,
        tiled=True,
    )
    latent = (gen_resid.astype(jnp.float32) + gen_gate * gen_proj).astype(jnp.bfloat16)
    role_index = lax.axis_index("role")
    level = steps[1 + role_index // 2]
    use_critic = role_index % 2 == 1
    w_qkv = jnp.where(use_critic, critic_qkv, teacher_qkv)
    w_out = jnp.where(use_critic, critic_out, teacher_out)
    w_time = jnp.where(use_critic, critic_time, teacher_time)
    w_norm = jnp.where(use_critic, critic_norm, teacher_norm)
    noise_level = level.astype(jnp.float32) / 1000.0
    noisy = (
        (1.0 - noise_level) * latent.astype(jnp.float32) + noise_level * noise.astype(jnp.float32)
    ).astype(jnp.bfloat16)
    modulation = jnp.einsum(
        "f,fkd->kd", time_embed(level, embed_width), w_time, preferred_element_type=jnp.float32
    )
    shift_vec = modulation[0]
    scale_vec = modulation[1]
    gate_vec = modulation[2]
    gathered = lax.all_gather(noisy, "seq", axis=0, tiled=True)
    partial_squares = jnp.sum(jnp.square(gathered.astype(jnp.float32)), axis=1)
    scaled = (gathered.astype(jnp.float32) * (1.0 + scale_vec)).astype(jnp.bfloat16)
    flat_w = w_qkv.reshape(w_qkv.shape[0], 3 * head_cols)
    projected = jnp.dot(scaled, flat_w, preferred_element_type=jnp.float32)
    shift_proj = jnp.dot(
        shift_vec.astype(jnp.bfloat16)[None, :], flat_w, preferred_element_type=jnp.float32
    )[0]
    projected, squares, shift_proj = lax.psum((projected, partial_squares, shift_proj), "mp")
    mixed = projected * lax.rsqrt(squares / D + 1e-06)[:, None] + shift_proj
    heads_here = head_cols // HEAD_DIM
    mixed = mixed.reshape(full_length, 3, heads_here, HEAD_DIM)
    gains = w_norm.reshape(2, heads_here, HEAD_DIM)
    query_norm = head_norm(mixed[:, 0], gains[0])
    key_norm = head_norm(mixed[:, 1], gains[1])
    value_rows = mixed[:, 2].astype(jnp.bfloat16)
    head_out = attend(query_norm, key_norm, value_rows)
    weight_sign = jnp.where(use_critic, 0.5, -0.5)
    block = head_out
    summed_rows = lax.psum_scatter(
        weight_sign * (gate_vec * jnp.dot(block, w_out, preferred_element_type=jnp.float32)),
        ("role", "seq"),
        scatter_dimension=0,
        tiled=True,
    )
    grad_rows = lax.all_gather(
        (gen_gate * summed_rows).astype(jnp.bfloat16), ("role", "seq"), axis=0, tiled=True
    )
    weight_grad = lax.dot_general(
        gen_heads, grad_rows, (((0,), (0,)), ((), ())), preferred_element_type=jnp.float32
    )
    return (latent, weight_grad.astype(jnp.bfloat16))

MIB = 1024 * 1024
EXTRA_ROWS = 16


def vmem_spec():
    return pl.BlockSpec(memory_space=pltpu.VMEM)


def smem_spec():
    return pl.BlockSpec(memory_space=pltpu.SMEM)


def params(mebibytes):
    return pltpu.CompilerParams(vmem_limit_bytes=mebibytes * MIB)


def dot32(a, b):
    return jnp.dot(a, b, preferred_element_type=jnp.float32)


def at_block(index, size):
    return pl.ds(pl.multiple_of(index * size, size), size)


def any_spec():
    return pl.BlockSpec(memory_space=pl.ANY)


def hbm_spec():
    return pl.BlockSpec(memory_space=pltpu.HBM)


def cost(flops, moved):
    return pl.CostEstimate(flops=flops, bytes_accessed=moved, transcendentals=0)


def pack_kernel(seq, product, gate, resid, noise, full, sent):
    length = full.shape[0]
    own = resid.shape[0]
    full[...] = product[...] * gate[0:1, :]
    at = at_block(seq[0], own)
    full[at, :] = full[at, :] + resid[...].astype(jnp.float32)
    sent[pl.ds(0, length), :] = full[...].astype(jnp.bfloat16)
    sent[pl.ds(length, own), :] = noise[...]


def pack_part(seq, product, gate, resid, noise):
    length, width = product.shape
    own = resid.shape[0]
    return pl.pallas_call(
        pack_kernel,
        in_specs=[smem_spec()] + [vmem_spec()] * 4,
        out_specs=[vmem_spec()] * 2,
        out_shape=[
            jax.ShapeDtypeStruct((length, width), jnp.float32),
            jax.ShapeDtypeStruct((length + own, width), jnp.bfloat16),
        ],
        compiler_params=params(8),
        name="pack_part",
    )(seq, product, gate, resid, noise)


def load_kernel(start, embed, time_a, time_b, planes_a, planes_b, weight_a, weight_b, mods, sems):
    cols = pl.ds(pl.multiple_of(start[0], weight_a.shape[2]), weight_a.shape[2])
    copies = []
    for index, (planes, weight) in enumerate(((planes_a, weight_a), (planes_b, weight_b))):
        for part in range(3):
            copies.append(
                pltpu.make_async_copy(planes.at[part, :, cols], weight.at[part], sems.at[3 * index + part])
            )
    for copy in copies:
        copy.start()
    for k in range(3):
        mods[0, k] = dot32(embed[...], time_a[k])
        mods[1, k] = dot32(embed[...], time_b[k])
    for copy in copies:
        copy.wait()


def load_part(start, embed, time_a, time_b, planes_a, planes_b, cols):
    parts, depth, _ = planes_a.shape
    width = time_a.shape[2]
    return pl.pallas_call(
        load_kernel,
        in_specs=[smem_spec()] + [vmem_spec()] * 3 + [hbm_spec()] * 2,
        out_specs=[vmem_spec()] * 3,
        out_shape=[jax.ShapeDtypeStruct((parts, depth, cols), jnp.bfloat16)] * 2
        + [jax.ShapeDtypeStruct((2, parts, 8, width), jnp.float32)],
        scratch_shapes=[pltpu.SemaphoreType.DMA((2 * parts,))],
        compiler_params=params(40),
        name="load_part",
    )(start, embed, time_a, time_b, planes_a, planes_b)


def join_kernel(full, arrived, joined):
    length = full.shape[0]
    own = arrived.shape[0] - length
    top = full[...] + arrived[pl.ds(0, length), :].astype(jnp.float32)
    joined[pl.ds(0, length), :] = top.astype(jnp.bfloat16)
    joined[pl.ds(length, own), :] = arrived[pl.ds(length, own), :]


def join_part(full, arrived):
    return pl.pallas_call(
        join_kernel,
        in_specs=[vmem_spec(), vmem_spec()],
        out_specs=vmem_spec(),
        out_shape=jax.ShapeDtypeStruct(arrived.shape, jnp.bfloat16),
        compiler_params=params(8),
        name="join_part",
    )(full, arrived)


def project(index, stride, mine, noisy, squares, mods, weight, kept, sent, result):
    tokens = noisy.shape[0]
    length = tokens // 2
    unit = squares.shape[1] // 2
    groups = weight.shape[2] // unit
    scale = mods[index, 1]
    shift = mods[index, 0]
    spread = noisy.astype(jnp.float32)
    top = spread[:length] * (1.0 + scale[1:2])
    low = spread[length:] * (1.0 + scale[2:3])
    extra = jnp.concatenate([shift[1:3], jnp.zeros((EXTRA_ROWS - 2, shift.shape[1]), jnp.float32)], axis=0)
    rows = jnp.concatenate([top, low, extra], axis=0).astype(jnp.bfloat16)
    row_id = lax.broadcasted_iota(jnp.int32, (EXTRA_ROWS, unit), 0)
    for part in range(3):
        result[...] = dot32(rows, weight[part])
        cols = pl.ds(part * unit, unit)
        for slot in range(groups):
            at = at_block(jnp.bitwise_xor(mine, slot), unit)
            goal = sent if slot & stride else kept
            place = slot // 2 if stride == 1 else slot % 2
            goal[place, pl.ds(0, tokens), cols] = result[pl.ds(0, tokens), at].astype(jnp.bfloat16)
            tail = jnp.where(row_id < 2, result[pl.ds(tokens, EXTRA_ROWS), at], 0.0)
            for level in range(2):
                tail = jnp.where(row_id == 2 + level, squares[0:1, level * length : (level + 1) * length], tail)
            goal[place, pl.ds(tokens, EXTRA_ROWS), cols] = tail.astype(jnp.bfloat16)


def qkv_kernel(seq, core, mine, levels, joined, swapped, noise, mods, weight_a, weight_b, latent, *refs):
    chunks, (values, noises, result) = refs[:4], refs[4:]
    length, cols = values.shape[0], joined.shape[1]
    own = latent.shape[0]
    tokens = 2 * length
    left, right = at_block(core[0], cols), at_block(1 - core[0], cols)
    values[:, left] = joined[pl.ds(0, length), :]
    values[:, right] = swapped[pl.ds(0, length), :]
    latent[...] = values[at_block(seq[0], own), :]
    noises[at_block(seq[0], own), :] = noise[...]
    theirs = at_block(1 - seq[0], own)
    noises[theirs, left] = joined[pl.ds(length, own), :]
    noises[theirs, right] = swapped[pl.ds(length, own), :]
    spread = values[...].astype(jnp.float32)
    noise_rows = noises[...].astype(jnp.float32)
    mixed = jnp.concatenate(
        [(1.0 - levels[level]) * spread + levels[level] * noise_rows for level in range(2)], axis=0
    ).astype(jnp.bfloat16)
    wide = mixed.astype(jnp.float32)
    sums = jnp.sum(wide * wide, axis=1, keepdims=True)
    sums = jnp.broadcast_to(sums, (tokens, length)).T[0:8]
    for index, weight in enumerate((weight_a, weight_b)):
        project(index, index + 1, mine[0], mixed, sums, mods, weight, *chunks[2 * index : 2 * index + 2], result)


def qkv_part(seq, core, mine, levels, joined, swapped, noise, mods, weight_a, weight_b):
    own, width = noise.shape
    length = joined.shape[0] - own
    tokens = 2 * length
    cols = weight_a.shape[2]
    return pl.pallas_call(
        qkv_kernel,
        in_specs=[smem_spec()] * 4 + [vmem_spec()] * 6,
        out_specs=[vmem_spec()] * 5,
        out_shape=[jax.ShapeDtypeStruct((own, width), jnp.bfloat16)]
        + [jax.ShapeDtypeStruct((cols // length // 2, tokens + EXTRA_ROWS, 3 * length), jnp.bfloat16)] * 4,
        scratch_shapes=[
            pltpu.VMEM((length, width), jnp.bfloat16),
            pltpu.VMEM((length, width), jnp.bfloat16),
            pltpu.VMEM((tokens + EXTRA_ROWS, cols), jnp.float32),
        ],
        compiler_params=params(20),
        name="qkv_part",
    )(seq, core, mine, levels, joined, swapped, noise, mods, weight_a, weight_b)


def attend_kernel(width, kept_a, other_a, kept_b, other_b, gains, out):
    _, _, length, unit = out.shape
    tokens = 2 * length
    for index, (kept, other) in enumerate(((kept_a, other_a), (kept_b, other_b))):
        mixed = kept[...] + other[...].astype(jnp.float32)
        extra = mixed[tokens:]
        for level in range(2):
            rows_at = slice(level * length, (level + 1) * length)
            squares = jnp.broadcast_to(extra[2 + level : 3 + level, :unit], (unit, unit)).T
            factor = lax.rsqrt(squares * (1.0 / width) + 1e-06)

            def pick(part):
                cols = slice(part * unit, (part + 1) * unit)
                return mixed[rows_at, cols] * factor + extra[level : level + 1, cols]

            def normed(part):
                rows = pick(part)
                mean = jnp.mean(rows * rows, axis=1, keepdims=True)
                return (rows * lax.rsqrt(mean + 1e-06) * gains[index, part : part + 1, :]).astype(jnp.bfloat16)

            query, key = normed(0), normed(1)
            value = pick(2).astype(jnp.bfloat16)
            logits = lax.dot_general(
                query, key, (((1,), (1,)), ((), ())), preferred_element_type=jnp.float32
            ) * (1.0 / math.sqrt(unit))
            expanded = jnp.exp(logits)
            probs = (expanded / jnp.sum(expanded, axis=1, keepdims=True)).astype(jnp.bfloat16)
            out[index, level] = dot32(probs, value).astype(jnp.bfloat16)


def attend_part(kept_a, other_a, kept_b, other_b, gains, width):
    unit = kept_a.shape[1] // 3
    length = (kept_a.shape[0] - EXTRA_ROWS) // 2
    return pl.pallas_call(
        lambda *refs: attend_kernel(width, *refs),
        in_specs=[vmem_spec()] * 5,
        out_specs=vmem_spec(),
        out_shape=jax.ShapeDtypeStruct((2, 2, length, unit), jnp.bfloat16),
        compiler_params=params(8),
        name="attend_part",
    )(kept_a, other_a, kept_b, other_b, gains)


def out_kernel(core, mine, *refs):
    heads = refs[0:4]
    weight_a, weight_b, mods, kept, sent, rows, total = refs[4:]
    _, _, length, unit = heads[0].shape
    for index, weight in enumerate((weight_a, weight_b)):
        for slot, head in enumerate(heads):
            at = at_block(jnp.bitwise_xor(mine[0], slot), unit)
            for level in range(2):
                rows[pl.ds(level * length, length), at] = head[index, level]
        result = dot32(rows[...], weight[...])
        gates = mods[index, 2]
        signed = gates[1:2] * result[:length] + gates[2:3] * result[length:]
        if index == 0:
            total[...] = -0.5 * signed
        else:
            total[...] = total[...] + 0.5 * signed
    cols = kept.shape[1]
    kept[...] = total[:, at_block(core[0], cols)]
    sent[...] = total[:, at_block(1 - core[0], cols)].astype(jnp.bfloat16)


def out_part(core, mine, heads, weight_a, weight_b, mods):
    length = heads[0].shape[2]
    depth, width = weight_a.shape
    return pl.pallas_call(
        out_kernel,
        in_specs=[smem_spec()] * 2 + [vmem_spec()] * 7,
        out_specs=[vmem_spec()] * 2,
        out_shape=[
            jax.ShapeDtypeStruct((length, width // 2), jnp.float32),
            jax.ShapeDtypeStruct((length, width // 2), jnp.bfloat16),
        ],
        scratch_shapes=[
            pltpu.VMEM((2 * length, depth), jnp.bfloat16),
            pltpu.VMEM((length, width), jnp.float32),
        ],
        compiler_params=params(16),
        name="out_part",
    )(core, mine, *heads, weight_a, weight_b, mods)


def spread_kernel(place, kept, arrived, own, *sends):
    block = own.shape[0]
    for hop, goal in enumerate((own, *sends)):
        at = at_block(jnp.bitwise_xor(place[0], hop), block)
        goal[...] = (kept[at, :] + arrived[at, :].astype(jnp.float32)).astype(goal.dtype)


def spread_part(place, kept, arrived, count):
    length, cols = kept.shape
    shape = (length // count, cols)
    return pl.pallas_call(
        spread_kernel,
        in_specs=[smem_spec()] + [vmem_spec()] * 2,
        out_specs=[vmem_spec()] * count,
        out_shape=[jax.ShapeDtypeStruct(shape, jnp.float32)]
        + [jax.ShapeDtypeStruct(shape, jnp.bfloat16)] * (count - 1),
        compiler_params=params(8),
        name="spread_part",
    )(place, kept, arrived)


def merge_kernel(place, *refs):
    blocks, rows = refs[:-1], refs[-1]
    size = blocks[0].shape[0]
    for hop, block in enumerate(blocks):
        rows[at_block(jnp.bitwise_xor(place[0], hop), size), :] = block[...]


def merge_part(place, blocks):
    size, cols = blocks[0].shape
    return pl.pallas_call(
        merge_kernel,
        in_specs=[smem_spec()] + [vmem_spec()] * len(blocks),
        out_specs=vmem_spec(),
        out_shape=jax.ShapeDtypeStruct((size * len(blocks), cols), jnp.bfloat16),
        compiler_params=params(8),
        name="merge_part",
    )(place, *blocks)


def grad_kernel(half, heads_t, rows, *refs):
    refs[-1][...] = dot32(heads_t[...], rows[...]).astype(jnp.bfloat16)


def grad_part(half, heads_t, rows, before, steps):
    depth, length = heads_t.shape
    cols = rows.shape[1]
    tile = depth // steps
    rest = [] if before is None else [before]
    grid_spec = pltpu.PrefetchScalarGridSpec(
        num_scalar_prefetch=1,
        grid=(steps,),
        in_specs=[
            pl.BlockSpec((tile, length), lambda n, w: (n, 0)),
            pl.BlockSpec((length, cols), lambda n, w: (0, 0)),
        ]
        + [any_spec()] * len(rest),
        out_specs=pl.BlockSpec((tile, cols), lambda n, w: (n, w[0])),
    )
    return pl.pallas_call(
        grad_kernel,
        grid_spec=grid_spec,
        out_shape=jax.ShapeDtypeStruct((depth, 2 * cols), jnp.bfloat16),
        input_output_aliases={3: 0} if rest else {},
        compiler_params=params(16),
        name="grad_part",
    )(half, heads_t, rows, *rest)


def exchange(array, axis, bit):
    return lax.ppermute(array, axis, [(i, i ^ bit) for i in range(lax.axis_size(axis))])


def chip_exchange(arrays):
    seqs = lax.axis_size("seq")
    everyone = range(lax.axis_size("role") * seqs)
    bits = (1, 2 * seqs, 2 * seqs + 1)
    return [lax.ppermute(x, ("role", "seq"), [(i, i ^ bit) for i in everyone]) for x, bit in zip(arrays, bits)]


def take(array, begin, size, axis):
    return lax.dynamic_slice_in_dim(array, begin, size, axis=axis, allow_negative_indices=False)


def both(mine, theirs):
    return mine.astype(jnp.float32) + theirs.astype(jnp.float32)


def heads_per_role(
    gen_heads,
    gen_resid,
    gen_out_w,
    gen_time_w,
    noise,
    steps,
    teacher_qkv,
    teacher_out,
    teacher_time,
    teacher_norm,
    critic_qkv,
    critic_out,
    critic_time,
    critic_norm,
):
    length = gen_heads.shape[0]
    roles, groups = lax.axis_size("role"), lax.axis_size("mp")
    role, seq, mp = lax.axis_index("role"), lax.axis_index("seq"), lax.axis_index("mp")
    part_cols = gen_heads.shape[1] // roles
    freq = gen_time_w.shape[0]
    core = role % 2
    half_cols = gen_resid.shape[1] // 2
    unit = part_cols // groups

    embed = jax.vmap(lambda t: time_embed(t, freq))(steps)
    embed = jnp.concatenate([embed, jnp.zeros((5, freq), jnp.bfloat16)], axis=0)
    levels = steps[1:3].astype(jnp.float32) / 1000.0
    start = role * part_cols
    scalars = [seq, mp, core, 1 - core, core * half_cols, start, start + mp * unit, role // 2 * 2 + seq]
    embed, *scalars = lax.optimization_barrier((embed, *scalars))
    seq_at, mine, core, other_core, start_at, place = [
        v.astype(jnp.int32).reshape(1) for v in scalars[:4] + scalars[5:6] + scalars[7:]
    ]
    begin, start, gain_at = scalars[4:7]
    weight, time_half, resid_half, noise_half = [
        take(w, begin, half_cols, 1) for w in (gen_out_w, gen_time_w, gen_resid, noise)
    ]
    gate = dot32(embed, time_half)
    full, sent = pack_part(seq_at, dot32(gen_heads, weight), gate, resid_half, noise_half)
    arrived = exchange(sent, "seq", 1)
    later, embed, _ = lax.optimization_barrier((start_at, embed, full))
    planes = [w.transpose(1, 0, 2) for w in (teacher_qkv, critic_qkv, teacher_time, critic_time)]
    weight_a, weight_b, mods = load_part(later, embed, planes[2], planes[3], planes[0], planes[1], part_cols)
    arrived, mods = lax.optimization_barrier((arrived, mods))
    joined = join_part(full, arrived)
    swapped = exchange(joined, "role", 1)

    latent, kept_a, sent_a, kept_b, sent_b = qkv_part(
        seq_at, core, mine, levels, joined, swapped, noise, mods, weight_a, weight_b
    )
    arrived_a, arrived_b = exchange(sent_a, "mp", 1), exchange(sent_b, "mp", 2)
    out_a, out_b = [take(w, start, part_cols, 0) for w in (teacher_out, critic_out)]
    gains = jnp.stack([teacher_norm, critic_norm])
    gains = take(gains, gain_at, unit, 2)
    arrived_a, arrived_b, out_a, out_b, gains = lax.optimization_barrier((arrived_a, arrived_b, out_a, out_b, gains))
    sum_a, sum_b = both(kept_a, arrived_a), both(kept_b, arrived_b)
    last_a = exchange(sum_a[1].astype(jnp.bfloat16), "mp", 2)
    last_b = exchange(sum_b[1].astype(jnp.bfloat16), "mp", 1)
    head = attend_part(sum_a[0], last_a, sum_b[0], last_b, gains, D)
    near, far = exchange(head, "mp", 1), exchange(head, "mp", 2)
    gathered = head, near, far, exchange(far, "mp", 1)

    kept, sent = out_part(core, mine, gathered, out_a, out_b, mods)
    own, *sends = spread_part(place, kept, exchange(sent, "role", 1), 4)
    arrived = chip_exchange(sends)
    rows = (gate[0:1] * (own + arrived[0].astype(jnp.float32) + both(*arrived[1:]))).astype(jnp.bfloat16)
    rows = merge_part(place, [rows, *chip_exchange([rows] * 3)])
    heads_t = gen_heads.T
    theirs = exchange(rows, "role", 1)
    weight_grad = grad_part(core, heads_t, rows, None, 2)
    weight_grad = grad_part(other_core, heads_t, theirs, weight_grad, 2)
    return latent, weight_grad


def solution(mesh):
    in_specs = (
        P(None, "seq"),
        P("seq", "mp"),
        P("seq", "mp"),
        P(None, "mp"),
        P("seq", "mp"),
        P(),
        P("mp", None, "seq"),
        P("seq", "mp"),
        P(None, None, "mp"),
        P(None, "seq"),
        P("mp", None, "seq"),
        P("seq", "mp"),
        P(None, None, "mp"),
        P(None, "seq"),
    )
    out_specs = (P("seq", "mp"), P("seq", "mp"))
    roles, seqs, groups = mesh.shape["role"], mesh.shape["seq"], mesh.shape["mp"]

    def on_device(*arrays):
        heads_here = arrays[0].shape[1] // HEAD_DIM
        length = arrays[0].shape[0]
        fits = (roles, seqs, groups) == (4, 2, 4) and heads_here == roles * groups and length == HEAD_DIM
        return heads_per_role(*arrays) if fits else pass_per_role(*arrays)

    return jax.shard_map(
        on_device, mesh=mesh, in_specs=in_specs, out_specs=out_specs, check_vma=False
    )
```

```python
import math

import jax
import jax.numpy as jnp
from jax import lax
from jax.experimental import pallas as pl
from jax.experimental.pallas import tpu as pltpu
from jax.sharding import PartitionSpec as P

D = 5120
HEAD_DIM = 128


def time_embed(step_value, width):
    half_width = width // 2
    positions = jnp.arange(half_width, dtype=jnp.float32)
    frequencies = jnp.exp(positions * (-math.log(10000.0) / half_width))
    angles = step_value.astype(jnp.float32) * frequencies
    return jnp.concatenate([jnp.cos(angles), jnp.sin(angles)]).astype(jnp.bfloat16)


def head_norm(values, gains):
    factor = lax.rsqrt(jnp.mean(values * values, axis=-1, keepdims=True) + 1e-06)
    return (values * factor * gains).astype(jnp.bfloat16)


def attend(query_norm, key_norm, value_rows):
    full_length, heads_here, head_width = query_norm.shape
    query_blocks = query_norm.reshape(
        full_length // full_length, full_length, heads_here, head_width
    )

    def one_block(query_block):
        logits = jnp.einsum(
            "qhd,khd->hqk", query_block, key_norm, preferred_element_type=jnp.float32
        ) * (1.0 / math.sqrt(head_width))
        expanded = jnp.exp(logits)
        probs = (expanded / jnp.sum(expanded, axis=2, keepdims=True)).astype(jnp.bfloat16)
        return jnp.einsum(
            "hqk,khd->qhd", probs, value_rows, preferred_element_type=jnp.float32
        ).astype(jnp.bfloat16)

    head_out = lax.map(one_block, query_blocks)
    return head_out.reshape(full_length, heads_here * head_width)


def pass_per_role(
    gen_heads,
    gen_resid,
    gen_out_w,
    gen_time_w,
    noise,
    steps,
    teacher_qkv,
    teacher_out,
    teacher_time,
    teacher_norm,
    critic_qkv,
    critic_out,
    critic_time,
    critic_norm,
):
    full_length = gen_heads.shape[0]
    head_cols = gen_heads.shape[1]
    embed_width = gen_time_w.shape[0]
    gen_gate = jnp.dot(
        time_embed(steps[0], embed_width)[None, :], gen_time_w, preferred_element_type=jnp.float32
    )[0]
    block = gen_heads
    gen_proj = lax.psum_scatter(
        jnp.dot(block, gen_out_w, preferred_element_type=jnp.float32),
        "seq",
        scatter_dimension=0,
        tiled=True,
    )
    latent = (gen_resid.astype(jnp.float32) + gen_gate * gen_proj).astype(jnp.bfloat16)
    role_index = lax.axis_index("role")
    level = steps[1 + role_index // 2]
    use_critic = role_index % 2 == 1
    w_qkv = jnp.where(use_critic, critic_qkv, teacher_qkv)
    w_out = jnp.where(use_critic, critic_out, teacher_out)
    w_time = jnp.where(use_critic, critic_time, teacher_time)
    w_norm = jnp.where(use_critic, critic_norm, teacher_norm)
    noise_level = level.astype(jnp.float32) / 1000.0
    noisy = (
        (1.0 - noise_level) * latent.astype(jnp.float32) + noise_level * noise.astype(jnp.float32)
    ).astype(jnp.bfloat16)
    modulation = jnp.einsum(
        "f,fkd->kd", time_embed(level, embed_width), w_time, preferred_element_type=jnp.float32
    )
    shift_vec = modulation[0]
    scale_vec = modulation[1]
    gate_vec = modulation[2]
    gathered = lax.all_gather(noisy, "seq", axis=0, tiled=True)
    partial_squares = jnp.sum(jnp.square(gathered.astype(jnp.float32)), axis=1)
    scaled = (gathered.astype(jnp.float32) * (1.0 + scale_vec)).astype(jnp.bfloat16)
    flat_w = w_qkv.reshape(w_qkv.shape[0], 3 * head_cols)
    projected = jnp.dot(scaled, flat_w, preferred_element_type=jnp.float32)
    shift_proj = jnp.dot(
        shift_vec.astype(jnp.bfloat16)[None, :], flat_w, preferred_element_type=jnp.float32
    )[0]
    projected, squares, shift_proj = lax.psum((projected, partial_squares, shift_proj), "mp")
    mixed = projected * lax.rsqrt(squares / D + 1e-06)[:, None] + shift_proj
    heads_here = head_cols // HEAD_DIM
    mixed = mixed.reshape(full_length, 3, heads_here, HEAD_DIM)
    gains = w_norm.reshape(2, heads_here, HEAD_DIM)
    query_norm = head_norm(mixed[:, 0], gains[0])
    key_norm = head_norm(mixed[:, 1], gains[1])
    value_rows = mixed[:, 2].astype(jnp.bfloat16)
    head_out = attend(query_norm, key_norm, value_rows)
    weight_sign = jnp.where(use_critic, 0.5, -0.5)
    block = head_out
    summed_rows = lax.psum_scatter(
        weight_sign * (gate_vec * jnp.dot(block, w_out, preferred_element_type=jnp.float32)),
        ("role", "seq"),
        scatter_dimension=0,
        tiled=True,
    )
    grad_rows = lax.all_gather(
        (gen_gate * summed_rows).astype(jnp.bfloat16), ("role", "seq"), axis=0, tiled=True
    )
    weight_grad = lax.dot_general(
        gen_heads, grad_rows, (((0,), (0,)), ((), ())), preferred_element_type=jnp.float32
    )
    return (latent, weight_grad.astype(jnp.bfloat16))

MIB = 1024 * 1024
EXTRA_ROWS = 16


def vmem_spec():
    return pl.BlockSpec(memory_space=pltpu.VMEM)


def smem_spec():
    return pl.BlockSpec(memory_space=pltpu.SMEM)


def params(mebibytes):
    return pltpu.CompilerParams(vmem_limit_bytes=mebibytes * MIB)


def dot32(a, b):
    return jnp.dot(a, b, preferred_element_type=jnp.float32)


def at_block(index, size):
    return pl.ds(pl.multiple_of(index * size, size), size)


def any_spec():
    return pl.BlockSpec(memory_space=pl.ANY)


def hbm_spec():
    return pl.BlockSpec(memory_space=pltpu.HBM)


def cost(flops, moved):
    return pl.CostEstimate(flops=flops, bytes_accessed=moved, transcendentals=0)


def pack_kernel(seq, product, gate, resid, noise, full, sent):
    length = full.shape[0]
    own = resid.shape[0]
    full[...] = product[...] * gate[0:1, :]
    at = at_block(seq[0], own)
    full[at, :] = full[at, :] + resid[...].astype(jnp.float32)
    sent[pl.ds(0, length), :] = full[...].astype(jnp.bfloat16)
    sent[pl.ds(length, own), :] = noise[...]


def pack_part(seq, product, gate, resid, noise):
    length, width = product.shape
    own = resid.shape[0]
    return pl.pallas_call(
        pack_kernel,
        in_specs=[smem_spec()] + [vmem_spec()] * 4,
        out_specs=[vmem_spec()] * 2,
        out_shape=[
            jax.ShapeDtypeStruct((length, width), jnp.float32),
            jax.ShapeDtypeStruct((length + own, width), jnp.bfloat16),
        ],
        compiler_params=params(8),
        name="pack_part",
    )(seq, product, gate, resid, noise)


def load_kernel(start, embed, time_a, time_b, planes_a, planes_b, weight_a, weight_b, mods, sems):
    cols = pl.ds(pl.multiple_of(start[0], weight_a.shape[2]), weight_a.shape[2])
    copies = []
    for index, (planes, weight) in enumerate(((planes_a, weight_a), (planes_b, weight_b))):
        for part in range(3):
            copies.append(
                pltpu.make_async_copy(planes.at[part, :, cols], weight.at[part], sems.at[3 * index + part])
            )
    for copy in copies:
        copy.start()
    for k in range(3):
        mods[0, k] = dot32(embed[...], time_a[k])
        mods[1, k] = dot32(embed[...], time_b[k])
    for copy in copies:
        copy.wait()


def load_part(start, embed, time_a, time_b, planes_a, planes_b, cols):
    parts, depth, _ = planes_a.shape
    width = time_a.shape[2]
    return pl.pallas_call(
        load_kernel,
        in_specs=[smem_spec()] + [vmem_spec()] * 3 + [hbm_spec()] * 2,
        out_specs=[vmem_spec()] * 3,
        out_shape=[jax.ShapeDtypeStruct((parts, depth, cols), jnp.bfloat16)] * 2
        + [jax.ShapeDtypeStruct((2, parts, 8, width), jnp.float32)],
        scratch_shapes=[pltpu.SemaphoreType.DMA((2 * parts,))],
        compiler_params=params(40),
        name="load_part",
    )(start, embed, time_a, time_b, planes_a, planes_b)


def join_kernel(full, arrived, joined):
    length = full.shape[0]
    own = arrived.shape[0] - length
    top = full[...] + arrived[pl.ds(0, length), :].astype(jnp.float32)
    joined[pl.ds(0, length), :] = top.astype(jnp.bfloat16)
    joined[pl.ds(length, own), :] = arrived[pl.ds(length, own), :]


def join_part(full, arrived):
    return pl.pallas_call(
        join_kernel,
        in_specs=[vmem_spec(), vmem_spec()],
        out_specs=vmem_spec(),
        out_shape=jax.ShapeDtypeStruct(arrived.shape, jnp.bfloat16),
        compiler_params=params(8),
        name="join_part",
    )(full, arrived)


def project(index, stride, mine, noisy, squares, mods, weight, kept, sent, result):
    tokens = noisy.shape[0]
    length = tokens // 2
    unit = squares.shape[1] // 2
    groups = weight.shape[2] // unit
    scale = mods[index, 1]
    shift = mods[index, 0]
    spread = noisy.astype(jnp.float32)
    top = spread[:length] * (1.0 + scale[1:2])
    low = spread[length:] * (1.0 + scale[2:3])
    extra = jnp.concatenate([shift[1:3], jnp.zeros((EXTRA_ROWS - 2, shift.shape[1]), jnp.float32)], axis=0)
    rows = jnp.concatenate([top, low, extra], axis=0).astype(jnp.bfloat16)
    row_id = lax.broadcasted_iota(jnp.int32, (EXTRA_ROWS, unit), 0)
    for part in range(3):
        result[...] = dot32(rows, weight[part])
        cols = pl.ds(part * unit, unit)
        for slot in range(groups):
            at = at_block(jnp.bitwise_xor(mine, slot), unit)
            goal = sent if slot & stride else kept
            place = slot // 2 if stride == 1 else slot % 2
            goal[place, pl.ds(0, tokens), cols] = result[pl.ds(0, tokens), at].astype(jnp.bfloat16)
            tail = jnp.where(row_id < 2, result[pl.ds(tokens, EXTRA_ROWS), at], 0.0)
            for level in range(2):
                tail = jnp.where(row_id == 2 + level, squares[0:1, level * length : (level + 1) * length], tail)
            goal[place, pl.ds(tokens, EXTRA_ROWS), cols] = tail.astype(jnp.bfloat16)


def qkv_kernel(seq, core, mine, levels, joined, swapped, noise, mods, weight_a, weight_b, latent, *refs):
    chunks, (values, noises, result) = refs[:4], refs[4:]
    length, cols = values.shape[0], joined.shape[1]
    own = latent.shape[0]
    tokens = 2 * length
    left, right = at_block(core[0], cols), at_block(1 - core[0], cols)
    values[:, left] = joined[pl.ds(0, length), :]
    values[:, right] = swapped[pl.ds(0, length), :]
    latent[...] = values[at_block(seq[0], own), :]
    noises[at_block(seq[0], own), :] = noise[...]
    theirs = at_block(1 - seq[0], own)
    noises[theirs, left] = joined[pl.ds(length, own), :]
    noises[theirs, right] = swapped[pl.ds(length, own), :]
    spread = values[...].astype(jnp.float32)
    noise_rows = noises[...].astype(jnp.float32)
    mixed = jnp.concatenate(
        [(1.0 - levels[level]) * spread + levels[level] * noise_rows for level in range(2)], axis=0
    ).astype(jnp.bfloat16)
    wide = mixed.astype(jnp.float32)
    sums = jnp.sum(wide * wide, axis=1, keepdims=True)
    sums = jnp.broadcast_to(sums, (tokens, length)).T[0:8]
    for index, weight in enumerate((weight_a, weight_b)):
        project(index, 2 - index, mine[0], mixed, sums, mods, weight, *chunks[2 * index : 2 * index + 2], result)


def qkv_part(seq, core, mine, levels, joined, swapped, noise, mods, weight_a, weight_b):
    own, width = noise.shape
    length = joined.shape[0] - own
    tokens = 2 * length
    cols = weight_a.shape[2]
    return pl.pallas_call(
        qkv_kernel,
        in_specs=[smem_spec()] * 4 + [vmem_spec()] * 6,
        out_specs=[vmem_spec()] * 5,
        out_shape=[jax.ShapeDtypeStruct((own, width), jnp.bfloat16)]
        + [jax.ShapeDtypeStruct((cols // length // 2, tokens + EXTRA_ROWS, 3 * length), jnp.bfloat16)] * 4,
        scratch_shapes=[
            pltpu.VMEM((length, width), jnp.bfloat16),
            pltpu.VMEM((length, width), jnp.bfloat16),
            pltpu.VMEM((tokens + EXTRA_ROWS, cols), jnp.float32),
        ],
        compiler_params=params(20),
        name="qkv_part",
    )(seq, core, mine, levels, joined, swapped, noise, mods, weight_a, weight_b)


def attend_kernel(width, kept_a, other_a, kept_b, other_b, gains, out):
    _, _, length, unit = out.shape
    tokens = 2 * length
    for index, (kept, other) in enumerate(((kept_a, other_a), (kept_b, other_b))):
        mixed = kept[...] + other[...].astype(jnp.float32)
        extra = mixed[tokens:]
        for level in range(2):
            rows_at = slice(level * length, (level + 1) * length)
            squares = jnp.broadcast_to(extra[2 + level : 3 + level, :unit], (unit, unit)).T
            factor = lax.rsqrt(squares * (1.0 / width) + 1e-06)

            def pick(part):
                cols = slice(part * unit, (part + 1) * unit)
                return mixed[rows_at, cols] * factor + extra[level : level + 1, cols]

            def normed(part):
                rows = pick(part)
                mean = jnp.mean(rows * rows, axis=1, keepdims=True)
                return (rows * lax.rsqrt(mean + 1e-06) * gains[index, part : part + 1, :]).astype(jnp.bfloat16)

            query, key = normed(0), normed(1)
            value = pick(2).astype(jnp.bfloat16)
            logits = lax.dot_general(
                query, key, (((1,), (1,)), ((), ())), preferred_element_type=jnp.float32
            ) * (1.0 / math.sqrt(unit))
            expanded = jnp.exp(logits)
            probs = (expanded / jnp.sum(expanded, axis=1, keepdims=True)).astype(jnp.bfloat16)
            out[index, level] = dot32(probs, value).astype(jnp.bfloat16)


def attend_part(kept_a, other_a, kept_b, other_b, gains, width):
    unit = kept_a.shape[1] // 3
    length = (kept_a.shape[0] - EXTRA_ROWS) // 2
    return pl.pallas_call(
        lambda *refs: attend_kernel(width, *refs),
        in_specs=[vmem_spec()] * 5,
        out_specs=vmem_spec(),
        out_shape=jax.ShapeDtypeStruct((2, 2, length, unit), jnp.bfloat16),
        compiler_params=params(8),
        name="attend_part",
    )(kept_a, other_a, kept_b, other_b, gains)


def out_kernel(core, mine, *refs):
    heads = refs[0:4]
    weight_a, weight_b, mods, kept, sent, rows, total = refs[4:]
    _, _, length, unit = heads[0].shape
    for index, weight in enumerate((weight_a, weight_b)):
        for slot, head in enumerate(heads):
            at = at_block(jnp.bitwise_xor(mine[0], slot), unit)
            for level in range(2):
                rows[pl.ds(level * length, length), at] = head[index, level]
        result = dot32(rows[...], weight[...])
        gates = mods[index, 2]
        signed = gates[1:2] * result[:length] + gates[2:3] * result[length:]
        if index == 0:
            total[...] = -0.5 * signed
        else:
            total[...] = total[...] + 0.5 * signed
    cols = kept.shape[1]
    kept[...] = total[:, at_block(core[0], cols)]
    sent[...] = total[:, at_block(1 - core[0], cols)].astype(jnp.bfloat16)


def out_part(core, mine, heads, weight_a, weight_b, mods):
    length = heads[0].shape[2]
    depth, width = weight_a.shape
    return pl.pallas_call(
        out_kernel,
        in_specs=[smem_spec()] * 2 + [vmem_spec()] * 7,
        out_specs=[vmem_spec()] * 2,
        out_shape=[
            jax.ShapeDtypeStruct((length, width // 2), jnp.float32),
            jax.ShapeDtypeStruct((length, width // 2), jnp.bfloat16),
        ],
        scratch_shapes=[
            pltpu.VMEM((2 * length, depth), jnp.bfloat16),
            pltpu.VMEM((length, width), jnp.float32),
        ],
        compiler_params=params(16),
        name="out_part",
    )(core, mine, *heads, weight_a, weight_b, mods)


def grad_kernel(half, heads_t, rows, *refs):
    refs[-1][...] = dot32(heads_t[...], rows[...]).astype(jnp.bfloat16)


def grad_part(half, heads_t, rows, before, steps):
    depth, length = heads_t.shape
    cols = rows.shape[1]
    tile = depth // steps
    rest = [] if before is None else [before]
    grid_spec = pltpu.PrefetchScalarGridSpec(
        num_scalar_prefetch=1,
        grid=(steps,),
        in_specs=[
            pl.BlockSpec((tile, length), lambda n, w: (n, 0)),
            pl.BlockSpec((length, cols), lambda n, w: (0, 0)),
        ]
        + [any_spec()] * len(rest),
        out_specs=pl.BlockSpec((tile, cols), lambda n, w: (n, w[0])),
    )
    return pl.pallas_call(
        grad_kernel,
        grid_spec=grid_spec,
        out_shape=jax.ShapeDtypeStruct((depth, 2 * cols), jnp.bfloat16),
        input_output_aliases={3: 0} if rest else {},
        compiler_params=params(16),
        name="grad_part",
    )(half, heads_t, rows, *rest)


def exchange(array, axis, bit):
    return lax.ppermute(array, axis, [(i, i ^ bit) for i in range(lax.axis_size(axis))])


def take(array, begin, size, axis):
    return lax.dynamic_slice_in_dim(array, begin, size, axis=axis, allow_negative_indices=False)


def both(mine, theirs):
    return mine.astype(jnp.float32) + theirs.astype(jnp.float32)


def heads_per_role(
    gen_heads,
    gen_resid,
    gen_out_w,
    gen_time_w,
    noise,
    steps,
    teacher_qkv,
    teacher_out,
    teacher_time,
    teacher_norm,
    critic_qkv,
    critic_out,
    critic_time,
    critic_norm,
):
    length = gen_heads.shape[0]
    roles, groups = lax.axis_size("role"), lax.axis_size("mp")
    role, seq, mp = lax.axis_index("role"), lax.axis_index("seq"), lax.axis_index("mp")
    part_cols = gen_heads.shape[1] // roles
    freq = gen_time_w.shape[0]
    core = role % 2
    half_cols = gen_resid.shape[1] // 2
    unit = part_cols // groups

    embed = jax.vmap(lambda t: time_embed(t, freq))(steps)
    embed = jnp.concatenate([embed, jnp.zeros((5, freq), jnp.bfloat16)], axis=0)
    levels = steps[1:3].astype(jnp.float32) / 1000.0
    start = role * part_cols
    scalars = [seq, mp, core, 1 - core, core * half_cols, start, start + mp * unit]
    gen_heads, *scalars = lax.optimization_barrier((gen_heads, *scalars))
    seq_at, mine, core, other_core, start_at = [v.astype(jnp.int32).reshape(1) for v in scalars[:4] + scalars[5:6]]
    begin, start, gain_at = scalars[4:]
    weight, time_half, resid_half, noise_half = [
        take(w, begin, half_cols, 1) for w in (gen_out_w, gen_time_w, gen_resid, noise)
    ]
    gate = dot32(embed, time_half)
    full, sent = pack_part(seq_at, dot32(gen_heads, weight), gate, resid_half, noise_half)
    arrived = exchange(sent, "seq", 1)
    later, embed, _ = lax.optimization_barrier((start_at, embed, full))
    planes = [w.transpose(1, 0, 2) for w in (teacher_qkv, critic_qkv, teacher_time, critic_time)]
    weight_a, weight_b, mods = load_part(later, embed, planes[2], planes[3], planes[0], planes[1], part_cols)
    arrived, mods = lax.optimization_barrier((arrived, mods))
    joined = join_part(full, arrived)
    swapped = exchange(joined, "role", 1)

    latent, kept_a, sent_a, kept_b, sent_b = qkv_part(
        seq_at, core, mine, levels, joined, swapped, noise, mods, weight_a, weight_b
    )
    arrived_a, arrived_b = exchange(sent_a, "mp", 2), exchange(sent_b, "mp", 1)
    out_a, out_b = [take(w, start, part_cols, 0) for w in (teacher_out, critic_out)]
    gains = jnp.stack([teacher_norm, critic_norm])
    gains = take(gains, gain_at, unit, 2)
    arrived_a, arrived_b, out_a, out_b, gains = lax.optimization_barrier((arrived_a, arrived_b, out_a, out_b, gains))
    sum_b = both(kept_b, arrived_b)
    send_b, arrived_a = lax.optimization_barrier((sum_b[1].astype(jnp.bfloat16), arrived_a))
    last_b = exchange(send_b, "mp", 2)
    sum_a = both(kept_a, arrived_a)
    last_a = exchange(sum_a[1].astype(jnp.bfloat16), "mp", 1)
    head = attend_part(sum_a[0], last_a, sum_b[0], last_b, gains, D)
    near, far = exchange(head, "mp", 1), exchange(head, "mp", 2)
    gathered = head, near, far, exchange(far, "mp", 1)

    kept, sent = out_part(core, mine, gathered, out_a, out_b, mods)
    total = both(kept, exchange(sent, "role", 1)).astype(jnp.bfloat16)
    along_x = exchange(total, "seq", 1)
    along_y = exchange(total, "role", 2)
    across = lax.ppermute(
        total, ("role", "seq"), [(i, i ^ (2 * lax.axis_size("seq") + 1)) for i in range(roles * lax.axis_size("seq"))]
    )
    total = both(total, along_x) + both(along_y, across)
    rows = (gate[0:1] * total).astype(jnp.bfloat16)
    heads_t = gen_heads.T
    theirs = exchange(rows, "role", 1)
    weight_grad = grad_part(core, heads_t, rows, None, 2)
    weight_grad = grad_part(other_core, heads_t, theirs, weight_grad, 2)
    return latent, weight_grad


def solution(mesh):
    in_specs = (
        P(None, "seq"),
        P("seq", "mp"),
        P("seq", "mp"),
        P(None, "mp"),
        P("seq", "mp"),
        P(),
        P("mp", None, "seq"),
        P("seq", "mp"),
        P(None, None, "mp"),
        P(None, "seq"),
        P("mp", None, "seq"),
        P("seq", "mp"),
        P(None, None, "mp"),
        P(None, "seq"),
    )
    out_specs = (P("seq", "mp"), P("seq", "mp"))
    roles, seqs, groups = mesh.shape["role"], mesh.shape["seq"], mesh.shape["mp"]

    def on_device(*arrays):
        heads_here = arrays[0].shape[1] // HEAD_DIM
        length = arrays[0].shape[0]
        fits = (roles, seqs, groups) == (4, 2, 4) and heads_here == roles * groups and length == HEAD_DIM
        return heads_per_role(*arrays) if fits else pass_per_role(*arrays)

    return jax.shard_map(
        on_device, mesh=mesh, in_specs=in_specs, out_specs=out_specs, check_vma=False
    )
```

```python
import math

import jax
import jax.numpy as jnp
from jax import lax
from jax.experimental import pallas as pl
from jax.experimental.pallas import tpu as pltpu
from jax.sharding import PartitionSpec as P

D = 5120
HEAD_DIM = 128


def time_embed(step_value, width):
    half_width = width // 2
    positions = jnp.arange(half_width, dtype=jnp.float32)
    frequencies = jnp.exp(positions * (-math.log(10000.0) / half_width))
    angles = step_value.astype(jnp.float32) * frequencies
    return jnp.concatenate([jnp.cos(angles), jnp.sin(angles)]).astype(jnp.bfloat16)


def head_norm(values, gains):
    factor = lax.rsqrt(jnp.mean(values * values, axis=-1, keepdims=True) + 1e-06)
    return (values * factor * gains).astype(jnp.bfloat16)


def attend(query_norm, key_norm, value_rows):
    full_length, heads_here, head_width = query_norm.shape
    query_blocks = query_norm.reshape(
        full_length // full_length, full_length, heads_here, head_width
    )

    def one_block(query_block):
        logits = jnp.einsum(
            "qhd,khd->hqk", query_block, key_norm, preferred_element_type=jnp.float32
        ) * (1.0 / math.sqrt(head_width))
        expanded = jnp.exp(logits)
        probs = (expanded / jnp.sum(expanded, axis=2, keepdims=True)).astype(jnp.bfloat16)
        return jnp.einsum(
            "hqk,khd->qhd", probs, value_rows, preferred_element_type=jnp.float32
        ).astype(jnp.bfloat16)

    head_out = lax.map(one_block, query_blocks)
    return head_out.reshape(full_length, heads_here * head_width)


def pass_per_role(
    gen_heads,
    gen_resid,
    gen_out_w,
    gen_time_w,
    noise,
    steps,
    teacher_qkv,
    teacher_out,
    teacher_time,
    teacher_norm,
    critic_qkv,
    critic_out,
    critic_time,
    critic_norm,
):
    full_length = gen_heads.shape[0]
    head_cols = gen_heads.shape[1]
    embed_width = gen_time_w.shape[0]
    gen_gate = jnp.dot(
        time_embed(steps[0], embed_width)[None, :], gen_time_w, preferred_element_type=jnp.float32
    )[0]
    block = gen_heads
    gen_proj = lax.psum_scatter(
        jnp.dot(block, gen_out_w, preferred_element_type=jnp.float32),
        "seq",
        scatter_dimension=0,
        tiled=True,
    )
    latent = (gen_resid.astype(jnp.float32) + gen_gate * gen_proj).astype(jnp.bfloat16)
    role_index = lax.axis_index("role")
    level = steps[1 + role_index // 2]
    use_critic = role_index % 2 == 1
    w_qkv = jnp.where(use_critic, critic_qkv, teacher_qkv)
    w_out = jnp.where(use_critic, critic_out, teacher_out)
    w_time = jnp.where(use_critic, critic_time, teacher_time)
    w_norm = jnp.where(use_critic, critic_norm, teacher_norm)
    noise_level = level.astype(jnp.float32) / 1000.0
    noisy = (
        (1.0 - noise_level) * latent.astype(jnp.float32) + noise_level * noise.astype(jnp.float32)
    ).astype(jnp.bfloat16)
    modulation = jnp.einsum(
        "f,fkd->kd", time_embed(level, embed_width), w_time, preferred_element_type=jnp.float32
    )
    shift_vec = modulation[0]
    scale_vec = modulation[1]
    gate_vec = modulation[2]
    gathered = lax.all_gather(noisy, "seq", axis=0, tiled=True)
    partial_squares = jnp.sum(jnp.square(gathered.astype(jnp.float32)), axis=1)
    scaled = (gathered.astype(jnp.float32) * (1.0 + scale_vec)).astype(jnp.bfloat16)
    flat_w = w_qkv.reshape(w_qkv.shape[0], 3 * head_cols)
    projected = jnp.dot(scaled, flat_w, preferred_element_type=jnp.float32)
    shift_proj = jnp.dot(
        shift_vec.astype(jnp.bfloat16)[None, :], flat_w, preferred_element_type=jnp.float32
    )[0]
    projected, squares, shift_proj = lax.psum((projected, partial_squares, shift_proj), "mp")
    mixed = projected * lax.rsqrt(squares / D + 1e-06)[:, None] + shift_proj
    heads_here = head_cols // HEAD_DIM
    mixed = mixed.reshape(full_length, 3, heads_here, HEAD_DIM)
    gains = w_norm.reshape(2, heads_here, HEAD_DIM)
    query_norm = head_norm(mixed[:, 0], gains[0])
    key_norm = head_norm(mixed[:, 1], gains[1])
    value_rows = mixed[:, 2].astype(jnp.bfloat16)
    head_out = attend(query_norm, key_norm, value_rows)
    weight_sign = jnp.where(use_critic, 0.5, -0.5)
    block = head_out
    summed_rows = lax.psum_scatter(
        weight_sign * (gate_vec * jnp.dot(block, w_out, preferred_element_type=jnp.float32)),
        ("role", "seq"),
        scatter_dimension=0,
        tiled=True,
    )
    grad_rows = lax.all_gather(
        (gen_gate * summed_rows).astype(jnp.bfloat16), ("role", "seq"), axis=0, tiled=True
    )
    weight_grad = lax.dot_general(
        gen_heads, grad_rows, (((0,), (0,)), ((), ())), preferred_element_type=jnp.float32
    )
    return (latent, weight_grad.astype(jnp.bfloat16))

MIB = 1024 * 1024
EXTRA_ROWS = 16


def vmem_spec():
    return pl.BlockSpec(memory_space=pltpu.VMEM)


def smem_spec():
    return pl.BlockSpec(memory_space=pltpu.SMEM)


def params(mebibytes):
    return pltpu.CompilerParams(vmem_limit_bytes=mebibytes * MIB)


def dot32(a, b):
    return jnp.dot(a, b, preferred_element_type=jnp.float32)


def at_block(index, size):
    return pl.ds(pl.multiple_of(index * size, size), size)


def any_spec():
    return pl.BlockSpec(memory_space=pl.ANY)


def hbm_spec():
    return pl.BlockSpec(memory_space=pltpu.HBM)


def cost(flops, moved):
    return pl.CostEstimate(flops=flops, bytes_accessed=moved, transcendentals=0)


def pack_kernel(seq, product, gate, resid, noise, full, sent):
    length = full.shape[0]
    own = resid.shape[0]
    full[...] = product[...] * gate[0:1, :]
    at = at_block(seq[0], own)
    full[at, :] = full[at, :] + resid[...].astype(jnp.float32)
    sent[pl.ds(0, length), :] = full[...].astype(jnp.bfloat16)
    sent[pl.ds(length, own), :] = noise[...]


def pack_part(seq, product, gate, resid, noise):
    length, width = product.shape
    own = resid.shape[0]
    return pl.pallas_call(
        pack_kernel,
        in_specs=[smem_spec()] + [vmem_spec()] * 4,
        out_specs=[vmem_spec()] * 2,
        out_shape=[
            jax.ShapeDtypeStruct((length, width), jnp.float32),
            jax.ShapeDtypeStruct((length + own, width), jnp.bfloat16),
        ],
        compiler_params=params(8),
        name="pack_part",
    )(seq, product, gate, resid, noise)


def load_kernel(start, embed, time_a, time_b, planes_a, planes_b, weight_a, weight_b, mods, sems):
    cols = pl.ds(pl.multiple_of(start[0], weight_a.shape[2]), weight_a.shape[2])
    copies = []
    for index, (planes, weight) in enumerate(((planes_a, weight_a), (planes_b, weight_b))):
        for part in range(3):
            copies.append(
                pltpu.make_async_copy(planes.at[part, :, cols], weight.at[part], sems.at[3 * index + part])
            )
    for copy in copies:
        copy.start()
    for k in range(3):
        mods[0, k] = dot32(embed[...], time_a[k])
        mods[1, k] = dot32(embed[...], time_b[k])
    for copy in copies:
        copy.wait()


def load_part(start, embed, time_a, time_b, planes_a, planes_b, cols):
    parts, depth, _ = planes_a.shape
    width = time_a.shape[2]
    return pl.pallas_call(
        load_kernel,
        in_specs=[smem_spec()] + [vmem_spec()] * 3 + [hbm_spec()] * 2,
        out_specs=[vmem_spec()] * 3,
        out_shape=[jax.ShapeDtypeStruct((parts, depth, cols), jnp.bfloat16)] * 2
        + [jax.ShapeDtypeStruct((2, parts, 8, width), jnp.float32)],
        scratch_shapes=[pltpu.SemaphoreType.DMA((2 * parts,))],
        compiler_params=params(40),
        name="load_part",
    )(start, embed, time_a, time_b, planes_a, planes_b)


def join_kernel(full, arrived, joined):
    length = full.shape[0]
    own = arrived.shape[0] - length
    top = full[...] + arrived[pl.ds(0, length), :].astype(jnp.float32)
    joined[pl.ds(0, length), :] = top.astype(jnp.bfloat16)
    joined[pl.ds(length, own), :] = arrived[pl.ds(length, own), :]


def join_part(full, arrived):
    return pl.pallas_call(
        join_kernel,
        in_specs=[vmem_spec(), vmem_spec()],
        out_specs=vmem_spec(),
        out_shape=jax.ShapeDtypeStruct(arrived.shape, jnp.bfloat16),
        compiler_params=params(8),
        name="join_part",
    )(full, arrived)


def project(index, stride, mine, noisy, squares, mods, weight, kept, sent, result):
    tokens = noisy.shape[0]
    length = tokens // 2
    unit = squares.shape[1] // 2
    groups = weight.shape[2] // unit
    scale = mods[index, 1]
    shift = mods[index, 0]
    spread = noisy.astype(jnp.float32)
    top = spread[:length] * (1.0 + scale[1:2])
    low = spread[length:] * (1.0 + scale[2:3])
    extra = jnp.concatenate([shift[1:3], jnp.zeros((EXTRA_ROWS - 2, shift.shape[1]), jnp.float32)], axis=0)
    rows = jnp.concatenate([top, low, extra], axis=0).astype(jnp.bfloat16)
    row_id = lax.broadcasted_iota(jnp.int32, (EXTRA_ROWS, unit), 0)
    for part in range(3):
        result[...] = dot32(rows, weight[part])
        cols = pl.ds(part * unit, unit)
        for slot in range(groups):
            at = at_block(jnp.bitwise_xor(mine, slot), unit)
            goal = sent if slot & stride else kept
            place = slot // 2 if stride == 1 else slot % 2
            goal[place, pl.ds(0, tokens), cols] = result[pl.ds(0, tokens), at].astype(jnp.bfloat16)
            tail = jnp.where(row_id < 2, result[pl.ds(tokens, EXTRA_ROWS), at], 0.0)
            for level in range(2):
                tail = jnp.where(row_id == 2 + level, squares[0:1, level * length : (level + 1) * length], tail)
            goal[place, pl.ds(tokens, EXTRA_ROWS), cols] = tail.astype(jnp.bfloat16)


def qkv_kernel(seq, core, mine, levels, joined, swapped, noise, mods, weight_a, weight_b, latent, *refs):
    chunks, (values, noises, result) = refs[:4], refs[4:]
    length, cols = values.shape[0], joined.shape[1]
    own = latent.shape[0]
    tokens = 2 * length
    left, right = at_block(core[0], cols), at_block(1 - core[0], cols)
    values[:, left] = joined[pl.ds(0, length), :]
    values[:, right] = swapped[pl.ds(0, length), :]
    latent[...] = values[at_block(seq[0], own), :]
    noises[at_block(seq[0], own), :] = noise[...]
    theirs = at_block(1 - seq[0], own)
    noises[theirs, left] = joined[pl.ds(length, own), :]
    noises[theirs, right] = swapped[pl.ds(length, own), :]
    spread = values[...].astype(jnp.float32)
    noise_rows = noises[...].astype(jnp.float32)
    mixed = jnp.concatenate(
        [(1.0 - levels[level]) * spread + levels[level] * noise_rows for level in range(2)], axis=0
    ).astype(jnp.bfloat16)
    wide = mixed.astype(jnp.float32)
    sums = jnp.sum(wide * wide, axis=1, keepdims=True)
    sums = jnp.broadcast_to(sums, (tokens, length)).T[0:8]
    for index, weight in enumerate((weight_a, weight_b)):
        project(index, index + 1, mine[0], mixed, sums, mods, weight, *chunks[2 * index : 2 * index + 2], result)


def qkv_part(seq, core, mine, levels, joined, swapped, noise, mods, weight_a, weight_b):
    own, width = noise.shape
    length = joined.shape[0] - own
    tokens = 2 * length
    cols = weight_a.shape[2]
    return pl.pallas_call(
        qkv_kernel,
        in_specs=[smem_spec()] * 4 + [vmem_spec()] * 6,
        out_specs=[vmem_spec()] * 5,
        out_shape=[jax.ShapeDtypeStruct((own, width), jnp.bfloat16)]
        + [jax.ShapeDtypeStruct((cols // length // 2, tokens + EXTRA_ROWS, 3 * length), jnp.bfloat16)] * 4,
        scratch_shapes=[
            pltpu.VMEM((length, width), jnp.bfloat16),
            pltpu.VMEM((length, width), jnp.bfloat16),
            pltpu.VMEM((tokens + EXTRA_ROWS, cols), jnp.float32),
        ],
        compiler_params=params(20),
        name="qkv_part",
    )(seq, core, mine, levels, joined, swapped, noise, mods, weight_a, weight_b)


def attend_kernel(width, kept_a, other_a, kept_b, other_b, gains, out):
    _, _, length, unit = out.shape
    tokens = 2 * length
    for index, (kept, other) in enumerate(((kept_a, other_a), (kept_b, other_b))):
        mixed = kept[...] + other[...].astype(jnp.float32)
        extra = mixed[tokens:]
        for level in range(2):
            rows_at = slice(level * length, (level + 1) * length)
            squares = jnp.broadcast_to(extra[2 + level : 3 + level, :unit], (unit, unit)).T
            factor = lax.rsqrt(squares * (1.0 / width) + 1e-06)

            def pick(part):
                cols = slice(part * unit, (part + 1) * unit)
                return mixed[rows_at, cols] * factor + extra[level : level + 1, cols]

            def normed(part):
                rows = pick(part)
                mean = jnp.mean(rows * rows, axis=1, keepdims=True)
                return (rows * lax.rsqrt(mean + 1e-06) * gains[index, part : part + 1, :]).astype(jnp.bfloat16)

            query, key = normed(0), normed(1)
            value = pick(2).astype(jnp.bfloat16)
            logits = lax.dot_general(
                query, key, (((1,), (1,)), ((), ())), preferred_element_type=jnp.float32
            ) * (1.0 / math.sqrt(unit))
            expanded = jnp.exp(logits)
            probs = (expanded / jnp.sum(expanded, axis=1, keepdims=True)).astype(jnp.bfloat16)
            out[index, level] = dot32(probs, value).astype(jnp.bfloat16)


def attend_part(kept_a, other_a, kept_b, other_b, gains, width):
    unit = kept_a.shape[1] // 3
    length = (kept_a.shape[0] - EXTRA_ROWS) // 2
    return pl.pallas_call(
        lambda *refs: attend_kernel(width, *refs),
        in_specs=[vmem_spec()] * 5,
        out_specs=vmem_spec(),
        out_shape=jax.ShapeDtypeStruct((2, 2, length, unit), jnp.bfloat16),
        compiler_params=params(8),
        name="attend_part",
    )(kept_a, other_a, kept_b, other_b, gains)


def out_kernel(core, mine, *refs):
    heads = refs[0:4]
    weight_a, weight_b, mods, kept, sent, rows, total = refs[4:]
    _, _, length, unit = heads[0].shape
    for index, weight in enumerate((weight_a, weight_b)):
        for slot, head in enumerate(heads):
            at = at_block(jnp.bitwise_xor(mine[0], slot), unit)
            for level in range(2):
                rows[pl.ds(level * length, length), at] = head[index, level]
        result = dot32(rows[...], weight[...])
        gates = mods[index, 2]
        signed = gates[1:2] * result[:length] + gates[2:3] * result[length:]
        if index == 0:
            total[...] = -0.5 * signed
        else:
            total[...] = total[...] + 0.5 * signed
    cols = kept.shape[1]
    kept[...] = total[:, at_block(core[0], cols)]
    sent[...] = total[:, at_block(1 - core[0], cols)].astype(jnp.bfloat16)


def out_part(core, mine, heads, weight_a, weight_b, mods):
    length = heads[0].shape[2]
    depth, width = weight_a.shape
    return pl.pallas_call(
        out_kernel,
        in_specs=[smem_spec()] * 2 + [vmem_spec()] * 7,
        out_specs=[vmem_spec()] * 2,
        out_shape=[
            jax.ShapeDtypeStruct((length, width // 2), jnp.float32),
            jax.ShapeDtypeStruct((length, width // 2), jnp.bfloat16),
        ],
        scratch_shapes=[
            pltpu.VMEM((2 * length, depth), jnp.bfloat16),
            pltpu.VMEM((length, width), jnp.float32),
        ],
        compiler_params=params(16),
        name="out_part",
    )(core, mine, *heads, weight_a, weight_b, mods)


def grad_kernel(half, heads_t, rows, *refs):
    refs[-1][...] = dot32(heads_t[...], rows[...]).astype(jnp.bfloat16)


def grad_part(half, heads_t, rows, before, steps):
    depth, length = heads_t.shape
    cols = rows.shape[1]
    tile = depth // steps
    rest = [] if before is None else [before]
    grid_spec = pltpu.PrefetchScalarGridSpec(
        num_scalar_prefetch=1,
        grid=(steps,),
        in_specs=[
            pl.BlockSpec((tile, length), lambda n, w: (n, 0)),
            pl.BlockSpec((length, cols), lambda n, w: (0, 0)),
        ]
        + [any_spec()] * len(rest),
        out_specs=pl.BlockSpec((tile, cols), lambda n, w: (n, w[0])),
    )
    return pl.pallas_call(
        grad_kernel,
        grid_spec=grid_spec,
        out_shape=jax.ShapeDtypeStruct((depth, 2 * cols), jnp.bfloat16),
        input_output_aliases={3: 0} if rest else {},
        compiler_params=params(16),
        name="grad_part",
    )(half, heads_t, rows, *rest)


def exchange(array, axis, bit):
    return lax.ppermute(array, axis, [(i, i ^ bit) for i in range(lax.axis_size(axis))])


def take(array, begin, size, axis):
    return lax.dynamic_slice_in_dim(array, begin, size, axis=axis, allow_negative_indices=False)


def both(mine, theirs):
    return mine.astype(jnp.float32) + theirs.astype(jnp.float32)


def heads_per_role(
    gen_heads,
    gen_resid,
    gen_out_w,
    gen_time_w,
    noise,
    steps,
    teacher_qkv,
    teacher_out,
    teacher_time,
    teacher_norm,
    critic_qkv,
    critic_out,
    critic_time,
    critic_norm,
):
    length = gen_heads.shape[0]
    roles, groups = lax.axis_size("role"), lax.axis_size("mp")
    role, seq, mp = lax.axis_index("role"), lax.axis_index("seq"), lax.axis_index("mp")
    part_cols = gen_heads.shape[1] // roles
    freq = gen_time_w.shape[0]
    core = role % 2
    half_cols = gen_resid.shape[1] // 2
    unit = part_cols // groups

    embed = jax.vmap(lambda t: time_embed(t, freq))(steps)
    embed = jnp.concatenate([embed, jnp.zeros((5, freq), jnp.bfloat16)], axis=0)
    levels = steps[1:3].astype(jnp.float32) / 1000.0
    start = role * part_cols
    scalars = [seq, mp, core, 1 - core, core * half_cols, start, start + mp * unit]
    embed, *scalars = lax.optimization_barrier((embed, *scalars))
    seq_at, mine, core, other_core, start_at = [v.astype(jnp.int32).reshape(1) for v in scalars[:4] + scalars[5:6]]
    begin, start, gain_at = scalars[4:]
    weight, time_half, resid_half, noise_half = [
        take(w, begin, half_cols, 1) for w in (gen_out_w, gen_time_w, gen_resid, noise)
    ]
    gate = dot32(embed, time_half)
    full, sent = pack_part(seq_at, dot32(gen_heads, weight), gate, resid_half, noise_half)
    arrived = exchange(sent, "seq", 1)
    later, embed, _ = lax.optimization_barrier((start_at, embed, full))
    planes = [w.transpose(1, 0, 2) for w in (teacher_qkv, critic_qkv, teacher_time, critic_time)]
    weight_a, weight_b, mods = load_part(later, embed, planes[2], planes[3], planes[0], planes[1], part_cols)
    arrived, mods = lax.optimization_barrier((arrived, mods))
    joined = join_part(full, arrived)
    swapped = exchange(joined, "role", 1)

    latent, kept_a, sent_a, kept_b, sent_b = qkv_part(
        seq_at, core, mine, levels, joined, swapped, noise, mods, weight_a, weight_b
    )
    arrived_b = exchange(sent_b, "mp", 2)
    arrived_a = exchange(sent_a, "mp", 1)
    out_a, out_b = [take(w, start, part_cols, 0) for w in (teacher_out, critic_out)]
    gains = jnp.stack([teacher_norm, critic_norm])
    gains = take(gains, gain_at, unit, 2)
    arrived_b, arrived_a, out_a, out_b, gains = lax.optimization_barrier((arrived_b, arrived_a, out_a, out_b, gains))
    sum_a, sum_b = both(kept_a, arrived_a), both(kept_b, arrived_b)
    last_a = exchange(sum_a[1].astype(jnp.bfloat16), "mp", 2)
    last_b = exchange(sum_b[1].astype(jnp.bfloat16), "mp", 1)
    head = attend_part(sum_a[0], last_a, sum_b[0], last_b, gains, D)
    near, far = exchange(head, "mp", 1), exchange(head, "mp", 2)
    gathered = head, near, far, exchange(far, "mp", 1)

    kept, sent = out_part(core, mine, gathered, out_a, out_b, mods)
    total = both(kept, exchange(sent, "role", 1)).astype(jnp.bfloat16)
    along_x = exchange(total, "seq", 1)
    along_y = exchange(total, "role", 2)
    across = lax.ppermute(
        total, ("role", "seq"), [(i, i ^ (2 * lax.axis_size("seq") + 1)) for i in range(roles * lax.axis_size("seq"))]
    )
    total = both(total, along_x) + both(along_y, across)
    rows = (gate[0:1] * total).astype(jnp.bfloat16)
    heads_t = gen_heads.T
    theirs = exchange(rows, "role", 1)
    weight_grad = grad_part(core, heads_t, rows, None, 2)
    weight_grad = grad_part(other_core, heads_t, theirs, weight_grad, 2)
    return latent, weight_grad


def solution(mesh):
    in_specs = (
        P(None, "seq"),
        P("seq", "mp"),
        P("seq", "mp"),
        P(None, "mp"),
        P("seq", "mp"),
        P(),
        P("mp", None, "seq"),
        P("seq", "mp"),
        P(None, None, "mp"),
        P(None, "seq"),
        P("mp", None, "seq"),
        P("seq", "mp"),
        P(None, None, "mp"),
        P(None, "seq"),
    )
    out_specs = (P("seq", "mp"), P("seq", "mp"))
    roles, seqs, groups = mesh.shape["role"], mesh.shape["seq"], mesh.shape["mp"]

    def on_device(*arrays):
        heads_here = arrays[0].shape[1] // HEAD_DIM
        length = arrays[0].shape[0]
        fits = (roles, seqs, groups) == (4, 2, 4) and heads_here == roles * groups and length == HEAD_DIM
        return heads_per_role(*arrays) if fits else pass_per_role(*arrays)

    return jax.shard_map(
        on_device, mesh=mesh, in_specs=in_specs, out_specs=out_specs, check_vma=False
    )
```

```python
import math

import jax
import jax.numpy as jnp
from jax import lax
from jax.experimental import pallas as pl
from jax.experimental.pallas import tpu as pltpu
from jax.sharding import PartitionSpec as P

D = 5120
HEAD_DIM = 128


def time_embed(step_value, width):
    half_width = width // 2
    positions = jnp.arange(half_width, dtype=jnp.float32)
    frequencies = jnp.exp(positions * (-math.log(10000.0) / half_width))
    angles = step_value.astype(jnp.float32) * frequencies
    return jnp.concatenate([jnp.cos(angles), jnp.sin(angles)]).astype(jnp.bfloat16)


def head_norm(values, gains):
    factor = lax.rsqrt(jnp.mean(values * values, axis=-1, keepdims=True) + 1e-06)
    return (values * factor * gains).astype(jnp.bfloat16)


def attend(query_norm, key_norm, value_rows):
    full_length, heads_here, head_width = query_norm.shape
    query_blocks = query_norm.reshape(
        full_length // full_length, full_length, heads_here, head_width
    )

    def one_block(query_block):
        logits = jnp.einsum(
            "qhd,khd->hqk", query_block, key_norm, preferred_element_type=jnp.float32
        ) * (1.0 / math.sqrt(head_width))
        expanded = jnp.exp(logits)
        probs = (expanded / jnp.sum(expanded, axis=2, keepdims=True)).astype(jnp.bfloat16)
        return jnp.einsum(
            "hqk,khd->qhd", probs, value_rows, preferred_element_type=jnp.float32
        ).astype(jnp.bfloat16)

    head_out = lax.map(one_block, query_blocks)
    return head_out.reshape(full_length, heads_here * head_width)


def pass_per_role(
    gen_heads,
    gen_resid,
    gen_out_w,
    gen_time_w,
    noise,
    steps,
    teacher_qkv,
    teacher_out,
    teacher_time,
    teacher_norm,
    critic_qkv,
    critic_out,
    critic_time,
    critic_norm,
):
    full_length = gen_heads.shape[0]
    head_cols = gen_heads.shape[1]
    embed_width = gen_time_w.shape[0]
    gen_gate = jnp.dot(
        time_embed(steps[0], embed_width)[None, :], gen_time_w, preferred_element_type=jnp.float32
    )[0]
    block = gen_heads
    gen_proj = lax.psum_scatter(
        jnp.dot(block, gen_out_w, preferred_element_type=jnp.float32),
        "seq",
        scatter_dimension=0,
        tiled=True,
    )
    latent = (gen_resid.astype(jnp.float32) + gen_gate * gen_proj).astype(jnp.bfloat16)
    role_index = lax.axis_index("role")
    level = steps[1 + role_index // 2]
    use_critic = role_index % 2 == 1
    w_qkv = jnp.where(use_critic, critic_qkv, teacher_qkv)
    w_out = jnp.where(use_critic, critic_out, teacher_out)
    w_time = jnp.where(use_critic, critic_time, teacher_time)
    w_norm = jnp.where(use_critic, critic_norm, teacher_norm)
    noise_level = level.astype(jnp.float32) / 1000.0
    noisy = (
        (1.0 - noise_level) * latent.astype(jnp.float32) + noise_level * noise.astype(jnp.float32)
    ).astype(jnp.bfloat16)
    modulation = jnp.einsum(
        "f,fkd->kd", time_embed(level, embed_width), w_time, preferred_element_type=jnp.float32
    )
    shift_vec = modulation[0]
    scale_vec = modulation[1]
    gate_vec = modulation[2]
    gathered = lax.all_gather(noisy, "seq", axis=0, tiled=True)
    partial_squares = jnp.sum(jnp.square(gathered.astype(jnp.float32)), axis=1)
    scaled = (gathered.astype(jnp.float32) * (1.0 + scale_vec)).astype(jnp.bfloat16)
    flat_w = w_qkv.reshape(w_qkv.shape[0], 3 * head_cols)
    projected = jnp.dot(scaled, flat_w, preferred_element_type=jnp.float32)
    shift_proj = jnp.dot(
        shift_vec.astype(jnp.bfloat16)[None, :], flat_w, preferred_element_type=jnp.float32
    )[0]
    projected, squares, shift_proj = lax.psum((projected, partial_squares, shift_proj), "mp")
    mixed = projected * lax.rsqrt(squares / D + 1e-06)[:, None] + shift_proj
    heads_here = head_cols // HEAD_DIM
    mixed = mixed.reshape(full_length, 3, heads_here, HEAD_DIM)
    gains = w_norm.reshape(2, heads_here, HEAD_DIM)
    query_norm = head_norm(mixed[:, 0], gains[0])
    key_norm = head_norm(mixed[:, 1], gains[1])
    value_rows = mixed[:, 2].astype(jnp.bfloat16)
    head_out = attend(query_norm, key_norm, value_rows)
    weight_sign = jnp.where(use_critic, 0.5, -0.5)
    block = head_out
    summed_rows = lax.psum_scatter(
        weight_sign * (gate_vec * jnp.dot(block, w_out, preferred_element_type=jnp.float32)),
        ("role", "seq"),
        scatter_dimension=0,
        tiled=True,
    )
    grad_rows = lax.all_gather(
        (gen_gate * summed_rows).astype(jnp.bfloat16), ("role", "seq"), axis=0, tiled=True
    )
    weight_grad = lax.dot_general(
        gen_heads, grad_rows, (((0,), (0,)), ((), ())), preferred_element_type=jnp.float32
    )
    return (latent, weight_grad.astype(jnp.bfloat16))

MIB = 1024 * 1024
EXTRA_ROWS = 16


def vmem_spec():
    return pl.BlockSpec(memory_space=pltpu.VMEM)


def smem_spec():
    return pl.BlockSpec(memory_space=pltpu.SMEM)


def params(mebibytes):
    return pltpu.CompilerParams(vmem_limit_bytes=mebibytes * MIB)


def dot32(a, b):
    return jnp.dot(a, b, preferred_element_type=jnp.float32)


def at_block(index, size):
    return pl.ds(pl.multiple_of(index * size, size), size)


def any_spec():
    return pl.BlockSpec(memory_space=pl.ANY)


def hbm_spec():
    return pl.BlockSpec(memory_space=pltpu.HBM)


def cost(flops, moved):
    return pl.CostEstimate(flops=flops, bytes_accessed=moved, transcendentals=0)


def pack_kernel(seq, product, gate, resid, noise, full, sent):
    length = full.shape[0]
    own = resid.shape[0]
    full[...] = product[...] * gate[0:1, :]
    at = at_block(seq[0], own)
    full[at, :] = full[at, :] + resid[...].astype(jnp.float32)
    sent[pl.ds(0, length), :] = full[...].astype(jnp.bfloat16)
    sent[pl.ds(length, own), :] = noise[...]


def pack_part(seq, product, gate, resid, noise):
    length, width = product.shape
    own = resid.shape[0]
    return pl.pallas_call(
        pack_kernel,
        in_specs=[smem_spec()] + [vmem_spec()] * 4,
        out_specs=[vmem_spec()] * 2,
        out_shape=[
            jax.ShapeDtypeStruct((length, width), jnp.float32),
            jax.ShapeDtypeStruct((length + own, width), jnp.bfloat16),
        ],
        compiler_params=params(8),
        name="pack_part",
    )(seq, product, gate, resid, noise)


def load_kernel(start, embed, time_a, time_b, planes_a, planes_b, weight_a, weight_b, mods, sems):
    cols = pl.ds(pl.multiple_of(start[0], weight_a.shape[2]), weight_a.shape[2])
    copies = []
    for index, (planes, weight) in enumerate(((planes_a, weight_a), (planes_b, weight_b))):
        for part in range(3):
            copies.append(
                pltpu.make_async_copy(planes.at[part, :, cols], weight.at[part], sems.at[3 * index + part])
            )
    for copy in copies:
        copy.start()
    for k in range(3):
        mods[0, k] = dot32(embed[...], time_a[k])
        mods[1, k] = dot32(embed[...], time_b[k])
    for copy in copies:
        copy.wait()


def load_part(start, embed, time_a, time_b, planes_a, planes_b, cols):
    parts, depth, _ = planes_a.shape
    width = time_a.shape[2]
    return pl.pallas_call(
        load_kernel,
        in_specs=[smem_spec()] + [vmem_spec()] * 3 + [hbm_spec()] * 2,
        out_specs=[vmem_spec()] * 3,
        out_shape=[jax.ShapeDtypeStruct((parts, depth, cols), jnp.bfloat16)] * 2
        + [jax.ShapeDtypeStruct((2, parts, 8, width), jnp.float32)],
        scratch_shapes=[pltpu.SemaphoreType.DMA((2 * parts,))],
        compiler_params=params(40),
        name="load_part",
    )(start, embed, time_a, time_b, planes_a, planes_b)


def join_kernel(full, arrived, joined):
    length = full.shape[0]
    own = arrived.shape[0] - length
    top = full[...] + arrived[pl.ds(0, length), :].astype(jnp.float32)
    joined[pl.ds(0, length), :] = top.astype(jnp.bfloat16)
    joined[pl.ds(length, own), :] = arrived[pl.ds(length, own), :]


def join_part(full, arrived):
    return pl.pallas_call(
        join_kernel,
        in_specs=[vmem_spec(), vmem_spec()],
        out_specs=vmem_spec(),
        out_shape=jax.ShapeDtypeStruct(arrived.shape, jnp.bfloat16),
        compiler_params=params(8),
        name="join_part",
    )(full, arrived)


def project(index, stride, mine, noisy, squares, mods, weight, kept, sent, result):
    tokens = noisy.shape[0]
    length = tokens // 2
    unit = squares.shape[1] // 2
    groups = weight.shape[2] // unit
    scale = mods[index, 1]
    shift = mods[index, 0]
    spread = noisy.astype(jnp.float32)
    top = spread[:length] * (1.0 + scale[1:2])
    low = spread[length:] * (1.0 + scale[2:3])
    extra = jnp.concatenate([shift[1:3], jnp.zeros((EXTRA_ROWS - 2, shift.shape[1]), jnp.float32)], axis=0)
    rows = jnp.concatenate([top, low, extra], axis=0).astype(jnp.bfloat16)
    row_id = lax.broadcasted_iota(jnp.int32, (EXTRA_ROWS, unit), 0)
    for part in range(3):
        result[...] = dot32(rows, weight[part])
        cols = pl.ds(part * unit, unit)
        for slot in range(groups):
            at = at_block(jnp.bitwise_xor(mine, slot), unit)
            goal = sent if slot & stride else kept
            place = slot // 2 if stride == 1 else slot % 2
            goal[place, pl.ds(0, tokens), cols] = result[pl.ds(0, tokens), at].astype(jnp.bfloat16)
            tail = jnp.where(row_id < 2, result[pl.ds(tokens, EXTRA_ROWS), at], 0.0)
            for level in range(2):
                tail = jnp.where(row_id == 2 + level, squares[0:1, level * length : (level + 1) * length], tail)
            goal[place, pl.ds(tokens, EXTRA_ROWS), cols] = tail.astype(jnp.bfloat16)


def far_kernel(seq, core, mine, levels, joined, swapped, noise, mods, weight, latent, noisy, squares, *refs):
    kept, sent, values, noises, result = refs
    length, cols = values.shape[0], joined.shape[1]
    own = latent.shape[0]
    tokens = 2 * length
    left, right = at_block(core[0], cols), at_block(1 - core[0], cols)
    values[:, left] = joined[pl.ds(0, length), :]
    values[:, right] = swapped[pl.ds(0, length), :]
    latent[...] = values[at_block(seq[0], own), :]
    noises[at_block(seq[0], own), :] = noise[...]
    theirs = at_block(1 - seq[0], own)
    noises[theirs, left] = joined[pl.ds(length, own), :]
    noises[theirs, right] = swapped[pl.ds(length, own), :]
    spread = values[...].astype(jnp.float32)
    noise_rows = noises[...].astype(jnp.float32)
    mixed = jnp.concatenate(
        [(1.0 - levels[level]) * spread + levels[level] * noise_rows for level in range(2)], axis=0
    ).astype(jnp.bfloat16)
    wide = mixed.astype(jnp.float32)
    sums = jnp.sum(wide * wide, axis=1, keepdims=True)
    sums = jnp.broadcast_to(sums, (tokens, length)).T[0:8]
    noisy[...] = mixed
    squares[...] = sums
    project(1, 2, mine[0], mixed, sums, mods, weight, kept, sent, result)


def near_kernel(mine, noisy, squares, mods, weight, kept, sent, result):
    project(0, 1, mine[0], noisy[...], squares[...], mods, weight, kept, sent, result)


def chunk_shapes(tokens, cols):
    unit = tokens // 2
    return [jax.ShapeDtypeStruct((cols // unit // 2, tokens + EXTRA_ROWS, 3 * unit), jnp.bfloat16)] * 2


def far_part(seq, core, mine, levels, joined, swapped, noise, mods, weight):
    own, width = noise.shape
    length = joined.shape[0] - own
    tokens = 2 * length
    cols = weight.shape[2]
    return pl.pallas_call(
        far_kernel,
        in_specs=[smem_spec()] * 4 + [vmem_spec()] * 5,
        out_specs=[vmem_spec()] * 5,
        out_shape=[
            jax.ShapeDtypeStruct((own, width), jnp.bfloat16),
            jax.ShapeDtypeStruct((tokens, width), jnp.bfloat16),
            jax.ShapeDtypeStruct((8, tokens), jnp.float32),
        ]
        + chunk_shapes(tokens, cols),
        scratch_shapes=[
            pltpu.VMEM((length, width), jnp.bfloat16),
            pltpu.VMEM((length, width), jnp.bfloat16),
            pltpu.VMEM((tokens + EXTRA_ROWS, cols), jnp.float32),
        ],
        compiler_params=params(20),
        name="far_part",
    )(seq, core, mine, levels, joined, swapped, noise, mods, weight)


def near_part(mine, noisy, squares, mods, weight):
    tokens = noisy.shape[0]
    cols = weight.shape[2]
    return pl.pallas_call(
        near_kernel,
        in_specs=[smem_spec()] + [vmem_spec()] * 4,
        out_specs=[vmem_spec()] * 2,
        out_shape=chunk_shapes(tokens, cols),
        scratch_shapes=[pltpu.VMEM((tokens + EXTRA_ROWS, cols), jnp.float32)],
        compiler_params=params(20),
        name="near_part",
    )(mine, noisy, squares, mods, weight)


def attend_kernel(width, kept_a, other_a, kept_b, other_b, gains, out):
    _, _, length, unit = out.shape
    tokens = 2 * length
    for index, (kept, other) in enumerate(((kept_a, other_a), (kept_b, other_b))):
        mixed = kept[...] + other[...].astype(jnp.float32)
        extra = mixed[tokens:]
        for level in range(2):
            rows_at = slice(level * length, (level + 1) * length)
            squares = jnp.broadcast_to(extra[2 + level : 3 + level, :unit], (unit, unit)).T
            factor = lax.rsqrt(squares * (1.0 / width) + 1e-06)

            def pick(part):
                cols = slice(part * unit, (part + 1) * unit)
                return mixed[rows_at, cols] * factor + extra[level : level + 1, cols]

            def normed(part):
                rows = pick(part)
                mean = jnp.mean(rows * rows, axis=1, keepdims=True)
                return (rows * lax.rsqrt(mean + 1e-06) * gains[index, part : part + 1, :]).astype(jnp.bfloat16)

            query, key = normed(0), normed(1)
            value = pick(2).astype(jnp.bfloat16)
            logits = lax.dot_general(
                query, key, (((1,), (1,)), ((), ())), preferred_element_type=jnp.float32
            ) * (1.0 / math.sqrt(unit))
            expanded = jnp.exp(logits)
            probs = (expanded / jnp.sum(expanded, axis=1, keepdims=True)).astype(jnp.bfloat16)
            out[index, level] = dot32(probs, value).astype(jnp.bfloat16)


def attend_part(kept_a, other_a, kept_b, other_b, gains, width):
    unit = kept_a.shape[1] // 3
    length = (kept_a.shape[0] - EXTRA_ROWS) // 2
    return pl.pallas_call(
        lambda *refs: attend_kernel(width, *refs),
        in_specs=[vmem_spec()] * 5,
        out_specs=vmem_spec(),
        out_shape=jax.ShapeDtypeStruct((2, 2, length, unit), jnp.bfloat16),
        compiler_params=params(8),
        name="attend_part",
    )(kept_a, other_a, kept_b, other_b, gains)


def out_kernel(core, mine, *refs):
    heads = refs[0:4]
    weight_a, weight_b, mods, kept, sent, rows, total = refs[4:]
    _, _, length, unit = heads[0].shape
    for index, weight in enumerate((weight_a, weight_b)):
        for slot, head in enumerate(heads):
            at = at_block(jnp.bitwise_xor(mine[0], slot), unit)
            for level in range(2):
                rows[pl.ds(level * length, length), at] = head[index, level]
        result = dot32(rows[...], weight[...])
        gates = mods[index, 2]
        signed = gates[1:2] * result[:length] + gates[2:3] * result[length:]
        if index == 0:
            total[...] = -0.5 * signed
        else:
            total[...] = total[...] + 0.5 * signed
    cols = kept.shape[1]
    kept[...] = total[:, at_block(core[0], cols)]
    sent[...] = total[:, at_block(1 - core[0], cols)].astype(jnp.bfloat16)


def out_part(core, mine, heads, weight_a, weight_b, mods):
    length = heads[0].shape[2]
    depth, width = weight_a.shape
    return pl.pallas_call(
        out_kernel,
        in_specs=[smem_spec()] * 2 + [vmem_spec()] * 7,
        out_specs=[vmem_spec()] * 2,
        out_shape=[
            jax.ShapeDtypeStruct((length, width // 2), jnp.float32),
            jax.ShapeDtypeStruct((length, width // 2), jnp.bfloat16),
        ],
        scratch_shapes=[
            pltpu.VMEM((2 * length, depth), jnp.bfloat16),
            pltpu.VMEM((length, width), jnp.float32),
        ],
        compiler_params=params(16),
        name="out_part",
    )(core, mine, *heads, weight_a, weight_b, mods)


def grad_kernel(half, heads_t, rows, *refs):
    refs[-1][...] = dot32(heads_t[...], rows[...]).astype(jnp.bfloat16)


def grad_part(half, heads_t, rows, before, steps):
    depth, length = heads_t.shape
    cols = rows.shape[1]
    tile = depth // steps
    rest = [] if before is None else [before]
    grid_spec = pltpu.PrefetchScalarGridSpec(
        num_scalar_prefetch=1,
        grid=(steps,),
        in_specs=[
            pl.BlockSpec((tile, length), lambda n, w: (n, 0)),
            pl.BlockSpec((length, cols), lambda n, w: (0, 0)),
        ]
        + [any_spec()] * len(rest),
        out_specs=pl.BlockSpec((tile, cols), lambda n, w: (n, w[0])),
    )
    return pl.pallas_call(
        grad_kernel,
        grid_spec=grid_spec,
        out_shape=jax.ShapeDtypeStruct((depth, 2 * cols), jnp.bfloat16),
        input_output_aliases={3: 0} if rest else {},
        compiler_params=params(16),
        name="grad_part",
    )(half, heads_t, rows, *rest)


def exchange(array, axis, bit):
    return lax.ppermute(array, axis, [(i, i ^ bit) for i in range(lax.axis_size(axis))])


def take(array, begin, size, axis):
    return lax.dynamic_slice_in_dim(array, begin, size, axis=axis, allow_negative_indices=False)


def both(mine, theirs):
    return mine.astype(jnp.float32) + theirs.astype(jnp.float32)


def heads_per_role(
    gen_heads,
    gen_resid,
    gen_out_w,
    gen_time_w,
    noise,
    steps,
    teacher_qkv,
    teacher_out,
    teacher_time,
    teacher_norm,
    critic_qkv,
    critic_out,
    critic_time,
    critic_norm,
):
    length = gen_heads.shape[0]
    roles, groups = lax.axis_size("role"), lax.axis_size("mp")
    role, seq, mp = lax.axis_index("role"), lax.axis_index("seq"), lax.axis_index("mp")
    part_cols = gen_heads.shape[1] // roles
    freq = gen_time_w.shape[0]
    core = role % 2
    half_cols = gen_resid.shape[1] // 2
    unit = part_cols // groups

    embed = jax.vmap(lambda t: time_embed(t, freq))(steps)
    embed = jnp.concatenate([embed, jnp.zeros((5, freq), jnp.bfloat16)], axis=0)
    levels = steps[1:3].astype(jnp.float32) / 1000.0
    start = role * part_cols
    scalars = [seq, mp, core, 1 - core, core * half_cols, start, start + mp * unit]
    embed, *scalars = lax.optimization_barrier((embed, *scalars))
    seq_at, mine, core, other_core, start_at = [v.astype(jnp.int32).reshape(1) for v in scalars[:4] + scalars[5:6]]
    begin, start, gain_at = scalars[4:]
    weight, time_half, resid_half, noise_half = [
        take(w, begin, half_cols, 1) for w in (gen_out_w, gen_time_w, gen_resid, noise)
    ]
    gate = dot32(embed, time_half)
    full, sent = pack_part(seq_at, dot32(gen_heads, weight), gate, resid_half, noise_half)
    arrived = exchange(sent, "seq", 1)
    later, embed, _ = lax.optimization_barrier((start_at, embed, full))
    planes = [w.transpose(1, 0, 2) for w in (teacher_qkv, critic_qkv, teacher_time, critic_time)]
    weight_a, weight_b, mods = load_part(later, embed, planes[2], planes[3], planes[0], planes[1], part_cols)
    arrived, mods = lax.optimization_barrier((arrived, mods))
    joined = join_part(full, arrived)
    swapped = exchange(joined, "role", 1)

    latent, noisy, squares, kept_b, sent_b = far_part(
        seq_at, core, mine, levels, joined, swapped, noise, mods, weight_b
    )
    arrived_b = exchange(sent_b, "mp", 2)
    kept_a, sent_a = near_part(mine, noisy, squares, mods, weight_a)
    arrived_a = exchange(sent_a, "mp", 1)
    out_a, out_b = [take(w, start, part_cols, 0) for w in (teacher_out, critic_out)]
    gains = jnp.stack([teacher_norm, critic_norm])
    gains = take(gains, gain_at, unit, 2)
    arrived_b, arrived_a, out_a, out_b, gains = lax.optimization_barrier((arrived_b, arrived_a, out_a, out_b, gains))
    sum_a, sum_b = both(kept_a, arrived_a), both(kept_b, arrived_b)
    last_a = exchange(sum_a[1].astype(jnp.bfloat16), "mp", 2)
    last_b = exchange(sum_b[1].astype(jnp.bfloat16), "mp", 1)
    head = attend_part(sum_a[0], last_a, sum_b[0], last_b, gains, D)
    near, far = exchange(head, "mp", 1), exchange(head, "mp", 2)
    gathered = head, near, far, exchange(far, "mp", 1)

    kept, sent = out_part(core, mine, gathered, out_a, out_b, mods)
    total = both(kept, exchange(sent, "role", 1)).astype(jnp.bfloat16)
    along_x = exchange(total, "seq", 1)
    along_y = exchange(total, "role", 2)
    across = lax.ppermute(
        total, ("role", "seq"), [(i, i ^ (2 * lax.axis_size("seq") + 1)) for i in range(roles * lax.axis_size("seq"))]
    )
    total = both(total, along_x) + both(along_y, across)
    rows = (gate[0:1] * total).astype(jnp.bfloat16)
    heads_t = gen_heads.T
    theirs = exchange(rows, "role", 1)
    weight_grad = grad_part(core, heads_t, rows, None, 2)
    weight_grad = grad_part(other_core, heads_t, theirs, weight_grad, 2)
    return latent, weight_grad


def solution(mesh):
    in_specs = (
        P(None, "seq"),
        P("seq", "mp"),
        P("seq", "mp"),
        P(None, "mp"),
        P("seq", "mp"),
        P(),
        P("mp", None, "seq"),
        P("seq", "mp"),
        P(None, None, "mp"),
        P(None, "seq"),
        P("mp", None, "seq"),
        P("seq", "mp"),
        P(None, None, "mp"),
        P(None, "seq"),
    )
    out_specs = (P("seq", "mp"), P("seq", "mp"))
    roles, seqs, groups = mesh.shape["role"], mesh.shape["seq"], mesh.shape["mp"]

    def on_device(*arrays):
        heads_here = arrays[0].shape[1] // HEAD_DIM
        length = arrays[0].shape[0]
        fits = (roles, seqs, groups) == (4, 2, 4) and heads_here == roles * groups and length == HEAD_DIM
        return heads_per_role(*arrays) if fits else pass_per_role(*arrays)

    return jax.shard_map(
        on_device, mesh=mesh, in_specs=in_specs, out_specs=out_specs, check_vma=False
    )
```

```python
import math

import jax
import jax.numpy as jnp
from jax import lax
from jax.experimental import pallas as pl
from jax.experimental.pallas import tpu as pltpu
from jax.sharding import PartitionSpec as P

D = 5120
HEAD_DIM = 128


def time_embed(step_value, width):
    half_width = width // 2
    positions = jnp.arange(half_width, dtype=jnp.float32)
    frequencies = jnp.exp(positions * (-math.log(10000.0) / half_width))
    angles = step_value.astype(jnp.float32) * frequencies
    return jnp.concatenate([jnp.cos(angles), jnp.sin(angles)]).astype(jnp.bfloat16)


def head_norm(values, gains):
    factor = lax.rsqrt(jnp.mean(values * values, axis=-1, keepdims=True) + 1e-06)
    return (values * factor * gains).astype(jnp.bfloat16)


def attend(query_norm, key_norm, value_rows):
    full_length, heads_here, head_width = query_norm.shape
    query_blocks = query_norm.reshape(
        full_length // full_length, full_length, heads_here, head_width
    )

    def one_block(query_block):
        logits = jnp.einsum(
            "qhd,khd->hqk", query_block, key_norm, preferred_element_type=jnp.float32
        ) * (1.0 / math.sqrt(head_width))
        expanded = jnp.exp(logits)
        probs = (expanded / jnp.sum(expanded, axis=2, keepdims=True)).astype(jnp.bfloat16)
        return jnp.einsum(
            "hqk,khd->qhd", probs, value_rows, preferred_element_type=jnp.float32
        ).astype(jnp.bfloat16)

    head_out = lax.map(one_block, query_blocks)
    return head_out.reshape(full_length, heads_here * head_width)


def pass_per_role(
    gen_heads,
    gen_resid,
    gen_out_w,
    gen_time_w,
    noise,
    steps,
    teacher_qkv,
    teacher_out,
    teacher_time,
    teacher_norm,
    critic_qkv,
    critic_out,
    critic_time,
    critic_norm,
):
    full_length = gen_heads.shape[0]
    head_cols = gen_heads.shape[1]
    embed_width = gen_time_w.shape[0]
    gen_gate = jnp.dot(
        time_embed(steps[0], embed_width)[None, :], gen_time_w, preferred_element_type=jnp.float32
    )[0]
    block = gen_heads
    gen_proj = lax.psum_scatter(
        jnp.dot(block, gen_out_w, preferred_element_type=jnp.float32),
        "seq",
        scatter_dimension=0,
        tiled=True,
    )
    latent = (gen_resid.astype(jnp.float32) + gen_gate * gen_proj).astype(jnp.bfloat16)
    role_index = lax.axis_index("role")
    level = steps[1 + role_index // 2]
    use_critic = role_index % 2 == 1
    w_qkv = jnp.where(use_critic, critic_qkv, teacher_qkv)
    w_out = jnp.where(use_critic, critic_out, teacher_out)
    w_time = jnp.where(use_critic, critic_time, teacher_time)
    w_norm = jnp.where(use_critic, critic_norm, teacher_norm)
    noise_level = level.astype(jnp.float32) / 1000.0
    noisy = (
        (1.0 - noise_level) * latent.astype(jnp.float32) + noise_level * noise.astype(jnp.float32)
    ).astype(jnp.bfloat16)
    modulation = jnp.einsum(
        "f,fkd->kd", time_embed(level, embed_width), w_time, preferred_element_type=jnp.float32
    )
    shift_vec = modulation[0]
    scale_vec = modulation[1]
    gate_vec = modulation[2]
    gathered = lax.all_gather(noisy, "seq", axis=0, tiled=True)
    partial_squares = jnp.sum(jnp.square(gathered.astype(jnp.float32)), axis=1)
    scaled = (gathered.astype(jnp.float32) * (1.0 + scale_vec)).astype(jnp.bfloat16)
    flat_w = w_qkv.reshape(w_qkv.shape[0], 3 * head_cols)
    projected = jnp.dot(scaled, flat_w, preferred_element_type=jnp.float32)
    shift_proj = jnp.dot(
        shift_vec.astype(jnp.bfloat16)[None, :], flat_w, preferred_element_type=jnp.float32
    )[0]
    projected, squares, shift_proj = lax.psum((projected, partial_squares, shift_proj), "mp")
    mixed = projected * lax.rsqrt(squares / D + 1e-06)[:, None] + shift_proj
    heads_here = head_cols // HEAD_DIM
    mixed = mixed.reshape(full_length, 3, heads_here, HEAD_DIM)
    gains = w_norm.reshape(2, heads_here, HEAD_DIM)
    query_norm = head_norm(mixed[:, 0], gains[0])
    key_norm = head_norm(mixed[:, 1], gains[1])
    value_rows = mixed[:, 2].astype(jnp.bfloat16)
    head_out = attend(query_norm, key_norm, value_rows)
    weight_sign = jnp.where(use_critic, 0.5, -0.5)
    block = head_out
    summed_rows = lax.psum_scatter(
        weight_sign * (gate_vec * jnp.dot(block, w_out, preferred_element_type=jnp.float32)),
        ("role", "seq"),
        scatter_dimension=0,
        tiled=True,
    )
    grad_rows = lax.all_gather(
        (gen_gate * summed_rows).astype(jnp.bfloat16), ("role", "seq"), axis=0, tiled=True
    )
    weight_grad = lax.dot_general(
        gen_heads, grad_rows, (((0,), (0,)), ((), ())), preferred_element_type=jnp.float32
    )
    return (latent, weight_grad.astype(jnp.bfloat16))

MIB = 1024 * 1024
EXTRA_ROWS = 16


def vmem_spec():
    return pl.BlockSpec(memory_space=pltpu.VMEM)


def smem_spec():
    return pl.BlockSpec(memory_space=pltpu.SMEM)


def params(mebibytes):
    return pltpu.CompilerParams(vmem_limit_bytes=mebibytes * MIB)


def dot32(a, b):
    return jnp.dot(a, b, preferred_element_type=jnp.float32)


def at_block(index, size):
    return pl.ds(pl.multiple_of(index * size, size), size)


def any_spec():
    return pl.BlockSpec(memory_space=pl.ANY)


def hbm_spec():
    return pl.BlockSpec(memory_space=pltpu.HBM)


def cost(flops, moved):
    return pl.CostEstimate(flops=flops, bytes_accessed=moved, transcendentals=0)


def pack_kernel(seq, product, gate, resid, noise, full, sent):
    length = full.shape[0]
    own = resid.shape[0]
    full[...] = product[...] * gate[0:1, :]
    at = at_block(seq[0], own)
    full[at, :] = full[at, :] + resid[...].astype(jnp.float32)
    sent[pl.ds(0, length), :] = full[...].astype(jnp.bfloat16)
    sent[pl.ds(length, own), :] = noise[...]


def pack_part(seq, product, gate, resid, noise):
    length, width = product.shape
    own = resid.shape[0]
    return pl.pallas_call(
        pack_kernel,
        in_specs=[smem_spec()] + [vmem_spec()] * 4,
        out_specs=[vmem_spec()] * 2,
        out_shape=[
            jax.ShapeDtypeStruct((length, width), jnp.float32),
            jax.ShapeDtypeStruct((length + own, width), jnp.bfloat16),
        ],
        compiler_params=params(8),
        name="pack_part",
    )(seq, product, gate, resid, noise)


def load_kernel(start, embed, time_a, time_b, planes_a, planes_b, weight_a, weight_b, mods, sems):
    cols = pl.ds(pl.multiple_of(start[0], weight_a.shape[2]), weight_a.shape[2])
    copies = []
    for index, (planes, weight) in enumerate(((planes_a, weight_a), (planes_b, weight_b))):
        for part in range(3):
            copies.append(
                pltpu.make_async_copy(planes.at[part, :, cols], weight.at[part], sems.at[3 * index + part])
            )
    for copy in copies:
        copy.start()
    for k in range(3):
        mods[0, k] = dot32(embed[...], time_a[k])
        mods[1, k] = dot32(embed[...], time_b[k])
    for copy in copies:
        copy.wait()


def load_part(start, embed, time_a, time_b, planes_a, planes_b, cols):
    parts, depth, _ = planes_a.shape
    width = time_a.shape[2]
    return pl.pallas_call(
        load_kernel,
        in_specs=[smem_spec()] + [vmem_spec()] * 3 + [hbm_spec()] * 2,
        out_specs=[vmem_spec()] * 3,
        out_shape=[jax.ShapeDtypeStruct((parts, depth, cols), jnp.bfloat16)] * 2
        + [jax.ShapeDtypeStruct((2, parts, 8, width), jnp.float32)],
        scratch_shapes=[pltpu.SemaphoreType.DMA((2 * parts,))],
        compiler_params=params(40),
        name="load_part",
    )(start, embed, time_a, time_b, planes_a, planes_b)


def join_kernel(full, arrived, joined):
    length = full.shape[0]
    own = arrived.shape[0] - length
    top = full[...] + arrived[pl.ds(0, length), :].astype(jnp.float32)
    joined[pl.ds(0, length), :] = top.astype(jnp.bfloat16)
    joined[pl.ds(length, own), :] = arrived[pl.ds(length, own), :]


def join_part(full, arrived):
    return pl.pallas_call(
        join_kernel,
        in_specs=[vmem_spec(), vmem_spec()],
        out_specs=vmem_spec(),
        out_shape=jax.ShapeDtypeStruct(arrived.shape, jnp.bfloat16),
        compiler_params=params(8),
        name="join_part",
    )(full, arrived)


def project(index, stride, mine, noisy, squares, mods, weight, kept, sent, result):
    tokens = noisy.shape[0]
    length = tokens // 2
    unit = squares.shape[1] // 2
    groups = weight.shape[2] // unit
    scale = mods[index, 1]
    shift = mods[index, 0]
    spread = noisy.astype(jnp.float32)
    top = spread[:length] * (1.0 + scale[1:2])
    low = spread[length:] * (1.0 + scale[2:3])
    extra = jnp.concatenate([shift[1:3], jnp.zeros((EXTRA_ROWS - 2, shift.shape[1]), jnp.float32)], axis=0)
    rows = jnp.concatenate([top, low, extra], axis=0).astype(jnp.bfloat16)
    row_id = lax.broadcasted_iota(jnp.int32, (EXTRA_ROWS, unit), 0)
    for part in range(3):
        result[...] = dot32(rows, weight[part])
        cols = pl.ds(part * unit, unit)
        for half, goal in enumerate((kept, sent)):
            tail = jnp.zeros((EXTRA_ROWS, unit), jnp.float32)
            for place in range(groups // 2):
                slot = 2 * place + half if stride == 1 else 2 * half + place
                at = at_block(jnp.bitwise_xor(mine, slot), unit)
                goal[pl.ds(place * tokens, tokens), cols] = result[pl.ds(0, tokens), at].astype(jnp.bfloat16)
                for level in range(2):
                    row = 4 * place + level
                    tail = jnp.where(row_id == row, result[pl.ds(tokens + level, 1), at], tail)
                    sums = squares[0:1, level * length : (level + 1) * length]
                    tail = jnp.where(row_id == row + 2, sums, tail)
            goal[pl.ds(2 * tokens, EXTRA_ROWS), cols] = tail.astype(jnp.bfloat16)


def qkv_kernel(seq, core, mine, levels, joined, swapped, noise, mods, weight_a, weight_b, latent, *refs):
    chunks, (values, noises, result) = refs[:4], refs[4:]
    length, cols = values.shape[0], joined.shape[1]
    own = latent.shape[0]
    tokens = 2 * length
    left, right = at_block(core[0], cols), at_block(1 - core[0], cols)
    values[:, left] = joined[pl.ds(0, length), :]
    values[:, right] = swapped[pl.ds(0, length), :]
    latent[...] = values[at_block(seq[0], own), :]
    noises[at_block(seq[0], own), :] = noise[...]
    theirs = at_block(1 - seq[0], own)
    noises[theirs, left] = joined[pl.ds(length, own), :]
    noises[theirs, right] = swapped[pl.ds(length, own), :]
    spread = values[...].astype(jnp.float32)
    noise_rows = noises[...].astype(jnp.float32)
    mixed = jnp.concatenate(
        [(1.0 - levels[level]) * spread + levels[level] * noise_rows for level in range(2)], axis=0
    ).astype(jnp.bfloat16)
    wide = mixed.astype(jnp.float32)
    sums = jnp.sum(wide * wide, axis=1, keepdims=True)
    sums = jnp.broadcast_to(sums, (tokens, length)).T[0:8]
    for index, weight in enumerate((weight_a, weight_b)):
        project(index, index + 1, mine[0], mixed, sums, mods, weight, *chunks[2 * index : 2 * index + 2], result)


def qkv_part(seq, core, mine, levels, joined, swapped, noise, mods, weight_a, weight_b):
    own, width = noise.shape
    length = joined.shape[0] - own
    tokens = 2 * length
    cols = weight_a.shape[2]
    return pl.pallas_call(
        qkv_kernel,
        in_specs=[smem_spec()] * 4 + [vmem_spec()] * 6,
        out_specs=[vmem_spec()] * 5,
        out_shape=[jax.ShapeDtypeStruct((own, width), jnp.bfloat16)]
        + [jax.ShapeDtypeStruct((cols // length // 2 * tokens + EXTRA_ROWS, 3 * length), jnp.bfloat16)] * 4,
        scratch_shapes=[
            pltpu.VMEM((length, width), jnp.bfloat16),
            pltpu.VMEM((length, width), jnp.bfloat16),
            pltpu.VMEM((tokens + EXTRA_ROWS, cols), jnp.float32),
        ],
        compiler_params=params(20),
        name="qkv_part",
    )(seq, core, mine, levels, joined, swapped, noise, mods, weight_a, weight_b)


def attend_kernel(width, kept_a, other_a, kept_b, other_b, gains, out):
    _, _, length, unit = out.shape
    tokens = 2 * length
    for index, (kept, other) in enumerate(((kept_a, other_a), (kept_b, other_b))):
        mixed = kept[pl.ds(0, tokens), :] + other[pl.ds(0, tokens), :].astype(jnp.float32)
        theirs = other[pl.ds(tokens, EXTRA_ROWS), :].astype(jnp.float32)
        extra = kept[pl.ds(2 * tokens, EXTRA_ROWS), :][0:4] + theirs[4:8]
        for level in range(2):
            rows_at = slice(level * length, (level + 1) * length)
            squares = jnp.broadcast_to(extra[2 + level : 3 + level, :unit], (unit, unit)).T
            factor = lax.rsqrt(squares * (1.0 / width) + 1e-06)

            def pick(part):
                cols = slice(part * unit, (part + 1) * unit)
                return mixed[rows_at, cols] * factor + extra[level : level + 1, cols]

            def normed(part):
                rows = pick(part)
                mean = jnp.mean(rows * rows, axis=1, keepdims=True)
                return (rows * lax.rsqrt(mean + 1e-06) * gains[index, part : part + 1, :]).astype(jnp.bfloat16)

            query, key = normed(0), normed(1)
            value = pick(2).astype(jnp.bfloat16)
            logits = lax.dot_general(
                query, key, (((1,), (1,)), ((), ())), preferred_element_type=jnp.float32
            ) * (1.0 / math.sqrt(unit))
            expanded = jnp.exp(logits)
            probs = (expanded / jnp.sum(expanded, axis=1, keepdims=True)).astype(jnp.bfloat16)
            out[index, level] = dot32(probs, value).astype(jnp.bfloat16)


def attend_part(kept_a, other_a, kept_b, other_b, gains, width):
    unit = kept_a.shape[1] // 3
    length = (kept_a.shape[0] - EXTRA_ROWS) // 4
    return pl.pallas_call(
        lambda *refs: attend_kernel(width, *refs),
        in_specs=[vmem_spec()] * 5,
        out_specs=vmem_spec(),
        out_shape=jax.ShapeDtypeStruct((2, 2, length, unit), jnp.bfloat16),
        compiler_params=params(8),
        name="attend_part",
    )(kept_a, other_a, kept_b, other_b, gains)


def out_kernel(core, mine, *refs):
    heads = refs[0:4]
    weight_a, weight_b, mods, kept, sent, rows, total = refs[4:]
    _, _, length, unit = heads[0].shape
    for index, weight in enumerate((weight_a, weight_b)):
        for slot, head in enumerate(heads):
            at = at_block(jnp.bitwise_xor(mine[0], slot), unit)
            for level in range(2):
                rows[pl.ds(level * length, length), at] = head[index, level]
        result = dot32(rows[...], weight[...])
        gates = mods[index, 2]
        signed = gates[1:2] * result[:length] + gates[2:3] * result[length:]
        if index == 0:
            total[...] = -0.5 * signed
        else:
            total[...] = total[...] + 0.5 * signed
    cols = kept.shape[1]
    kept[...] = total[:, at_block(core[0], cols)]
    sent[...] = total[:, at_block(1 - core[0], cols)].astype(jnp.bfloat16)


def out_part(core, mine, heads, weight_a, weight_b, mods):
    length = heads[0].shape[2]
    depth, width = weight_a.shape
    return pl.pallas_call(
        out_kernel,
        in_specs=[smem_spec()] * 2 + [vmem_spec()] * 7,
        out_specs=[vmem_spec()] * 2,
        out_shape=[
            jax.ShapeDtypeStruct((length, width // 2), jnp.float32),
            jax.ShapeDtypeStruct((length, width // 2), jnp.bfloat16),
        ],
        scratch_shapes=[
            pltpu.VMEM((2 * length, depth), jnp.bfloat16),
            pltpu.VMEM((length, width), jnp.float32),
        ],
        compiler_params=params(16),
        name="out_part",
    )(core, mine, *heads, weight_a, weight_b, mods)


def grad_kernel(half, heads_t, rows, *refs):
    refs[-1][...] = dot32(heads_t[...], rows[...]).astype(jnp.bfloat16)


def grad_part(half, heads_t, rows, before, steps):
    depth, length = heads_t.shape
    cols = rows.shape[1]
    tile = depth // steps
    rest = [] if before is None else [before]
    grid_spec = pltpu.PrefetchScalarGridSpec(
        num_scalar_prefetch=1,
        grid=(steps,),
        in_specs=[
            pl.BlockSpec((tile, length), lambda n, w: (n, 0)),
            pl.BlockSpec((length, cols), lambda n, w: (0, 0)),
        ]
        + [any_spec()] * len(rest),
        out_specs=pl.BlockSpec((tile, cols), lambda n, w: (n, w[0])),
    )
    return pl.pallas_call(
        grad_kernel,
        grid_spec=grid_spec,
        out_shape=jax.ShapeDtypeStruct((depth, 2 * cols), jnp.bfloat16),
        input_output_aliases={3: 0} if rest else {},
        compiler_params=params(16),
        name="grad_part",
    )(half, heads_t, rows, *rest)


def exchange(array, axis, bit):
    return lax.ppermute(array, axis, [(i, i ^ bit) for i in range(lax.axis_size(axis))])


def take(array, begin, size, axis):
    return lax.dynamic_slice_in_dim(array, begin, size, axis=axis, allow_negative_indices=False)


def both(mine, theirs):
    return mine.astype(jnp.float32) + theirs.astype(jnp.float32)


def heads_per_role(
    gen_heads,
    gen_resid,
    gen_out_w,
    gen_time_w,
    noise,
    steps,
    teacher_qkv,
    teacher_out,
    teacher_time,
    teacher_norm,
    critic_qkv,
    critic_out,
    critic_time,
    critic_norm,
):
    length = gen_heads.shape[0]
    roles, groups = lax.axis_size("role"), lax.axis_size("mp")
    role, seq, mp = lax.axis_index("role"), lax.axis_index("seq"), lax.axis_index("mp")
    part_cols = gen_heads.shape[1] // roles
    freq = gen_time_w.shape[0]
    core = role % 2
    half_cols = gen_resid.shape[1] // 2
    unit = part_cols // groups

    embed = jax.vmap(lambda t: time_embed(t, freq))(steps)
    embed = jnp.concatenate([embed, jnp.zeros((5, freq), jnp.bfloat16)], axis=0)
    levels = steps[1:3].astype(jnp.float32) / 1000.0
    start = role * part_cols
    scalars = [seq, mp, core, 1 - core, core * half_cols, start, start + mp * unit]
    embed, *scalars = lax.optimization_barrier((embed, *scalars))
    seq_at, mine, core, other_core, start_at = [v.astype(jnp.int32).reshape(1) for v in scalars[:4] + scalars[5:6]]
    begin, start, gain_at = scalars[4:]
    weight, time_half, resid_half, noise_half = [
        take(w, begin, half_cols, 1) for w in (gen_out_w, gen_time_w, gen_resid, noise)
    ]
    gate = dot32(embed, time_half)
    full, sent = pack_part(seq_at, dot32(gen_heads, weight), gate, resid_half, noise_half)
    arrived = exchange(sent, "seq", 1)
    later, embed, _ = lax.optimization_barrier((start_at, embed, full))
    planes = [w.transpose(1, 0, 2) for w in (teacher_qkv, critic_qkv, teacher_time, critic_time)]
    weight_a, weight_b, mods = load_part(later, embed, planes[2], planes[3], planes[0], planes[1], part_cols)
    arrived, mods = lax.optimization_barrier((arrived, mods))
    joined = join_part(full, arrived)
    swapped = exchange(joined, "role", 1)

    latent, kept_a, sent_a, kept_b, sent_b = qkv_part(
        seq_at, core, mine, levels, joined, swapped, noise, mods, weight_a, weight_b
    )
    arrived_b = exchange(sent_b, "mp", 2)
    arrived_a = exchange(sent_a, "mp", 1)
    out_a, out_b = [take(w, start, part_cols, 0) for w in (teacher_out, critic_out)]
    gains = jnp.stack([teacher_norm, critic_norm])
    gains = take(gains, gain_at, unit, 2)
    arrived_b, arrived_a, out_a, out_b, gains = lax.optimization_barrier((arrived_b, arrived_a, out_a, out_b, gains))
    sum_a, sum_b = both(kept_a, arrived_a), both(kept_b, arrived_b)
    second = (sum_a.shape[0] - EXTRA_ROWS) // 2
    last_a = exchange(sum_a[second:].astype(jnp.bfloat16), "mp", 2)
    last_b = exchange(sum_b[second:].astype(jnp.bfloat16), "mp", 1)
    head = attend_part(sum_a, last_a, sum_b, last_b, gains, D)
    near, far = exchange(head, "mp", 1), exchange(head, "mp", 2)
    gathered = head, near, far, exchange(far, "mp", 1)

    kept, sent = out_part(core, mine, gathered, out_a, out_b, mods)
    total = both(kept, exchange(sent, "role", 1)).astype(jnp.bfloat16)
    along_x = exchange(total, "seq", 1)
    along_y = exchange(total, "role", 2)
    across = lax.ppermute(
        total, ("role", "seq"), [(i, i ^ (2 * lax.axis_size("seq") + 1)) for i in range(roles * lax.axis_size("seq"))]
    )
    total = both(total, along_x) + both(along_y, across)
    rows = (gate[0:1] * total).astype(jnp.bfloat16)
    heads_t = gen_heads.T
    theirs = exchange(rows, "role", 1)
    weight_grad = grad_part(core, heads_t, rows, None, 2)
    weight_grad = grad_part(other_core, heads_t, theirs, weight_grad, 2)
    return latent, weight_grad


def solution(mesh):
    in_specs = (
        P(None, "seq"),
        P("seq", "mp"),
        P("seq", "mp"),
        P(None, "mp"),
        P("seq", "mp"),
        P(),
        P("mp", None, "seq"),
        P("seq", "mp"),
        P(None, None, "mp"),
        P(None, "seq"),
        P("mp", None, "seq"),
        P("seq", "mp"),
        P(None, None, "mp"),
        P(None, "seq"),
    )
    out_specs = (P("seq", "mp"), P("seq", "mp"))
    roles, seqs, groups = mesh.shape["role"], mesh.shape["seq"], mesh.shape["mp"]

    def on_device(*arrays):
        heads_here = arrays[0].shape[1] // HEAD_DIM
        length = arrays[0].shape[0]
        fits = (roles, seqs, groups) == (4, 2, 4) and heads_here == roles * groups and length == HEAD_DIM
        return heads_per_role(*arrays) if fits else pass_per_role(*arrays)

    return jax.shard_map(
        on_device, mesh=mesh, in_specs=in_specs, out_specs=out_specs, check_vma=False
    )
```

```python
import math

import jax
import jax.numpy as jnp
from jax import lax
from jax.experimental import pallas as pl
from jax.experimental.pallas import tpu as pltpu
from jax.sharding import PartitionSpec as P

D = 5120
HEAD_DIM = 128


def time_embed(step_value, width):
    half_width = width // 2
    positions = jnp.arange(half_width, dtype=jnp.float32)
    frequencies = jnp.exp(positions * (-math.log(10000.0) / half_width))
    angles = step_value.astype(jnp.float32) * frequencies
    return jnp.concatenate([jnp.cos(angles), jnp.sin(angles)]).astype(jnp.bfloat16)


def head_norm(values, gains):
    factor = lax.rsqrt(jnp.mean(values * values, axis=-1, keepdims=True) + 1e-06)
    return (values * factor * gains).astype(jnp.bfloat16)


def attend(query_norm, key_norm, value_rows):
    full_length, heads_here, head_width = query_norm.shape
    query_blocks = query_norm.reshape(
        full_length // full_length, full_length, heads_here, head_width
    )

    def one_block(query_block):
        logits = jnp.einsum(
            "qhd,khd->hqk", query_block, key_norm, preferred_element_type=jnp.float32
        ) * (1.0 / math.sqrt(head_width))
        expanded = jnp.exp(logits)
        probs = (expanded / jnp.sum(expanded, axis=2, keepdims=True)).astype(jnp.bfloat16)
        return jnp.einsum(
            "hqk,khd->qhd", probs, value_rows, preferred_element_type=jnp.float32
        ).astype(jnp.bfloat16)

    head_out = lax.map(one_block, query_blocks)
    return head_out.reshape(full_length, heads_here * head_width)


def pass_per_role(
    gen_heads,
    gen_resid,
    gen_out_w,
    gen_time_w,
    noise,
    steps,
    teacher_qkv,
    teacher_out,
    teacher_time,
    teacher_norm,
    critic_qkv,
    critic_out,
    critic_time,
    critic_norm,
):
    full_length = gen_heads.shape[0]
    head_cols = gen_heads.shape[1]
    embed_width = gen_time_w.shape[0]
    gen_gate = jnp.dot(
        time_embed(steps[0], embed_width)[None, :], gen_time_w, preferred_element_type=jnp.float32
    )[0]
    block = gen_heads
    gen_proj = lax.psum_scatter(
        jnp.dot(block, gen_out_w, preferred_element_type=jnp.float32),
        "seq",
        scatter_dimension=0,
        tiled=True,
    )
    latent = (gen_resid.astype(jnp.float32) + gen_gate * gen_proj).astype(jnp.bfloat16)
    role_index = lax.axis_index("role")
    level = steps[1 + role_index // 2]
    use_critic = role_index % 2 == 1
    w_qkv = jnp.where(use_critic, critic_qkv, teacher_qkv)
    w_out = jnp.where(use_critic, critic_out, teacher_out)
    w_time = jnp.where(use_critic, critic_time, teacher_time)
    w_norm = jnp.where(use_critic, critic_norm, teacher_norm)
    noise_level = level.astype(jnp.float32) / 1000.0
    noisy = (
        (1.0 - noise_level) * latent.astype(jnp.float32) + noise_level * noise.astype(jnp.float32)
    ).astype(jnp.bfloat16)
    modulation = jnp.einsum(
        "f,fkd->kd", time_embed(level, embed_width), w_time, preferred_element_type=jnp.float32
    )
    shift_vec = modulation[0]
    scale_vec = modulation[1]
    gate_vec = modulation[2]
    gathered = lax.all_gather(noisy, "seq", axis=0, tiled=True)
    partial_squares = jnp.sum(jnp.square(gathered.astype(jnp.float32)), axis=1)
    scaled = (gathered.astype(jnp.float32) * (1.0 + scale_vec)).astype(jnp.bfloat16)
    flat_w = w_qkv.reshape(w_qkv.shape[0], 3 * head_cols)
    projected = jnp.dot(scaled, flat_w, preferred_element_type=jnp.float32)
    shift_proj = jnp.dot(
        shift_vec.astype(jnp.bfloat16)[None, :], flat_w, preferred_element_type=jnp.float32
    )[0]
    projected, squares, shift_proj = lax.psum((projected, partial_squares, shift_proj), "mp")
    mixed = projected * lax.rsqrt(squares / D + 1e-06)[:, None] + shift_proj
    heads_here = head_cols // HEAD_DIM
    mixed = mixed.reshape(full_length, 3, heads_here, HEAD_DIM)
    gains = w_norm.reshape(2, heads_here, HEAD_DIM)
    query_norm = head_norm(mixed[:, 0], gains[0])
    key_norm = head_norm(mixed[:, 1], gains[1])
    value_rows = mixed[:, 2].astype(jnp.bfloat16)
    head_out = attend(query_norm, key_norm, value_rows)
    weight_sign = jnp.where(use_critic, 0.5, -0.5)
    block = head_out
    summed_rows = lax.psum_scatter(
        weight_sign * (gate_vec * jnp.dot(block, w_out, preferred_element_type=jnp.float32)),
        ("role", "seq"),
        scatter_dimension=0,
        tiled=True,
    )
    grad_rows = lax.all_gather(
        (gen_gate * summed_rows).astype(jnp.bfloat16), ("role", "seq"), axis=0, tiled=True
    )
    weight_grad = lax.dot_general(
        gen_heads, grad_rows, (((0,), (0,)), ((), ())), preferred_element_type=jnp.float32
    )
    return (latent, weight_grad.astype(jnp.bfloat16))

MIB = 1024 * 1024
EXTRA_ROWS = 16


def vmem_spec():
    return pl.BlockSpec(memory_space=pltpu.VMEM)


def smem_spec():
    return pl.BlockSpec(memory_space=pltpu.SMEM)


def params(mebibytes):
    return pltpu.CompilerParams(vmem_limit_bytes=mebibytes * MIB)


def dot32(a, b):
    return jnp.dot(a, b, preferred_element_type=jnp.float32)


def at_block(index, size):
    return pl.ds(pl.multiple_of(index * size, size), size)


def any_spec():
    return pl.BlockSpec(memory_space=pl.ANY)


def hbm_spec():
    return pl.BlockSpec(memory_space=pltpu.HBM)


def cost(flops, moved):
    return pl.CostEstimate(flops=flops, bytes_accessed=moved, transcendentals=0)


def pack_kernel(seq, product, gate, resid, noise, full, sent):
    length = full.shape[0]
    own = resid.shape[0]
    full[...] = product[...] * gate[0:1, :]
    at = at_block(seq[0], own)
    full[at, :] = full[at, :] + resid[...].astype(jnp.float32)
    sent[pl.ds(0, length), :] = full[...].astype(jnp.bfloat16)
    sent[pl.ds(length, own), :] = noise[...]


def pack_part(seq, product, gate, resid, noise):
    length, width = product.shape
    own = resid.shape[0]
    return pl.pallas_call(
        pack_kernel,
        in_specs=[smem_spec()] + [vmem_spec()] * 4,
        out_specs=[vmem_spec()] * 2,
        out_shape=[
            jax.ShapeDtypeStruct((length, width), jnp.float32),
            jax.ShapeDtypeStruct((length + own, width), jnp.bfloat16),
        ],
        compiler_params=params(8),
        name="pack_part",
    )(seq, product, gate, resid, noise)


def load_kernel(start, embed, time_a, time_b, planes_a, planes_b, weight_a, weight_b, mods, sems):
    cols = pl.ds(pl.multiple_of(start[0], weight_a.shape[2]), weight_a.shape[2])
    copies = []
    for index, (planes, weight) in enumerate(((planes_a, weight_a), (planes_b, weight_b))):
        for part in range(3):
            copies.append(
                pltpu.make_async_copy(planes.at[part, :, cols], weight.at[part], sems.at[3 * index + part])
            )
    for copy in copies:
        copy.start()
    for k in range(3):
        mods[0, k] = dot32(embed[...], time_a[k])
        mods[1, k] = dot32(embed[...], time_b[k])
    for copy in copies:
        copy.wait()


def load_part(start, embed, time_a, time_b, planes_a, planes_b, cols):
    parts, depth, _ = planes_a.shape
    width = time_a.shape[2]
    return pl.pallas_call(
        load_kernel,
        in_specs=[smem_spec()] + [vmem_spec()] * 3 + [hbm_spec()] * 2,
        out_specs=[vmem_spec()] * 3,
        out_shape=[jax.ShapeDtypeStruct((parts, depth, cols), jnp.bfloat16)] * 2
        + [jax.ShapeDtypeStruct((2, parts, 8, width), jnp.float32)],
        scratch_shapes=[pltpu.SemaphoreType.DMA((2 * parts,))],
        compiler_params=params(40),
        name="load_part",
    )(start, embed, time_a, time_b, planes_a, planes_b)


def join_kernel(full, arrived, joined):
    length = full.shape[0]
    own = arrived.shape[0] - length
    top = full[...] + arrived[pl.ds(0, length), :].astype(jnp.float32)
    joined[pl.ds(0, length), :] = top.astype(jnp.bfloat16)
    joined[pl.ds(length, own), :] = arrived[pl.ds(length, own), :]


def join_part(full, arrived):
    return pl.pallas_call(
        join_kernel,
        in_specs=[vmem_spec(), vmem_spec()],
        out_specs=vmem_spec(),
        out_shape=jax.ShapeDtypeStruct(arrived.shape, jnp.bfloat16),
        compiler_params=params(8),
        name="join_part",
    )(full, arrived)


def project(index, stride, mine, noisy, squares, mods, weight, kept, sent, result):
    tokens = noisy.shape[0]
    length = tokens // 2
    unit = squares.shape[1] // 2
    groups = weight.shape[2] // unit
    scale = mods[index, 1]
    shift = mods[index, 0]
    spread = noisy.astype(jnp.float32)
    top = spread[:length] * (1.0 + scale[1:2])
    low = spread[length:] * (1.0 + scale[2:3])
    extra = jnp.concatenate([shift[1:3], jnp.zeros((EXTRA_ROWS - 2, shift.shape[1]), jnp.float32)], axis=0)
    rows = jnp.concatenate([top, low, extra], axis=0).astype(jnp.bfloat16)
    row_id = lax.broadcasted_iota(jnp.int32, (EXTRA_ROWS, unit), 0)
    for part in range(3):
        result[...] = dot32(rows, weight[part])
        cols = pl.ds(part * unit, unit)
        for half, goal in enumerate((kept, sent)):
            tail = jnp.zeros((EXTRA_ROWS, unit), jnp.float32)
            for place in range(groups // 2):
                slot = 2 * place + half if stride == 1 else 2 * half + place
                at = at_block(jnp.bitwise_xor(mine, slot), unit)
                goal[pl.ds(place * tokens, tokens), cols] = result[pl.ds(0, tokens), at].astype(jnp.bfloat16)
                for level in range(2):
                    row = 4 * place + level
                    tail = jnp.where(row_id == row, result[pl.ds(tokens + level, 1), at], tail)
                    sums = squares[0:1, level * length : (level + 1) * length]
                    tail = jnp.where(row_id == row + 2, sums, tail)
            goal[pl.ds(2 * tokens, EXTRA_ROWS), cols] = tail.astype(jnp.bfloat16)


def qkv_kernel(seq, core, mine, levels, joined, swapped, noise, mods, weight_a, weight_b, latent, *refs):
    chunks, (values, noises, result) = refs[:4], refs[4:]
    length, cols = values.shape[0], joined.shape[1]
    own = latent.shape[0]
    tokens = 2 * length
    left, right = at_block(core[0], cols), at_block(1 - core[0], cols)
    values[:, left] = joined[pl.ds(0, length), :]
    values[:, right] = swapped[pl.ds(0, length), :]
    latent[...] = values[at_block(seq[0], own), :]
    noises[at_block(seq[0], own), :] = noise[...]
    theirs = at_block(1 - seq[0], own)
    noises[theirs, left] = joined[pl.ds(length, own), :]
    noises[theirs, right] = swapped[pl.ds(length, own), :]
    spread = values[...].astype(jnp.float32)
    noise_rows = noises[...].astype(jnp.float32)
    mixed = jnp.concatenate(
        [(1.0 - levels[level]) * spread + levels[level] * noise_rows for level in range(2)], axis=0
    ).astype(jnp.bfloat16)
    wide = mixed.astype(jnp.float32)
    sums = jnp.sum(wide * wide, axis=1, keepdims=True)
    sums = jnp.broadcast_to(sums, (tokens, length)).T[0:8]
    for index, weight in enumerate((weight_a, weight_b)):
        project(index, index + 1, mine[0], mixed, sums, mods, weight, *chunks[2 * index : 2 * index + 2], result)


def qkv_part(seq, core, mine, levels, joined, swapped, noise, mods, weight_a, weight_b):
    own, width = noise.shape
    length = joined.shape[0] - own
    tokens = 2 * length
    cols = weight_a.shape[2]
    return pl.pallas_call(
        qkv_kernel,
        in_specs=[smem_spec()] * 4 + [vmem_spec()] * 6,
        out_specs=[vmem_spec()] * 5,
        out_shape=[jax.ShapeDtypeStruct((own, width), jnp.bfloat16)]
        + [jax.ShapeDtypeStruct((cols // length // 2 * tokens + EXTRA_ROWS, 3 * length), jnp.bfloat16)] * 4,
        scratch_shapes=[
            pltpu.VMEM((length, width), jnp.bfloat16),
            pltpu.VMEM((length, width), jnp.bfloat16),
            pltpu.VMEM((tokens + EXTRA_ROWS, cols), jnp.float32),
        ],
        compiler_params=params(20),
        name="qkv_part",
    )(seq, core, mine, levels, joined, swapped, noise, mods, weight_a, weight_b)


def attend_kernel(width, kept_a, other_a, kept_b, other_b, gains, out):
    _, _, length, unit = out.shape
    tokens = 2 * length
    for index, (kept, other) in enumerate(((kept_a, other_a), (kept_b, other_b))):
        mixed = kept[pl.ds(0, tokens), :] + other[pl.ds(0, tokens), :].astype(jnp.float32)
        theirs = other[pl.ds(tokens, EXTRA_ROWS), :].astype(jnp.float32)
        extra = kept[pl.ds(2 * tokens, EXTRA_ROWS), :][0:4] + theirs[4:8]
        for level in range(2):
            rows_at = slice(level * length, (level + 1) * length)
            squares = jnp.broadcast_to(extra[2 + level : 3 + level, :unit], (unit, unit)).T
            factor = lax.rsqrt(squares * (1.0 / width) + 1e-06)

            def pick(part):
                cols = slice(part * unit, (part + 1) * unit)
                return mixed[rows_at, cols] * factor + extra[level : level + 1, cols]

            def normed(part):
                rows = pick(part)
                mean = jnp.mean(rows * rows, axis=1, keepdims=True)
                return (rows * lax.rsqrt(mean + 1e-06) * gains[index, part : part + 1, :]).astype(jnp.bfloat16)

            query, key = normed(0), normed(1)
            value = pick(2).astype(jnp.bfloat16)
            logits = lax.dot_general(
                query, key, (((1,), (1,)), ((), ())), preferred_element_type=jnp.float32
            ) * (1.0 / math.sqrt(unit))
            expanded = jnp.exp(logits)
            probs = (expanded / jnp.sum(expanded, axis=1, keepdims=True)).astype(jnp.bfloat16)
            out[index, level] = dot32(probs, value).astype(jnp.bfloat16)


def attend_part(kept_a, other_a, kept_b, other_b, gains, width):
    unit = kept_a.shape[1] // 3
    length = (kept_a.shape[0] - EXTRA_ROWS) // 4
    return pl.pallas_call(
        lambda *refs: attend_kernel(width, *refs),
        in_specs=[vmem_spec()] * 5,
        out_specs=vmem_spec(),
        out_shape=jax.ShapeDtypeStruct((2, 2, length, unit), jnp.bfloat16),
        compiler_params=params(8),
        name="attend_part",
    )(kept_a, other_a, kept_b, other_b, gains)


def out_kernel(core, mine, *refs):
    heads = refs[0:4]
    weight_a, weight_b, mods, kept, sent, rows, total = refs[4:]
    _, _, length, unit = heads[0].shape
    for index, weight in enumerate((weight_a, weight_b)):
        for slot, head in enumerate(heads):
            at = at_block(jnp.bitwise_xor(mine[0], slot), unit)
            for level in range(2):
                rows[pl.ds(level * length, length), at] = head[index, level]
        result = dot32(rows[...], weight[...])
        gates = mods[index, 2]
        signed = gates[1:2] * result[:length] + gates[2:3] * result[length:]
        if index == 0:
            total[...] = -0.5 * signed
        else:
            total[...] = total[...] + 0.5 * signed
    cols = kept.shape[1]
    kept[...] = total[:, at_block(core[0], cols)]
    sent[...] = total[:, at_block(1 - core[0], cols)].astype(jnp.bfloat16)


def out_part(core, mine, heads, weight_a, weight_b, mods):
    length = heads[0].shape[2]
    depth, width = weight_a.shape
    return pl.pallas_call(
        out_kernel,
        in_specs=[smem_spec()] * 2 + [vmem_spec()] * 7,
        out_specs=[vmem_spec()] * 2,
        out_shape=[
            jax.ShapeDtypeStruct((length, width // 2), jnp.float32),
            jax.ShapeDtypeStruct((length, width // 2), jnp.bfloat16),
        ],
        scratch_shapes=[
            pltpu.VMEM((2 * length, depth), jnp.bfloat16),
            pltpu.VMEM((length, width), jnp.float32),
        ],
        compiler_params=params(16),
        name="out_part",
    )(core, mine, *heads, weight_a, weight_b, mods)


def grad_kernel(half, heads_t, rows, *refs):
    refs[-1][...] = dot32(heads_t[...], rows[...]).astype(jnp.bfloat16)


def grad_part(half, heads_t, rows, before, steps):
    depth, length = heads_t.shape
    cols = rows.shape[1]
    tile = depth // steps
    rest = [] if before is None else [before]
    grid_spec = pltpu.PrefetchScalarGridSpec(
        num_scalar_prefetch=1,
        grid=(steps,),
        in_specs=[
            pl.BlockSpec((tile, length), lambda n, w: (n, 0)),
            pl.BlockSpec((length, cols), lambda n, w: (0, 0)),
        ]
        + [any_spec()] * len(rest),
        out_specs=pl.BlockSpec((tile, cols), lambda n, w: (n, w[0])),
    )
    return pl.pallas_call(
        grad_kernel,
        grid_spec=grid_spec,
        out_shape=jax.ShapeDtypeStruct((depth, 2 * cols), jnp.bfloat16),
        input_output_aliases={3: 0} if rest else {},
        compiler_params=params(16),
        name="grad_part",
    )(half, heads_t, rows, *rest)


def exchange(array, axis, bit):
    return lax.ppermute(array, axis, [(i, i ^ bit) for i in range(lax.axis_size(axis))])


def take(array, begin, size, axis):
    return lax.dynamic_slice_in_dim(array, begin, size, axis=axis, allow_negative_indices=False)


def both(mine, theirs):
    return mine.astype(jnp.float32) + theirs.astype(jnp.float32)


def heads_per_role(
    gen_heads,
    gen_resid,
    gen_out_w,
    gen_time_w,
    noise,
    steps,
    teacher_qkv,
    teacher_out,
    teacher_time,
    teacher_norm,
    critic_qkv,
    critic_out,
    critic_time,
    critic_norm,
):
    length = gen_heads.shape[0]
    roles, groups = lax.axis_size("role"), lax.axis_size("mp")
    role, seq, mp = lax.axis_index("role"), lax.axis_index("seq"), lax.axis_index("mp")
    part_cols = gen_heads.shape[1] // roles
    freq = gen_time_w.shape[0]
    core = role % 2
    half_cols = gen_resid.shape[1] // 2
    unit = part_cols // groups

    embed = jax.vmap(lambda t: time_embed(t, freq))(steps)
    embed = jnp.concatenate([embed, jnp.zeros((5, freq), jnp.bfloat16)], axis=0)
    levels = steps[1:3].astype(jnp.float32) / 1000.0
    start = role * part_cols
    scalars = [seq, mp, core, 1 - core, core * half_cols, start, start + mp * unit]
    embed, *scalars = lax.optimization_barrier((embed, *scalars))
    seq_at, mine, core, other_core, start_at = [v.astype(jnp.int32).reshape(1) for v in scalars[:4] + scalars[5:6]]
    begin, start, gain_at = scalars[4:]
    weight, time_half, resid_half, noise_half = [
        take(w, begin, half_cols, 1) for w in (gen_out_w, gen_time_w, gen_resid, noise)
    ]
    gate = dot32(embed, time_half)
    full, sent = pack_part(seq_at, dot32(gen_heads, weight), gate, resid_half, noise_half)
    arrived = exchange(sent, "seq", 1)
    later, embed, _ = lax.optimization_barrier((start_at, embed, full))
    planes = [w.transpose(1, 0, 2) for w in (teacher_qkv, critic_qkv, teacher_time, critic_time)]
    weight_a, weight_b, mods = load_part(later, embed, planes[2], planes[3], planes[0], planes[1], part_cols)
    arrived, mods = lax.optimization_barrier((arrived, mods))
    joined = join_part(full, arrived)
    swapped = exchange(joined, "role", 1)

    latent, kept_a, sent_a, kept_b, sent_b = qkv_part(
        seq_at, core, mine, levels, joined, swapped, noise, mods, weight_a, weight_b
    )
    arrived_b = exchange(sent_b, "mp", 2)
    arrived_a = exchange(sent_a, "mp", 1)
    out_a, out_b = [take(w, start, part_cols, 0) for w in (teacher_out, critic_out)]
    gains = jnp.stack([teacher_norm, critic_norm])
    gains = take(gains, gain_at, unit, 2)
    arrived_b, arrived_a, out_a, out_b, gains = lax.optimization_barrier((arrived_b, arrived_a, out_a, out_b, gains))
    sum_a, sum_b = both(kept_a, arrived_a), both(kept_b, arrived_b)
    second = (sum_a.shape[0] - EXTRA_ROWS) // 2
    last_a = exchange(sum_a[second:].astype(jnp.bfloat16), "mp", 2)
    last_b = exchange(sum_b[second:].astype(jnp.bfloat16), "mp", 1)
    head = attend_part(sum_a, last_a, sum_b, last_b, gains, D)
    near, far = exchange(head, "mp", 1), exchange(head, "mp", 2)
    gathered = head, near, far, exchange(far, "mp", 1)

    kept, sent = out_part(core, mine, gathered, out_a, out_b, mods)
    total = both(kept, exchange(sent, "role", 1)).astype(jnp.bfloat16)
    along_x = exchange(total, "seq", 1)
    along_y = exchange(total, "role", 2)
    across = lax.ppermute(
        total, ("role", "seq"), [(i, i ^ (2 * lax.axis_size("seq") + 1)) for i in range(roles * lax.axis_size("seq"))]
    )
    total = both(total, along_x) + both(along_y, across)
    rows = (gate[0:1] * total).astype(jnp.bfloat16)
    heads_t = gen_heads.T
    theirs = exchange(rows, "role", 1)
    weight_grad = grad_part(core, heads_t, rows, None, 1)
    weight_grad = grad_part(other_core, heads_t, theirs, weight_grad, 1)
    return latent, weight_grad


def solution(mesh):
    in_specs = (
        P(None, "seq"),
        P("seq", "mp"),
        P("seq", "mp"),
        P(None, "mp"),
        P("seq", "mp"),
        P(),
        P("mp", None, "seq"),
        P("seq", "mp"),
        P(None, None, "mp"),
        P(None, "seq"),
        P("mp", None, "seq"),
        P("seq", "mp"),
        P(None, None, "mp"),
        P(None, "seq"),
    )
    out_specs = (P("seq", "mp"), P("seq", "mp"))
    roles, seqs, groups = mesh.shape["role"], mesh.shape["seq"], mesh.shape["mp"]

    def on_device(*arrays):
        heads_here = arrays[0].shape[1] // HEAD_DIM
        length = arrays[0].shape[0]
        fits = (roles, seqs, groups) == (4, 2, 4) and heads_here == roles * groups and length == HEAD_DIM
        return heads_per_role(*arrays) if fits else pass_per_role(*arrays)

    return jax.shard_map(
        on_device, mesh=mesh, in_specs=in_specs, out_specs=out_specs, check_vma=False
    )
```

```python
import math

import jax
import jax.numpy as jnp
from jax import lax
from jax.experimental import pallas as pl
from jax.experimental.pallas import tpu as pltpu
from jax.sharding import PartitionSpec as P

D = 5120
HEAD_DIM = 128


def time_embed(step_value, width):
    half_width = width // 2
    positions = jnp.arange(half_width, dtype=jnp.float32)
    frequencies = jnp.exp(positions * (-math.log(10000.0) / half_width))
    angles = step_value.astype(jnp.float32) * frequencies
    return jnp.concatenate([jnp.cos(angles), jnp.sin(angles)]).astype(jnp.bfloat16)


def head_norm(values, gains):
    factor = lax.rsqrt(jnp.mean(values * values, axis=-1, keepdims=True) + 1e-06)
    return (values * factor * gains).astype(jnp.bfloat16)


def attend(query_norm, key_norm, value_rows):
    full_length, heads_here, head_width = query_norm.shape
    query_blocks = query_norm.reshape(
        full_length // full_length, full_length, heads_here, head_width
    )

    def one_block(query_block):
        logits = jnp.einsum(
            "qhd,khd->hqk", query_block, key_norm, preferred_element_type=jnp.float32
        ) * (1.0 / math.sqrt(head_width))
        expanded = jnp.exp(logits)
        probs = (expanded / jnp.sum(expanded, axis=2, keepdims=True)).astype(jnp.bfloat16)
        return jnp.einsum(
            "hqk,khd->qhd", probs, value_rows, preferred_element_type=jnp.float32
        ).astype(jnp.bfloat16)

    head_out = lax.map(one_block, query_blocks)
    return head_out.reshape(full_length, heads_here * head_width)


def pass_per_role(
    gen_heads,
    gen_resid,
    gen_out_w,
    gen_time_w,
    noise,
    steps,
    teacher_qkv,
    teacher_out,
    teacher_time,
    teacher_norm,
    critic_qkv,
    critic_out,
    critic_time,
    critic_norm,
):
    full_length = gen_heads.shape[0]
    head_cols = gen_heads.shape[1]
    embed_width = gen_time_w.shape[0]
    gen_gate = jnp.dot(
        time_embed(steps[0], embed_width)[None, :], gen_time_w, preferred_element_type=jnp.float32
    )[0]
    block = gen_heads
    gen_proj = lax.psum_scatter(
        jnp.dot(block, gen_out_w, preferred_element_type=jnp.float32),
        "seq",
        scatter_dimension=0,
        tiled=True,
    )
    latent = (gen_resid.astype(jnp.float32) + gen_gate * gen_proj).astype(jnp.bfloat16)
    role_index = lax.axis_index("role")
    level = steps[1 + role_index // 2]
    use_critic = role_index % 2 == 1
    w_qkv = jnp.where(use_critic, critic_qkv, teacher_qkv)
    w_out = jnp.where(use_critic, critic_out, teacher_out)
    w_time = jnp.where(use_critic, critic_time, teacher_time)
    w_norm = jnp.where(use_critic, critic_norm, teacher_norm)
    noise_level = level.astype(jnp.float32) / 1000.0
    noisy = (
        (1.0 - noise_level) * latent.astype(jnp.float32) + noise_level * noise.astype(jnp.float32)
    ).astype(jnp.bfloat16)
    modulation = jnp.einsum(
        "f,fkd->kd", time_embed(level, embed_width), w_time, preferred_element_type=jnp.float32
    )
    shift_vec = modulation[0]
    scale_vec = modulation[1]
    gate_vec = modulation[2]
    gathered = lax.all_gather(noisy, "seq", axis=0, tiled=True)
    partial_squares = jnp.sum(jnp.square(gathered.astype(jnp.float32)), axis=1)
    scaled = (gathered.astype(jnp.float32) * (1.0 + scale_vec)).astype(jnp.bfloat16)
    flat_w = w_qkv.reshape(w_qkv.shape[0], 3 * head_cols)
    projected = jnp.dot(scaled, flat_w, preferred_element_type=jnp.float32)
    shift_proj = jnp.dot(
        shift_vec.astype(jnp.bfloat16)[None, :], flat_w, preferred_element_type=jnp.float32
    )[0]
    projected, squares, shift_proj = lax.psum((projected, partial_squares, shift_proj), "mp")
    mixed = projected * lax.rsqrt(squares / D + 1e-06)[:, None] + shift_proj
    heads_here = head_cols // HEAD_DIM
    mixed = mixed.reshape(full_length, 3, heads_here, HEAD_DIM)
    gains = w_norm.reshape(2, heads_here, HEAD_DIM)
    query_norm = head_norm(mixed[:, 0], gains[0])
    key_norm = head_norm(mixed[:, 1], gains[1])
    value_rows = mixed[:, 2].astype(jnp.bfloat16)
    head_out = attend(query_norm, key_norm, value_rows)
    weight_sign = jnp.where(use_critic, 0.5, -0.5)
    block = head_out
    summed_rows = lax.psum_scatter(
        weight_sign * (gate_vec * jnp.dot(block, w_out, preferred_element_type=jnp.float32)),
        ("role", "seq"),
        scatter_dimension=0,
        tiled=True,
    )
    grad_rows = lax.all_gather(
        (gen_gate * summed_rows).astype(jnp.bfloat16), ("role", "seq"), axis=0, tiled=True
    )
    weight_grad = lax.dot_general(
        gen_heads, grad_rows, (((0,), (0,)), ((), ())), preferred_element_type=jnp.float32
    )
    return (latent, weight_grad.astype(jnp.bfloat16))

MIB = 1024 * 1024
EXTRA_ROWS = 16


def vmem_spec():
    return pl.BlockSpec(memory_space=pltpu.VMEM)


def smem_spec():
    return pl.BlockSpec(memory_space=pltpu.SMEM)


def params(mebibytes):
    return pltpu.CompilerParams(vmem_limit_bytes=mebibytes * MIB)


def dot32(a, b):
    return jnp.dot(a, b, preferred_element_type=jnp.float32)


def at_block(index, size):
    return pl.ds(pl.multiple_of(index * size, size), size)


def any_spec():
    return pl.BlockSpec(memory_space=pl.ANY)


def hbm_spec():
    return pl.BlockSpec(memory_space=pltpu.HBM)


def cost(flops, moved):
    return pl.CostEstimate(flops=flops, bytes_accessed=moved, transcendentals=0)


def pack_kernel(seq, product, gate, resid, noise, full, sent):
    length = full.shape[0]
    own = resid.shape[0]
    full[...] = product[...] * gate[0:1, :]
    at = at_block(seq[0], own)
    full[at, :] = full[at, :] + resid[...].astype(jnp.float32)
    sent[pl.ds(0, length), :] = full[...].astype(jnp.bfloat16)
    sent[pl.ds(length, own), :] = noise[...]


def pack_part(seq, product, gate, resid, noise):
    length, width = product.shape
    own = resid.shape[0]
    return pl.pallas_call(
        pack_kernel,
        in_specs=[smem_spec()] + [vmem_spec()] * 4,
        out_specs=[vmem_spec()] * 2,
        out_shape=[
            jax.ShapeDtypeStruct((length, width), jnp.float32),
            jax.ShapeDtypeStruct((length + own, width), jnp.bfloat16),
        ],
        compiler_params=params(8),
        name="pack_part",
    )(seq, product, gate, resid, noise)


def load_kernel(start, embed, time_a, time_b, planes_a, planes_b, weight_a, weight_b, mods, sems):
    cols = pl.ds(pl.multiple_of(start[0], weight_a.shape[2]), weight_a.shape[2])
    copies = []
    for index, (planes, weight) in enumerate(((planes_a, weight_a), (planes_b, weight_b))):
        for part in range(3):
            copies.append(
                pltpu.make_async_copy(planes.at[part, :, cols], weight.at[part], sems.at[3 * index + part])
            )
    for copy in copies:
        copy.start()
    for k in range(3):
        mods[0, k] = dot32(embed[...], time_a[k])
        mods[1, k] = dot32(embed[...], time_b[k])
    for copy in copies:
        copy.wait()


def load_part(start, embed, time_a, time_b, planes_a, planes_b, cols):
    parts, depth, _ = planes_a.shape
    width = time_a.shape[2]
    return pl.pallas_call(
        load_kernel,
        in_specs=[smem_spec()] + [vmem_spec()] * 3 + [hbm_spec()] * 2,
        out_specs=[vmem_spec()] * 3,
        out_shape=[jax.ShapeDtypeStruct((parts, depth, cols), jnp.bfloat16)] * 2
        + [jax.ShapeDtypeStruct((2, parts, 8, width), jnp.float32)],
        scratch_shapes=[pltpu.SemaphoreType.DMA((2 * parts,))],
        compiler_params=params(40),
        name="load_part",
    )(start, embed, time_a, time_b, planes_a, planes_b)


def join_kernel(full, arrived, joined):
    length = full.shape[0]
    own = arrived.shape[0] - length
    top = full[...] + arrived[pl.ds(0, length), :].astype(jnp.float32)
    joined[pl.ds(0, length), :] = top.astype(jnp.bfloat16)
    joined[pl.ds(length, own), :] = arrived[pl.ds(length, own), :]


def join_part(full, arrived):
    return pl.pallas_call(
        join_kernel,
        in_specs=[vmem_spec(), vmem_spec()],
        out_specs=vmem_spec(),
        out_shape=jax.ShapeDtypeStruct(arrived.shape, jnp.bfloat16),
        compiler_params=params(8),
        name="join_part",
    )(full, arrived)


def project(index, stride, mine, noisy, squares, mods, weight, kept, sent, result):
    tokens = noisy.shape[0]
    length = tokens // 2
    unit = squares.shape[1] // 2
    groups = weight.shape[2] // unit
    scale = mods[index, 1]
    shift = mods[index, 0]
    spread = noisy.astype(jnp.float32)
    top = spread[:length] * (1.0 + scale[1:2])
    low = spread[length:] * (1.0 + scale[2:3])
    extra = jnp.concatenate([shift[1:3], jnp.zeros((EXTRA_ROWS - 2, shift.shape[1]), jnp.float32)], axis=0)
    rows = jnp.concatenate([top, low, extra], axis=0).astype(jnp.bfloat16)
    row_id = lax.broadcasted_iota(jnp.int32, (EXTRA_ROWS, unit), 0)
    for part in range(3):
        result[...] = dot32(rows, weight[part])
        cols = pl.ds(part * unit, unit)
        for half, goal in enumerate((kept, sent)):
            tail = jnp.zeros((EXTRA_ROWS, unit), jnp.float32)
            for place in range(groups // 2):
                slot = 2 * place + half if stride == 1 else 2 * half + place
                at = at_block(jnp.bitwise_xor(mine, slot), unit)
                goal[pl.ds(place * tokens, tokens), cols] = result[pl.ds(0, tokens), at].astype(jnp.bfloat16)
                for level in range(2):
                    row = 4 * place + level
                    tail = jnp.where(row_id == row, result[pl.ds(tokens + level, 1), at], tail)
                    sums = squares[0:1, level * length : (level + 1) * length]
                    tail = jnp.where(row_id == row + 2, sums, tail)
            goal[pl.ds(2 * tokens, EXTRA_ROWS), cols] = tail.astype(jnp.bfloat16)


def qkv_kernel(seq, core, mine, levels, joined, swapped, noise, mods, weight_a, weight_b, latent, *refs):
    chunks, (values, noises, result) = refs[:4], refs[4:]
    length, cols = values.shape[0], joined.shape[1]
    own = latent.shape[0]
    tokens = 2 * length
    left, right = at_block(core[0], cols), at_block(1 - core[0], cols)
    values[:, left] = joined[pl.ds(0, length), :]
    values[:, right] = swapped[pl.ds(0, length), :]
    latent[...] = values[at_block(seq[0], own), :]
    noises[at_block(seq[0], own), :] = noise[...]
    theirs = at_block(1 - seq[0], own)
    noises[theirs, left] = joined[pl.ds(length, own), :]
    noises[theirs, right] = swapped[pl.ds(length, own), :]
    spread = values[...].astype(jnp.float32)
    noise_rows = noises[...].astype(jnp.float32)
    mixed = jnp.concatenate(
        [(1.0 - levels[level]) * spread + levels[level] * noise_rows for level in range(2)], axis=0
    ).astype(jnp.bfloat16)
    wide = mixed.astype(jnp.float32)
    sums = jnp.sum(wide * wide, axis=1, keepdims=True)
    sums = jnp.broadcast_to(sums, (tokens, length)).T[0:8]
    for index, weight in enumerate((weight_a, weight_b)):
        project(index, index + 1, mine[0], mixed, sums, mods, weight, *chunks[2 * index : 2 * index + 2], result)


def qkv_part(seq, core, mine, levels, joined, swapped, noise, mods, weight_a, weight_b):
    own, width = noise.shape
    length = joined.shape[0] - own
    tokens = 2 * length
    cols = weight_a.shape[2]
    return pl.pallas_call(
        qkv_kernel,
        in_specs=[smem_spec()] * 4 + [vmem_spec()] * 6,
        out_specs=[vmem_spec()] * 5,
        out_shape=[jax.ShapeDtypeStruct((own, width), jnp.bfloat16)]
        + [jax.ShapeDtypeStruct((cols // length // 2 * tokens + EXTRA_ROWS, 3 * length), jnp.bfloat16)] * 4,
        scratch_shapes=[
            pltpu.VMEM((length, width), jnp.bfloat16),
            pltpu.VMEM((length, width), jnp.bfloat16),
            pltpu.VMEM((tokens + EXTRA_ROWS, cols), jnp.float32),
        ],
        compiler_params=params(20),
        name="qkv_part",
    )(seq, core, mine, levels, joined, swapped, noise, mods, weight_a, weight_b)


def attend_kernel(width, kept_a, other_a, kept_b, other_b, gains, out):
    _, _, length, unit = out.shape
    tokens = 2 * length
    for index, (kept, other) in enumerate(((kept_a, other_a), (kept_b, other_b))):
        mixed = kept[pl.ds(0, tokens), :] + other[pl.ds(0, tokens), :].astype(jnp.float32)
        theirs = other[pl.ds(tokens, EXTRA_ROWS), :].astype(jnp.float32)
        extra = kept[pl.ds(2 * tokens, EXTRA_ROWS), :][0:4] + theirs[4:8]
        for level in range(2):
            rows_at = slice(level * length, (level + 1) * length)
            squares = jnp.broadcast_to(extra[2 + level : 3 + level, :unit], (unit, unit)).T
            factor = lax.rsqrt(squares * (1.0 / width) + 1e-06)

            def pick(part):
                cols = slice(part * unit, (part + 1) * unit)
                return mixed[rows_at, cols] * factor + extra[level : level + 1, cols]

            def normed(part):
                rows = pick(part)
                mean = jnp.mean(rows * rows, axis=1, keepdims=True)
                return (rows * lax.rsqrt(mean + 1e-06) * gains[index, part : part + 1, :]).astype(jnp.bfloat16)

            query, key = normed(0), normed(1)
            value = pick(2).astype(jnp.bfloat16)
            logits = lax.dot_general(
                query, key, (((1,), (1,)), ((), ())), preferred_element_type=jnp.float32
            ) * (1.0 / math.sqrt(unit))
            expanded = jnp.exp(logits)
            probs = (expanded / jnp.sum(expanded, axis=1, keepdims=True)).astype(jnp.bfloat16)
            out[index, level] = dot32(probs, value).astype(jnp.bfloat16)


def attend_part(kept_a, other_a, kept_b, other_b, gains, width):
    unit = kept_a.shape[1] // 3
    length = (kept_a.shape[0] - EXTRA_ROWS) // 4
    return pl.pallas_call(
        lambda *refs: attend_kernel(width, *refs),
        in_specs=[vmem_spec()] * 5,
        out_specs=vmem_spec(),
        out_shape=jax.ShapeDtypeStruct((2, 2, length, unit), jnp.bfloat16),
        compiler_params=params(8),
        name="attend_part",
    )(kept_a, other_a, kept_b, other_b, gains)


def out_kernel(core, mine, *refs):
    heads = refs[0:4]
    weight_a, weight_b, mods, kept, sent, rows, total = refs[4:]
    _, _, length, unit = heads[0].shape
    for index, weight in enumerate((weight_a, weight_b)):
        for slot, head in enumerate(heads):
            at = at_block(jnp.bitwise_xor(mine[0], slot), unit)
            for level in range(2):
                rows[pl.ds(level * length, length), at] = head[index, level]
        result = dot32(rows[...], weight[...])
        gates = mods[index, 2]
        signed = gates[1:2] * result[:length] + gates[2:3] * result[length:]
        if index == 0:
            total[...] = -0.5 * signed
        else:
            total[...] = total[...] + 0.5 * signed
    cols = kept.shape[1]
    kept[...] = total[:, at_block(core[0], cols)]
    sent[...] = total[:, at_block(1 - core[0], cols)].astype(jnp.bfloat16)


def out_part(core, mine, heads, weight_a, weight_b, mods):
    length = heads[0].shape[2]
    depth, width = weight_a.shape
    return pl.pallas_call(
        out_kernel,
        in_specs=[smem_spec()] * 2 + [vmem_spec()] * 7,
        out_specs=[vmem_spec()] * 2,
        out_shape=[
            jax.ShapeDtypeStruct((length, width // 2), jnp.float32),
            jax.ShapeDtypeStruct((length, width // 2), jnp.bfloat16),
        ],
        scratch_shapes=[
            pltpu.VMEM((2 * length, depth), jnp.bfloat16),
            pltpu.VMEM((length, width), jnp.float32),
        ],
        compiler_params=params(16),
        name="out_part",
    )(core, mine, *heads, weight_a, weight_b, mods)


def grad_kernel(half, heads_t, rows, *refs):
    refs[-1][...] = dot32(heads_t[...], rows[...]).astype(jnp.bfloat16)


def grad_part(half, heads_t, rows, before, steps):
    depth, length = heads_t.shape
    cols = rows.shape[1]
    tile = depth // steps
    rest = [] if before is None else [before]
    grid_spec = pltpu.PrefetchScalarGridSpec(
        num_scalar_prefetch=1,
        grid=(steps,),
        in_specs=[
            pl.BlockSpec((tile, length), lambda n, w: (n, 0)),
            pl.BlockSpec((length, cols), lambda n, w: (0, 0)),
        ]
        + [any_spec()] * len(rest),
        out_specs=pl.BlockSpec((tile, cols), lambda n, w: (n, w[0])),
    )
    return pl.pallas_call(
        grad_kernel,
        grid_spec=grid_spec,
        out_shape=jax.ShapeDtypeStruct((depth, 2 * cols), jnp.bfloat16),
        input_output_aliases={3: 0} if rest else {},
        compiler_params=params(16),
        name="grad_part",
    )(half, heads_t, rows, *rest)


def exchange(array, axis, bit):
    return lax.ppermute(array, axis, [(i, i ^ bit) for i in range(lax.axis_size(axis))])


def take(array, begin, size, axis):
    return lax.dynamic_slice_in_dim(array, begin, size, axis=axis, allow_negative_indices=False)


def both(mine, theirs):
    return mine.astype(jnp.float32) + theirs.astype(jnp.float32)


def heads_per_role(
    gen_heads,
    gen_resid,
    gen_out_w,
    gen_time_w,
    noise,
    steps,
    teacher_qkv,
    teacher_out,
    teacher_time,
    teacher_norm,
    critic_qkv,
    critic_out,
    critic_time,
    critic_norm,
):
    length = gen_heads.shape[0]
    roles, groups = lax.axis_size("role"), lax.axis_size("mp")
    role, seq, mp = lax.axis_index("role"), lax.axis_index("seq"), lax.axis_index("mp")
    part_cols = gen_heads.shape[1] // roles
    freq = gen_time_w.shape[0]
    core = role % 2
    half_cols = gen_resid.shape[1] // 2
    unit = part_cols // groups

    embed = jax.vmap(lambda t: time_embed(t, freq))(steps)
    embed = jnp.concatenate([embed, jnp.zeros((5, freq), jnp.bfloat16)], axis=0)
    levels = steps[1:3].astype(jnp.float32) / 1000.0
    start = role * part_cols
    scalars = [seq, mp, core, 1 - core, core * half_cols, start, start + mp * unit]
    embed, *scalars = lax.optimization_barrier((embed, *scalars))
    seq_at, mine, core, other_core, start_at = [v.astype(jnp.int32).reshape(1) for v in scalars[:4] + scalars[5:6]]
    begin, start, gain_at = scalars[4:]
    weight, time_half, resid_half, noise_half = [
        take(w, begin, half_cols, 1) for w in (gen_out_w, gen_time_w, gen_resid, noise)
    ]
    gate = dot32(embed, time_half)
    full, sent = pack_part(seq_at, dot32(gen_heads, weight), gate, resid_half, noise_half)
    arrived = exchange(sent, "seq", 1)
    later, embed, _ = lax.optimization_barrier((start_at, embed, full))
    planes = [w.transpose(1, 0, 2) for w in (teacher_qkv, critic_qkv, teacher_time, critic_time)]
    weight_a, weight_b, mods = load_part(later, embed, planes[2], planes[3], planes[0], planes[1], part_cols)
    arrived, mods = lax.optimization_barrier((arrived, mods))
    joined = join_part(full, arrived)
    swapped = exchange(joined, "role", 1)

    latent, kept_a, sent_a, kept_b, sent_b = qkv_part(
        seq_at, core, mine, levels, joined, swapped, noise, mods, weight_a, weight_b
    )
    arrived_b = exchange(sent_b, "mp", 2)
    arrived_a = exchange(sent_a, "mp", 1)
    out_a, out_b = [take(w, start, part_cols, 0) for w in (teacher_out, critic_out)]
    gains = jnp.stack([teacher_norm, critic_norm])
    gains = take(gains, gain_at, unit, 2)
    arrived_b, arrived_a, out_a, out_b, gains = lax.optimization_barrier((arrived_b, arrived_a, out_a, out_b, gains))
    sum_a, sum_b = both(kept_a, arrived_a), both(kept_b, arrived_b)
    second = (sum_a.shape[0] - EXTRA_ROWS) // 2
    last_a = exchange(sum_a[second:].astype(jnp.bfloat16), "mp", 2)
    last_b = exchange(sum_b[second:].astype(jnp.bfloat16), "mp", 1)
    head = attend_part(sum_a, last_a, sum_b, last_b, gains, D)
    near, far = exchange(head, "mp", 1), exchange(head, "mp", 2)
    gathered = head, near, far, exchange(far, "mp", 1)

    kept, sent = out_part(core, mine, gathered, out_a, out_b, mods)
    total = both(kept, exchange(sent, "role", 1)).astype(jnp.bfloat16)
    along_x = exchange(total, "seq", 1)
    along_y = exchange(total, "role", 2)
    across = lax.ppermute(
        total, ("role", "seq"), [(i, i ^ (2 * lax.axis_size("seq") + 1)) for i in range(roles * lax.axis_size("seq"))]
    )
    total = both(total, along_x) + both(along_y, across)
    rows = (gate[0:1] * total).astype(jnp.bfloat16)
    heads_t = gen_heads.T
    theirs = exchange(rows, "role", 1)
    weight_grad = grad_part(core, heads_t, rows, None, 2)
    weight_grad = grad_part(other_core, heads_t, theirs, weight_grad, 4)
    return latent, weight_grad


def solution(mesh):
    in_specs = (
        P(None, "seq"),
        P("seq", "mp"),
        P("seq", "mp"),
        P(None, "mp"),
        P("seq", "mp"),
        P(),
        P("mp", None, "seq"),
        P("seq", "mp"),
        P(None, None, "mp"),
        P(None, "seq"),
        P("mp", None, "seq"),
        P("seq", "mp"),
        P(None, None, "mp"),
        P(None, "seq"),
    )
    out_specs = (P("seq", "mp"), P("seq", "mp"))
    roles, seqs, groups = mesh.shape["role"], mesh.shape["seq"], mesh.shape["mp"]

    def on_device(*arrays):
        heads_here = arrays[0].shape[1] // HEAD_DIM
        length = arrays[0].shape[0]
        fits = (roles, seqs, groups) == (4, 2, 4) and heads_here == roles * groups and length == HEAD_DIM
        return heads_per_role(*arrays) if fits else pass_per_role(*arrays)

    return jax.shard_map(
        on_device, mesh=mesh, in_specs=in_specs, out_specs=out_specs, check_vma=False
    )
```
